32 devices in a mesh: blk: 8 (over z, x), head: 4 (over y, core).
Axes of the slice: x: 2, y: 2, z: 4, core: 2. Of those that a mesh axis runs over, the one named last changes fastest.
Arguments:
- inputs: bfloat16 [2, 2048, 1024], P(None, ('blk', 'head')), may hold values from -6 to 6
- cotangent: bfloat16 [2, 2048, 1024], P(None, ('blk', 'head')), may hold values from -6 to 6
- doc_starts: int32 [2, 2], replicated, may hold values from 1 to 2047, as said below
- norm_one: bfloat16 [1024], P(('blk', 'head')), may hold values from 0.5 to 1.5
- mixer_in: bfloat16 [1024, 3352], P(('blk', 'head')), may hold values from -0.1875 to 0.1875
- conv_weight: float32 [4, 1792], replicated, may hold values from -3 to 3
- conv_bias: float32 [1792], replicated, may hold values from -3 to 3
- dt_bias: float32 [24], replicated, may hold values from -7 to -2.25
- a_log: float32 [24], replicated, may hold values from -1 to 1
- d_skip: float32 [24], replicated, may hold values from 0.5 to 1.5
- ssm_gain: float32 [1536], replicated, may hold values from 0.5 to 1.5
- mixer_out: bfloat16 [1536, 1024], P(None, ('blk', 'head')), may hold values from -0.15625 to 0.15625
- attn_in: bfloat16 [1024, 768], P(('blk', 'head')), may hold values from -0.1875 to 0.1875
- attn_out: bfloat16 [512, 1024], P(None, ('blk', 'head')), may hold values from -0.75 to 0.75
- norm_two: bfloat16 [1024], P(('blk', 'head')), may hold values from 0.5 to 1.5
- ffn_in: bfloat16 [1024, 4096], P(('blk', 'head')), may hold values from -0.1875 to 0.1875
- ffn_out: bfloat16 [2048, 1024], P(None, ('blk', 'head')), may hold values from -0.125 to 0.125
Outputs:
- output: float32 [2, 2048, 1024], P(None, ('blk', 'head'))
- grad_inputs: float32 [2, 2048, 1024], P(None, ('blk', 'head'))
- grad_norm_one: float32 [1024], replicated
- grad_mixer_in: float32 [1024, 3352], P('blk', 'head')
- grad_conv_weight: float32 [4, 1792], replicated
- grad_conv_bias: float32 [1792], replicated
- grad_dt_bias: float32 [24], replicated
- grad_a_log: float32 [24], replicated
- grad_d_skip: float32 [24], replicated
- grad_ssm_gain: float32 [1536], replicated
- grad_mixer_out: float32 [1536, 1024], P('blk', 'head')
- grad_attn_in: float32 [1024, 768], P('blk', 'head')
- grad_attn_out: float32 [512, 1024], P('blk', 'head')
- grad_norm_two: float32 [1024], replicated
- grad_ffn_in: float32 [1024, 4096], P('blk', 'head')
- grad_ffn_out: float32 [2048, 1024], P('blk', 'head')
The draws below stay inside these ranges and needn't reach their ends.
Inputs may be any that keep to these rules, and one draw needn't show every extreme that they name: `doc_starts`: each row is strictly ascending; every document it bounds (from token 0 to the first start, between consecutive starts, from the last start to the end of the 2048 tokens) is at most 1024 tokens long, and one of them is exactly 1024 long.
All inputs are finite; a program needn't handle non-finite values.
Results may differ from the reference program's by a relative error of at most 0.04.
Values may be sent and summed in bfloat16 or wider, within the bound.
A program may use at most 192 MiB of HBM per device.

```python
import jax
import jax.numpy as jnp
from jax import lax

D = 1024
MHEADS = 24
MHDIM = 64
STATE = 128
CONVK = 4
QHEADS = 8
KVHEADS = 2
HDIM = 64
FF = 2048
MB = 2
DI = 1536
EDGE = 256
TOKENS = 2048
MAXDOC = 1024
NDOC = 2
N_HEAD = 4


def draw_doc_starts(key, part):
    key = jax.random.fold_in(key, 11)
    half_len = MAXDOC // 2
    cell_count = TOKENS // half_len
    order = jnp.arange(NDOC, dtype=jnp.int32)
    cell_index = jnp.arange(cell_count, dtype=jnp.int32)
    row_list = []
    for micro_index in range(MB):
        pick_key, offset_key = jax.random.split(jax.random.fold_in(key, micro_index))
        skipped = jax.random.randint(pick_key, (), 1, cell_count - 1, dtype=jnp.int32)
        offsets = jax.random.randint(offset_key, (cell_count,), 0, half_len, dtype=jnp.int32)
        offsets = jnp.where(cell_index == 0, 0, offsets)
        offsets = jnp.where(cell_index == skipped + 1, offsets[skipped - 1], offsets)
        cells = jnp.where(order + 1 < skipped, order + 1, order + 2)
        row_list.append(cells * half_len + offsets[cells])
    return jnp.stack(row_list).astype(jnp.int32)


def shard_levels(stream_key, shape, shards, least, high):
    factor_of = 1.0
    for dim, shards_of in shards:
        heights = jax.random.uniform(jax.random.fold_in(jax.random.fold_in(stream_key, 6), dim), (shards_of,), jnp.float32, least / len(shards), high / len(shards))
        factor_of = factor_of * jnp.repeat(jnp.exp(heights), shape[dim] // shards_of).reshape((-1,) + (1,) * (len(shape) - 1 - dim))
    return factor_of


def bell_draw(own_key, dims, width, limit, shards=(), held_as=jnp.bfloat16):
    factor_of = shard_levels(own_key, dims, shards, -0.22, 0.18) if shards else 1.0
    entries = jax.random.normal(own_key, dims, jnp.float32) * width * factor_of
    return jnp.minimum(jnp.maximum(entries, -limit), limit).astype(held_as)


def setup_inputs(seed: int = 0) -> dict:
    arg_keys = jax.random.split(jax.random.key(seed), 18)
    return {
        "inputs": bell_draw(arg_keys[0], (MB, TOKENS, D), 1.0, 6.0, ((1, 32),)),
        "cotangent": bell_draw(arg_keys[1], (MB, TOKENS, D), 1.0, 6.0, ((1, 32),)),
        "doc_starts": draw_doc_starts(jax.random.fold_in(arg_keys[17], 71), 0),
        "norm_one": jnp.clip(1.0 + 0.1 * jax.random.normal(arg_keys[3], (D,), jnp.float32), 0.5, 1.5).astype(jnp.bfloat16),
        "mixer_in": bell_draw(arg_keys[4], (D, 2 * DI + 2 * STATE + MHEADS), D ** -0.5, 0.1875, ((0, 32),)),
        "conv_weight": bell_draw(arg_keys[5], (CONVK, DI + 2 * STATE), 0.5, 3.0, (), jnp.float32),
        "conv_bias": bell_draw(arg_keys[6], (DI + 2 * STATE,), 0.5, 3.0, (), jnp.float32),
        "dt_bias": jnp.clip(jax.random.uniform(arg_keys[7], (MHEADS,), jnp.float32, -7.0, -2.25), -7.0, -2.25),
        "a_log": jnp.clip(jax.random.uniform(arg_keys[8], (MHEADS,), jnp.float32, -1.0, 1.0), -1.0, 1.0),
        "d_skip": jnp.clip(jax.random.uniform(arg_keys[9], (MHEADS,), jnp.float32, 0.5, 1.5), 0.5, 1.5),
        "ssm_gain": jnp.clip(1.0 + 0.1 * jax.random.normal(arg_keys[10], (DI,), jnp.float32), 0.5, 1.5),
        "mixer_out": bell_draw(arg_keys[11], (DI, D), DI ** -0.5, 0.15625, ((1, 32),)),
        "attn_in": bell_draw(arg_keys[12], (D, (QHEADS + 2 * KVHEADS) * HDIM), D ** -0.5, 0.1875, ((0, 32),)),
        "attn_out": bell_draw(arg_keys[13], (QHEADS * HDIM, D), HDIM ** -0.5, 0.75, ((1, 32),)),
        "norm_two": jnp.clip(1.0 + 0.1 * jax.random.normal(arg_keys[14], (D,), jnp.float32), 0.5, 1.5).astype(jnp.bfloat16),
        "ffn_in": bell_draw(arg_keys[15], (D, 2 * FF), D ** -0.5, 0.1875, ((0, 32),)),
        "ffn_out": bell_draw(arg_keys[16], (FF, D), FF ** -0.5, 0.125, ((1, 32),)),
    }


@jax.custom_vjp
def low(v):
    return lax.optimization_barrier(v.astype(jnp.bfloat16)).astype(jnp.float32)

@jax.custom_vjp
def low_back(v):
    return v

def low_keep(v):
    return (low(v), None)

def low_pass(kept, grad):
    return (grad,)

def back_keep(v):
    return (v, None)

def back_low(kept, grad):
    return (low(grad),)
low.defvjp(low_keep, low_pass)
low_back.defvjp(back_keep, back_low)
eps_norm = 1e-05
rope_base = 10000.0
far_negative = -1e+30
highest = lax.Precision.HIGHEST

def rms_norm(values, gain):
    scaling = lax.rsqrt(lax.optimization_barrier(jnp.mean(values * values, axis=-1, keepdims=True)) + eps_norm)
    return values * scaling * gain

def matmul_high(left_op, right_op):
    return jnp.dot(left_op, right_op, precision=highest, preferred_element_type=jnp.float32)

def rotate(values, positions):
    half_dim = values.shape[-1] // 2
    frequency = rope_base ** (-(jnp.arange(half_dim).astype(jnp.float32) * 2.0 / values.shape[-1]))
    angles = positions.astype(jnp.float32)[:, None] * frequency[None, :]
    cosine = jnp.cos(angles)[:, None, :]
    sine_part = jnp.sin(angles)[:, None, :]
    front_half = values[..., :half_dim]
    back_half = values[..., half_dim:]
    return jnp.concatenate([front_half * cosine - back_half * sine_part, back_half * cosine + front_half * sine_part], axis=-1)

def conv_silu(conv_input, edge_rows, edge_seg, segment, weight, offsets):
    tap_count = weight.shape[0]
    row_total = conv_input.shape[0]
    padded = jnp.concatenate([edge_rows, conv_input], axis=0)
    seg_pad = jnp.concatenate([edge_seg, segment], axis=0)
    summed = jnp.zeros_like(conv_input) + offsets[None, :]
    for tap_index in range(tap_count):
        shifted = padded[tap_index:tap_index + row_total]
        same_doc = (seg_pad[tap_index:tap_index + row_total] == segment)[:, None]
        summed = summed + jnp.where(same_doc, shifted * weight[tap_index][None, :], 0.0)
    return jax.nn.silu(summed)

def decay_sums(step_size, a_neg):
    return jnp.cumsum(step_size * a_neg[None, :], axis=0)

def intra_block(x_heads, bmat, cmat, step_size, cumulative, segment):
    ordering = jnp.arange(x_heads.shape[0])
    same_doc = (segment[:, None] == segment[None, :]) & (ordering[:, None] >= ordering[None, :])
    products = matmul_high(cmat, bmat.T)
    gaps = jnp.where(same_doc[:, :, None], cumulative[:, None, :] - cumulative[None, :, :], far_negative)
    weights = jnp.exp(gaps) * products[:, :, None] * step_size[None, :, :]
    return jnp.einsum('tsh,shp->thp', weights, x_heads, precision=highest)

def read_state(cmat, cumulative, segment, seg_prev, state_in):
    is_live = (segment == seg_prev)[:, None, None]
    carried = jnp.einsum('tn,hpn->thp', cmat, state_in, precision=highest)
    return jnp.where(is_live, carried * jnp.exp(cumulative)[:, :, None], 0.0)

def block_state(x_heads, bmat, step_size, cumulative, segment, seg_prev):
    kept_rows = (segment == segment[-1])[:, None]
    weights = jnp.where(kept_rows, jnp.exp(cumulative[-1][None, :] - cumulative) * step_size, 0.0)
    own_state = jnp.einsum('th,thp,tn->hpn', weights, x_heads, bmat, precision=highest)
    decays = jnp.where(segment[-1] == seg_prev, jnp.exp(cumulative[-1]), 0.0)
    return (own_state, decays)

def ssm_scan(x_heads, bmat, cmat, step_size, a_neg, skip_gain, segment):
    block_count = x_heads.shape[0] // EDGE
    heads_group = x_heads.shape[1]
    prior_seg = jnp.concatenate([jnp.full((1,), -1, jnp.int32), segment.reshape(block_count, EDGE)[:-1, -1]])

    def advance(state_in, block_data):
        x_blk, b_blk, c_blk, s_blk, seg_blk, prev_seg = block_data
        cumulative = decay_sums(s_blk, a_neg)
        result = intra_block(x_blk, b_blk, c_blk, s_blk, cumulative, seg_blk) + read_state(c_blk, cumulative, seg_blk, prev_seg, state_in) + skip_gain[None, :, None] * x_blk
        own_state, decays = block_state(x_blk, b_blk, s_blk, cumulative, seg_blk, prev_seg)
        return (decays[:, None, None] * state_in + own_state, result)
    blocks = (x_heads.reshape(block_count, EDGE, heads_group, x_heads.shape[2]), bmat.reshape(block_count, EDGE, bmat.shape[1]), cmat.reshape(block_count, EDGE, cmat.shape[1]), step_size.reshape(block_count, EDGE, heads_group), segment.reshape(block_count, EDGE), prior_seg)
    start_state = jnp.zeros((heads_group, x_heads.shape[2], bmat.shape[1]), jnp.float32)
    final_state, outputs = lax.scan(jax.checkpoint(advance), start_state, blocks)
    return outputs.reshape(x_heads.shape)

def attend_all(queries, key_rows, value_rows, segment, positions):
    row_total = queries.shape[0]
    scaling = queries.shape[-1] ** (-0.5)

    def one_block(block_index):
        row_start = block_index * EDGE
        query_blk = lax.dynamic_slice_in_dim(queries, row_start, EDGE, 0)
        seg_blk = lax.dynamic_slice_in_dim(segment, row_start, EDGE, 0)
        pos_blk = lax.dynamic_slice_in_dim(positions, row_start, EDGE, 0)
        scores = low_back(jnp.einsum('qhd,kd->hqk', query_blk, key_rows, precision=highest) * scaling)
        allowed = (seg_blk[:, None] == segment[None, :]) & (pos_blk[:, None] >= positions[None, :])
        scores = jnp.where(allowed[None], scores, far_negative)
        weights = low(jax.nn.softmax(scores, axis=-1))
        return jnp.einsum('hqk,kd->qhd', weights, value_rows, precision=highest)
    blocks = lax.map(jax.checkpoint(one_block), jnp.arange(row_total // EDGE).astype(jnp.int32))
    return blocks.reshape(row_total, queries.shape[1], queries.shape[2])

def layer(values, starts, norm_one, mixer_in, conv_weight, conv_bias, dt_bias, a_log, d_skip, ssm_gain, mixer_out, attn_in, attn_out, norm_two, ffn_in, ffn_out):
    row_total = values.shape[0]
    positions = jnp.arange(row_total).astype(jnp.int32)
    segment = lax.optimization_barrier(jnp.sum((starts[None, :] <= positions[:, None]).astype(jnp.int32), axis=1)).astype(jnp.int32)
    normed = low(rms_norm(values, norm_one))
    proj_m = low_back(matmul_high(normed, mixer_in))
    proj_a = low_back(matmul_high(normed, attn_in))
    gate_z = proj_m[:, :DI]
    conv_in = low(proj_m[:, DI:2 * DI + 2 * STATE])
    dt_raw = low(proj_m[:, 2 * DI + 2 * STATE:])
    heads_dev = MHEADS // N_HEAD
    x_cols = heads_dev * MHDIM
    edge_rows = jnp.zeros((CONVK - 1, x_cols + 2 * STATE), jnp.float32)
    edge_seg = jnp.full((CONVK - 1,), -1, jnp.int32)
    ssm_parts = []
    for group_index in range(N_HEAD):
        columns = low_back(jnp.concatenate([conv_in[:, group_index * x_cols:(group_index + 1) * x_cols], conv_in[:, DI:]], axis=1))
        weight = jnp.concatenate([conv_weight[:, group_index * x_cols:(group_index + 1) * x_cols], conv_weight[:, DI:]], axis=1)
        offsets = jnp.concatenate([conv_bias[group_index * x_cols:(group_index + 1) * x_cols], conv_bias[DI:]], axis=0)
        convolved = conv_silu(columns, edge_rows, edge_seg, segment, weight, offsets)
        x_heads = convolved[:, :x_cols].reshape(row_total, heads_dev, MHDIM)
        bmat = convolved[:, x_cols:x_cols + STATE]
        cmat = convolved[:, x_cols + STATE:]
        first_head = group_index * heads_dev
        dt_group = low_back(dt_raw[:, first_head:first_head + heads_dev])
        step_size = jax.nn.softplus(dt_group + dt_bias[first_head:first_head + heads_dev][None, :])
        a_neg = -jnp.exp(a_log[first_head:first_head + heads_dev])
        result = ssm_scan(x_heads, bmat, cmat, step_size, a_neg, d_skip[first_head:first_head + heads_dev], segment)
        ssm_parts.append(low(low_back(result.reshape(row_total, x_cols))))
    mixed = jnp.concatenate(ssm_parts, axis=1)
    query_all = low(rotate(proj_a[:, :QHEADS * HDIM].reshape(row_total, QHEADS, HDIM), positions))
    key_all = low(rotate(proj_a[:, QHEADS * HDIM:(QHEADS + KVHEADS) * HDIM].reshape(row_total, KVHEADS, HDIM), positions))
    value_all = low(proj_a[:, (QHEADS + KVHEADS) * HDIM:].reshape(row_total, KVHEADS, HDIM))
    query_dev = QHEADS // N_HEAD
    group_size = QHEADS // KVHEADS
    attn_parts = []
    for group_index in range(N_HEAD):
        kv_head = group_index * query_dev // group_size
        query_group = low_back(query_all[:, group_index * query_dev:(group_index + 1) * query_dev])
        key_group = low_back(key_all[:, kv_head])
        value_group = low_back(value_all[:, kv_head])
        result = attend_all(query_group, key_group, value_group, segment, positions)
        attn_parts.append(result.reshape(row_total, query_dev * HDIM))
    attended = low(low_back(jnp.concatenate(attn_parts, axis=1)))
    gated = low(rms_norm(mixed * jax.nn.silu(gate_z), ssm_gain))
    hidden = values + low_back(matmul_high(gated, mixer_out)) + low_back(matmul_high(attended, attn_out))
    normed_two = low(rms_norm(hidden, norm_two))
    gate_up = low_back(matmul_high(normed_two, ffn_in))
    activated = low(jax.nn.silu(gate_up[:, :FF]) * gate_up[:, FF:])
    return hidden + matmul_high(activated, ffn_out)

def reference(inputs, cotangent, doc_starts, norm_one, mixer_in, conv_weight, conv_bias, dt_bias, a_log, d_skip, ssm_gain, mixer_out, attn_in, attn_out, norm_two, ffn_in, ffn_out):
    params = tuple((one_param.astype(jnp.float32) for one_param in (norm_one, mixer_in, conv_weight, conv_bias, dt_bias, a_log, d_skip, ssm_gain, mixer_out, attn_in, attn_out, norm_two, ffn_in, ffn_out)))
    results = []
    input_grads = []
    totals = None
    for micro_index in range(MB):
        starts = doc_starts[micro_index]

        def forward(values, *weights):
            return layer(values, starts, *weights)
        result, pullback = jax.vjp(forward, inputs[micro_index].astype(jnp.float32), *params)
        gradients = pullback(cotangent[micro_index].astype(jnp.float32))
        results.append(result)
        input_grads.append(gradients[0])
        if totals is None:
            totals = tuple(gradients[1:])
        else:
            totals = tuple((earlier + extra for earlier, extra in zip(totals, gradients[1:])))
    return (jnp.stack(results), jnp.stack(input_grads), totals[0], totals[1], totals[2], totals[3], totals[4], totals[5], totals[6], totals[7], totals[8], totals[9], totals[10], totals[11], totals[12], totals[13])
```

```python
import functools

import jax
import jax.numpy as jnp
import numpy as np
from jax import lax
from jax.experimental import pallas as pl
from jax.experimental.pallas import tpu as pltpu
from jax.sharding import PartitionSpec as P

MHEADS = 24
MHDIM = 64
STATE = 128
QHEADS = 8
HDIM = 64
FF = 2048
DI = 1536
D = 1024
MAXLEN = 4096
NH = 4
HG = MHEADS // NH
XC = HG * MHDIM
FG = FF // NH
W1C = 2 * XC + 3 * 128
WRC = 2 * FG + XC + 128 + FG
LAG = 16
EPS = 1e-5
FAR = -1e30
SCALE = HDIM**-0.5
MESH = pl.DeviceIdType.MESH
BF = jnp.bfloat16
F32 = jnp.float32
VMEM_LIMIT = 60 * 2**20
high = lax.Precision.HIGHEST


def nn(a, b):
    return lax.dot_general(a, b, (((1,), (0,)), ((), ())), preferred_element_type=F32)


def nt(a, b):
    return lax.dot_general(a, b, (((1,), (1,)), ((), ())), preferred_element_type=F32)


def tn(a, b):
    return lax.dot_general(a, b, (((0,), (0,)), ((), ())), preferred_element_type=F32)


def other(index, step):
    return index + step - 2 * step * lax.rem(index // step, 2)


def copy_to(src, dst, send, recv, where):
    return pltpu.make_async_remote_copy(
        src_ref=src, dst_ref=dst, send_sem=send, recv_sem=recv, device_id=where, device_id_type=MESH
    )


def barrier(edges):
    sem = pltpu.get_barrier_semaphore()
    for there, where in edges:
        if there is True:
            pl.semaphore_signal(sem, inc=1, device_id=where, device_id_type=MESH)
        else:

            @pl.when(there)
            def _():
                pl.semaphore_signal(sem, inc=1, device_id=where, device_id_type=MESH)

    total = 0
    for there, _ in edges:
        total = total + (1 if there is True else there.astype(jnp.int32))
    pl.semaphore_wait(sem, total)


def lanes(shape):
    return lax.broadcasted_iota(jnp.int32, shape, len(shape) - 1)


def rows_of(shape):
    return lax.broadcasted_iota(jnp.int32, shape, len(shape) - 2)


def sigmoid(v):
    return 1.0 / (1.0 + jnp.exp(-v))


def widen(cols, first, count=HG, width=MHDIM):
    return jnp.concatenate(
        [
            jnp.broadcast_to(cols[:, first + i : first + i + 1], (cols.shape[0], width))
            for i in range(count)
        ],
        axis=1,
    )


class LineGather:
    def __init__(self, piece, b, h, nb, sems):
        self.piece, self.h, self.nz = piece, h, nb // 2
        self.z, self.x = b // 2, lax.rem(b, 2)
        self.line_recv, self.send_r, self.send_l, self.x_send, self.x_recv = sems

    @staticmethod
    def scratch(nb):
        return [pltpu.SemaphoreType.DMA((nb // 2,))] * 5

    def at(self, z, x=None):
        return self.piece(2 * z + (self.x if x is None else x))

    def to_x(self, z):
        return copy_to(
            self.at(z), self.at(z), self.x_send.at[z], self.x_recv.at[z], (2 * self.z + 1 - self.x, self.h)
        )

    def to_z(self, z, way):
        send = self.send_r if way > 0 else self.send_l
        return copy_to(
            self.at(z), self.at(z), send.at[z], self.line_recv.at[z], (2 * (self.z + way) + self.x, self.h)
        )

    def begin(self):
        self.to_x(self.z).start()
        self.hop(0)

    def hop(self, s):
        @pl.when((self.z - s >= 0) & (self.z + 1 < self.nz))
        def _():
            self.to_z(self.z - s, 1).start()

        @pl.when((self.z + s < self.nz) & (self.z >= 1))
        def _():
            self.to_z(self.z + s, -1).start()

    def advance(self, s):
        left, right = self.z - 1 - s, self.z + 1 + s

        @pl.when(left >= 0)
        def _():
            self.to_z(left, 1).wait_recv()
            self.to_x(left).start()

        @pl.when(right < self.nz)
        def _():
            self.to_z(right, -1).wait_recv()
            self.to_x(right).start()

        if s + 1 < self.nz - 1:
            self.hop(s + 1)

    def finish(self):
        for z in range(self.nz):
            copy_to(
                self.at(z, 1 - self.x),
                self.at(z, 1 - self.x),
                self.x_send.at[z],
                self.x_recv.at[z],
                (2 * self.z + 1 - self.x, self.h),
            ).wait_recv()
        for z in range(self.nz):
            self.to_x(z).wait_send()

            @pl.when((z <= self.z) & (self.z + 1 < self.nz))
            def _():
                self.to_z(z, 1).wait_send()

            @pl.when((z >= self.z) & (self.z >= 1))
            def _():
                self.to_z(z, -1).wait_send()

    def edges(self):
        return line_edges(2 * self.z + self.x, self.h, 2 * self.nz)


def line_edges(b, h, nb):
    return [
        (True, (other(b, 1), h)),
        (b >= 2, (b - 2, h)),
        (b + 2 < nb, (b + 2, h)),
    ]


def head_edges(b, h):
    return [(True, (b, other(h, 1))), (True, (b, other(h, 2))), (True, (b, NH - 1 - h))]


class HeadGather:
    def __init__(self, rows, b, h, sems):
        self.rows, self.b, self.h = rows, b, h
        self.send, self.recv = sems

    @staticmethod
    def scratch():
        return [pltpu.SemaphoreType.DMA((3,))] * 2

    def copy(self, i):
        pair, across = other(self.h, 1), other(self.h, 2)
        rows = self.rows(self.h if i < 2 else across)
        return copy_to(rows, rows, self.send.at[i], self.recv.at[i], (self.b, across if i == 1 else pair))

    def begin(self):
        self.copy(1).start()
        self.copy(0).start()

    def forward(self):
        self.copy(1).wait_recv()
        self.copy(2).start()

    def finish(self):
        self.copy(0).wait_recv()
        self.copy(2).wait_recv()
        for i in range(3):
            self.copy(i).wait_send()


class HeadScatter:
    def __init__(self, full, b, h, bufs, sems):
        self.full, self.b, self.h = full, b, h
        self.send_c, self.recv_c, self.send_y, self.recv_y = bufs
        self.send, self.recv = sems

    @staticmethod
    def scratch(rows, width=D):
        return [
            pltpu.VMEM((2, 2, rows, width), BF),
            pltpu.VMEM((2, 2, rows, width), BF),
            pltpu.VMEM((2, rows, width), BF),
            pltpu.VMEM((2, rows, width), BF),
            pltpu.SemaphoreType.DMA((2,)),
            pltpu.SemaphoreType.DMA((2,)),
        ]

    def copy(self, i):
        src, dst = ((self.send_c, self.recv_c), (self.send_y, self.recv_y))[i]
        return copy_to(src, dst, self.send.at[i], self.recv.at[i], (self.b, other(self.h, i + 1)))

    def begin(self):
        core = lax.rem(self.h, 2)
        for y in range(2):
            for m in range(2):
                self.send_c[y, m] = self.full(m, 2 * y + 1 - core).astype(BF)
        self.copy(0).start()

    def middle(self):
        core, y = lax.rem(self.h, 2), self.h // 2
        self.copy(0).wait_recv()
        for m in range(2):
            self.send_y[m] = (
                self.full(m, 2 * (1 - y) + core) + self.recv_c[1 - y, m].astype(F32)
            ).astype(BF)
        self.copy(1).start()

    def finish(self):
        self.copy(1).wait_recv()
        self.copy(0).wait_send()
        self.copy(1).wait_send()

    def result(self, m):
        y = self.h // 2
        return self.full(m, self.h) + self.recv_c[y, m].astype(F32) + self.recv_y[m].astype(F32)


def place():
    return lax.axis_index("blk"), lax.axis_index("head")


def rotate_pair(v, cosine, sine):
    lane = lax.rem(lanes(v.shape), HDIM)
    front = lane < HDIM // 2
    partner = jnp.where(front, pltpu.roll(v, 128 - HDIM // 2, 1), pltpu.roll(v, HDIM // 2, 1))
    return v * cosine + jnp.where(front, -partner, partner) * sine


def rope_tables(freq_ref, b, rows, ref_cos, ref_sin):
    pos = (b * rows + rows_of((rows, 128))).astype(F32)
    angle = pos * freq_ref[...]
    ref_cos[...] = jnp.cos(angle)
    ref_sin[...] = jnp.sin(angle)


def front_kernel(
    nb, T, local_pieces,
    x_ref, cot_ref, w1p_ref, wrp_ref, freq_ref,
    normed_ref, gate_ref, xin_ref, bc_ref, q_ref, kv_ref, dt_ref, cotg_ref, w1_ref, wr_ref, gains_ref,
    cos_ref, sin_ref,
    xg, sx0, sx1, sc0, sc1, sp, rp, l0, l1, l2, l3, l4, k0, k1, k2, k3, k4, halo_s, halo_r, own_s, pair_s, pair_r,
):
    b, h = place()
    tok = T // NH
    rpb = D // nb
    piece = rpb // NH
    barrier(
        head_edges(b, h)
        + line_edges(b, h, nb)
        + [((h == NH - 1) & (b + 1 < nb), (b + 1, jnp.int32(i))) for i in range(NH)]
        + [(b >= 1, (b - 1, jnp.int32(NH - 1)))]
    )
    gather_x = HeadGather(lambda i: xg.at[:, pl.ds(LAG + i * tok, tok)], b, h, (sx0, sx1))
    gather_c = HeadGather(lambda i: cotg_ref.at[:, pl.ds(i * tok, tok)], b, h, (sc0, sc1))
    line1 = LineGather(lambda i: w1_ref.at[pl.ds(i * rpb, rpb)], b, h, nb, (l0, l1, l2, l3, l4))
    line2 = LineGather(lambda i: wr_ref.at[pl.ds(i * rpb, rpb)], b, h, nb, (k0, k1, k2, k3, k4))

    sent = []
    if local_pieces:
        for n, (src, dst) in enumerate(((w1p_ref, w1_ref), (wrp_ref, wr_ref))):
            for i, to in enumerate((other(h, 1), other(h, 2), NH - 1 - h)):
                mine = dst.at[pl.ds(b * rpb + h * piece, piece)]
                sent.append(copy_to(src.at[to], mine, sp.at[3 * n + i], rp.at[3 * n + i], (b, to)))
            if n == 0:
                for c in sent:
                    c.start()
                w1_ref[pl.ds(b * rpb + h * piece, piece), :] = w1p_ref[h]
    else:
        w1_ref[pl.ds(b * rpb, rpb), :] = w1p_ref[...]
    for m in range(2):
        xg[m, pl.ds(LAG + h * tok, tok), :] = x_ref[m]
        cotg_ref[m, pl.ds(h * tok, tok), :] = cot_ref[m]
    gather_x.begin()

    def halo(i):
        return copy_to(
            x_ref.at[:, pl.ds(tok - LAG, LAG)], xg.at[:, pl.ds(0, LAG)], halo_s.at[i], halo_r.at[0], (b + 1, jnp.int32(i))
        )

    @pl.when((h == NH - 1) & (b + 1 < nb))
    def _():
        for i in range(NH):
            halo(i).start()

    @pl.when(b == 0)
    def _():
        xg[:, 0:LAG, :] = jnp.zeros((2, LAG, D), BF)

    if local_pieces:
        for i in range(3):
            sent[i].wait_recv()
    line1.begin()
    gather_c.begin()
    if local_pieces:
        for i in range(3):
            sent[3 + i].start()
        own = pltpu.make_async_copy(wrp_ref.at[h], wr_ref.at[pl.ds(b * rpb + h * piece, piece)], own_s.at[0])
    else:
        own = pltpu.make_async_copy(wrp_ref, wr_ref.at[pl.ds(b * rpb, rpb)], own_s.at[0])
    own.start()
    rope_tables(freq_ref, b, T, cos_ref, sin_ref)
    gather_x.forward()
    gather_c.forward()
    gather_x.finish()

    @pl.when(b >= 1)
    def _():
        halo(0).wait_recv()

    @pl.when((h == NH - 1) & (b + 1 < nb))
    def _():
        for i in range(NH):
            halo(i).wait_send()

    own.wait()
    if local_pieces:
        for i in range(3):
            sent[3 + i].wait_recv()
    for s in range(nb // 2 - 1):
        line1.advance(s)
    line1.finish()
    line2.begin()

    last = w1_ref[:, W1C - 128 :].astype(F32).T
    gains_ref[...] = last[HDIM + HG + 2 - 8 : HDIM + HG + 2]
    n1 = gains_ref[6:7, :]
    for m in range(2):
        v = xg[m].astype(F32)
        scale = lax.rsqrt(jnp.mean(v * v, axis=1, keepdims=True) + EPS)
        normed_ref[m] = (v * scale * n1).astype(BF)
    core = lax.rem(h, 2)
    small = 2 * XC
    lane = lanes((T, 128))
    kv, dt = [], []
    for m in range(2):
        bc = nn(normed_ref[m], w1_ref[:, small : small + 128])
        bc_ref[m, :, pl.ds(pl.multiple_of(core * 128, 128), 128)] = bc.astype(BF)
        kv.append(nn(normed_ref[m, LAG:], w1_ref[:, small + 256 : small + 384]))
    packed = jnp.where(lane < HDIM, kv[0], pltpu.roll(kv[1], HDIM, 1))
    turned = rotate_pair(packed, cos_ref[...], sin_ref[...])
    kv_ref[core] = jnp.where(core == 0, turned, packed).astype(BF)
    pair = (
        copy_to(kv_ref.at[core], kv_ref.at[core], pair_s.at[0], pair_r.at[0], (b, other(h, 1))),
        copy_to(
            bc_ref.at[:, :, pl.ds(pl.multiple_of(core * 128, 128), 128)],
            bc_ref.at[:, :, pl.ds(pl.multiple_of(core * 128, 128), 128)],
            pair_s.at[1], pair_r.at[1], (b, other(h, 1)),
        ),
    )
    for c in pair:
        c.start()
    line2.advance(0)
    dt = [pltpu.roll(kv[0], 128 - HDIM, 1), pltpu.roll(kv[1], 128 - HDIM + 8, 1)]
    dt_ref[...] = (
        jnp.where(lane < HG, dt[0], jnp.where((lane >= 8) & (lane < 8 + HG), dt[1], 0.0)).astype(BF).astype(F32)
    )
    for m in range(2):
        q = nn(normed_ref[m, LAG:], w1_ref[:, small + 128 : small + 256])
        q_ref[m] = rotate_pair(q, cos_ref[...], sin_ref[...]).astype(BF)
        xin_ref[m] = nn(normed_ref[m], w1_ref[:, XC : 2 * XC]).astype(BF)
        gate_ref[m] = nn(normed_ref[m, LAG:], w1_ref[:, :XC])
    for s in range(1, nb // 2 - 1):
        line2.advance(s)
    line2.finish()
    for c in pair:
        c.wait()
    gather_c.finish()
    for c in sent:
        c.wait_send()


def vm(shape, dtype):
    return jax.ShapeDtypeStruct(shape, dtype)


def call(kernel, outs, scratch, args, name, cid, smem=(), hbm=(), hbm_out=(), **cost):
    in_specs = [
        pl.BlockSpec(memory_space=pltpu.SMEM if i in smem else (pl.ANY if i in hbm else pltpu.VMEM))
        for i in range(len(args))
    ]
    out_specs = [
        pl.BlockSpec(memory_space=pl.ANY if i in hbm_out else pltpu.VMEM) for i in range(len(outs))
    ]
    return pl.pallas_call(
        kernel,
        out_shape=outs,
        in_specs=in_specs,
        out_specs=out_specs,
        scratch_shapes=scratch,
        compiler_params=pltpu.CompilerParams(
            collective_id=cid, has_side_effects=True, vmem_limit_bytes=VMEM_LIMIT
        ),
        name=name,
    )(*args)


def front(nb, x, cot, w1p, wrp, freq, local_pieces):
    tok = x.shape[1]
    T = tok * NH
    dma = pltpu.SemaphoreType.DMA
    outs = [
        vm((2, LAG + T, D), BF), vm((2, T, XC), F32), vm((2, LAG + T, XC), BF), vm((2, LAG + T, 256), BF),
        vm((2, T, 128), BF), vm((2, T, 128), BF), vm((T, 128), F32), vm((2, T, D), BF),
        vm((D, W1C), BF), vm((D, WRC), BF), vm((8, D), F32), vm((T, 128), F32), vm((T, 128), F32),
    ]
    scratch = (
        [pltpu.VMEM((2, LAG + T, D), BF)]
        + HeadGather.scratch() + HeadGather.scratch()
        + [dma((6,)), dma((6,))]
        + LineGather.scratch(nb) + LineGather.scratch(nb)
        + [dma((NH,)), dma((1,)), dma((1,)), dma((2,)), dma((2,))]
    )
    return call(
        functools.partial(front_kernel, nb, T, local_pieces), outs, scratch, (x, cot, w1p, wrp, freq), "front", 1,
    )


def doc_start(starts_ref, m, pos):
    first = jnp.zeros(pos.shape, jnp.int32)
    for k in range(starts_ref.shape[1]):
        s = starts_ref[m, k]
        first = jnp.where(pos >= s, s, first)
    return first


def head_row(ref, h, count=2):
    lane = lanes((1, 128))
    row = jnp.zeros((1, 128), F32)
    for i in range(HG):
        for m in range(count):
            row = jnp.where(lane == 8 * m + i, ref[h * HG + i], row)
    return row


def wide_row(ref, h):
    lane = lanes((1, XC)) // MHDIM
    row = jnp.zeros((1, XC), F32)
    for i in range(HG):
        row = jnp.where(lane == i, ref[h * HG + i], row)
    return row


def valid_row():
    lane = lanes((1, 128))
    return (lane < 16) & (lax.rem(lane, 8) < HG)


def triangle(n, upper=False):
    r, c = rows_of((n, n)), lanes((n, n))
    return ((c >= r) if upper else (c <= r)).astype(F32)


class Scan:
    ROWS = XC + 16

    def __init__(self, way, b, h, nb, reach, bufs):
        self.way, self.b, self.h, self.nb = way, b, h, nb
        self.steps = Scan.step_list(reach)
        self.send_buf, self.recv_buf, self.sums, self.send, self.recv = bufs

    @staticmethod
    def step_list(reach):
        steps, d = [], 1
        while d < reach:
            steps.append(d)
            d *= 2
        return steps + [1]

    @staticmethod
    def scratch(reach):
        n = len(Scan.step_list(reach))
        return [
            pltpu.VMEM((n, 2, Scan.ROWS, 128), BF),
            pltpu.VMEM((n, 2, Scan.ROWS, 128), BF),
            pltpu.VMEM((2, Scan.ROWS, 128), F32),
            pltpu.SemaphoreType.DMA((n,)),
            pltpu.SemaphoreType.DMA((n,)),
        ]

    @staticmethod
    def edges(b, h, nb, reach):
        out = []
        for d in sorted(set(Scan.step_list(reach))):
            out += [(b + d < nb, (b + d, h)), (b >= d, (b - d, h))]
        return out

    def has_to(self, d):
        return (self.b + d < self.nb) if self.way > 0 else (self.b >= d)

    def has_from(self, d):
        return (self.b >= d) if self.way > 0 else (self.b + d < self.nb)

    def copy(self, i):
        return copy_to(
            self.send_buf.at[i], self.recv_buf.at[i], self.send.at[i], self.recv.at[i],
            (self.b + self.way * self.steps[i], self.h),
        )

    def send_step(self, i):
        self.send_buf[i] = self.sums[...].astype(BF)

        @pl.when(self.has_to(self.steps[i]))
        def _():
            self.copy(i).start()

    def receive(self, i):
        there = self.has_from(self.steps[i])

        @pl.when(there)
        def _():
            self.copy(i).wait_recv()

        @pl.when(jnp.logical_not(there))
        def _():
            self.recv_buf[i] = jnp.zeros((2, Scan.ROWS, 128), BF)

    def join(self, i):
        self.receive(i)
        for m in range(2):
            early = self.recv_buf[i, m].astype(F32)
            for j in range(HG):
                mine = pl.ds(j * MHDIM, MHDIM)
                decay = self.sums[m, pl.ds(XC + j, 1), :]
                self.sums[m, mine, :] = self.sums[m, mine, :] + decay * early[j * MHDIM : (j + 1) * MHDIM]
            self.sums[m, pl.ds(XC, 8), :] = self.sums[m, pl.ds(XC, 8), :] * early[XC : XC + 8]

    def finish(self):
        for i, d in enumerate(self.steps):

            @pl.when(self.has_to(d))
            def _():
                self.copy(i).wait_send()


def halo_edges(b, h, nb, reach):
    out = []
    for d in range(1, reach + 1):
        out += [(b + d < nb, (b + d, h)), (b >= d, (b - d, h))]
    return out


class Halo:
    def __init__(self, way, src, dst, b, h, nb, reach, sems):
        self.way, self.src, self.dst, self.b, self.h, self.nb, self.reach = way, src, dst, b, h, nb, reach
        self.send, self.recv = sems

    @staticmethod
    def scratch(reach):
        return [pltpu.SemaphoreType.DMA((reach + 1,))] * 2

    def there(self, d, way):
        return (self.b + d < self.nb) if way > 0 else (self.b >= d)

    def copy(self, d):
        return copy_to(
            self.src(d), self.dst(d), self.send.at[d], self.recv.at[d], (self.b + self.way * d, self.h)
        )

    def begin(self):
        for d in range(1, self.reach + 1):

            @pl.when(self.there(d, self.way))
            def _():
                self.copy(d).start()

    def finish_recv(self):
        for d in range(1, self.reach + 1):

            @pl.when(self.there(d, -self.way))
            def _():
                self.copy(d).wait_recv()

    def finish_send(self):
        for d in range(1, self.reach + 1):

            @pl.when(self.there(d, self.way))
            def _():
                self.copy(d).wait_send()


class HeadSum:
    def __init__(self, b, h, bufs):
        self.b, self.h = b, h
        self.buf, self.send, self.recv = bufs

    @staticmethod
    def scratch(T):
        return [pltpu.VMEM((4, 8, T), F32), pltpu.SemaphoreType.DMA((3,)), pltpu.SemaphoreType.DMA((3,))]

    def copies(self):
        return [
            copy_to(self.buf.at[0], self.buf.at[1 + i], self.send.at[i], self.recv.at[i], (self.b, to))
            for i, to in enumerate((other(self.h, 1), other(self.h, 2), NH - 1 - self.h))
        ]

    def begin(self, cols):
        T = self.buf.shape[2]
        lane = lanes((T, 128))
        packed = jnp.where(lane == 0, cols[0], jnp.where(lane == 1, cols[1], 0.0))
        self.buf[0] = packed.T[:8]
        for c in self.copies():
            c.start()

    def finish(self):
        for c in self.copies():
            c.wait()
        T = self.buf.shape[2]
        total = self.buf[0] + self.buf[1] + self.buf[2] + self.buf[3]
        cols = jnp.concatenate([total, jnp.zeros((120, T), F32)], axis=0).T
        return [cols[:, 0:1], cols[:, 1:2]]


def group_taps(h, w_ref, b_ref, chunk):
    if chunk < XC // 128:
        at = pl.ds(pl.multiple_of(h * XC + chunk * 128, 128), 128)
    else:
        at = pl.ds(DI + (chunk - XC // 128) * 128, 128)
    return w_ref[:, at], b_ref[:, at]


def decays_of(dt_ref, bias_ref, alog_ref, h, T):
    valid = valid_row()
    z = dt_ref[...] + head_row(bias_ref, h)
    step = jnp.where(valid, jnp.maximum(z, 0.0) + jnp.log1p(jnp.exp(-jnp.abs(z))), 0.0)
    a_neg = jnp.where(valid, -jnp.exp(head_row(alog_ref, h)), 0.0)
    cum = jnp.dot(triangle(T), step * a_neg, precision=high, preferred_element_type=F32)
    return z, step, a_neg, cum


def by_batch(pick):
    first, second = pick(0), pick(1)
    return jnp.where(lanes((first.shape[0], 128)) < 8, first, second)


def mixer_kernel(
    nb, T, reach,
    xin_ref, bc_ref, q_ref, kv_ref, dt_ref, gate_ref, starts_ref, cw_ref, cb_ref, dtb_ref, alog_ref, skip_ref, gain_ref,
    ylow_ref, gated_ref, attnf_ref, attnl_ref, r_ref, lse_ref, pre_ref, sin_ref, kvh_ref,
    cin, xs, bs, cs, ybuf, sbuf, cumt, stept, c0, c1, c2, c3, c4, h0, h1, t0, t1, t2,
):
    b, h = place()
    barrier(head_edges(b, h) + Scan.edges(b, h, nb, reach) + halo_edges(b, h, nb, reach))
    scan = Scan(1, b, h, nb, reach, (c0, c1, c2, c3, c4))
    halo = Halo(1, lambda d: kv_ref, lambda d: kvh_ref.at[d], b, h, nb, reach, (h0, h1))
    sums = HeadSum(b, h, (t0, t1, t2))
    halo.begin()
    pos = b * T + rows_of((T, 1))
    first = [doc_start(starts_ref, m, pos) for m in range(2)]
    last = [f[T - 1 :, :] for f in first]
    for d in range(1, reach + 1):

        @pl.when(b < d)
        def _():
            kvh_ref[d] = jnp.zeros((2, T, 128), BF)

    kvh_ref[0] = kv_ref[...]
    for m in range(2):
        cin[:, 0:XC] = xin_ref[m].astype(F32)
        cin[:, XC:] = bc_ref[m].astype(F32)
        for chunk in range((XC + 256) // 128):
            cols = pl.ds(chunk * 128, 128)
            taps, bias = group_taps(h, cw_ref, cb_ref, chunk)
            total = jnp.broadcast_to(bias, (T, 128))
            for j in range(4):
                back = 3 - j
                total = total + jnp.where(pos - first[m] >= back, cin[pl.ds(LAG - back, T), cols] * taps[j : j + 1], 0.0)
            pre_ref[m, :, cols] = total
            act = total * sigmoid(total)
            if chunk < XC // 128:
                xs[m, :, cols] = act
            elif chunk == XC // 128:
                bs[m] = act.astype(BF)
            else:
                cs[m] = act.astype(BF)
    z, step, a_neg, cum = decays_of(dt_ref, dtb_ref, alog_ref, h, T)
    cumt[...] = cum.T[:16]
    stept[...] = step.T[:16]
    cum_last = cum[T - 1 :, :]
    kept = by_batch(lambda m: jnp.broadcast_to((pos >= last[m]).astype(F32), (T, 128)))
    omega = jnp.exp(cum_last - cum) * step * kept
    for m in range(2):
        weighted = (xs[m] * widen(omega, 8 * m)).astype(BF)
        scan.sums[m, 0:XC, :] = tn(weighted, bs[m])
        decay = jnp.where(last[m] < b * T, jnp.exp(cumt[8 * m : 8 * m + 8, T - 1 : T]), 0.0)
        scan.sums[m, XC : XC + 8, :] = jnp.broadcast_to(decay, (8, 128))
        scan.sums[m, XC + 8 :, :] = jnp.zeros((8, 128), F32)
    scan.send_step(0)

    seen = lanes((T, T)) + b * T
    for m in range(2):
        both = nt(cs[m], bs[m])
        allowed = (seen <= pos) & (seen >= first[m])
        for i in range(HG):
            l = 8 * m + i
            gap = jnp.where(allowed, cum[:, l : l + 1] - cumt[l : l + 1, :], FAR)
            weights = (jnp.exp(gap) * both * stept[l : l + 1, :]).astype(BF)
            ybuf[m, :, i * MHDIM : (i + 1) * MHDIM] = nn(weights, xs[m, :, i * MHDIM : (i + 1) * MHDIM].astype(BF))
        ybuf[m] = ybuf[m] + wide_row(skip_ref, h) * xs[m]
        if m == 0:
            scan.join(0)
            scan.send_step(1)
    halo.finish_recv()

    lane = lanes((T, 128))
    lse_all = jnp.zeros((T, 128), F32)
    for m in range(2):
        for i in range(2):
            query = q_ref[m, :, i * HDIM : (i + 1) * HDIM]

            def score(d, top):
                at = seen - d * T
                keys = kvh_ref[d, 0, :, m * HDIM : (m + 1) * HDIM]
                s = jnp.where((at <= pos) & (at >= first[m]), nt(query, keys) * SCALE, FAR)
                sbuf[d] = s
                return jnp.maximum(top, jnp.max(s, axis=1, keepdims=True))

            top = lax.fori_loop(0, reach + 1, score, jnp.full((T, 1), FAR, F32))

            def weigh(d, total):
                e = jnp.exp(sbuf[d] - top)
                sbuf[d] = e
                return total + jnp.sum(e, axis=1, keepdims=True)

            total = lax.fori_loop(0, reach + 1, weigh, jnp.zeros((T, 1), F32))
            inverse = 1.0 / total

            def take(d, acc):
                probs = (sbuf[d] * inverse).astype(BF)
                return acc + nn(probs, kvh_ref[d, 1, :, m * HDIM : (m + 1) * HDIM])

            attnf_ref[m, :, i * HDIM : (i + 1) * HDIM] = lax.fori_loop(0, reach + 1, take, jnp.zeros((T, HDIM), F32))
            lse_all = jnp.where(lane == 2 * m + i, top + jnp.log(total), lse_all)
        attnl_ref[m] = attnf_ref[m].astype(BF)
        if len(scan.steps) > 2 and m == 0:
            scan.join(1)
            scan.send_step(2)
    lse_ref[...] = lse_all
    for i in range(2, len(scan.steps) - 1):
        scan.join(i)
        scan.send_step(i + 1)
    end = len(scan.steps) - 1
    scan.receive(end)
    sin_ref[...] = c1[end]
    squares = []
    for m in range(2):
        live = jnp.where(first[m] < b * T, jnp.exp(cum), 0.0)
        y = ybuf[m] + nt(cs[m], sin_ref[m, 0:XC]) * widen(live, 8 * m)
        low = y.astype(BF)
        ylow_ref[m] = low
        gate = gate_ref[m]
        g = low.astype(F32) * gate * sigmoid(gate)
        ybuf[m] = g
        squares.append(jnp.sum(g * g, axis=1, keepdims=True))
    sums.begin(squares)
    scan.finish()
    halo.finish_send()
    gain = gain_ref[:, pl.ds(pl.multiple_of(h * XC, 128), XC)]
    totals = sums.finish()
    scales = [lax.rsqrt(t * (1.0 / DI) + EPS) for t in totals]
    for m in range(2):
        gated_ref[m] = (ybuf[m] * scales[m] * gain).astype(BF)
    r_ref[...] = jnp.where(lane == 0, scales[0], jnp.where(lane == 1, scales[1], 0.0))


def mixer(nb, reach, xin, bc, q, kv, dt, gate, starts, cw, cb, dtb, alog, skip, gain):
    T = q.shape[1]
    outs = [
        vm((2, T, XC), BF), vm((2, T, XC), BF), vm((2, T, 128), F32), vm((2, T, 128), BF), vm((T, 128), F32),
        vm((T, 128), F32), vm((2, T, XC + 256), F32), vm((2, Scan.ROWS, 128), BF), vm((reach + 1, 2, T, 128), BF),
    ]
    scratch = (
        [
            pltpu.VMEM((LAG + T, XC + 256), F32), pltpu.VMEM((2, T, XC), F32), pltpu.VMEM((2, T, 128), BF),
            pltpu.VMEM((2, T, 128), BF), pltpu.VMEM((2, T, XC), F32), pltpu.VMEM((reach + 1, T, T), F32),
            pltpu.VMEM((16, T), F32), pltpu.VMEM((16, T), F32),
        ]
        + Scan.scratch(reach) + Halo.scratch(reach) + HeadSum.scratch(T)
    )
    return call(
        functools.partial(mixer_kernel, nb, T, reach), outs, scratch,
        (xin, bc, q, kv, dt, gate, starts, cw, cb, dtb, alog, skip, gain), "mixer", 2, smem=(6, 9, 10, 11),
    )


def norm_back(value, scale, gain, upstream):
    n = value * scale
    uw = upstream * gain
    grad = scale * (uw - n * jnp.mean(n * uw, axis=1, keepdims=True))
    return grad, jnp.sum(upstream * n, axis=0, keepdims=True)


def arrange(per, width, first):
    total = XC + 128
    share, mix, att = total // per, XC // per, 128 // per
    n, src = lanes((width, total)), rows_of((width, total))
    i, u = n // share, lax.rem(n, share)
    if first == 0:
        hit = (u < mix) & (src == i * mix + u)
    else:
        hit = (u >= mix) & (src == i * att + u - mix)
    return hit.astype(F32).astype(BF)


def feed_kernel(
    nb, T,
    gated_ref, attnl_ref, x_ref, cot_ref, cotg_ref, wr_ref, gains_ref, ylow_ref, gate_ref, r_ref, gain_ref,
    out_ref, gh_ref, gy_ref, ggate_ref, gattn_ref, gwr_ref, gn2_ref, ggain_ref,
    part, part2, secg, hlg, act, ggu, gact, hid, w0, w1, w2, w3, w4, w5, v0, v1, v2, v3, v4, v5, u0, u1, u2, u3, u4, u5,
    a0, a1, b0, b1, t0, t1, t2,
):
    b, h = place()
    tok = T // NH
    barrier(head_edges(b, h))
    n2 = gains_ref[7:8, :]

    def rows(ref):
        return lambda m, head: ref[m, pl.ds(pl.multiple_of(head * tok, tok), tok), :]

    at_gate, at_mix, at_att, at_out = 0, 2 * FG, 2 * FG + XC, 2 * FG + XC + 128
    for m in range(2):
        part[m] = nt(gated_ref[m], wr_ref[:, at_mix:at_att]) + nt(attnl_ref[m], wr_ref[:, at_att:at_out])
    first = HeadScatter(rows(part), b, h, (w0, w1, w2, w3), (w4, w5))
    first.begin()
    gact[0] = nn(cotg_ref[0], wr_ref[:, at_out:])
    first.middle()
    gact[1] = nn(cotg_ref[1], wr_ref[:, at_out:])
    first.finish()
    gather_s = HeadGather(lambda i: secg.at[:, pl.ds(i * tok, tok)], b, h, (a0, a1))
    for m in range(2):
        value = x_ref[m].astype(F32) + first.result(m)
        hid[m] = value
        scale = lax.rsqrt(jnp.mean(value * value, axis=1, keepdims=True) + EPS)
        secg[m, pl.ds(pl.multiple_of(h * tok, tok), tok), :] = (value * scale * n2).astype(BF)
    gather_s.begin()
    gather_s.forward()
    gather_s.finish()
    for m in range(2):
        a = nn(secg[m], wr_ref[:, 0:FG])
        u = nn(secg[m], wr_ref[:, FG : 2 * FG])
        sg = sigmoid(a)
        si = a * sg
        act[m] = (si * u).astype(BF)
        ggu[m, :, 0:FG] = (gact[m] * u * (sg * (1.0 + a * (1.0 - sg)))).astype(BF)
        ggu[m, :, FG:] = (gact[m] * si).astype(BF)
    for m in range(2):
        part[m] = nt(ggu[m], wr_ref[:, 0 : 2 * FG])
    second = HeadScatter(rows(part), b, h, (v0, v1, v2, v3), (v4, v5))
    second.begin()
    part2[0] = nt(act[0], wr_ref[:, at_out:])
    second.middle()
    part2[1] = nt(act[1], wr_ref[:, at_out:])
    second.finish()
    third = HeadScatter(rows(part2), b, h, (u0, u1, u2, u3), (u4, u5))
    gather_h = HeadGather(lambda i: hlg.at[:, pl.ds(i * tok, tok)], b, h, (b0, b1))
    gn2 = jnp.zeros((1, D), F32)
    for m in range(2):
        value = hid[m]
        scale = lax.rsqrt(jnp.mean(value * value, axis=1, keepdims=True) + EPS)
        grad, gain_part = norm_back(value, scale, n2, second.result(m))
        grad = grad + cot_ref[m].astype(F32)
        gh_ref[m] = grad
        gn2 = gn2 + gain_part
        hlg[m, pl.ds(pl.multiple_of(h * tok, tok), tok), :] = grad.astype(BF)
    gn2_ref[...] = gn2
    gather_h.begin()
    third.begin()

    def both(ref, cols):
        return [ref[m, :, cols] for m in range(2)]

    for k in range(4):
        cols = slice(k * FG // 2, (k + 1) * FG // 2)
        gwr_ref[:, cols] = sum(tn(secg[m], ggu[m, :, cols]) for m in range(2)).astype(BF)
        if k == 0:
            gather_h.forward()
        if k == 1:
            third.middle()
    for k in range(2):
        cols = slice(k * FG // 2, (k + 1) * FG // 2)
        gwr_ref[:, at_out + cols.start : at_out + cols.stop] = sum(
            tn(cotg_ref[m], act[m, :, cols]) for m in range(2)
        ).astype(BF)
    gather_h.finish()
    sums = HeadSum(b, h, (t0, t1, t2))
    gain = gain_ref[:, pl.ds(pl.multiple_of(h * XC, 128), XC)]
    dots = []
    ggain = jnp.zeros((1, XC), F32)
    for m in range(2):
        part[m, :, 0:XC] = nn(hlg[m], wr_ref[:, at_mix:at_att])
        gattn_ref[m] = nn(hlg[m], wr_ref[:, at_att:at_out]).astype(BF)
        gate = gate_ref[m]
        si = gate * sigmoid(gate)
        n = ylow_ref[m].astype(F32) * si * r_ref[:, m : m + 1]
        up = part[m, :, 0:XC]
        ggain = ggain + jnp.sum(up * n, axis=0, keepdims=True)
        dots.append(jnp.sum(up * gain * n, axis=1, keepdims=True))
    ggain_ref[...] = ggain
    sums.begin(dots)
    third.finish()
    for m in range(2):
        out_ref[m] = hid[m] + third.result(m)
    per = max(nb // NH, 1)
    mix_to, att_to = arrange(per, XC, 0), arrange(per, 128, 1)
    for m in range(2):
        act[m] = (nn(gated_ref[m], mix_to) + nn(attnl_ref[m], att_to)).astype(BF)
    for k in range(2):
        cols = slice(k * FG // 2, (k + 1) * FG // 2)
        gwr_ref[:, at_mix + cols.start : at_mix + cols.stop] = sum(tn(hlg[m], act[m, :, cols]) for m in range(2)).astype(BF)
    totals = sums.finish()
    for m in range(2):
        gate = gate_ref[m]
        sg = sigmoid(gate)
        si = gate * sg
        low = ylow_ref[m].astype(F32)
        scale = r_ref[:, m : m + 1]
        n = low * si * scale
        grad = scale * (part[m, :, 0:XC] * gain - n * (totals[m] * (1.0 / DI)))
        gy_ref[m] = (grad * si).astype(BF)
        ggate_ref[m] = (grad * low * (sg * (1.0 + gate * (1.0 - sg)))).astype(BF)


def feed(nb, gated, attnl, x, cot, cotg, wr, gains, ylow, gate, r, gain):
    T = gated.shape[1]
    tok = T // NH
    outs = [
        vm((2, tok, D), F32), vm((2, tok, D), F32), vm((2, T, XC), BF), vm((2, T, XC), BF), vm((2, T, 128), BF),
        vm((D, WRC), BF), vm((1, D), F32), vm((1, XC), F32),
    ]
    scratch = (
        [
            pltpu.VMEM((2, T, D), F32), pltpu.VMEM((2, T, D), F32), pltpu.VMEM((2, T, D), BF), pltpu.VMEM((2, T, D), BF),
            pltpu.VMEM((2, T, FG), BF), pltpu.VMEM((2, T, 2 * FG), BF), pltpu.VMEM((2, T, FG), F32),
            pltpu.VMEM((2, tok, D), F32),
        ]
        + HeadScatter.scratch(tok) * 3 + HeadGather.scratch() * 2 + HeadSum.scratch(T)
    )
    return call(
        functools.partial(feed_kernel, nb, T), outs, scratch,
        (gated, attnl, x, cot, cotg, wr, gains, ylow, gate, r, gain), "feed", 3,
    )


def head_select(m):
    return (lanes((XC, 128)) == 8 * m + rows_of((XC, 128)) // MHDIM).astype(F32)


def exact(a, b):
    return jnp.dot(a, b, precision=high, preferred_element_type=F32)


def back_kernel(
    nb, T, reach,
    gy_ref, gattn_ref, q_ref, kvh_ref, attnf_ref, lse_ref, pre_ref, xin_ref, bc_ref, dt_ref, sin_ref, ggate_ref,
    starts_ref, cw_ref, cb_ref, dtb_ref, alog_ref, skip_ref, cos_ref, sine_ref, normed_ref, w1_ref, x_ref, gh_ref, gains_ref,
    gin_ref, gw1_ref, gcw_ref, gsmall_ref, gn1_ref,
    cin, xs, bs, cs, cumt, stept, gx, gbm, gcm, gcin, gq, gkv, gkvs, gkvr, gproj, gnp, rowq,
    pair_b, pair_k, pair_kr, pair_r, yb_s, yb_r, edge_s, edge_r,
    c0, c1, c2, c3, c4, h0, h1, w0, w1, w2, w3, w4, w5, es, er, ps, pr,
):
    b, h = place()
    tok = T // NH
    core, y = lax.rem(h, 2), h // 2
    barrier(
        head_edges(b, h) + Scan.edges(b, h, nb, reach) + halo_edges(b, h, nb, reach)
        + [((h == NH - 1) & (b + 1 < nb), (b + 1, jnp.int32(i))) for i in range(NH)]
        + [(b >= 1, (b - 1, jnp.int32(NH - 1)))]
    )
    scan = Scan(-1, b, h, nb, reach, (c0, c1, c2, c3, c4))
    halo = Halo(-1, lambda d: gkvs.at[d], lambda d: gkvr.at[d], b, h, nb, reach, (h0, h1))
    pos = b * T + rows_of((T, 1))
    first = [doc_start(starts_ref, m, pos) for m in range(2)]
    last = [f[T - 1 :, :] for f in first]
    seen = lanes((T, T)) + b * T
    lane = lanes((T, 128))
    for m in range(2):
        for chunk in range((XC + 256) // 128):
            cols = pl.ds(chunk * 128, 128)
            total = pre_ref[m, :, cols]
            act = total * sigmoid(total)
            if chunk < XC // 128:
                xs[m, :, cols] = act
            elif chunk == XC // 128:
                bs[m] = act.astype(BF)
            else:
                cs[m] = act.astype(BF)
    z, step, a_neg, cum = decays_of(dt_ref, dtb_ref, alog_ref, h, T)
    cumt[...] = cum.T[:16]
    stept[...] = step.T[:16]
    cum_last = cum[T - 1 :, :]
    live = jnp.exp(cum) * by_batch(lambda m: jnp.broadcast_to((first[m] < b * T).astype(F32), (T, 128)))
    kept = jnp.exp(cum_last - cum) * by_batch(lambda m: jnp.broadcast_to((pos >= last[m]).astype(F32), (T, 128)))
    omega = kept * step
    for m in range(2):
        u = (gy_ref[m].astype(F32) * widen(live, 8 * m)).astype(BF)
        scan.sums[m, 0:XC, :] = tn(u, cs[m])
        decay = jnp.where(last[m] < b * T, jnp.exp(cumt[8 * m : 8 * m + 8, T - 1 : T]), 0.0)
        scan.sums[m, XC : XC + 8, :] = jnp.broadcast_to(decay, (8, 128))
        scan.sums[m, XC + 8 :, :] = jnp.zeros((8, 128), F32)
    scan.send_step(0)

    gkv[...] = jnp.zeros_like(gkv)
    for m in range(2):
        for i in range(2):
            mine = slice(i * HDIM, (i + 1) * HDIM)
            query, grad = q_ref[m, :, mine], gattn_ref[m, :, mine]
            delta = jnp.sum(grad.astype(F32) * attnf_ref[m, :, mine], axis=1, keepdims=True)
            lse = lse_ref[:, 2 * m + i : 2 * m + i + 1]

            def block(d, acc):
                at = seen - d * T
                keys = kvh_ref[d, 0, :, m * HDIM : (m + 1) * HDIM]
                vals = kvh_ref[d, 1, :, m * HDIM : (m + 1) * HDIM]
                probs = jnp.where((at <= pos) & (at >= first[m]), jnp.exp(nt(query, keys) * SCALE - lse), 0.0)
                ds = (probs * (nt(grad, vals) - delta)).astype(BF)
                gkv[d, 0, :, m * HDIM : (m + 1) * HDIM] += tn(ds, query) * SCALE
                gkv[d, 1, :, m * HDIM : (m + 1) * HDIM] += tn(probs.astype(BF), grad)
                return acc + nn(ds, keys)

            gq[m, :, mine] = lax.fori_loop(0, reach + 1, block, jnp.zeros((T, HDIM), F32)) * SCALE
    gkvs[...] = gkv[...].astype(BF)
    halo.begin()
    scan.join(0)
    scan.send_step(1)

    row_sums = jnp.zeros((T, 128), F32)
    rowq[...] = jnp.zeros_like(rowq)
    skip = wide_row(skip_ref, h)
    gskip = jnp.zeros((1, 128), F32)
    for m in range(2):
        both = nt(cs[m], bs[m])
        allowed = (seen <= pos) & (seen >= first[m])
        gboth = jnp.zeros((T, T), F32)
        for i in range(HG):
            l = 8 * m + i
            mine = slice(i * MHDIM, (i + 1) * MHDIM)
            grad = gy_ref[m, :, mine]
            decay = jnp.exp(jnp.where(allowed, cum[:, l : l + 1] - cumt[l : l + 1, :], FAR))
            srow = stept[l : l + 1, :]
            ld = decay * nt(grad, xs[m, :, mine].astype(BF))
            gboth = gboth + ld * srow
            q = ld * both
            rowq[l : l + 1, :] = jnp.sum(q, axis=0, keepdims=True)
            row_sums = jnp.where(lane == l, jnp.sum(q * srow, axis=1, keepdims=True), row_sums)
            gx[m, :, mine] = tn((decay * both * srow).astype(BF), grad)
        low = gboth.astype(BF)
        gcm[m] = nn(low, bs[m])
        gbm[m] = tn(low, cs[m])
        gyf = gy_ref[m].astype(F32)
        gskip = gskip + exact(jnp.sum(gyf * xs[m], axis=0, keepdims=True), head_select(m))
        gx[m] = gx[m] + skip * gyf
        u = gyf * widen(live, 8 * m)
        carried = nt(cs[m], sin_ref[m, 0:XC])
        row_sums = row_sums + exact(u * carried, head_select(m))
        gcm[m] += nn(u.astype(BF), sin_ref[m, 0:XC])
        if m == 0 and len(scan.steps) > 2:
            scan.join(1)
            scan.send_step(2)
    for i in range(2, len(scan.steps) - 1):
        scan.join(i)
        scan.send_step(i + 1)

    halo.finish_recv()
    for k in range(2):
        total = gkv[0, k]
        for d in range(1, reach + 1):
            total = total + jnp.where(b + d < nb, gkvr[d, k].astype(F32), 0.0)
        gkv[0, k] = total
    pair_k[...] = gkv[0, 1 - core].astype(BF)
    swap_k = copy_to(pair_k, pair_kr, ps.at[0], pr.at[0], (b, other(h, 1)))
    swap_k.start()

    end = len(scan.steps) - 1
    scan.receive(end)
    colq = jnp.concatenate([rowq[...], jnp.zeros((112, T), F32)], axis=0).T
    gstep = colq
    gcum = row_sums - step * colq
    glast = jnp.zeros((1, 128), F32)
    for m in range(2):
        adjoint = c1[end, m, 0:XC]
        read = nt(bs[m], adjoint)
        wide = widen(omega, 8 * m)
        gx[m] += wide * read
        gbm[m] += nn((xs[m] * wide).astype(BF), adjoint)
        gw = exact(xs[m] * read, head_select(m))
        gstep = gstep + kept * gw
        term = omega * gw
        gcum = gcum - term
        glast = glast + jnp.sum(term, axis=0, keepdims=True)
        through = jnp.where(last[m] < b * T, jnp.exp(cum_last), 0.0)
        overlap = adjoint.astype(F32) * sin_ref[m, 0:XC].astype(F32)
        per_head = jnp.sum(
            lax.dot_general(overlap, head_select(m), (((0,), (0,)), ((), ())), precision=high, preferred_element_type=F32),
            axis=0, keepdims=True,
        )
        glast = glast + through * per_head
    gcum = gcum + jnp.where(rows_of((T, 128)) == T - 1, glast, 0.0)
    gda = exact(triangle(T, upper=True), gcum)
    gstep = gstep + gda * a_neg
    gz = jnp.where(valid_row(), gstep * sigmoid(z), 0.0)
    small = jnp.concatenate(
        [
            jnp.sum(gz, axis=0, keepdims=True),
            jnp.sum(gda * step, axis=0, keepdims=True) * a_neg,
            gskip,
            jnp.zeros((5, 128), F32),
        ],
        axis=0,
    )
    gsmall_ref[...] = small + pltpu.roll(small, 120, 1)

    gcw_ref[...] = jnp.zeros_like(gcw_ref)
    gcin[...] = jnp.zeros_like(gcin)
    for m in range(2):
        cin[:, 0:XC] = xin_ref[m].astype(F32)
        cin[:, XC:] = bc_ref[m].astype(F32)
        for chunk in range((XC + 256) // 128):
            cols = pl.ds(chunk * 128, 128)
            taps, _ = group_taps(h, cw_ref, cb_ref, chunk)
            pre = pre_ref[m, :, cols]
            sg = sigmoid(pre)
            if chunk < XC // 128:
                up = gx[m, :, cols]
            elif chunk == XC // 128:
                up = gbm[m]
            else:
                up = gcm[m]
            gs = up * (sg * (1.0 + pre * (1.0 - sg)))
            gcw_ref[4:5, cols] += jnp.sum(gs, axis=0, keepdims=True)
            for back in range(4):
                j = 3 - back
                kept_gs = jnp.where(pos - first[m] >= back, gs, 0.0)
                gcw_ref[j : j + 1, cols] += jnp.sum(
                    jnp.where(pos - first[m] >= back, gs * cin[pl.ds(LAG - back, T), cols], 0.0), axis=0, keepdims=True
                )
                gcin[m, pl.ds(LAG - back, T), cols] += kept_gs * taps[j : j + 1]

    for m in range(2):
        pair_b[m] = gcin[m, :, pl.ds(pl.multiple_of(XC + (1 - core) * 128, 128), 128)].astype(BF)
    swap_b = copy_to(pair_b, pair_r, ps.at[1], pr.at[1], (b, other(h, 1)))
    swap_b.start()
    swap_k.wait()
    packed = gkv[0, core] + pair_kr[...].astype(F32)
    turned = rotate_pair(packed, cos_ref[...], -sine_ref[...])
    packed = jnp.where(core == 0, turned, packed)
    for m in range(2):
        gproj[m, 0:LAG, 0:XC] = jnp.zeros((LAG, XC), BF)
        gproj[m, LAG:, 0:XC] = ggate_ref[m]
        gproj[m, :, XC : 2 * XC] = gcin[m, :, 0:XC].astype(BF)
        gproj[m, 0:LAG, 2 * XC + 128 :] = jnp.zeros((LAG, 256), BF)
        gproj[m, LAG:, 2 * XC + 128 : 2 * XC + 256] = rotate_pair(gq[m], cos_ref[...], -sine_ref[...]).astype(BF)
        mine = packed if m == 0 else pltpu.roll(packed, HDIM, 1)
        gdt = pltpu.roll(gz, HDIM - 8 * m, 1)
        gproj[m, LAG:, 2 * XC + 256 :] = jnp.where(
            lane < HDIM, mine, jnp.where(lane < HDIM + HG, gdt, 0.0)
        ).astype(BF)
    swap_b.wait()
    for m in range(2):
        total = gcin[m, :, pl.ds(pl.multiple_of(XC + core * 128, 128), 128)] + pair_r[m].astype(F32)
        gcin[m, :, 0:128] = total
        yb_s[m] = total.astype(BF)
    swap_y = copy_to(yb_s, yb_r, ps.at[2], pr.at[2], (b, other(h, 2)))
    swap_y.start()
    swap_y.wait()
    half = lanes((LAG + T, 128)) // HDIM == y
    for m in range(2):
        total = gcin[m, :, 0:128] + yb_r[m].astype(F32)
        gproj[m, :, 2 * XC : 2 * XC + 128] = jnp.where(half, total, 0.0).astype(BF)

    for m in range(2):
        gnp[m] = nt(gproj[m], w1_ref[...])
    scatter = HeadScatter(
        lambda m, head: gnp[m, pl.ds(pl.multiple_of(LAG + head * tok, LAG), tok), :], b, h, (w0, w1, w2, w3), (w4, w5)
    )
    scatter.begin()
    for m in range(2):
        edge_s[m] = gnp[m, 0:LAG, :].astype(BF)

    def edge(i):
        return copy_to(edge_s, edge_r.at[i], es.at[0], er.at[i], (b - 1, jnp.int32(NH - 1)))

    @pl.when(b >= 1)
    def _():
        edge(h).start()

    scatter.middle()
    third = W1C // 3
    for k in range(3):
        cols = slice(k * third, (k + 1) * third)
        gw1_ref[:, cols] = sum(tn(normed_ref[m], gproj[m, :, cols]) for m in range(2)).astype(BF)
    scatter.finish()

    @pl.when(b >= 1)
    def _():
        edge(h).wait_send()

    mine = (h == NH - 1) & (b + 1 < nb)

    @pl.when(mine)
    def _():
        for i in range(NH):
            edge(i).wait_recv()

    @pl.when(jnp.logical_not(mine))
    def _():
        edge_r[...] = jnp.zeros_like(edge_r)

    n1 = gains_ref[6:7, :]
    gn1 = jnp.zeros((1, D), F32)
    for m in range(2):
        gnp[m, 0:tok, :] = scatter.result(m)
        gnp[m, tok - LAG : tok, :] += sum(edge_r[i, m].astype(F32) for i in range(NH))
        value = x_ref[m].astype(F32)
        scale = lax.rsqrt(jnp.mean(value * value, axis=1, keepdims=True) + EPS)
        grad, part = norm_back(value, scale, n1, gnp[m, 0:tok, :])
        gn1 = gn1 + part
        gin_ref[m] = gh_ref[m] + grad
    gn1_ref[...] = gn1
    scan.finish()
    halo.finish_send()


def back(nb, reach, *args):
    gy, q = args[0], args[2]
    T = q.shape[1]
    tok = T // NH
    dma = pltpu.SemaphoreType.DMA
    outs = [vm((2, tok, D), F32), vm((D, W1C), BF), vm((8, XC + 256), F32), vm((8, 128), F32), vm((1, D), F32)]
    scratch = (
        [
            pltpu.VMEM((LAG + T, XC + 256), F32), pltpu.VMEM((2, T, XC), F32), pltpu.VMEM((2, T, 128), BF),
            pltpu.VMEM((2, T, 128), BF), pltpu.VMEM((16, T), F32), pltpu.VMEM((16, T), F32),
            pltpu.VMEM((2, T, XC), F32), pltpu.VMEM((2, T, 128), F32), pltpu.VMEM((2, T, 128), F32),
            pltpu.VMEM((2, LAG + T, XC + 256), F32), pltpu.VMEM((2, T, 128), F32),
            pltpu.VMEM((reach + 1, 2, T, 128), F32), pltpu.VMEM((reach + 1, 2, T, 128), BF),
            pltpu.VMEM((reach + 1, 2, T, 128), BF), pltpu.VMEM((2, LAG + T, W1C), BF),
            pltpu.VMEM((2, LAG + T, D), F32), pltpu.VMEM((16, T), F32),
            pltpu.VMEM((2, LAG + T, 128), BF), pltpu.VMEM((T, 128), BF), pltpu.VMEM((T, 128), BF),
            pltpu.VMEM((2, LAG + T, 128), BF),
            pltpu.VMEM((2, LAG + T, 128), BF), pltpu.VMEM((2, LAG + T, 128), BF),
            pltpu.VMEM((2, LAG, D), BF), pltpu.VMEM((NH, 2, LAG, D), BF),
        ]
        + Scan.scratch(reach) + Halo.scratch(reach) + HeadScatter.scratch(tok)
        + [dma((1,)), dma((NH,)), dma((3,)), dma((3,))]
    )
    return call(functools.partial(back_kernel, nb, T, reach), outs, scratch, args, "back", 4, smem=(12, 15, 16, 17))


class LineReduce:
    def __init__(self, src, bufs, b, h, nb):
        self.src, self.h, self.nz = src, h, nb // 2
        self.z, self.x = b // 2, lax.rem(b, 2)
        self.total, self.from_x, self.from_l, self.from_r, self.xs, self.xr, self.ls, self.lr, self.rs, self.rr = bufs
        order, low, top = [], 0, self.nz - 1
        while low <= top:
            order += [top] if low == top else [top, low]
            low, top = low + 1, top - 1
        self.order = order

    @staticmethod
    def scratch(nb, cols):
        nz, rpb = nb // 2, D // nb
        return [pltpu.VMEM((nz, rpb, cols), BF)] * 4 + [pltpu.SemaphoreType.DMA((nz,))] * 6

    def to_x(self, z):
        return copy_to(
            self.src.at[z, 1 - self.x], self.from_x.at[z], self.xs.at[z], self.xr.at[z], (2 * self.z + 1 - self.x, self.h)
        )

    def up(self, z):
        return copy_to(
            self.total.at[z], self.from_l.at[z], self.rs.at[z], self.lr.at[z], (2 * (self.z + 1) + self.x, self.h)
        )

    def down(self, z):
        return copy_to(
            self.total.at[z], self.from_r.at[z], self.ls.at[z], self.rr.at[z], (2 * (self.z - 1) + self.x, self.h)
        )

    def begin(self):
        for z in self.order:
            self.to_x(z).start()

    def step(self, k):
        z = self.order[k]
        self.to_x(z).wait_recv()
        self.total[z] = (self.src[z, self.x].astype(F32) + self.from_x[z].astype(F32)).astype(BF)

        @pl.when(self.z < z)
        def _():
            @pl.when(self.z >= 1)
            def _():
                self.up(z).wait_recv()
                self.total[z] = (self.total[z].astype(F32) + self.from_l[z].astype(F32)).astype(BF)

            self.up(z).start()

        @pl.when(self.z > z)
        def _():
            @pl.when(self.z + 1 < self.nz)
            def _():
                self.down(z).wait_recv()
                self.total[z] = (self.total[z].astype(F32) + self.from_r[z].astype(F32)).astype(BF)

            self.down(z).start()

    def finish(self, result):
        for z in range(self.nz):
            self.to_x(z).wait_send()

            @pl.when(self.z < z)
            def _():
                self.up(z).wait_send()

            @pl.when(self.z > z)
            def _():
                self.down(z).wait_send()

            @pl.when(self.z == z)
            def _():
                result[...] = self.src[z, self.x].astype(F32) + self.from_x[z].astype(F32)

                @pl.when(self.z >= 1)
                def _():
                    self.up(z).wait_recv()
                    result[...] += self.from_l[z].astype(F32)

                @pl.when(self.z + 1 < self.nz)
                def _():
                    self.down(z).wait_recv()
                    result[...] += self.from_r[z].astype(F32)


class Sum:
    def __init__(self, bufs, b, h, nb):
        self.b, self.h, self.nb = b, h, nb
        self.acc, self.got, self.send, self.recv = bufs
        self.steps = Sum.step_list(nb)

    @staticmethod
    def step_list(nb):
        steps = [("h", 1), ("h", 2)]
        d = 1
        while d < nb:
            steps.append(("b", d))
            d *= 2
        return steps

    @staticmethod
    def scratch(nb, shape):
        n = len(Sum.step_list(nb))
        return [
            pltpu.VMEM((n + 1,) + shape, F32), pltpu.VMEM((n,) + shape, F32),
            pltpu.SemaphoreType.DMA((n,)), pltpu.SemaphoreType.DMA((n,)),
        ]

    def peer(self, i):
        kind, d = self.steps[i]
        return (self.b, other(self.h, d)) if kind == "h" else (other(self.b, d), self.h)

    def edges(self):
        return [(True, self.peer(i)) for i in range(len(self.steps))]

    def copy(self, i):
        return copy_to(self.acc.at[i], self.got.at[i], self.send.at[i], self.recv.at[i], self.peer(i))

    def begin(self, value):
        self.acc[0] = value
        self.copy(0).start()

    def step(self, i):
        self.copy(i).wait()
        self.acc[i + 1] = self.acc[i] + self.got[i]
        if i + 1 < len(self.steps):
            self.copy(i + 1).start()

    def result(self):
        return self.acc[len(self.steps)]


def reduce_kernel(
    nb,
    gwr_ref, gw1_ref, small_ref,
    w1all_ref, *rest,
):
    b, h = place()
    rpb = D // nb
    per = nb // NH
    share = (XC + 128) // per
    easy = share % 128 == 0
    if easy:
        ffn_ref, mix_ref, att_ref, fo_ref, small_out = rest[:5]
        rest = rest[5:]
    else:
        wr_out, small_out = rest[:2]
        rest = rest[2:]
    a, rest = rest[:10], rest[10:]
    c, rest = rest[:10], rest[10:]
    s, rest = rest[:4], rest[4:]
    res1, res2, g0, g1 = rest[:4]
    rest = rest[4:]
    line2, line1 = LineReduce(gwr_ref, a, b, h, nb), LineReduce(gw1_ref, c, b, h, nb)
    total = Sum(s, b, h, nb)
    edges = head_edges(b, h) + line_edges(b, h, nb) + total.edges()
    if easy:
        msg, got, fmsg, fgot, msend, mrecv, fsend, frecv = rest
        target = [(per * h + i, b // per) for i in range(per)]
        source = [(per * h + i, b // per) for i in range(per)]
        for i in range(per):
            away = (target[i][0] != b) | (target[i][1] != h)
            edges.append((away, target[i]))
    barrier(edges)
    line2.begin()
    line1.begin()
    total.begin(small_ref[...])
    n = len(line2.order)
    for k in range(n):
        line2.step(k)
        if k < len(total.steps):
            total.step(k)
    line2.finish(res2)
    if easy:
        for i, to in enumerate((h // 2, 2 + h // 2)):
            fmsg[i] = res2[:, i * FG : (i + 1) * FG].astype(BF)
            slot = lax.rem(h, 2)

            @pl.when(to != h)
            def _():
                copy_to(fmsg.at[i], fgot.at[slot], fsend.at[i], frecv.at[slot], (b, to)).start()

            @pl.when(to == h)
            def _():
                fgot[slot] = fmsg[i]

        for i in range(per):
            for j in range(2):
                msg[i, j] = res2[:, 2 * FG + j * FG + i * share : 2 * FG + j * FG + (i + 1) * share].astype(BF)
            bb, hh = target[i]
            slot = lax.rem(b, per)
            away = (bb != b) | (hh != h)

            @pl.when(away)
            def _():
                copy_to(msg.at[i], got.at[slot], msend.at[i], mrecv.at[slot], (bb, hh)).start()

            @pl.when(jnp.logical_not(away))
            def _():
                got[slot] = msg[i]
    else:
        wr_out[...] = res2[...]
    for k in range(n):
        line1.step(k)
        if n + k < len(total.steps):
            total.step(n + k)
    for k in range(2 * n, len(total.steps)):
        total.step(k)
    line1.finish(res1)
    w1all_ref[h] = res1[...].astype(BF)
    gather = HeadGather(lambda i: w1all_ref.at[i], b, h, (g0, g1))
    gather.begin()
    small_out[...] = total.result()
    if easy:
        for j in range(2):
            src_h = 2 * lax.rem(h, 2) + j

            @pl.when(src_h != h)
            def _():
                copy_to(fmsg.at[0], fgot.at[j], fsend.at[0], frecv.at[j], (b, src_h)).wait_recv()

            ffn_ref[:, j * FG : (j + 1) * FG] = fgot[j].astype(F32)
        for j in range(per):
            bb, hh = source[j]

            @pl.when((bb != b) | (hh != h))
            def _():
                copy_to(msg.at[0], got.at[j], msend.at[0], mrecv.at[j], (bb, hh)).wait_recv()

            out = got[j, 0].astype(F32).T
            cols = slice(j * rpb, (j + 1) * rpb)
            mix_ref[:, cols] = out[: XC // per]
            att_ref[:, cols] = out[XC // per :]
            fo_ref[:, cols] = got[j, 1].astype(F32).T
        for i, to in enumerate((h // 2, 2 + h // 2)):

            @pl.when(to != h)
            def _():
                copy_to(fmsg.at[i], fgot.at[0], fsend.at[i], frecv.at[0], (b, to)).wait_send()

        for i in range(per):
            bb, hh = target[i]

            @pl.when((bb != b) | (hh != h))
            def _():
                copy_to(msg.at[i], got.at[0], msend.at[i], mrecv.at[0], (bb, hh)).wait_send()

    gather.forward()
    gather.finish()


def reduce(nb, gwr, gw1, small):
    rpb, per = D // nb, nb // NH
    share = (XC + 128) // per
    easy = share % 128 == 0
    dma = pltpu.SemaphoreType.DMA
    outs = [vm((NH, rpb, W1C), BF)]
    if easy:
        outs += [
            vm((rpb, 2 * FG), F32), vm((XC // per, per * rpb), F32), vm((128 // per, per * rpb), F32),
            vm((FG // per, per * rpb), F32), vm(small.shape, F32),
        ]
    else:
        outs += [vm((rpb, WRC), F32), vm(small.shape, F32)]
    scratch = (
        LineReduce.scratch(nb, WRC) + LineReduce.scratch(nb, W1C) + Sum.scratch(nb, small.shape)
        + [pltpu.VMEM((rpb, W1C), F32), pltpu.VMEM((rpb, WRC), F32)] + HeadGather.scratch()
    )
    if easy:
        scratch += [
            pltpu.VMEM((per, 2, rpb, share), BF), pltpu.VMEM((per, 2, rpb, share), BF),
            pltpu.VMEM((2, rpb, FG), BF), pltpu.VMEM((2, rpb, FG), BF),
            dma((per,)), dma((per,)), dma((2,)), dma((2,)),
        ]
    shape = (nb // 2, 2, rpb)
    return call(
        functools.partial(reduce_kernel, nb), outs, scratch,
        (gwr.reshape(shape + (WRC,)), gw1.reshape(shape + (W1C,)), small), "reduce", 5,
    )


def on_device(
    inputs, cotangent, doc_starts, norm_one, mixer_in, conv_weight, conv_bias, dt_bias, a_log, d_skip, ssm_gain,
    mixer_out, attn_in, attn_out, norm_two, ffn_in, ffn_out,
):
    nb = lax.axis_size("blk")
    head = lax.axis_index("head")
    tok = inputs.shape[1]
    T = tok * NH
    longest = min(MAXLEN, T * nb // 2)
    reach = (longest + T - 2) // T
    shard = mixer_in.shape[0]
    rpb = shard * NH

    gains = jnp.stack([norm_one, norm_two], axis=1)
    mix_t, att_t, ffn_t = mixer_out.T, attn_out.T, ffn_out.T
    first, rest = [], []
    for i in range(NH):
        kv = QHEADS * HDIM + 128 * (i % 2) + HDIM * (i // 2)
        first.append(
            jnp.concatenate(
                [
                    mixer_in[:, i * XC : (i + 1) * XC],
                    mixer_in[:, DI + i * XC : DI + (i + 1) * XC],
                    mixer_in[:, 2 * DI + 128 * (i % 2) : 2 * DI + 128 * (i % 2) + 128],
                    attn_in[:, i * 128 : (i + 1) * 128],
                    attn_in[:, kv : kv + HDIM],
                    mixer_in[:, 2 * DI + 2 * STATE + i * HG : 2 * DI + 2 * STATE + (i + 1) * HG],
                    gains,
                    jnp.zeros((shard, 128 - HDIM - HG - 2), BF),
                ],
                axis=1,
            )
        )
        rest.append(
            jnp.concatenate(
                [
                    ffn_in[:, i * FG : (i + 1) * FG],
                    ffn_in[:, FF + i * FG : FF + (i + 1) * FG],
                    mix_t[:, i * XC : (i + 1) * XC],
                    att_t[:, i * 128 : (i + 1) * 128],
                    ffn_t[:, i * FG : (i + 1) * FG],
                ],
                axis=1,
            )
        )
    first, rest = jnp.stack(first), jnp.stack(rest)
    local_pieces = shard % 16 == 0
    if not local_pieces:
        first, rest = (
            lax.all_to_all(v, "head", split_axis=0, concat_axis=0, tiled=True).reshape(rpb, v.shape[2])
            for v in (first, rest)
        )
    lane = np.arange(128) % HDIM % (HDIM // 2)
    freq = jnp.asarray((10000.0 ** (-(lane.astype(np.float32) * 2.0 / HDIM))).astype(np.float32))[None, :]
    conv_b, gain = conv_bias[None, :], ssm_gain[None, :]

    (normed, gate, xin, bc, q, kv, dt, cotg, w1, wr, gain_rows, cosine, sine) = front(
        nb, inputs, cotangent, first, rest, freq, local_pieces
    )
    ylow, gated, attnf, attnl, r, lse, pre, state, kvh = mixer(
        nb, reach, xin, bc, q, kv, dt, gate, doc_starts, conv_weight, conv_b, dt_bias, a_log, d_skip, gain
    )
    result, gh, gy, ggate, gattn, gwr, gn2, ggain = feed(
        nb, gated, attnl, inputs, cotangent, cotg, wr, gain_rows, ylow, gate, r, gain
    )
    gin, gw1, gcw, gsmall, gn1 = back(
        nb, reach, gy, gattn, q, kvh, attnf, lse, pre, xin, bc, dt, state, ggate, doc_starts, conv_weight, conv_b,
        dt_bias, a_log, d_skip, cosine, sine, normed, w1, inputs, gh, gain_rows,
    )
    wide = DI + 2 * STATE
    conv = lax.dynamic_update_slice(jnp.zeros((5, DI), F32), gcw[:5, :XC], (0, head * XC))
    rows = [
        jnp.concatenate([conv, gcw[:5, XC:]], axis=1),
        lax.dynamic_update_slice(jnp.zeros((1, wide), F32), ggain, (0, head * XC)),
        jnp.pad(jnp.concatenate([gn1, gn2], axis=0), ((0, 0), (0, wide - D))),
        lax.dynamic_update_slice(jnp.zeros((8, wide), F32), gsmall[:3, :HG], (0, head * HG)),
    ]
    reduced = reduce(nb, gwr, gw1, jnp.concatenate(rows, axis=0))
    w1all, small = reduced[0].astype(F32), reduced[-1]
    part = lambda i, a, b: w1all[i, :, a:b]
    groups = range(NH)
    bc0, q0, kv0 = 2 * XC, 2 * XC + 128, 2 * XC + 256
    full_m = jnp.concatenate(
        [part(i, 0, XC) for i in groups]
        + [part(i, XC, 2 * XC) for i in groups]
        + [part(i + 2 * y, bc0 + HDIM * y, bc0 + HDIM * (y + 1)) for i in range(2) for y in range(2)]
        + [part(i, kv0 + HDIM, kv0 + HDIM + HG) for i in groups],
        axis=1,
    )
    full_a = jnp.concatenate(
        [part(i, q0, q0 + 128) for i in groups] + [part(i + 2 * y, kv0, kv0 + HDIM) for i in range(2) for y in range(2)],
        axis=1,
    )
    wide_m, wide_a = full_m.shape[1] // NH, full_a.shape[1] // NH
    g_mix_in = lax.dynamic_slice_in_dim(full_m, head * wide_m, wide_m, 1)
    g_att_in = lax.dynamic_slice_in_dim(full_a, head * wide_a, wide_a, 1)
    if len(reduced) == 6:
        g_ffn_in, g_mix_out, g_att_out, g_ffn_out = reduced[1:5]
    else:
        per = nb // NH
        blk = lax.axis_index("blk")
        mine = lax.all_gather(reduced[1][:, : 2 * FG].astype(BF), "head").reshape(NH, rpb, 2, FG)
        ffn = jnp.transpose(mine, (1, 2, 0, 3)).reshape(rpb, 2 * FF)
        g_ffn_in = lax.dynamic_slice_in_dim(ffn, head * (2 * FF // NH), 2 * FF // NH, 1).astype(F32)
        outs = lax.all_gather(reduced[1][:, 2 * FG :].astype(BF), ("blk", "head")).reshape(nb, NH, rpb, 2 * FG)
        outs = jnp.transpose(outs, (1, 3, 0, 2)).reshape(NH, 2, per, FG // per, D)
        outs = lax.dynamic_slice_in_dim(outs, head * (D // NH), D // NH, 4)
        outs = jnp.transpose(outs, (0, 2, 1, 3, 4)).reshape(nb, 2, FG // per, D // NH)
        outs = lax.dynamic_index_in_dim(outs, blk, 0, False).astype(F32)
        g_mix_out, g_att_out, g_ffn_out = outs[0, : XC // per], outs[0, XC // per :], outs[1]
    return (
        result, gin, small[6, :D], g_mix_in, small[:4], small[4], small[8, :MHEADS], small[9, :MHEADS],
        small[10, :MHEADS], small[5, :DI], g_mix_out, g_att_in, g_att_out, small[7, :D], g_ffn_in, g_ffn_out,
    )


def solution(mesh):
    both = ("blk", "head")
    tokens, rows, cols = P(None, both, None), P(both, None), P(None, both)
    split = P("blk", "head")
    return jax.shard_map(
        on_device,
        mesh=mesh,
        in_specs=(
            tokens, tokens, P(), P(both), rows, P(), P(), P(), P(), P(), P(), cols, rows, cols, P(both), rows, cols,
        ),
        out_specs=(
            tokens, tokens, P(), split, P(), P(), P(), P(), P(), P(), split, split, split, P(), split, split,
        ),
        check_vma=False,
    )
```

```python
import functools
import types

import jax
import jax.numpy as jnp
import numpy as np
from jax import lax
from jax.experimental import pallas as pl
from jax.experimental.pallas import tpu as pltpu
from jax.sharding import PartitionSpec as P

MHEADS = 24
MHDIM = 64
STATE = 128
QHEADS = 8
HDIM = 64
FF = 2048
DI = 1536
D = 1024
MAXLEN = 4096
NH = 4
HG = MHEADS // NH
XC = HG * MHDIM
FG = FF // NH
WA = XC + 3 * 128
WB = 2 * XC + 128
WC = 3 * FG
LAG = 16
EPS = 1e-5
FAR = -1e30
SCALE = HDIM**-0.5
MESH = pl.DeviceIdType.MESH
BF = jnp.bfloat16
F32 = jnp.float32
VMEM_LIMIT = 62 * 2**20
high = lax.Precision.HIGHEST


def nn(a, b):
    return lax.dot_general(a, b, (((1,), (0,)), ((), ())), preferred_element_type=F32)


def nt(a, b):
    return lax.dot_general(a, b, (((1,), (1,)), ((), ())), preferred_element_type=F32)


def tn(a, b):
    return lax.dot_general(a, b, (((0,), (0,)), ((), ())), preferred_element_type=F32)


def other(index, step):
    return index + step - 2 * step * lax.rem(index // step, 2)


def copy_to(src, dst, send, recv, where):
    return pltpu.make_async_remote_copy(
        src_ref=src, dst_ref=dst, send_sem=send, recv_sem=recv, device_id=where, device_id_type=MESH
    )


def barrier(edges):
    sem = pltpu.get_barrier_semaphore()
    for there, where in edges:
        if there is True:
            pl.semaphore_signal(sem, inc=1, device_id=where, device_id_type=MESH)
        else:

            @pl.when(there)
            def _():
                pl.semaphore_signal(sem, inc=1, device_id=where, device_id_type=MESH)

    total = 0
    for there, _ in edges:
        total = total + (1 if there is True else there.astype(jnp.int32))
    pl.semaphore_wait(sem, total)


def lanes(shape):
    return lax.broadcasted_iota(jnp.int32, shape, len(shape) - 1)


def rows_of(shape):
    return lax.broadcasted_iota(jnp.int32, shape, len(shape) - 2)


def sigmoid(v):
    return 1.0 / (1.0 + jnp.exp(-v))


def widen(cols, first, count=HG, width=MHDIM):
    return jnp.concatenate(
        [
            jnp.broadcast_to(cols[:, first + i : first + i + 1], (cols.shape[0], width))
            for i in range(count)
        ],
        axis=1,
    )


class LineGather:
    def __init__(self, piece, b, h, nb, sems):
        self.piece, self.h, self.nz = piece, h, nb // 2
        self.z, self.x = b // 2, lax.rem(b, 2)
        self.line_recv, self.send_r, self.send_l, self.x_send, self.x_recv = sems

    @staticmethod
    def scratch(nb):
        return [pltpu.SemaphoreType.DMA((nb // 2,))] * 5

    def at(self, z, x=None):
        return self.piece(2 * z + (self.x if x is None else x))

    def to_x(self, z):
        return copy_to(
            self.at(z), self.at(z), self.x_send.at[z], self.x_recv.at[z], (2 * self.z + 1 - self.x, self.h)
        )

    def to_z(self, z, way):
        send = self.send_r if way > 0 else self.send_l
        return copy_to(
            self.at(z), self.at(z), send.at[z], self.line_recv.at[z], (2 * (self.z + way) + self.x, self.h)
        )

    def begin(self):
        self.hop(0)
        self.to_x(self.z).start()

    def hop(self, s):
        @pl.when((self.z - s >= 0) & (self.z + 1 < self.nz))
        def _():
            self.to_z(self.z - s, 1).start()

        @pl.when((self.z + s < self.nz) & (self.z >= 1))
        def _():
            self.to_z(self.z + s, -1).start()

    def advance(self, s):
        left, right = self.z - 1 - s, self.z + 1 + s
        more = s + 1 < self.nz - 1

        @pl.when(left >= 0)
        def _():
            self.to_z(left, 1).wait_recv()
            if more:

                @pl.when(self.z + 1 < self.nz)
                def _():
                    self.to_z(left, 1).start()

            self.to_x(left).start()

        @pl.when(right < self.nz)
        def _():
            self.to_z(right, -1).wait_recv()
            if more:

                @pl.when(self.z >= 1)
                def _():
                    self.to_z(right, -1).start()

            self.to_x(right).start()

    def finish(self):
        for z in range(self.nz):
            copy_to(
                self.at(z, 1 - self.x),
                self.at(z, 1 - self.x),
                self.x_send.at[z],
                self.x_recv.at[z],
                (2 * self.z + 1 - self.x, self.h),
            ).wait_recv()

    def done(self):
        for z in range(self.nz):
            self.to_x(z).wait_send()

            @pl.when((z <= self.z) & (self.z + 1 < self.nz))
            def _():
                self.to_z(z, 1).wait_send()

            @pl.when((z >= self.z) & (self.z >= 1))
            def _():
                self.to_z(z, -1).wait_send()


def line_edges(b, h, nb):
    return [
        (True, (other(b, 1), h)),
        (b >= 2, (b - 2, h)),
        (b + 2 < nb, (b + 2, h)),
    ]


def head_edges(b, h):
    return [(True, (b, other(h, 1))), (True, (b, other(h, 2))), (True, (b, NH - 1 - h))]


class HeadGather:
    def __init__(self, rows, b, h, sems):
        self.rows, self.b, self.h = rows, b, h
        self.send, self.recv = sems

    @staticmethod
    def scratch():
        return [pltpu.SemaphoreType.DMA((2, 3))] * 2

    def copy(self, m, i):
        pair, across = other(self.h, 1), other(self.h, 2)
        rows = self.rows(m, self.h if i < 2 else across)
        return copy_to(rows, rows, self.send.at[m, i], self.recv.at[m, i], (self.b, across if i == 1 else pair))

    def begin(self, m):
        self.copy(m, 1).start()
        self.copy(m, 0).start()

    def forward(self, m):
        self.copy(m, 1).wait_recv()
        self.copy(m, 2).start()

    def finish(self, m):
        self.copy(m, 0).wait_recv()
        self.copy(m, 2).wait_recv()

    def done(self):
        for m in range(2):
            for i in range(3):
                self.copy(m, i).wait_send()


class HeadScatter:
    def __init__(self, full, b, h, bufs):
        self.full, self.b, self.h = full, b, h
        self.send_c, self.recv_c, self.send_y, self.recv_y, self.send, self.recv = bufs

    @staticmethod
    def scratch(rows):
        return [
            pltpu.VMEM((2, 2, rows, D), BF),
            pltpu.VMEM((2, 2, rows, D), BF),
            pltpu.VMEM((2, rows, D), BF),
            pltpu.VMEM((2, rows, D), BF),
            pltpu.SemaphoreType.DMA((2, 2)),
            pltpu.SemaphoreType.DMA((2, 2)),
        ]

    def copy(self, m, i):
        src, dst = ((self.send_c, self.recv_c), (self.send_y, self.recv_y))[i]
        return copy_to(src.at[m], dst.at[m], self.send.at[m, i], self.recv.at[m, i], (self.b, other(self.h, i + 1)))

    def begin(self, m):
        core = lax.rem(self.h, 2)
        for y in range(2):
            self.send_c[m, y] = self.full(m, 2 * y + 1 - core).astype(BF)
        self.copy(m, 0).start()

    def middle(self, m):
        core, y = lax.rem(self.h, 2), self.h // 2
        self.copy(m, 0).wait_recv()
        self.send_y[m] = (self.full(m, 2 * (1 - y) + core) + self.recv_c[m, 1 - y].astype(F32)).astype(BF)
        self.copy(m, 1).start()

    def finish(self, m):
        self.copy(m, 1).wait_recv()

    def result(self, m):
        y = self.h // 2
        return self.full(m, self.h) + self.recv_c[m, y].astype(F32) + self.recv_y[m].astype(F32)

    def done(self):
        for m in range(2):
            for i in range(2):
                self.copy(m, i).wait_send()


class Todo:
    def __init__(self):
        self.steps = []

    def add(self, *steps):
        self.steps += steps

    def tick(self, count=1):
        for _ in range(min(count, len(self.steps))):
            self.steps.pop(0)()

    def drain(self, left=0):
        self.tick(max(len(self.steps) - left, 0))


def place():
    return lax.axis_index("blk"), lax.axis_index("head")


def rotate_pair(v, cosine, sine):
    lane = lax.rem(lanes(v.shape), HDIM)
    front = lane < HDIM // 2
    partner = jnp.where(front, pltpu.roll(v, 128 - HDIM // 2, 1), pltpu.roll(v, HDIM // 2, 1))
    return v * cosine + jnp.where(front, -partner, partner) * sine


def rope_tables(freq_ref, b, rows, ref_cos, ref_sin):
    pos = (b * rows + rows_of((rows, 128))).astype(F32)
    angle = pos * freq_ref[...]
    ref_cos[...] = jnp.cos(angle)
    ref_sin[...] = jnp.sin(angle)


def vm(shape, dtype):
    return jax.ShapeDtypeStruct(shape, dtype)


def run(body, ins, outs, scratch, name, cid, smem=(), hbm=()):
    names = list(ins) + list(outs) + list(scratch)

    def kernel(*refs):
        body(types.SimpleNamespace(**dict(zip(names, refs))))

    def space(n):
        return pl.BlockSpec(memory_space=pltpu.SMEM if n in smem else (pl.ANY if n in hbm else pltpu.VMEM))

    got = pl.pallas_call(
        kernel,
        out_shape=list(outs.values()),
        in_specs=[space(n) for n in ins],
        out_specs=[space(n) for n in outs],
        scratch_shapes=list(scratch.values()),
        compiler_params=pltpu.CompilerParams(
            collective_id=cid, has_side_effects=cid is not None, vmem_limit_bytes=VMEM_LIMIT
        ),
        name=name,
    )(*ins.values())
    return types.SimpleNamespace(**dict(zip(outs, got)))


class Moves:
    def __init__(self, refs, names, out):
        self.refs, self.names, self.out = refs, names, out
        self.waiting = []

    def copy(self, name):
        far, near = getattr(self.refs, name), getattr(self.refs, "v_" + name)
        src, dst = (near, far) if self.out else (far, near)
        return pltpu.make_async_copy(src, dst, self.refs.moved.at[self.names.index(name)])

    def start(self, *names):
        for n in names:
            self.copy(n).start()
            self.waiting.append(n)

    def wait(self, *names):
        for n in names:
            self.copy(n).wait()
            self.waiting.remove(n)

    def wait_all(self):
        self.wait(*list(self.waiting))


def group(prefix, shapes):
    return {f"{prefix}{i}": s for i, s in enumerate(shapes)}


def members(refs, prefix, count):
    return [getattr(refs, f"{prefix}{i}") for i in range(count)]


def doc_start(starts_ref, m, pos):
    first = jnp.zeros(pos.shape, jnp.int32)
    for k in range(starts_ref.shape[1]):
        s = starts_ref[m, k]
        first = jnp.where(pos >= s, s, first)
    return first


def head_row(ref, h, count=2):
    lane = lanes((1, 128))
    row = jnp.zeros((1, 128), F32)
    for i in range(HG):
        for m in range(count):
            row = jnp.where(lane == 8 * m + i, ref[h * HG + i], row)
    return row


def wide_row(ref, h):
    lane = lanes((1, XC)) // MHDIM
    row = jnp.zeros((1, XC), F32)
    for i in range(HG):
        row = jnp.where(lane == i, ref[h * HG + i], row)
    return row


def valid_row():
    lane = lanes((1, 128))
    return (lane < 16) & (lax.rem(lane, 8) < HG)


def triangle(n, upper=False):
    r, c = rows_of((n, n)), lanes((n, n))
    return ((c >= r) if upper else (c <= r)).astype(F32)


class Scan:
    ROWS = XC + 16

    def __init__(self, way, b, h, nb, reach, bufs):
        self.way, self.b, self.h, self.nb = way, b, h, nb
        self.steps = Scan.step_list(reach)
        self.send_buf, self.recv_buf, self.sums, self.send, self.recv = bufs

    @staticmethod
    def step_list(reach):
        steps, d = [], 1
        while d < reach:
            steps.append(d)
            d *= 2
        return steps + [1]

    @staticmethod
    def scratch(reach):
        n = len(Scan.step_list(reach))
        return [
            pltpu.VMEM((n, Scan.ROWS, 128), BF),
            pltpu.VMEM((n, Scan.ROWS, 128), BF),
            pltpu.VMEM((Scan.ROWS, 128), F32),
            pltpu.SemaphoreType.DMA((n,)),
            pltpu.SemaphoreType.DMA((n,)),
        ]

    @staticmethod
    def edges(b, h, nb, reach):
        out = []
        for d in sorted(set(Scan.step_list(reach))):
            out += [(b + d < nb, (b + d, h)), (b >= d, (b - d, h))]
        return out

    def has_to(self, d):
        return (self.b + d < self.nb) if self.way > 0 else (self.b >= d)

    def has_from(self, d):
        return (self.b >= d) if self.way > 0 else (self.b + d < self.nb)

    def copy(self, i):
        return copy_to(
            self.send_buf.at[i], self.recv_buf.at[i], self.send.at[i], self.recv.at[i],
            (self.b + self.way * self.steps[i], self.h),
        )

    def set(self, state, decay):
        self.sums[0:XC, :] = state
        self.sums[XC : XC + 8, :] = jnp.broadcast_to(decay, (8, 128))
        self.sums[XC + 8 :, :] = jnp.zeros((8, 128), F32)
        self.send_step(0)

    def send_step(self, i):
        self.send_buf[i] = self.sums[...].astype(BF)

        @pl.when(self.has_to(self.steps[i]))
        def _():
            self.copy(i).start()

    def receive(self, i):
        there = self.has_from(self.steps[i])

        @pl.when(there)
        def _():
            self.copy(i).wait_recv()

        @pl.when(jnp.logical_not(there))
        def _():
            self.recv_buf[i] = jnp.zeros((Scan.ROWS, 128), BF)

    def join(self, i):
        if i + 1 >= len(self.steps):
            return
        self.receive(i)
        early = self.recv_buf[i].astype(F32)
        for j in range(HG):
            mine = pl.ds(j * MHDIM, MHDIM)
            decay = self.sums[pl.ds(XC + j, 1), :]
            self.sums[mine, :] = self.sums[mine, :] + decay * early[j * MHDIM : (j + 1) * MHDIM]
        self.sums[pl.ds(XC, 8), :] = self.sums[pl.ds(XC, 8), :] * early[XC : XC + 8]
        self.send_step(i + 1)

    def last(self):
        end = len(self.steps) - 1
        self.receive(end)
        return self.recv_buf.at[end]

    def finish(self):
        for i, d in enumerate(self.steps):

            @pl.when(self.has_to(d))
            def _():
                self.copy(i).wait_send()


def halo_edges(b, h, nb, reach):
    out = []
    for d in range(1, reach + 1):
        out += [(b + d < nb, (b + d, h)), (b >= d, (b - d, h))]
    return out


class Halo:
    def __init__(self, way, src, dst, b, h, nb, reach, sems):
        self.way, self.src, self.dst, self.b, self.h, self.nb, self.reach = way, src, dst, b, h, nb, reach
        self.send, self.recv = sems

    @staticmethod
    def scratch(reach):
        return [pltpu.SemaphoreType.DMA((reach + 1,))] * 2

    def there(self, d, way):
        return (self.b + d < self.nb) if way > 0 else (self.b >= d)

    def copy(self, d):
        return copy_to(
            self.src(d), self.dst(d), self.send.at[d], self.recv.at[d], (self.b + self.way * d, self.h)
        )

    def begin(self):
        for d in range(1, self.reach + 1):

            @pl.when(self.there(d, self.way))
            def _():
                self.copy(d).start()

    def finish_recv(self):
        for d in range(1, self.reach + 1):

            @pl.when(self.there(d, -self.way))
            def _():
                self.copy(d).wait_recv()

    def finish_send(self):
        for d in range(1, self.reach + 1):

            @pl.when(self.there(d, self.way))
            def _():
                self.copy(d).wait_send()


class HeadSum:
    def __init__(self, b, h, bufs):
        self.b, self.h = b, h
        self.buf, self.send, self.recv = bufs

    @staticmethod
    def scratch(T):
        return [pltpu.VMEM((4, 8, T), F32), pltpu.SemaphoreType.DMA((3,)), pltpu.SemaphoreType.DMA((3,))]

    def copies(self):
        return [
            copy_to(self.buf.at[0], self.buf.at[1 + i], self.send.at[i], self.recv.at[i], (self.b, to))
            for i, to in enumerate((other(self.h, 1), other(self.h, 2), NH - 1 - self.h))
        ]

    def begin(self, column):
        T = self.buf.shape[2]
        self.buf[0] = jnp.broadcast_to(column, (T, 128)).T[:8]
        for c in self.copies():
            c.start()

    def finish(self):
        for c in self.copies():
            c.wait()
        T = self.buf.shape[2]
        total = self.buf[0] + self.buf[1] + self.buf[2] + self.buf[3]
        return jnp.concatenate([total, jnp.zeros((120, T), F32)], axis=0).T[:, 0:1]


def group_taps(h, w_ref, b_ref, chunk):
    if chunk < XC // 128:
        at = pl.ds(pl.multiple_of(h * XC + chunk * 128, 128), 128)
    else:
        at = pl.ds(DI + (chunk - XC // 128) * 128, 128)
    return w_ref[:, at], (None if b_ref is None else b_ref[:, at])


def decays_of(dt_ref, bias_ref, alog_ref, h, T):
    valid = valid_row()
    z = dt_ref[...] + head_row(bias_ref, h)
    step = jnp.where(valid, jnp.maximum(z, 0.0) + jnp.log1p(jnp.exp(-jnp.abs(z))), 0.0)
    a_neg = jnp.where(valid, -jnp.exp(head_row(alog_ref, h)), 0.0)
    cum = jnp.dot(triangle(T), step * a_neg, precision=high, preferred_element_type=F32)
    return z, step, a_neg, cum


def by_batch(pick):
    first, second = pick(0), pick(1)
    return jnp.where(lanes((first.shape[0], 128)) < 8, first, second)


def norm_back(value, scale, gain, upstream):
    n = value * scale
    uw = upstream * gain
    grad = scale * (uw - n * jnp.mean(n * uw, axis=1, keepdims=True))
    return grad, jnp.sum(upstream * n, axis=0, keepdims=True)


def arrange(per, width, first):
    total = XC + 128
    share, mix, att = total // per, XC // per, 128 // per
    n, src = lanes((width, total)), rows_of((width, total))
    i, u = n // share, lax.rem(n, share)
    if first == 0:
        hit = (u < mix) & (src == i * mix + u)
    else:
        hit = (u >= mix) & (src == i * att + u - mix)
    return hit.astype(F32).astype(BF)


def head_select(m):
    return (lanes((XC, 128)) == 8 * m + rows_of((XC, 128)) // MHDIM).astype(F32)


def exact(a, b):
    return jnp.dot(a, b, precision=high, preferred_element_type=F32)


class LineReduce:
    def __init__(self, src, bufs, b, h, nb):
        self.src, self.h, self.nz = src, h, nb // 2
        self.z, self.x = b // 2, lax.rem(b, 2)
        self.whole = len(bufs) == 10
        if self.whole:
            self.total, self.from_l, self.from_r, self.ls, self.lr, self.rs, self.rr, self.from_x, self.xs, self.xr = bufs
        else:
            self.total, self.from_l, self.from_r, self.ls, self.lr, self.rs, self.rr = bufs

    @staticmethod
    def scratch(nb, cols, whole=True):
        nz, rpb = nb // 2, D // nb
        buf, sem = pltpu.VMEM((nz, rpb, cols), BF), pltpu.SemaphoreType.DMA((nz,))
        return [buf] * 3 + [sem] * 4 + ([buf] + [sem] * 2 if whole else [])

    def to_x(self, z):
        return copy_to(
            self.src.at[z, 1 - self.x], self.from_x.at[z], self.xs.at[z], self.xr.at[z], (2 * self.z + 1 - self.x, self.h)
        )

    def up(self, z):
        return copy_to(
            self.total.at[z], self.from_l.at[z], self.rs.at[z], self.lr.at[z], (2 * (self.z + 1) + self.x, self.h)
        )

    def down(self, z):
        return copy_to(
            self.total.at[z], self.from_r.at[z], self.ls.at[z], self.rr.at[z], (2 * (self.z - 1) + self.x, self.h)
        )

    def start_x(self, j):
        self.to_x(jnp.where(self.z < self.nz // 2, self.nz - 1 - j, j)).start()

    def start_some(self, part, parts=4):
        for j in range(part * self.nz // parts, (part + 1) * self.nz // parts):
            self.start_x(j)

    def paired(self, z):
        if not self.whole:
            return self.src[z].astype(F32)
        self.to_x(z).wait_recv()
        return self.src[z, self.x].astype(F32) + self.from_x[z].astype(F32)

    def step(self, t):
        z_up, z_down = self.nz - 1 - t + self.z, t - (self.nz - 1) + self.z

        @pl.when(t >= self.z)
        def _():
            value = self.paired(z_up)

            @pl.when(self.z == 0)
            def _():
                self.total[z_up] = value.astype(BF)

            @pl.when(self.z > 0)
            def _():
                self.up(z_up).wait_recv()
                self.total[z_up] = (value + self.from_l[z_up].astype(F32)).astype(BF)

            self.up(z_up).start()

        @pl.when(z_down >= 0)
        def _():
            value = self.paired(z_down)

            @pl.when(self.z == self.nz - 1)
            def _():
                self.total[z_down] = value.astype(BF)

            @pl.when(self.z < self.nz - 1)
            def _():
                self.down(z_down).wait_recv()
                self.total[z_down] = (value + self.from_r[z_down].astype(F32)).astype(BF)

            self.down(z_down).start()

    def step_some(self, part, parts=3):
        for t in range(part * (self.nz - 1) // parts, (part + 1) * (self.nz - 1) // parts):
            self.step(t)

    def finish(self, result):
        z = self.z
        result[...] = self.paired(z)

        @pl.when(z >= 1)
        def _():
            self.up(z).wait_recv()
            result[...] += self.from_l[z].astype(F32)

        @pl.when(z + 1 < self.nz)
        def _():
            self.down(z).wait_recv()
            result[...] += self.from_r[z].astype(F32)

    def done(self):
        for z in range(self.nz):
            if self.whole:
                self.to_x(z).wait_send()

            @pl.when(self.z < z)
            def _():
                self.up(z).wait_send()

            @pl.when(self.z > z)
            def _():
                self.down(z).wait_send()


class PairReduce:
    def __init__(self, src, bufs, b, h, nb):
        self.src, self.h, self.nz = src, h, nb // 2
        self.z, self.x = b // 2, lax.rem(b, 2)
        self.from_x, self.xs, self.xr = bufs

    @staticmethod
    def scratch(nb, cols):
        nz, rpb = nb // 2, D // nb
        return [pltpu.VMEM((nz, rpb, cols), BF)] + [pltpu.SemaphoreType.DMA((nz,))] * 2

    def to_x(self, z):
        return copy_to(
            self.src.at[z, 1 - self.x], self.from_x.at[z], self.xs.at[z], self.xr.at[z], (2 * self.z + 1 - self.x, self.h)
        )

    def begin(self):
        for z in range(self.nz):
            self.to_x(z).start()

    def finish(self, out, cols):
        for z in range(self.nz):
            self.to_x(z).wait_recv()
            out[z, :, cols] = (self.src[z, self.x].astype(F32) + self.from_x[z].astype(F32)).astype(BF)

    def done(self):
        for z in range(self.nz):
            self.to_x(z).wait_send()


class Sum:
    def __init__(self, bufs, b, h, nb):
        self.b, self.h, self.nb = b, h, nb
        self.acc, self.got, self.send, self.recv = bufs
        self.steps = Sum.step_list(nb)

    @staticmethod
    def step_list(nb):
        steps = [("h", 1), ("h", 2)]
        d = 1
        while d < nb:
            steps.append(("b", d))
            d *= 2
        return steps

    @staticmethod
    def scratch(nb, shape):
        n = len(Sum.step_list(nb))
        return [
            pltpu.VMEM((n + 1,) + shape, F32), pltpu.VMEM((n,) + shape, F32),
            pltpu.SemaphoreType.DMA((n,)), pltpu.SemaphoreType.DMA((n,)),
        ]

    def peer(self, i):
        kind, d = self.steps[i]
        return (self.b, other(self.h, d)) if kind == "h" else (other(self.b, d), self.h)

    def edges(self):
        return [(True, self.peer(i)) for i in range(len(self.steps))]

    def copy(self, i):
        return copy_to(self.acc.at[i], self.got.at[i], self.send.at[i], self.recv.at[i], self.peer(i))

    def begin(self, value):
        self.acc[0] = value
        self.copy(0).start()

    def step(self, i):
        self.copy(i).wait()
        self.acc[i + 1] = self.acc[i] + self.got[i]
        if i + 1 < len(self.steps):
            self.copy(i + 1).start()

    def result(self):
        return self.acc[len(self.steps)]


def pack_rows(R, S):
    eye = (rows_of((S, S)) == lanes((S, S))).astype(F32)
    gain_cols = [jnp.sum(eye * ref[...].astype(F32), axis=1, keepdims=True) for ref in (R.n1, R.n2)]
    lane = lanes((S, 128))
    for i in range(NH):
        R.pa[i, :, 0:XC] = R.mixer_in[:, DI + i * XC : DI + (i + 1) * XC]
        bc = 2 * DI + 128 * (i % 2)
        R.pa[i, :, XC : XC + 128] = R.mixer_in[:, bc : bc + 128]
        R.pa[i, :, XC + 128 : XC + 256] = R.attn_in[:, i * 128 : (i + 1) * 128]
        kv = QHEADS * HDIM + 128 * (i % 2)
        kv = R.attn_in[:, kv : kv + 128].astype(F32)
        if i >= 2:
            kv = pltpu.roll(kv, HDIM, 1)
        pick = (rows_of((MHEADS, 128)) == i * HG + lanes((MHEADS, 128)) - HDIM) & (lanes((MHEADS, 128)) >= HDIM)
        pick = pick & (lanes((MHEADS, 128)) < HDIM + HG)
        dt = nn(R.mixer_in[:, 2 * DI + 2 * STATE :], pick.astype(F32).astype(BF))
        last = jnp.where(lane < HDIM, kv, dt)
        for k in range(2):
            last = jnp.where(lane == HDIM + HG + k, gain_cols[k], last)
        R.pa[i, :, XC + 256 :] = last.astype(BF)
    for i in range(NH):
        R.pb[i, :, 0:XC] = R.mixer_in[:, i * XC : (i + 1) * XC]
        R.pb[i, :, XC : 2 * XC] = R.mixer_out[:, i * XC : (i + 1) * XC]
        R.pb[i, :, 2 * XC :] = R.attn_out[:, i * 128 : (i + 1) * 128]
        R.pc[i, :, 0:FG] = R.ffn_out[:, i * FG : (i + 1) * FG]
        R.pc[i, :, FG : 2 * FG] = R.ffn_in[:, i * FG : (i + 1) * FG]
        R.pc[i, :, 2 * FG :] = R.ffn_in[:, FF + i * FG : FF + (i + 1) * FG]


LATE_OUT = ["normed", "xin", "bc", "q", "pre", "wa", "wb", "kvh", "gw_out"]


def forward_body(nb, T, reach, local, R):
    b, h = place()
    moves = Moves(R, LATE_OUT, True)
    core, y = lax.rem(h, 2), h // 2
    tok, rpb = T // NH, D // nb
    S, nz = rpb // NH, nb // 2
    pair = (b, other(h, 1))
    peers = (other(h, 1), other(h, 2), NH - 1 - h)
    if local:
        pack_rows(R, S)
    R.cb2[...] = R.cb[...].reshape(1, DI + 256)
    R.gain2[...] = R.gain[...].reshape(1, DI)
    barrier(
        head_edges(b, h)
        + line_edges(b, h, nb)
        + [((h == NH - 1) & (b + 1 < nb), (b + 1, jnp.int32(i))) for i in range(NH)]
        + [(b >= 1, (b - 1, jnp.int32(NH - 1)))]
        + Scan.edges(b, h, nb, reach)
        + halo_edges(b, h, nb, reach)
    )
    packs, weights = (R.pa, R.pb, R.pc), (R.v_wa, R.v_wb, R.wc)
    gather_x = HeadGather(lambda m, i: R.xg.at[m, pl.ds(LAG + i * tok, tok)], b, h, members(R, "gx", 2))
    gather_c = HeadGather(lambda m, i: R.cotg.at[m, pl.ds(i * tok, tok)], b, h, members(R, "gc", 2))
    spots = [(R.v_wa, slice(XC, WA)), (R.v_wa, slice(0, XC)), (R.v_wb, slice(0, WB))] + [(R.wc, slice(k * FG, (k + 1) * FG)) for k in range(3)]
    lines = [
        LineGather(
            lambda i, w=w, cols=cols: w.at[pl.ds(i * rpb, rpb), cols], b, h, nb, members(R, f"line{k}_", 5)
        )
        for k, (w, cols) in enumerate(spots)
    ]

    def piece(k, i):
        mine = weights[k].at[pl.ds(b * rpb + h * S, S)]
        return copy_to(packs[k].at[peers[i]], mine, R.ps.at[k, i], R.pr.at[k, i], (b, peers[i]))

    def start_pieces(k):
        if local:
            for i in range(3):
                piece(k, i).start()
            weights[k][pl.ds(b * rpb + h * S, S), :] = packs[k][h]
        else:
            weights[k][pl.ds(b * rpb, rpb), :] = packs[k][...]

    def wait_pieces(k):
        if local:
            for i in range(3):
                piece(k, i).wait_recv()

    start_pieces(0)
    for m in range(2):
        R.xg[m, pl.ds(LAG + h * tok, tok), :] = R.x[m]
        R.cotg[m, pl.ds(h * tok, tok), :] = R.cot[m]
    for m in range(2):
        gather_x.begin(m)

    def edge(i):
        return copy_to(
            R.x.at[:, pl.ds(tok - LAG, LAG)], R.xg.at[:, pl.ds(0, LAG)], R.es.at[i], R.er.at[0], (b + 1, jnp.int32(i))
        )

    @pl.when((h == NH - 1) & (b + 1 < nb))
    def _():
        for i in range(NH):
            edge(i).start()

    @pl.when(b == 0)
    def _():
        R.xg[:, 0:LAG, :] = jnp.zeros((2, LAG, D), BF)

    start_pieces(1)
    wait_pieces(0)
    lines[0].begin()
    lines[1].begin()
    rope_tables(R.freq, b, T, R.cosine, R.sine)
    for m in range(2):
        gather_x.forward(m)
    for m in range(2):
        gather_x.finish(m)

    @pl.when(b >= 1)
    def _():
        edge(0).wait_recv()

    for m in range(2):
        v = R.xg[m].astype(F32)
        R.wide[m] = v * lax.rsqrt(jnp.mean(v * v, axis=1, keepdims=True) + EPS)
    share = lambda part: range(part * (nz - 1) // 3, (part + 1) * (nz - 1) // 3)

    def ahead(part, *which):
        for s in share(part):
            for k in which:
                lines[k].advance(s)

    ahead(0, 0, 1)
    wait_pieces(1)
    start_pieces(2)
    for m in range(2):
        gather_c.begin(m)
    ahead(1, 0, 1)
    lines[2].begin()
    ahead(2, 0, 1)
    lines[0].finish()

    last = R.v_wa[:, XC + 256 :].astype(F32).T
    R.gains[...] = last[HDIM + HG + 2 - 8 : HDIM + HG + 2]
    n1 = R.gains[6:7, :]
    for m in range(2):
        R.v_normed[m] = (R.wide[m] * n1).astype(BF)
    lane = lanes((T, 128))
    mine_bc = pl.ds(pl.multiple_of(core * 128, 128), 128)
    kv = [nn(R.v_normed[m, LAG:], R.v_wa[:, XC + 256 :]) for m in range(2)]
    packed = jnp.where(lane < HDIM, kv[0], pltpu.roll(kv[1], HDIM, 1))
    turned = rotate_pair(packed, R.cosine[...], R.sine[...])
    R.v_kvh[0, core] = jnp.where(core == 0, turned, packed).astype(BF)
    halo = Halo(1, lambda d: R.v_kvh.at[0, core], lambda d: R.v_kvh.at[d, core], b, h, nb, reach, members(R, "halo", 2))
    halo.begin()
    for m in range(2):
        R.v_bc[m, :, mine_bc] = nn(R.v_normed[m], R.v_wa[:, XC : XC + 128]).astype(BF)
    swap = (
        lambda: copy_to(R.v_bc.at[:, :, mine_bc], R.v_bc.at[:, :, mine_bc], R.ss.at[0], R.sr.at[0], pair),
        lambda: copy_to(R.v_kvh.at[0, core], R.v_kvh.at[0, core], R.ss.at[1], R.sr.at[1], pair),
    )
    for c in swap:
        c().start()
    wait_pieces(2)
    lines[3].begin()
    dt = [pltpu.roll(kv[0], 128 - HDIM, 1), pltpu.roll(kv[1], 128 - HDIM + 8, 1)]
    R.dt[...] = (
        jnp.where(lane < HG, dt[0], jnp.where((lane >= 8) & (lane < 8 + HG), dt[1], 0.0)).astype(BF).astype(F32)
    )
    for m in range(2):
        q = nn(R.v_normed[m, LAG:], R.v_wa[:, XC + 128 : XC + 256])
        R.v_q[m] = rotate_pair(q, R.cosine[...], R.sine[...]).astype(BF)
    lines[1].finish()
    for m in range(2):
        R.v_xin[m] = nn(R.v_normed[m], R.v_wa[:, 0:XC]).astype(BF)

    scans = [Scan(1, b, h, nb, reach, members(R, f"scan{m}_", 5)) for m in range(2)]
    sums = [HeadSum(b, h, members(R, f"sumf{m}_", 3)) for m in range(2)]
    back_sums = [HeadSum(b, h, members(R, f"sumb{m}_", 3)) for m in range(2)]
    pos = b * T + rows_of((T, 1))
    first = [doc_start(R.starts, m, pos) for m in range(2)]
    tail = [f[T - 1 :, :] for f in first]
    for d in range(1, reach + 1):

        @pl.when(b < d)
        def _():
            R.v_kvh[d] = jnp.zeros((2, T, 128), BF)

    def convolve(m, chunks):
        for chunk in chunks:
            cols = pl.ds(chunk * 128, 128)
            taps, bias = group_taps(h, R.cw, R.cb2, chunk)
            total = jnp.broadcast_to(bias, (T, 128))
            for j in range(4):
                back = 3 - j
                total = total + jnp.where(
                    pos - first[m] >= back, R.cin[m, pl.ds(LAG - back, T), cols] * taps[j : j + 1], 0.0
                )
            R.v_pre[m, :, cols] = total
            act = total * sigmoid(total)
            if chunk < XC // 128:
                R.xs[m, :, cols] = act
            elif chunk == XC // 128:
                R.bs[m] = act.astype(BF)
            else:
                R.cs[m] = act.astype(BF)

    z, step, a_neg, cum = decays_of(R.dt, R.dtb, R.alog, h, T)
    R.cumt[...] = cum.T[:16]
    R.stept[...] = step.T[:16]
    cum_last = cum[T - 1 :, :]
    kept = by_batch(lambda m: jnp.broadcast_to((pos >= tail[m]).astype(F32), (T, 128)))
    omega = jnp.exp(cum_last - cum) * step * kept
    for m in range(2):
        if m == 1:
            lines[4].begin()
        R.cin[m, :, 0:XC] = R.v_xin[m].astype(F32)
        convolve(m, range(XC // 128))
        if m == 0:
            swap[0]().wait_recv()
        R.cin[m, :, XC:] = R.v_bc[m].astype(F32)
        convolve(m, (XC // 128, XC // 128 + 1))
        weighted = (R.xs[m] * widen(omega, 8 * m)).astype(BF)
        decay = jnp.where(tail[m] < b * T, jnp.exp(R.cumt[8 * m : 8 * m + 8, T - 1 : T]), 0.0)
        scans[m].set(tn(weighted, R.bs[m]), decay)
    lines[5].begin()
    ahead(0, 2, 3)

    seen = lanes((T, T)) + b * T
    lane = lanes((T, 128))

    def inside(m, between):
        both = nt(R.cs[m], R.bs[m])
        allowed = (seen <= pos) & (seen >= first[m])
        for i in range(HG):
            l = 8 * m + i
            gap = jnp.where(allowed, cum[:, l : l + 1] - R.cumt[l : l + 1, :], FAR)
            weights_ts = (jnp.exp(gap) * both * R.stept[l : l + 1, :]).astype(BF)
            R.ybuf[m, :, i * MHDIM : (i + 1) * MHDIM] = nn(weights_ts, R.xs[m, :, i * MHDIM : (i + 1) * MHDIM].astype(BF))
            if i == HG // 2 - 1:
                between()
        R.ybuf[m] = R.ybuf[m] + wide_row(R.skip, h) * R.xs[m]

    def on_to_pair(d):
        return copy_to(R.v_kvh.at[d, core], R.v_kvh.at[d, core], R.hs.at[d], R.hr.at[d], pair)

    R.lse[...] = jnp.zeros((T, 128), F32)

    def attend(m, i):
        query = R.v_q[m, :, i * HDIM : (i + 1) * HDIM]

        def score(d, top):
            at = seen - d * T
            keys = R.v_kvh[d, 0, :, m * HDIM : (m + 1) * HDIM]
            s = jnp.where((at <= pos) & (at >= first[m]), nt(query, keys) * SCALE, FAR)
            R.sbuf[d] = s
            return jnp.maximum(top, jnp.max(s, axis=1, keepdims=True))

        top = lax.fori_loop(0, reach + 1, score, jnp.full((T, 1), FAR, F32))

        def weigh(d, total):
            e = jnp.exp(R.sbuf[d] - top)
            R.sbuf[d] = e
            return total + jnp.sum(e, axis=1, keepdims=True)

        total = lax.fori_loop(0, reach + 1, weigh, jnp.zeros((T, 1), F32))
        inverse = 1.0 / total

        def take(d, acc):
            probs = (R.sbuf[d] * inverse).astype(BF)
            return acc + nn(probs, R.v_kvh[d, 1, :, m * HDIM : (m + 1) * HDIM])

        out = lax.fori_loop(0, reach + 1, take, jnp.zeros((T, HDIM), F32))
        R.attnf[m, :, i * HDIM : (i + 1) * HDIM] = out
        R.attnl[m, :, i * HDIM : (i + 1) * HDIM] = out.astype(BF)
        R.lse[...] = jnp.where(lane == 2 * m + i, top + jnp.log(total), R.lse[...])

    def mixed(m):
        gate = nn(R.v_normed[m, LAG:], R.v_wb[:, 0:XC])
        R.gate[m] = gate
        R.sin[m] = scans[m].last()[...]
        live = jnp.where(first[m] < b * T, jnp.exp(cum), 0.0)
        yv = R.ybuf[m] + nt(R.cs[m], R.sin[m, 0:XC]) * widen(live, 8 * m)
        low = yv.astype(BF)
        R.ylow[m] = low
        g = low.astype(F32) * gate * sigmoid(gate)
        R.ybuf[m] = g
        sums[m].begin(jnp.sum(g * g, axis=1, keepdims=True))

    gain = R.gain2[:, pl.ds(pl.multiple_of(h * XC, 128), XC)]
    n2 = R.gains[7:8, :]
    scales = [None, None]

    def rows(ref):
        return lambda m, head: ref[m, pl.ds(pl.multiple_of(head * tok, tok), tok), :]

    def own(ref, m):
        return ref.at[m, pl.ds(pl.multiple_of(h * tok, tok), tok), :]

    out1 = HeadScatter(rows(R.wide), b, h, members(R, "sc1_", 6))
    out2 = HeadScatter(rows(R.wide), b, h, members(R, "sc2_", 6))
    out3 = HeadScatter(rows(R.part), b, h, members(R, "sc3_", 6))
    gather_s = HeadGather(lambda m, i: R.secg.at[m, pl.ds(i * tok, tok)], b, h, members(R, "gs", 2))
    gather_h = HeadGather(lambda m, i: R.hlg.at[m, pl.ds(i * tok, tok)], b, h, members(R, "gh", 2))
    w_mix, w_att, w_out, w_in = (
        lambda: R.v_wb[:, XC : 2 * XC], lambda: R.v_wb[:, 2 * XC :], lambda: R.wc[:, 0:FG], lambda: R.wc[:, FG:]
    )

    def project(m):
        scales[m] = lax.rsqrt(sums[m].finish() * (1.0 / DI) + EPS)
        R.gated[m] = (R.ybuf[m] * scales[m] * gain).astype(BF)
        R.wide[m, 0:T, :] = nt(R.gated[m], w_mix()) + nt(R.attnl[m], w_att())
        out1.begin(m)

    def second_norm(m):
        out1.finish(m)
        value = R.x[m].astype(F32) + out1.result(m)
        R.hid[m] = value
        scale = lax.rsqrt(jnp.mean(value * value, axis=1, keepdims=True) + EPS)
        own(R.secg, m)[...] = (value * scale * n2).astype(BF)
        gather_s.begin(m)

    def feed(m):
        gather_c.finish(m)
        R.gact[m] = nn(R.cotg[m], w_out())
        gather_s.finish(m)
        a = nn(R.secg[m], R.wc[:, FG : 2 * FG])
        u = nn(R.secg[m], R.wc[:, 2 * FG :])
        sg = sigmoid(a)
        si = a * sg
        R.act[m] = (si * u).astype(BF)
        R.ggu[m, :, 0:FG] = (R.gact[m] * u * (sg * (1.0 + a * (1.0 - sg)))).astype(BF)
        R.ggu[m, :, FG:] = (R.gact[m] * si).astype(BF)
        R.wide[m, 0:T, :] = nt(R.ggu[m], w_in())
        out2.begin(m)
        R.part[m] = nt(R.act[m], w_out())

    def hidden_back(m):
        out2.finish(m)
        value = R.hid[m]
        scale = lax.rsqrt(jnp.mean(value * value, axis=1, keepdims=True) + EPS)
        grad, gain_part = norm_back(value, scale, n2, out2.result(m))
        grad = grad + R.cot[m].astype(F32)
        R.gh[m] = grad
        R.gn2[...] = gain_part if m == 0 else R.gn2[...] + gain_part
        own(R.hlg, m)[...] = grad.astype(BF)
        gather_h.begin(m)

    def project_back(m):
        gather_h.finish(m)
        R.up[m] = nn(R.hlg[m], w_mix())
        gate = R.gate[m]
        n = R.ylow[m].astype(F32) * gate * sigmoid(gate) * scales[m]
        up = R.up[m]
        part = jnp.sum(up * n, axis=0, keepdims=True)
        R.ggain[...] = part if m == 0 else R.ggain[...] + part
        back_sums[m].begin(jnp.sum(up * gain * n, axis=1, keepdims=True))
        R.gattn[m] = nn(R.hlg[m], w_att()).astype(BF)

    def mixed_back(m):
        total = back_sums[m].finish()
        gate = R.gate[m]
        sg = sigmoid(gate)
        si = gate * sg
        low = R.ylow[m].astype(F32)
        n = low * si * scales[m]
        grad = scales[m] * (R.up[m] * gain - n * (total * (1.0 / DI)))
        R.gy[m] = (grad * si).astype(BF)
        R.ggate[m] = (grad * low * (sg * (1.0 + gate * (1.0 - sg)))).astype(BF)

    def weight_grad(ref, at, left, right, cols):
        ref[:, at + cols.start : at + cols.stop] = sum(tn(left[m], right[m, :, cols]) for m in range(2)).astype(BF)

    pairs = [PairReduce(getattr(R, f"gi{k}"), members(R, f"pair{k}_", 3), b, h, nb) for k in range(2)]

    def in_grad(k, q):
        cols = slice(k * FG + q * FG // 2, k * FG + (q + 1) * FG // 2)
        grad = sum(tn(R.secg[m], R.ggu[m, :, cols]) for m in range(2)).astype(BF)
        pairs[k].src[:, :, :, q * FG // 2 : (q + 1) * FG // 2] = grad.reshape(nz, 2, rpb, FG // 2)

    moves.start("normed", "xin", "bc", "q", "pre", "wa")
    inside(0, lambda: ahead(0, 4))
    for m in range(2):
        scans[m].join(0)
    ahead(0, 5)
    halo.finish_recv()
    for d in range(1, reach + 1):

        @pl.when(b >= d)
        def _():
            on_to_pair(d).start()

    swap[1]().wait_recv()
    for d in range(1, reach + 1):

        @pl.when(b >= d)
        def _():
            on_to_pair(d).wait_recv()

    attend(0, 0)
    ahead(1, 2)
    for i in range(1, len(scans[0].steps) - 1):
        for m in range(2):
            scans[m].join(i)
    attend(0, 1)
    ahead(1, 3)
    for m in range(2):
        gather_c.forward(m)
    inside(1, lambda: ahead(1, 4))
    ahead(2, 2)
    lines[2].finish()
    moves.start("wb", "kvh")
    mixed(0)
    ahead(1, 5)
    attend(1, 0)
    project(0)
    ahead(2, 3)
    attend(1, 1)
    out1.middle(0)
    ahead(2, 4)
    mixed(1)
    second_norm(0)
    project(1)
    ahead(2, 5)
    gather_s.forward(0)
    out1.middle(1)
    for k in range(3, 6):
        lines[k].finish()
    feed(0)
    second_norm(1)
    out2.middle(0)
    gather_s.forward(1)
    feed(1)
    out2.middle(1)
    in_grad(0, 0)
    in_grad(0, 1)
    pairs[0].begin()
    hidden_back(0)
    for m in range(2):
        out3.begin(m)
    gather_h.forward(0)
    in_grad(1, 0)
    hidden_back(1)
    in_grad(1, 1)
    pairs[1].begin()
    project_back(0)
    gather_h.forward(1)
    out3.middle(0)
    out3.middle(1)
    half = [slice(k * FG // 2, (k + 1) * FG // 2) for k in range(2)]
    for k in range(2):
        weight_grad(R.v_gw_out, FG, R.cotg, R.act, half[k])
    project_back(1)
    mixed_back(0)
    per = max(nb // NH, 1)
    mix_to, att_to = arrange(per, XC, 0), arrange(per, 128, 1)
    for m in range(2):
        R.act[m] = (nn(R.gated[m], mix_to) + nn(R.attnl[m], att_to)).astype(BF)
    for k in range(2):
        weight_grad(R.v_gw_out, 0, R.hlg, R.act, half[k])
    moves.start("gw_out")
    mixed_back(1)
    for m in range(2):
        out3.finish(m)
        R.out[m] = R.hid[m] + out3.result(m)
    for k in range(2):
        pairs[k].finish(R.gw_in, slice(k * FG, (k + 1) * FG))

    if local:
        for k in range(3):
            for i in range(3):
                piece(k, i).wait_send()

    @pl.when((h == NH - 1) & (b + 1 < nb))
    def _():
        for i in range(NH):
            edge(i).wait_send()

    for c in swap:
        c().wait_send()
    for d in range(1, reach + 1):

        @pl.when(b >= d)
        def _():
            on_to_pair(d).wait_send()

    moves.wait_all()
    for g in lines + pairs + [gather_x, gather_c, gather_s, gather_h, out1, out2, out3]:
        g.done()
    for scan in scans:
        scan.finish()
    halo.finish_send()


def forward(nb, reach, ins, local):
    tok = ins["x"].shape[1]
    T, rpb = tok * NH, D // nb
    S = rpb // NH
    dma = pltpu.SemaphoreType.DMA
    outs = dict(
        normed=vm((2, LAG + T, D), BF), xin=vm((2, LAG + T, XC), BF), bc=vm((2, LAG + T, 256), BF), q=vm((2, T, 128), BF),
        kvh=vm((reach + 1, 2, T, 128), BF), dt=vm((T, 128), F32), pre=vm((2, T, XC + 256), F32),
        sin=vm((2, Scan.ROWS, 128), BF), attnf=vm((2, T, 128), F32), lse=vm((T, 128), F32), gy=vm((2, T, XC), BF),
        ggate=vm((2, T, XC), BF), gattn=vm((2, T, 128), BF), gw_in=vm((nb // 2, rpb, 2 * FG), BF), gw_out=vm((D, 2 * FG), BF), gn2=vm((1, D), F32),
        ggain=vm((1, XC), F32), out=vm((2, tok, D), F32), gh=vm((2, tok, D), F32), wa=vm((D, WA), BF), wb=vm((D, WB), BF),
        gains=vm((8, D), F32), cosine=vm((T, 128), F32), sine=vm((T, 128), F32),
    )
    V = pltpu.VMEM
    scratch = dict(
        xg=V((2, LAG + T, D), BF), cotg=V((2, T, D), BF), wc=V((D, WC), BF), wide=V((2, LAG + T, D), F32),
        gate=V((2, T, XC), F32), cin=V((2, LAG + T, XC + 256), F32), xs=V((2, T, XC), F32), bs=V((2, T, 128), BF),
        cs=V((2, T, 128), BF), ybuf=V((2, T, XC), F32), sbuf=V((reach + 1, T, T), F32), cumt=V((16, T), F32),
        stept=V((16, T), F32), ylow=V((2, T, XC), BF), gated=V((2, T, XC), BF), attnl=V((2, T, 128), BF),
        part=V((2, T, D), F32), secg=V((2, T, D), BF), hlg=V((2, T, D), BF), act=V((2, T, FG), BF),
        ggu=V((2, T, 2 * FG), BF), gact=V((2, T, FG), F32), hid=V((2, tok, D), F32), up=V((2, T, XC), F32),
        cb2=V((1, DI + 256), F32), gain2=V((1, DI), F32),
        ps=dma((3, 3)), pr=dma((3, 3)), es=dma((NH,)), er=dma((1,)), ss=dma((2,)), sr=dma((2,)),
        hs=dma((reach + 1,)), hr=dma((reach + 1,)),
    )
    scratch.update({"v_" + n: V(outs[n].shape, outs[n].dtype) for n in LATE_OUT}, moved=dma((len(LATE_OUT),)))
    if local:
        scratch.update(pa=V((NH, S, WA), BF), pb=V((NH, S, WB), BF), pc=V((NH, S, WC), BF))
    for name in ("gx", "gc", "gs", "gh"):
        scratch.update(group(name, HeadGather.scratch()))
    for k in range(2):
        scratch.update(group(f"pair{k}_", PairReduce.scratch(nb, FG)))
        scratch[f"gi{k}"] = V((nb // 2, 2, rpb, FG), BF)
    for k in range(6):
        scratch.update(group(f"line{k}_", LineGather.scratch(nb)))
    for k in range(3):
        scratch.update(group(f"sc{k + 1}_", HeadScatter.scratch(tok)))
    for m in range(2):
        scratch.update(group(f"scan{m}_", Scan.scratch(reach)))
        scratch.update(group(f"sumf{m}_", HeadSum.scratch(T)))
        scratch.update(group(f"sumb{m}_", HeadSum.scratch(T)))
    scratch.update(group("halo", Halo.scratch(reach)))
    body = functools.partial(forward_body, nb, T, reach, local)
    return run(body, ins, outs, scratch, "forward", 1, smem=("starts", "dtb", "alog", "skip"), hbm=LATE_OUT)


LATE_IN = ["pre", "gw_out", "kvh", "normed", "ggate", "xin", "bc", "wa", "wb", "gh"]


def backward_body(nb, T, reach, easy, R):
    b, h = place()
    moves = Moves(R, LATE_IN, False)
    tok, rpb = T // NH, D // nb
    nz, per = nb // 2, nb // NH
    share = (XC + 128) // per
    core, y = lax.rem(h, 2), h // 2
    pair, across = (b, other(h, 1)), (b, other(h, 2))
    total_sum = Sum(members(R, "sum", 4), b, h, nb)
    targets = [(per * h + i, b // per) for i in range(per)] if easy else []

    def away(device):
        return (device[0] != b) | (device[1] != h)

    barrier(
        head_edges(b, h) + line_edges(b, h, nb) + Scan.edges(b, h, nb, reach) + halo_edges(b, h, nb, reach)
        + [((h == NH - 1) & (b + 1 < nb), (b + 1, jnp.int32(i))) for i in range(NH)]
        + [(b >= 1, (b - 1, jnp.int32(NH - 1)))]
        + total_sum.edges()
        + [(away(t), t) for t in targets]
    )
    lines = [
        LineReduce(src, members(R, f"line{k}_", 10 if k else 7), b, h, nb)
        for k, src in enumerate((R.gw_in, R.v_gw_out, R.gwb, R.gwx, R.gwc))
    ]

    def send_ffn():
        lines[0].finish(R.res0)
        if easy:
            for i, to in enumerate((h // 2, 2 + h // 2)):
                R.fmsg[i] = R.res0[:, i * FG : (i + 1) * FG].astype(BF)
                slot = lax.rem(h, 2)

                @pl.when(to != h)
                def _():
                    copy_to(R.fmsg.at[i], R.fgot.at[slot], R.fs.at[i], R.fr.at[slot], (b, to)).start()

                @pl.when(to == h)
                def _():
                    R.fgot[slot] = R.fmsg[i]
        else:
            R.raw[:, 0 : 2 * FG] = R.res0[...].astype(BF)

    def send_out():
        lines[1].finish(R.res1)
        if easy:
            slot = lax.rem(b, per)
            for i, to in enumerate(targets):
                for j in range(2):
                    R.msg[i, j] = R.res1[:, j * FG + i * share : j * FG + (i + 1) * share].astype(BF)

                @pl.when(away(to))
                def _():
                    copy_to(R.msg.at[i], R.got.at[slot], R.ms.at[i], R.mr.at[slot], to).start()

                @pl.when(jnp.logical_not(away(to)))
                def _():
                    R.got[slot] = R.msg[i]
        else:
            R.raw[:, 2 * FG :] = R.res1[...].astype(BF)

    gather = HeadGather(lambda m, i: (R.w1b, R.w1c)[m].at[i], b, h, members(R, "gw", 2))

    def send_gate():
        lines[2].finish(R.res2)
        R.w1b[h] = R.res2[...].astype(BF)
        gather.begin(0)

    moves.start("pre", "gw_out", "kvh", "normed", "ggate", "xin", "bc", "wa", "wb", "gh")
    lines[0].step_some(0)
    moves.wait("pre", "gw_out")
    lines[1].start_some(0)
    scans = [Scan(-1, b, h, nb, reach, members(R, f"scan{m}_", 5)) for m in range(2)]
    halo = Halo(-1, lambda d: R.gkvs.at[d], lambda d: R.gkvr.at[d], b, h, nb, reach, members(R, "halo", 2))
    pos = b * T + rows_of((T, 1))
    first = [doc_start(R.starts, m, pos) for m in range(2)]
    tail = [f[T - 1 :, :] for f in first]
    seen = lanes((T, T)) + b * T
    lane = lanes((T, 128))
    for m in range(2):
        for chunk in range((XC + 256) // 128):
            cols = pl.ds(chunk * 128, 128)
            value = R.v_pre[m, :, cols]
            act = value * sigmoid(value)
            if chunk < XC // 128:
                R.xs[m, :, cols] = act
            elif chunk == XC // 128:
                R.bs[m] = act.astype(BF)
            else:
                R.cs[m] = act.astype(BF)
    z, step, a_neg, cum = decays_of(R.dt, R.dtb, R.alog, h, T)
    R.cumt[...] = cum.T[:16]
    R.stept[...] = step.T[:16]
    cum_last = cum[T - 1 :, :]
    live = jnp.exp(cum) * by_batch(lambda m: jnp.broadcast_to((first[m] < b * T).astype(F32), (T, 128)))
    kept = jnp.exp(cum_last - cum) * by_batch(lambda m: jnp.broadcast_to((pos >= tail[m]).astype(F32), (T, 128)))
    omega = kept * step
    for m in range(2):
        u = (R.gy[m].astype(F32) * widen(live, 8 * m)).astype(BF)
        decay = jnp.where(tail[m] < b * T, jnp.exp(R.cumt[8 * m : 8 * m + 8, T - 1 : T]), 0.0)
        scans[m].set(tn(u, R.cs[m]), decay)
    lines[0].step_some(1)
    lines[1].start_some(1)
    moves.wait("kvh")

    R.gkv[...] = jnp.zeros_like(R.gkv)
    for m in range(2):
        for i in range(2):
            mine = slice(i * HDIM, (i + 1) * HDIM)
            query, grad = R.q[m, :, mine], R.gattn[m, :, mine]
            delta = jnp.sum(grad.astype(F32) * R.attnf[m, :, mine], axis=1, keepdims=True)
            lse = R.lse[:, 2 * m + i : 2 * m + i + 1]

            def block(d, acc):
                at = seen - d * T
                keys = R.v_kvh[d, 0, :, m * HDIM : (m + 1) * HDIM]
                vals = R.v_kvh[d, 1, :, m * HDIM : (m + 1) * HDIM]
                probs = jnp.where((at <= pos) & (at >= first[m]), jnp.exp(nt(query, keys) * SCALE - lse), 0.0)
                ds = (probs * (nt(grad, vals) - delta)).astype(BF)
                R.gkv[d, 0, :, m * HDIM : (m + 1) * HDIM] += tn(ds, query) * SCALE
                R.gkv[d, 1, :, m * HDIM : (m + 1) * HDIM] += tn(probs.astype(BF), grad)
                return acc + nn(ds, keys)

            R.gq[m, :, mine] = lax.fori_loop(0, reach + 1, block, jnp.zeros((T, HDIM), F32)) * SCALE
            if m == 0 and i == 1:
                lines[0].step_some(2)
                lines[1].start_some(2)
            elif m == 1 and i == 0:
                lines[1].step_some(0)
            elif m == 1:
                lines[1].start_some(3)
                send_ffn()
        if m == 0:
            for scan in scans:
                scan.join(0)
    for d in range(reach + 1):
        R.pair_k[d] = R.gkv[d, 1 - core].astype(BF)
    swap_k = lambda: copy_to(R.pair_k, R.pair_kr, R.ss.at[0], R.sr.at[0], pair)
    swap_k().start()

    moves.wait("normed", "ggate")
    for m in range(2):
        R.gproj[m, 0:LAG, WA:] = jnp.zeros((LAG, XC), BF)
        R.gproj[m, LAG:, WA:] = R.v_ggate[m]
        R.gproj[m, 0:LAG, XC + 128 :WA] = jnp.zeros((LAG, 256), BF)
        R.gproj[m, LAG:, XC + 128 : XC + 256] = rotate_pair(R.gq[m], R.cosine[...], -R.sine[...]).astype(BF)


    def weight_grad(ref, at, cols):
        grad = sum(tn(R.v_normed[m], R.gproj[m, :, cols]) for m in range(2)).astype(BF)
        ref[:, :, :, at : at + cols.stop - cols.start] = grad.reshape(nz, 2, rpb, cols.stop - cols.start)

    weight_grad(R.gwb, 0, slice(WA, WA + XC))
    weight_grad(R.gwb, XC, slice(XC + 128, XC + 256))
    swap_k().wait_recv()
    for d in range(reach + 1):
        value = R.gkv[d, core] + R.pair_kr[d].astype(F32)
        if d == 0:
            R.gkv[0, core] = value
        else:
            R.gkvs[d] = value.astype(BF)
    halo.begin()
    lines[1].step_some(1)

    row_sums = jnp.zeros((T, 128), F32)
    R.rowq[...] = jnp.zeros_like(R.rowq)
    skip = wide_row(R.skip, h)
    gskip = jnp.zeros((1, 128), F32)
    for m in range(2):
        both = nt(R.cs[m], R.bs[m])
        allowed = (seen <= pos) & (seen >= first[m])
        gboth = jnp.zeros((T, T), F32)
        for i in range(HG):
            l = 8 * m + i
            mine = slice(i * MHDIM, (i + 1) * MHDIM)
            grad = R.gy[m, :, mine]
            decay = jnp.exp(jnp.where(allowed, cum[:, l : l + 1] - R.cumt[l : l + 1, :], FAR))
            srow = R.stept[l : l + 1, :]
            ld = decay * nt(grad, R.xs[m, :, mine].astype(BF))
            gboth = gboth + ld * srow
            q = ld * both
            R.rowq[l : l + 1, :] = jnp.sum(q, axis=0, keepdims=True)
            row_sums = jnp.where(lane == l, jnp.sum(q * srow, axis=1, keepdims=True), row_sums)
            R.gx[m, :, mine] = tn((decay * both * srow).astype(BF), grad)
            if i == HG // 2:
                if m == 0:
                    lines[1].step_some(2)
                else:
                    send_out()
        low = gboth.astype(BF)
        R.gcm[m] = nn(low, R.bs[m])
        R.gbm[m] = tn(low, R.cs[m])
        gyf = R.gy[m].astype(F32)
        gskip = gskip + exact(jnp.sum(gyf * R.xs[m], axis=0, keepdims=True), head_select(m))
        R.gx[m] = R.gx[m] + skip * gyf
        u = gyf * widen(live, 8 * m)
        carried = nt(R.cs[m], R.sin[m, 0:XC])
        row_sums = row_sums + exact(u * carried, head_select(m))
        R.gcm[m] += nn(u.astype(BF), R.sin[m, 0:XC])
        if m == 0:
            for scan in scans:
                scan.join(1)
            lines[2].start_some(0)
            lines[2].start_some(1)
    for scan in scans:
        for i in range(2, len(scan.steps) - 1):
            scan.join(i)

    colq = jnp.concatenate([R.rowq[...], jnp.zeros((112, T), F32)], axis=0).T
    gstep = colq
    gcum = row_sums - step * colq
    glast = jnp.zeros((1, 128), F32)
    for m in range(2):
        adjoint = scans[m].last()[0:XC, :]
        read = nt(R.bs[m], adjoint)
        wide = widen(omega, 8 * m)
        R.gx[m] += wide * read
        R.gbm[m] += nn((R.xs[m] * wide).astype(BF), adjoint)
        gw = exact(R.xs[m] * read, head_select(m))
        gstep = gstep + kept * gw
        term = omega * gw
        gcum = gcum - term
        glast = glast + jnp.sum(term, axis=0, keepdims=True)
        through = jnp.where(tail[m] < b * T, jnp.exp(cum_last), 0.0)
        overlap = adjoint.astype(F32) * R.sin[m, 0:XC].astype(F32)
        per_head = jnp.sum(
            lax.dot_general(overlap, head_select(m), (((0,), (0,)), ((), ())), precision=high, preferred_element_type=F32),
            axis=0, keepdims=True,
        )
        glast = glast + through * per_head
    gcum = gcum + jnp.where(rows_of((T, 128)) == T - 1, glast, 0.0)
    gda = exact(triangle(T, upper=True), gcum)
    gstep = gstep + gda * a_neg
    gz = jnp.where(valid_row(), gstep * sigmoid(z), 0.0)
    lines[2].start_some(2)
    lines[2].start_some(3)
    lines[2].step_some(0)
    moves.wait("xin", "bc")

    conv_grad = [[], []]
    R.gcin[...] = jnp.zeros_like(R.gcin)
    R.gcw[...] = jnp.zeros_like(R.gcw)
    for m in range(2):
        R.cin[:, 0:XC] = R.v_xin[m].astype(F32)
        R.cin[:, XC:] = R.v_bc[m].astype(F32)
        for chunk in range((XC + 256) // 128):
            cols = pl.ds(chunk * 128, 128)
            taps, _ = group_taps(h, R.cw, None, chunk)
            pre = R.v_pre[m, :, cols]
            sg = sigmoid(pre)
            if chunk < XC // 128:
                up = R.gx[m, :, cols]
            elif chunk == XC // 128:
                up = R.gbm[m]
            else:
                up = R.gcm[m]
            gs = up * (sg * (1.0 + pre * (1.0 - sg)))
            R.gcw[4:5, cols] += jnp.sum(gs, axis=0, keepdims=True)
            for back in range(4):
                j = 3 - back
                near = jnp.where(pos - first[m] >= back, gs, 0.0)
                R.gcw[j : j + 1, cols] += jnp.sum(near * R.cin[pl.ds(LAG - back, T), cols], axis=0, keepdims=True)
                R.gcin[m, pl.ds(LAG - back, T), cols] += near * taps[j : j + 1]

    mine_bc = pl.ds(pl.multiple_of(XC + core * 128, 128), 128)
    pair_bc = pl.ds(pl.multiple_of(XC + (1 - core) * 128, 128), 128)
    for m in range(2):
        R.pair_b[m] = R.gcin[m, :, pair_bc].astype(BF)
    swap_b = lambda: copy_to(R.pair_b, R.pair_br, R.ss.at[1], R.sr.at[1], pair)
    swap_b().start()
    for m in range(2):
        R.gproj[m, :, 0:XC] = R.gcin[m, :, 0:XC].astype(BF)
    weight_grad(R.gwx, 0, slice(0, XC))
    for k in range(4):
        lines[3].start_some(k)
    lines[2].step_some(1)
    halo.finish_recv()
    packed = R.gkv[0, core]
    for d in range(1, reach + 1):
        packed = packed + jnp.where(b + d < nb, R.gkvr[d].astype(F32), 0.0)
    turned = rotate_pair(packed, R.cosine[...], -R.sine[...])
    packed = jnp.where(core == 0, turned, packed)
    swap_b().wait_recv()
    for m in range(2):
        value = R.gcin[m, :, mine_bc] + R.pair_br[m].astype(F32)
        R.sum_b[m] = value
        R.across_b[m] = value.astype(BF)
    swap_y = lambda: copy_to(R.across_b, R.across_br, R.ss.at[2], R.sr.at[2], across)
    swap_y().start()
    for m in range(2):
        mine = packed if m == 0 else pltpu.roll(packed, HDIM, 1)
        gdt = pltpu.roll(gz, HDIM - 8 * m, 1)
        R.gproj[m, LAG:, XC + 256 : WA] = jnp.where(
            lane < HDIM, mine, jnp.where(lane < HDIM + HG, gdt, 0.0)
        ).astype(BF)
    weight_grad(R.gwc, 128, slice(XC + 256, WA))
    swap_y().wait_recv()
    half = lanes((LAG + T, 128)) // HDIM == y
    for m in range(2):
        R.gproj[m, :, XC : XC + 128] = jnp.where(half, R.sum_b[m] + R.across_br[m].astype(F32), 0.0).astype(BF)
    weight_grad(R.gwc, 0, slice(XC, XC + 128))
    for k in range(4):
        lines[4].start_some(k)
    lines[2].step_some(2)
    moves.wait("wa", "wb")

    scatter = HeadScatter(
        lambda m, head: R.gnp[m, pl.ds(pl.multiple_of(LAG + head * tok, LAG), tok), :], b, h, members(R, "sc", 6)
    )
    for m in range(2):
        R.gnp[m] = nt(R.gproj[m, :, 0:WA], R.v_wa[...]) + nt(R.gproj[m, :, WA:], R.v_wb[:, 0:XC])
        scatter.begin(m)
        R.edge_s[m] = R.gnp[m, 0:LAG, :].astype(BF)

    n1 = R.gains[6:7, :]
    small = jnp.concatenate(
        [
            jnp.sum(gz, axis=0, keepdims=True),
            jnp.sum(gda * step, axis=0, keepdims=True) * a_neg,
            gskip,
            jnp.zeros((5, 128), F32),
        ],
        axis=0,
    )
    small = jnp.where(lanes((8, 128)) < HG, small + pltpu.roll(small, 120, 1), 0.0)
    small = pltpu.roll(small, h * HG, 1)
    R.pay[...] = jnp.zeros_like(R.pay)
    wide_x = pl.ds(pl.multiple_of(h * XC, 128), XC)
    R.pay[0:5, wide_x] = R.gcw[0:5, 0:XC]
    R.pay[0:5, DI:] = R.gcw[0:5, XC:]
    R.pay[5:6, wide_x] = R.ggain[...]
    gn1 = sum(jnp.sum(R.gnp[m] * R.v_normed[m].astype(F32), axis=0, keepdims=True) for m in range(2))
    R.pay[6:7, 0:D] = gn1 / n1
    R.pay[7:8, 0:D] = R.gn2[...]
    for k in range(3):
        R.pay[6:7, D + 128 * k : D + 128 * (k + 1)] = small[k : k + 1]
    total_sum.begin(R.pay[...])

    def edge(i):
        return copy_to(R.edge_s, R.edge_r.at[i], R.es.at[0], R.er.at[i], (b - 1, jnp.int32(NH - 1)))

    @pl.when(b >= 1)
    def _():
        edge(h).start()

    for m in range(2):
        scatter.middle(m)
    moves.wait("gh")
    lines[3].step_some(0)
    total_sum.step(0)
    lines[4].step_some(0)
    send_gate()
    mine = (h == NH - 1) & (b + 1 < nb)

    @pl.when(mine)
    def _():
        for i in range(NH):
            edge(i).wait_recv()

    @pl.when(jnp.logical_not(mine))
    def _():
        R.edge_r[...] = jnp.zeros_like(R.edge_r)

    for m in range(2):
        scatter.finish(m)
        R.up[m] = scatter.result(m)
        R.up[m, tok - LAG : tok, :] += sum(R.edge_r[i, m].astype(F32) for i in range(NH))
        value = R.x[m].astype(F32)
        scale = lax.rsqrt(jnp.mean(value * value, axis=1, keepdims=True) + EPS)
        R.gin[m] = R.v_gh[m] + norm_back(value, scale, n1, R.up[m])[0]
    lines[3].step_some(1)
    total_sum.step(1)
    lines[4].step_some(1)
    lines[3].step_some(2)
    total_sum.step(2)
    lines[4].step_some(2)
    gather.forward(0)
    lines[3].finish(R.res3)
    R.w1c[h, :, 0:XC] = R.res3[...].astype(BF)
    total_sum.step(3)
    lines[4].finish(R.res4)
    R.w1c[h, :, XC:] = R.res4[...].astype(BF)
    gather.begin(1)
    for k in range(4, len(total_sum.steps)):
        total_sum.step(k)
    gather.forward(1)
    R.small[...] = total_sum.result()
    if easy:
        for j in range(2):
            src = 2 * lax.rem(h, 2) + j

            @pl.when(src != h)
            def _():
                copy_to(R.fmsg.at[0], R.fgot.at[j], R.fs.at[0], R.fr.at[j], (b, src)).wait_recv()

        for j in range(per):

            @pl.when(away(targets[j]))
            def _():
                copy_to(R.msg.at[0], R.got.at[j], R.ms.at[0], R.mr.at[j], targets[j]).wait_recv()

        for i, to in enumerate((h // 2, 2 + h // 2)):

            @pl.when(to != h)
            def _():
                copy_to(R.fmsg.at[i], R.fgot.at[0], R.fs.at[i], R.fr.at[0], (b, to)).wait_send()

        for i in range(per):

            @pl.when(away(targets[i]))
            def _():
                copy_to(R.msg.at[i], R.got.at[0], R.ms.at[i], R.mr.at[0], targets[i]).wait_send()

    for m in range(2):
        gather.finish(m)
    for line in lines:
        line.done()

    @pl.when(b >= 1)
    def _():
        edge(h).wait_send()

    for c in (swap_k, swap_b, swap_y):
        c().wait_send()
    gather.done()
    scatter.done()
    for scan in scans:
        scan.finish()
    halo.finish_send()


def backward(nb, reach, ins):
    tok = ins["x"].shape[1]
    T, rpb, nz, per = tok * NH, D // nb, nb // 2, nb // NH
    share = (XC + 128) // per
    easy = share % 128 == 0
    dma, V = pltpu.SemaphoreType.DMA, pltpu.VMEM
    outs = dict(
        gin=vm((2, tok, D), F32), w1b=vm((NH, rpb, XC + 128), BF), w1c=vm((NH, rpb, XC + 256), BF),
        small=vm((8, DI + 256), F32),
    )
    if easy:
        outs.update(fgot=vm((2, rpb, FG), BF), got=vm((per, 2, rpb, share), BF))
    else:
        outs.update(raw=vm((rpb, 4 * FG), BF))
    scratch = dict(
        xs=V((2, T, XC), F32), bs=V((2, T, 128), BF), cs=V((2, T, 128), BF), cumt=V((16, T), F32), stept=V((16, T), F32),
        gkv=V((reach + 1, 2, T, 128), F32), gkvs=V((reach + 1, T, 128), BF), gkvr=V((reach + 1, T, 128), BF),
        pair_k=V((reach + 1, T, 128), BF), pair_kr=V((reach + 1, T, 128), BF), gq=V((2, T, 128), F32),
        gproj=V((2, LAG + T, WA + XC), BF), gwb=V((nz, 2, rpb, XC + 128), BF), gwx=V((nz, 2, rpb, XC), BF), gwc=V((nz, 2, rpb, 256), BF),
        rowq=V((16, T), F32), gx=V((2, T, XC), F32), gbm=V((2, T, 128), F32), gcm=V((2, T, 128), F32),
        gcin=V((2, LAG + T, XC + 256), F32), gcw=V((8, XC + 256), F32), cin=V((LAG + T, XC + 256), F32),
        pair_b=V((2, LAG + T, 128), BF), pair_br=V((2, LAG + T, 128), BF), sum_b=V((2, LAG + T, 128), F32),
        across_b=V((2, LAG + T, 128), BF), across_br=V((2, LAG + T, 128), BF), gnp=V((2, LAG + T, D), F32),
        edge_s=V((2, LAG, D), BF), edge_r=V((NH, 2, LAG, D), BF), up=V((2, tok, D), F32), pay=V((8, DI + 256), F32),
        res0=V((rpb, 2 * FG), F32), res1=V((rpb, 2 * FG), F32), res2=V((rpb, XC + 128), F32), res3=V((rpb, XC), F32), res4=V((rpb, 256), F32),
        ss=dma((3,)), sr=dma((3,)), es=dma((1,)), er=dma((NH,)), moved=dma((len(LATE_IN),)),
    )
    scratch.update({"v_" + n: V(ins[n].shape, ins[n].dtype) for n in LATE_IN})
    if easy:
        scratch.update(
            fmsg=V((2, rpb, FG), BF), msg=V((per, 2, rpb, share), BF), fs=dma((2,)), fr=dma((2,)), ms=dma((per,)), mr=dma((per,)),
        )
    for k, cols in enumerate((2 * FG, 2 * FG, XC + 128, XC, 256)):
        scratch.update(group(f"line{k}_", LineReduce.scratch(nb, cols, k > 0)))
    scratch.update(group("sum", Sum.scratch(nb, (8, DI + 256))))
    for m in range(2):
        scratch.update(group(f"scan{m}_", Scan.scratch(reach)))
    scratch.update(group("halo", Halo.scratch(reach)))
    scratch.update(group("sc", HeadScatter.scratch(tok)))
    scratch.update(group("gw", HeadGather.scratch()))
    body = functools.partial(backward_body, nb, T, reach, easy)
    return run(body, ins, outs, scratch, "backward", 2, smem=("starts", "dtb", "alog", "skip"), hbm=LATE_IN)


def finish_body(nb, R):
    h = lax.axis_index("head")
    rpb, per = D // nb, nb // NH
    R.out[...] = R.out_in[...]
    R.gin[...] = R.gin_in[...]
    kv = XC + 128
    for i in range(NH):
        first, second = R.w1b[i].astype(F32).T, R.w1c[i].astype(F32).T
        R.full[i * XC : (i + 1) * XC] = first[:XC]
        R.full[DI + i * XC : DI + (i + 1) * XC] = second[:XC]
        R.fatt[i * 128 : (i + 1) * 128] = first[XC:]
        half = HDIM * (i // 2)
        at = 2 * DI + 128 * (i % 2) + half
        R.full[at : at + HDIM] = second[XC + half : XC + half + HDIM]
        at = QHEADS * HDIM + 128 * (i % 2) + half
        R.fatt[at : at + HDIM] = second[kv : kv + HDIM]
        at = 2 * DI + 256 + i * HG
        R.full[at : at + HG] = second[kv + HDIM : kv + HDIM + HG]
    for ref, out in ((R.full, R.mix_in), (R.fatt, R.att_in)):
        width = out.shape[0]
        out[...] = ref[pl.ds(h * width, width), :]
    R.cw[...] = R.small[0:4, :]
    R.cb[...] = R.small[4:5, :].reshape(DI + 256)
    R.gain[...] = R.small[5:6, 0:DI].reshape(DI)
    R.n1[...] = R.small[6:7, 0:D].reshape(D)
    R.n2[...] = R.small[7:8, 0:D].reshape(D)
    for k, ref in enumerate((R.dtb, R.alog, R.skip)):
        ref[...] = R.small[6:7, D + 128 * k : D + 128 * k + MHEADS].reshape(MHEADS)
    if hasattr(R, "got"):
        for j in range(2):
            R.ffn[:, j * FG : (j + 1) * FG] = R.fgot[j].astype(F32)
        for j in range(per):
            cols = slice(j * rpb, (j + 1) * rpb)
            both = R.got[j, 0].astype(F32).T
            R.mix_out[:, cols] = both[: XC // per]
            R.att_out[:, cols] = both[XC // per :]
            R.ffn_out[:, cols] = R.got[j, 1].astype(F32).T


def finish(nb, ins, mix_cols, att_cols):
    rpb, per = D // nb, nb // NH
    outs = dict(
        out=vm(ins["out_in"].shape, F32), gin=vm(ins["gin_in"].shape, F32), mix_in=vm((mix_cols, rpb), F32),
        att_in=vm((att_cols, rpb), F32), cw=vm((4, DI + 256), F32), cb=vm((DI + 256,), F32), gain=vm((DI,), F32),
        n1=vm((D,), F32), n2=vm((D,), F32), dtb=vm((MHEADS,), F32), alog=vm((MHEADS,), F32), skip=vm((MHEADS,), F32),
    )
    if "got" in ins:
        outs.update(
            ffn=vm((rpb, 2 * FG), F32), mix_out=vm((XC // per, per * rpb), F32), att_out=vm((128 // per, per * rpb), F32),
            ffn_out=vm((FG // per, per * rpb), F32),
        )
    V = pltpu.VMEM
    scratch = dict(full=V((NH * mix_cols, rpb), F32), fatt=V((NH * att_cols, rpb), F32))
    return run(functools.partial(finish_body, nb), ins, outs, scratch, "finish", None)


def pack_columns(mixer_in, attn_in, mixer_out, attn_out, ffn_in, ffn_out, norm_one, norm_two):
    shard = mixer_in.shape[0]
    mix_t, att_t, ffn_t = mixer_out.T, attn_out.T, ffn_out.T
    sets = ([], [], [])
    for i in range(NH):
        kv = QHEADS * HDIM + 128 * (i % 2) + HDIM * (i // 2)
        bc, dt = 2 * DI + 128 * (i % 2), 2 * DI + 2 * STATE + i * HG
        sets[0].append(
            [
                mixer_in[:, DI + i * XC : DI + (i + 1) * XC], mixer_in[:, bc : bc + 128],
                attn_in[:, i * 128 : (i + 1) * 128], attn_in[:, kv : kv + HDIM], mixer_in[:, dt : dt + HG],
                norm_one[:, None], norm_two[:, None], jnp.zeros((shard, 128 - HDIM - HG - 2), BF),
            ]
        )
        sets[1].append(
            [
                mixer_in[:, i * XC : (i + 1) * XC], mix_t[:, i * XC : (i + 1) * XC], att_t[:, i * 128 : (i + 1) * 128],
            ]
        )
        sets[2].append(
            [
                ffn_t[:, i * FG : (i + 1) * FG], ffn_in[:, i * FG : (i + 1) * FG],
                ffn_in[:, FF + i * FG : FF + (i + 1) * FG],
            ]
        )
    out = []
    for parts in sets:
        v = jnp.stack([jnp.concatenate(p, axis=1) for p in parts])
        out.append(lax.all_to_all(v, "head", split_axis=0, concat_axis=0, tiled=True).reshape(shard * NH, v.shape[2]))
    return out


def on_device(
    inputs, cotangent, doc_starts, norm_one, mixer_in, conv_weight, conv_bias, dt_bias, a_log, d_skip, ssm_gain,
    mixer_out, attn_in, attn_out, norm_two, ffn_in, ffn_out,
):
    nb = lax.axis_size("blk")
    T = inputs.shape[1] * NH
    longest = min(MAXLEN, T * nb // 2)
    reach = (longest + T - 2) // T
    shard = mixer_in.shape[0]
    rpb, nz = shard * NH, nb // 2
    local = shard % 16 == 0

    lane = np.arange(128) % HDIM % (HDIM // 2)
    freq = jnp.asarray((10000.0 ** (-(lane.astype(np.float32) * 2.0 / HDIM))).astype(np.float32))[None, :]
    small = dict(
        starts=doc_starts, cw=conv_weight, dtb=dt_bias, alog=a_log, skip=d_skip
    )
    if local:
        weights = dict(
            mixer_in=mixer_in, attn_in=attn_in, mixer_out=mixer_out.T, attn_out=attn_out.T, ffn_in=ffn_in,
            ffn_out=ffn_out.T, n1=norm_one[None, :], n2=norm_two[None, :],
        )
    else:
        weights = dict(
            zip(("pa", "pb", "pc"), pack_columns(mixer_in, attn_in, mixer_out, attn_out, ffn_in, ffn_out, norm_one, norm_two))
        )
    f = forward(nb, reach, dict(x=inputs, cot=cotangent, freq=freq, cb=conv_bias, gain=ssm_gain, **small, **weights), local)
    shape = (nz, 2, rpb, 2 * FG)
    kept = (
        "gy", "gattn", "q", "kvh", "attnf", "lse", "pre", "xin", "bc", "dt", "sin", "ggate", "cosine", "sine", "normed", "wa",
        "wb", "gh", "gains", "gn2", "ggain",
    )
    b = backward(
        nb, reach,
        dict(
            x=inputs, gw_in=f.gw_in, gw_out=f.gw_out.reshape(shape), **small,
            **{n: getattr(f, n) for n in kept},
        ),
    )
    ins = dict(out_in=f.out, gin_in=b.gin, w1b=b.w1b, w1c=b.w1c, small=b.small)
    easy = hasattr(b, "got")
    if easy:
        ins.update(fgot=b.fgot, got=b.got)
    r = finish(nb, ins, mixer_in.shape[1] // NH, attn_in.shape[1] // NH)
    if easy:
        g_ffn_in, g_mix_out, g_att_out, g_ffn_out = r.ffn, r.mix_out, r.att_out, r.ffn_out
    else:
        per = nb // NH
        head, blk = lax.axis_index("head"), lax.axis_index("blk")
        mine = lax.all_gather(b.raw[:, : 2 * FG], "head").reshape(NH, rpb, 2, FG)
        ffn = jnp.transpose(mine, (1, 2, 0, 3)).reshape(rpb, 2 * FF)
        g_ffn_in = lax.dynamic_slice_in_dim(ffn, head * (2 * FF // NH), 2 * FF // NH, 1).astype(F32)
        outs = lax.all_gather(b.raw[:, 2 * FG :], ("blk", "head")).reshape(nb, NH, rpb, 2 * FG)
        outs = jnp.transpose(outs, (1, 3, 0, 2)).reshape(NH, 2, per, FG // per, D)
        outs = lax.dynamic_slice_in_dim(outs, head * (D // NH), D // NH, 4)
        outs = jnp.transpose(outs, (0, 2, 1, 3, 4)).reshape(nb, 2, FG // per, D // NH)
        outs = lax.dynamic_index_in_dim(outs, blk, 0, False).astype(F32)
        g_mix_out, g_att_out, g_ffn_out = outs[0, : XC // per], outs[0, XC // per :], outs[1]
    return (
        r.out, r.gin, r.n1, r.mix_in.T, r.cw, r.cb, r.dtb, r.alog, r.skip, r.gain, g_mix_out, r.att_in.T, g_att_out, r.n2,
        g_ffn_in, g_ffn_out,
    )


def solution(mesh):
    both = ("blk", "head")
    tokens, rows, cols = P(None, both, None), P(both, None), P(None, both)
    split = P("blk", "head")
    return jax.shard_map(
        on_device,
        mesh=mesh,
        in_specs=(
            tokens, tokens, P(), P(both), rows, P(), P(), P(), P(), P(), P(), cols, rows, cols, P(both), rows, cols,
        ),
        out_specs=(
            tokens, tokens, P(), split, P(), P(), P(), P(), P(), P(), split, split, split, P(), split, split,
        ),
        check_vma=False,
    )
```

```python
import functools
import types

import jax
import jax.numpy as jnp
import numpy as np
from jax import lax
from jax.experimental import pallas as pl
from jax.experimental.pallas import tpu as pltpu
from jax.sharding import PartitionSpec as P

MHEADS = 24
MHDIM = 64
STATE = 128
QHEADS = 8
HDIM = 64
FF = 2048
DI = 1536
D = 1024
MAXLEN = 4096
NH = 4
HG = MHEADS // NH
XC = HG * MHDIM
FG = FF // NH
WA = XC + 3 * 128
WB = 2 * XC + 128
WC = 3 * FG
LAG = 16
EPS = 1e-5
FAR = -1e30
SCALE = HDIM**-0.5
MESH = pl.DeviceIdType.MESH
BF = jnp.bfloat16
F32 = jnp.float32
VMEM_LIMIT = 62 * 2**20
high = lax.Precision.HIGHEST


def nn(a, b):
    return lax.dot_general(a, b, (((1,), (0,)), ((), ())), preferred_element_type=F32)


def nt(a, b):
    return lax.dot_general(a, b, (((1,), (1,)), ((), ())), preferred_element_type=F32)


def tn(a, b):
    return lax.dot_general(a, b, (((0,), (0,)), ((), ())), preferred_element_type=F32)


def other(index, step):
    return index + step - 2 * step * lax.rem(index // step, 2)


def copy_to(src, dst, send, recv, where):
    return pltpu.make_async_remote_copy(
        src_ref=src, dst_ref=dst, send_sem=send, recv_sem=recv, device_id=where, device_id_type=MESH
    )


def barrier(edges):
    sem = pltpu.get_barrier_semaphore()
    for there, where in edges:
        if there is True:
            pl.semaphore_signal(sem, inc=1, device_id=where, device_id_type=MESH)
        else:

            @pl.when(there)
            def _():
                pl.semaphore_signal(sem, inc=1, device_id=where, device_id_type=MESH)

    total = 0
    for there, _ in edges:
        total = total + (1 if there is True else there.astype(jnp.int32))
    pl.semaphore_wait(sem, total)


def lanes(shape):
    return lax.broadcasted_iota(jnp.int32, shape, len(shape) - 1)


def rows_of(shape):
    return lax.broadcasted_iota(jnp.int32, shape, len(shape) - 2)


def sigmoid(v):
    return 1.0 / (1.0 + jnp.exp(-v))


def widen(cols, first, count=HG, width=MHDIM):
    return jnp.concatenate(
        [
            jnp.broadcast_to(cols[:, first + i : first + i + 1], (cols.shape[0], width))
            for i in range(count)
        ],
        axis=1,
    )


class LineGather:
    def __init__(self, piece, b, h, nb, sems):
        self.piece, self.h, self.nz = piece, h, nb // 2
        self.z, self.x = b // 2, lax.rem(b, 2)
        self.line_recv, self.send_r, self.send_l, self.x_send, self.x_recv = sems

    @staticmethod
    def scratch(nb):
        return [pltpu.SemaphoreType.DMA((nb // 2,))] * 5

    def at(self, z, x=None):
        return self.piece(2 * z + (self.x if x is None else x))

    def to_x(self, z):
        return copy_to(
            self.at(z), self.at(z), self.x_send.at[z], self.x_recv.at[z], (2 * self.z + 1 - self.x, self.h)
        )

    def to_z(self, z, way):
        send = self.send_r if way > 0 else self.send_l
        return copy_to(
            self.at(z), self.at(z), send.at[z], self.line_recv.at[z], (2 * (self.z + way) + self.x, self.h)
        )

    def begin(self):
        self.hop(0)
        self.to_x(self.z).start()

    def hop(self, s):
        @pl.when((self.z - s >= 0) & (self.z + 1 < self.nz))
        def _():
            self.to_z(self.z - s, 1).start()

        @pl.when((self.z + s < self.nz) & (self.z >= 1))
        def _():
            self.to_z(self.z + s, -1).start()

    def advance(self, s):
        left, right = self.z - 1 - s, self.z + 1 + s
        more = s + 1 < self.nz - 1

        @pl.when(left >= 0)
        def _():
            self.to_z(left, 1).wait_recv()
            if more:

                @pl.when(self.z + 1 < self.nz)
                def _():
                    self.to_z(left, 1).start()

            self.to_x(left).start()

        @pl.when(right < self.nz)
        def _():
            self.to_z(right, -1).wait_recv()
            if more:

                @pl.when(self.z >= 1)
                def _():
                    self.to_z(right, -1).start()

            self.to_x(right).start()

    def finish(self):
        for z in range(self.nz):
            copy_to(
                self.at(z, 1 - self.x),
                self.at(z, 1 - self.x),
                self.x_send.at[z],
                self.x_recv.at[z],
                (2 * self.z + 1 - self.x, self.h),
            ).wait_recv()

    def done(self):
        for z in range(self.nz):
            self.to_x(z).wait_send()

            @pl.when((z <= self.z) & (self.z + 1 < self.nz))
            def _():
                self.to_z(z, 1).wait_send()

            @pl.when((z >= self.z) & (self.z >= 1))
            def _():
                self.to_z(z, -1).wait_send()


def line_edges(b, h, nb):
    return [
        (True, (other(b, 1), h)),
        (b >= 2, (b - 2, h)),
        (b + 2 < nb, (b + 2, h)),
    ]


def head_edges(b, h):
    return [(True, (b, other(h, 1))), (True, (b, other(h, 2))), (True, (b, NH - 1 - h))]


class HeadGather:
    def __init__(self, rows, b, h, sems):
        self.rows, self.b, self.h = rows, b, h
        self.send, self.recv = sems

    @staticmethod
    def scratch():
        return [pltpu.SemaphoreType.DMA((2, 3))] * 2

    def copy(self, m, i):
        pair, across = other(self.h, 1), other(self.h, 2)
        rows = self.rows(m, self.h if i < 2 else across)
        return copy_to(rows, rows, self.send.at[m, i], self.recv.at[m, i], (self.b, across if i == 1 else pair))

    def begin(self, m):
        self.copy(m, 1).start()
        self.copy(m, 0).start()

    def forward(self, m):
        self.copy(m, 1).wait_recv()
        self.copy(m, 2).start()

    def finish(self, m):
        self.copy(m, 0).wait_recv()
        self.copy(m, 2).wait_recv()

    def done(self):
        for m in range(2):
            for i in range(3):
                self.copy(m, i).wait_send()


class HeadScatter:
    def __init__(self, full, b, h, bufs):
        self.full, self.b, self.h = full, b, h
        self.send_c, self.recv_c, self.send_y, self.recv_y, self.send, self.recv = bufs

    @staticmethod
    def scratch(rows):
        return [
            pltpu.VMEM((2, 2, rows, D), BF),
            pltpu.VMEM((2, 2, rows, D), BF),
            pltpu.VMEM((2, rows, D), BF),
            pltpu.VMEM((2, rows, D), BF),
            pltpu.SemaphoreType.DMA((2, 2)),
            pltpu.SemaphoreType.DMA((2, 2)),
        ]

    def copy(self, m, i):
        src, dst = ((self.send_c, self.recv_c), (self.send_y, self.recv_y))[i]
        return copy_to(src.at[m], dst.at[m], self.send.at[m, i], self.recv.at[m, i], (self.b, other(self.h, i + 1)))

    def begin(self, m):
        core = lax.rem(self.h, 2)
        for y in range(2):
            self.send_c[m, y] = self.full(m, 2 * y + 1 - core).astype(BF)
        self.copy(m, 0).start()

    def middle(self, m):
        core, y = lax.rem(self.h, 2), self.h // 2
        self.copy(m, 0).wait_recv()
        self.send_y[m] = (self.full(m, 2 * (1 - y) + core) + self.recv_c[m, 1 - y].astype(F32)).astype(BF)
        self.copy(m, 1).start()

    def finish(self, m):
        self.copy(m, 1).wait_recv()

    def result(self, m):
        y = self.h // 2
        return self.full(m, self.h) + self.recv_c[m, y].astype(F32) + self.recv_y[m].astype(F32)

    def done(self):
        for m in range(2):
            for i in range(2):
                self.copy(m, i).wait_send()


class Todo:
    def __init__(self):
        self.steps = []

    def add(self, *steps):
        self.steps += steps

    def tick(self, count=1):
        for _ in range(min(count, len(self.steps))):
            self.steps.pop(0)()

    def drain(self, left=0):
        self.tick(max(len(self.steps) - left, 0))


def place():
    return lax.axis_index("blk"), lax.axis_index("head")


def rotate_pair(v, cosine, sine):
    lane = lax.rem(lanes(v.shape), HDIM)
    front = lane < HDIM // 2
    partner = jnp.where(front, pltpu.roll(v, 128 - HDIM // 2, 1), pltpu.roll(v, HDIM // 2, 1))
    return v * cosine + jnp.where(front, -partner, partner) * sine


def rope_tables(freq_ref, b, rows, ref_cos, ref_sin):
    pos = (b * rows + rows_of((rows, 128))).astype(F32)
    angle = pos * freq_ref[...]
    ref_cos[...] = jnp.cos(angle)
    ref_sin[...] = jnp.sin(angle)


def vm(shape, dtype):
    return jax.ShapeDtypeStruct(shape, dtype)


def run(body, ins, outs, scratch, name, cid, smem=(), hbm=()):
    names = list(ins) + list(outs) + list(scratch)

    def kernel(*refs):
        body(types.SimpleNamespace(**dict(zip(names, refs))))

    def space(n):
        return pl.BlockSpec(memory_space=pltpu.SMEM if n in smem else (pl.ANY if n in hbm else pltpu.VMEM))

    got = pl.pallas_call(
        kernel,
        out_shape=list(outs.values()),
        in_specs=[space(n) for n in ins],
        out_specs=[space(n) for n in outs],
        scratch_shapes=list(scratch.values()),
        compiler_params=pltpu.CompilerParams(
            collective_id=cid, has_side_effects=cid is not None, vmem_limit_bytes=VMEM_LIMIT
        ),
        name=name,
    )(*ins.values())
    return types.SimpleNamespace(**dict(zip(outs, got)))


class Moves:
    def __init__(self, refs, names, out):
        self.refs, self.names, self.out = refs, names, out
        self.waiting = []

    def copy(self, name):
        far, near = getattr(self.refs, name), getattr(self.refs, "v_" + name)
        src, dst = (near, far) if self.out else (far, near)
        return pltpu.make_async_copy(src, dst, self.refs.moved.at[self.names.index(name)])

    def start(self, *names):
        for n in names:
            self.copy(n).start()
            self.waiting.append(n)

    def wait(self, *names):
        for n in names:
            self.copy(n).wait()
            self.waiting.remove(n)

    def wait_all(self):
        self.wait(*list(self.waiting))


def group(prefix, shapes):
    return {f"{prefix}{i}": s for i, s in enumerate(shapes)}


def members(refs, prefix, count):
    return [getattr(refs, f"{prefix}{i}") for i in range(count)]


def doc_start(starts_ref, m, pos):
    first = jnp.zeros(pos.shape, jnp.int32)
    for k in range(starts_ref.shape[1]):
        s = starts_ref[m, k]
        first = jnp.where(pos >= s, s, first)
    return first


def head_row(ref, h, count=2):
    lane = lanes((1, 128))
    row = jnp.zeros((1, 128), F32)
    for i in range(HG):
        for m in range(count):
            row = jnp.where(lane == 8 * m + i, ref[h * HG + i], row)
    return row


def wide_row(ref, h):
    lane = lanes((1, XC)) // MHDIM
    row = jnp.zeros((1, XC), F32)
    for i in range(HG):
        row = jnp.where(lane == i, ref[h * HG + i], row)
    return row


def valid_row():
    lane = lanes((1, 128))
    return (lane < 16) & (lax.rem(lane, 8) < HG)


def triangle(n, upper=False):
    r, c = rows_of((n, n)), lanes((n, n))
    return ((c >= r) if upper else (c <= r)).astype(F32)


class Scan:
    ROWS = XC + 16

    def __init__(self, way, b, h, nb, reach, bufs):
        self.way, self.b, self.h, self.nb = way, b, h, nb
        self.steps = Scan.step_list(reach)
        self.send_buf, self.recv_buf, self.sums, self.send, self.recv = bufs

    @staticmethod
    def step_list(reach):
        steps, d = [], 1
        while d < reach:
            steps.append(d)
            d *= 2
        return steps + [1]

    @staticmethod
    def scratch(reach):
        n = len(Scan.step_list(reach))
        return [
            pltpu.VMEM((n, Scan.ROWS, 128), BF),
            pltpu.VMEM((n, Scan.ROWS, 128), BF),
            pltpu.VMEM((Scan.ROWS, 128), F32),
            pltpu.SemaphoreType.DMA((n,)),
            pltpu.SemaphoreType.DMA((n,)),
        ]

    @staticmethod
    def edges(b, h, nb, reach):
        out = []
        for d in sorted(set(Scan.step_list(reach))):
            out += [(b + d < nb, (b + d, h)), (b >= d, (b - d, h))]
        return out

    def has_to(self, d):
        return (self.b + d < self.nb) if self.way > 0 else (self.b >= d)

    def has_from(self, d):
        return (self.b >= d) if self.way > 0 else (self.b + d < self.nb)

    def copy(self, i):
        return copy_to(
            self.send_buf.at[i], self.recv_buf.at[i], self.send.at[i], self.recv.at[i],
            (self.b + self.way * self.steps[i], self.h),
        )

    def set(self, state, decay):
        self.sums[0:XC, :] = state
        self.sums[XC : XC + 8, :] = jnp.broadcast_to(decay, (8, 128))
        self.sums[XC + 8 :, :] = jnp.zeros((8, 128), F32)
        self.send_step(0)

    def send_step(self, i):
        self.send_buf[i] = self.sums[...].astype(BF)

        @pl.when(self.has_to(self.steps[i]))
        def _():
            self.copy(i).start()

    def receive(self, i):
        there = self.has_from(self.steps[i])

        @pl.when(there)
        def _():
            self.copy(i).wait_recv()

        @pl.when(jnp.logical_not(there))
        def _():
            self.recv_buf[i] = jnp.zeros((Scan.ROWS, 128), BF)

    def join(self, i):
        if i + 1 >= len(self.steps):
            return
        self.receive(i)
        early = self.recv_buf[i].astype(F32)
        for j in range(HG):
            mine = pl.ds(j * MHDIM, MHDIM)
            decay = self.sums[pl.ds(XC + j, 1), :]
            self.sums[mine, :] = self.sums[mine, :] + decay * early[j * MHDIM : (j + 1) * MHDIM]
        self.sums[pl.ds(XC, 8), :] = self.sums[pl.ds(XC, 8), :] * early[XC : XC + 8]
        self.send_step(i + 1)

    def last(self):
        end = len(self.steps) - 1
        self.receive(end)
        return self.recv_buf.at[end]

    def finish(self):
        for i, d in enumerate(self.steps):

            @pl.when(self.has_to(d))
            def _():
                self.copy(i).wait_send()


def halo_edges(b, h, nb, reach):
    out = []
    for d in range(1, reach + 1):
        out += [(b + d < nb, (b + d, h)), (b >= d, (b - d, h))]
    return out


class Halo:
    def __init__(self, way, src, dst, b, h, nb, reach, sems):
        self.way, self.src, self.dst, self.b, self.h, self.nb, self.reach = way, src, dst, b, h, nb, reach
        self.send, self.recv = sems

    @staticmethod
    def scratch(reach):
        return [pltpu.SemaphoreType.DMA((reach + 1,))] * 2

    def there(self, d, way):
        return (self.b + d < self.nb) if way > 0 else (self.b >= d)

    def copy(self, d):
        return copy_to(
            self.src(d), self.dst(d), self.send.at[d], self.recv.at[d], (self.b + self.way * d, self.h)
        )

    def begin(self):
        for d in range(1, self.reach + 1):

            @pl.when(self.there(d, self.way))
            def _():
                self.copy(d).start()

    def finish_recv(self):
        for d in range(1, self.reach + 1):

            @pl.when(self.there(d, -self.way))
            def _():
                self.copy(d).wait_recv()

    def finish_send(self):
        for d in range(1, self.reach + 1):

            @pl.when(self.there(d, self.way))
            def _():
                self.copy(d).wait_send()


class HeadSum:
    def __init__(self, b, h, bufs):
        self.b, self.h = b, h
        self.buf, self.send, self.recv = bufs

    @staticmethod
    def scratch(T):
        return [pltpu.VMEM((4, 8, T), F32), pltpu.SemaphoreType.DMA((3,)), pltpu.SemaphoreType.DMA((3,))]

    def copies(self):
        return [
            copy_to(self.buf.at[0], self.buf.at[1 + i], self.send.at[i], self.recv.at[i], (self.b, to))
            for i, to in enumerate((other(self.h, 1), other(self.h, 2), NH - 1 - self.h))
        ]

    def begin(self, column):
        T = self.buf.shape[2]
        self.buf[0] = jnp.broadcast_to(column, (T, 128)).T[:8]
        for c in self.copies():
            c.start()

    def finish(self):
        for c in self.copies():
            c.wait()
        T = self.buf.shape[2]
        total = self.buf[0] + self.buf[1] + self.buf[2] + self.buf[3]
        return jnp.concatenate([total, jnp.zeros((120, T), F32)], axis=0).T[:, 0:1]


def group_taps(h, w_ref, b_ref, chunk):
    if chunk < XC // 128:
        at = pl.ds(pl.multiple_of(h * XC + chunk * 128, 128), 128)
    else:
        at = pl.ds(DI + (chunk - XC // 128) * 128, 128)
    return w_ref[:, at], (None if b_ref is None else b_ref[:, at])


def decays_of(dt_ref, bias_ref, alog_ref, h, T):
    valid = valid_row()
    z = dt_ref[...] + head_row(bias_ref, h)
    step = jnp.where(valid, jnp.maximum(z, 0.0) + jnp.log1p(jnp.exp(-jnp.abs(z))), 0.0)
    a_neg = jnp.where(valid, -jnp.exp(head_row(alog_ref, h)), 0.0)
    cum = jnp.dot(triangle(T), step * a_neg, precision=high, preferred_element_type=F32)
    return z, step, a_neg, cum


def by_batch(pick):
    first, second = pick(0), pick(1)
    return jnp.where(lanes((first.shape[0], 128)) < 8, first, second)


def norm_back(value, scale, gain, upstream):
    n = value * scale
    uw = upstream * gain
    grad = scale * (uw - n * jnp.mean(n * uw, axis=1, keepdims=True))
    return grad, jnp.sum(upstream * n, axis=0, keepdims=True)


def arrange(per, width, first):
    total = XC + 128
    share, mix, att = total // per, XC // per, 128 // per
    n, src = lanes((width, total)), rows_of((width, total))
    i, u = n // share, lax.rem(n, share)
    if first == 0:
        hit = (u < mix) & (src == i * mix + u)
    else:
        hit = (u >= mix) & (src == i * att + u - mix)
    return hit.astype(F32).astype(BF)


def head_select(m):
    return (lanes((XC, 128)) == 8 * m + rows_of((XC, 128)) // MHDIM).astype(F32)


def exact(a, b):
    return jnp.dot(a, b, precision=high, preferred_element_type=F32)


class LineReduce:
    def __init__(self, src, bufs, b, h, nb):
        self.src, self.h, self.nz = src, h, nb // 2
        self.z, self.x = b // 2, lax.rem(b, 2)
        self.whole = len(bufs) == 10
        if self.whole:
            self.total, self.from_l, self.from_r, self.ls, self.lr, self.rs, self.rr, self.from_x, self.xs, self.xr = bufs
        else:
            self.total, self.from_l, self.from_r, self.ls, self.lr, self.rs, self.rr = bufs

    @staticmethod
    def scratch(nb, cols, whole=True):
        nz, rpb = nb // 2, D // nb
        buf, sem = pltpu.VMEM((nz, rpb, cols), BF), pltpu.SemaphoreType.DMA((nz,))
        return [buf] * 3 + [sem] * 4 + ([buf] + [sem] * 2 if whole else [])

    def to_x(self, z):
        return copy_to(
            self.src.at[z, 1 - self.x], self.from_x.at[z], self.xs.at[z], self.xr.at[z], (2 * self.z + 1 - self.x, self.h)
        )

    def up(self, z):
        return copy_to(
            self.total.at[z], self.from_l.at[z], self.rs.at[z], self.lr.at[z], (2 * (self.z + 1) + self.x, self.h)
        )

    def down(self, z):
        return copy_to(
            self.total.at[z], self.from_r.at[z], self.ls.at[z], self.rr.at[z], (2 * (self.z - 1) + self.x, self.h)
        )

    def start_x(self, j):
        self.to_x(jnp.where(self.z < self.nz // 2, self.nz - 1 - j, j)).start()

    def start_some(self, part, parts=4):
        for j in range(part * self.nz // parts, (part + 1) * self.nz // parts):
            self.start_x(j)

    def paired(self, z):
        if not self.whole:
            return self.src[z].astype(F32)
        self.to_x(z).wait_recv()
        return self.src[z, self.x].astype(F32) + self.from_x[z].astype(F32)

    def step(self, t):
        z_up, z_down = self.nz - 1 - t + self.z, t - (self.nz - 1) + self.z

        @pl.when(t >= self.z)
        def _():
            value = self.paired(z_up)

            @pl.when(self.z == 0)
            def _():
                self.total[z_up] = value.astype(BF)

            @pl.when(self.z > 0)
            def _():
                self.up(z_up).wait_recv()
                self.total[z_up] = (value + self.from_l[z_up].astype(F32)).astype(BF)

            self.up(z_up).start()

        @pl.when(z_down >= 0)
        def _():
            value = self.paired(z_down)

            @pl.when(self.z == self.nz - 1)
            def _():
                self.total[z_down] = value.astype(BF)

            @pl.when(self.z < self.nz - 1)
            def _():
                self.down(z_down).wait_recv()
                self.total[z_down] = (value + self.from_r[z_down].astype(F32)).astype(BF)

            self.down(z_down).start()

    def step_some(self, part, parts=3):
        for t in range(part * (self.nz - 1) // parts, (part + 1) * (self.nz - 1) // parts):
            self.step(t)

    def finish(self, result):
        z = self.z
        result[...] = self.paired(z)

        @pl.when(z >= 1)
        def _():
            self.up(z).wait_recv()
            result[...] += self.from_l[z].astype(F32)

        @pl.when(z + 1 < self.nz)
        def _():
            self.down(z).wait_recv()
            result[...] += self.from_r[z].astype(F32)

    def done(self):
        for z in range(self.nz):
            if self.whole:
                self.to_x(z).wait_send()

            @pl.when(self.z < z)
            def _():
                self.up(z).wait_send()

            @pl.when(self.z > z)
            def _():
                self.down(z).wait_send()


class PairReduce:
    def __init__(self, src, bufs, b, h, nb):
        self.src, self.h, self.nz = src, h, nb // 2
        self.z, self.x = b // 2, lax.rem(b, 2)
        self.from_x, self.xs, self.xr = bufs

    @staticmethod
    def scratch(nb, cols):
        nz, rpb = nb // 2, D // nb
        return [pltpu.VMEM((nz, rpb, cols), BF)] + [pltpu.SemaphoreType.DMA((nz,))] * 2

    def to_x(self, z):
        return copy_to(
            self.src.at[z, 1 - self.x], self.from_x.at[z], self.xs.at[z], self.xr.at[z], (2 * self.z + 1 - self.x, self.h)
        )

    def begin(self):
        for z in range(self.nz):
            self.to_x(z).start()

    def finish(self, out, cols):
        for z in range(self.nz):
            self.to_x(z).wait_recv()
            out[z, :, cols] = (self.src[z, self.x].astype(F32) + self.from_x[z].astype(F32)).astype(BF)

    def done(self):
        for z in range(self.nz):
            self.to_x(z).wait_send()


class Sum:
    def __init__(self, bufs, b, h, nb):
        self.b, self.h, self.nb = b, h, nb
        self.acc, self.got, self.send, self.recv = bufs
        self.steps = Sum.step_list(nb)

    @staticmethod
    def step_list(nb):
        steps = [("h", 1), ("h", 2)]
        d = 1
        while d < nb:
            steps.append(("b", d))
            d *= 2
        return steps

    @staticmethod
    def scratch(nb, shape):
        n = len(Sum.step_list(nb))
        return [
            pltpu.VMEM((n + 1,) + shape, F32), pltpu.VMEM((n,) + shape, F32),
            pltpu.SemaphoreType.DMA((n,)), pltpu.SemaphoreType.DMA((n,)),
        ]

    def peer(self, i):
        kind, d = self.steps[i]
        return (self.b, other(self.h, d)) if kind == "h" else (other(self.b, d), self.h)

    def edges(self):
        return [(True, self.peer(i)) for i in range(len(self.steps))]

    def copy(self, i):
        return copy_to(self.acc.at[i], self.got.at[i], self.send.at[i], self.recv.at[i], self.peer(i))

    def begin(self, value):
        self.acc[0] = value
        self.copy(0).start()

    def step(self, i):
        self.copy(i).wait()
        self.acc[i + 1] = self.acc[i] + self.got[i]
        if i + 1 < len(self.steps):
            self.copy(i + 1).start()

    def result(self):
        return self.acc[len(self.steps)]


def pack_rows(R, S):
    eye = (rows_of((S, S)) == lanes((S, S))).astype(F32)
    gain_cols = [jnp.sum(eye * ref[...].astype(F32), axis=1, keepdims=True) for ref in (R.n1, R.n2)]
    lane = lanes((S, 128))
    for i in range(NH):
        R.pa[i, :, 0:XC] = R.mixer_in[:, DI + i * XC : DI + (i + 1) * XC]
        bc = 2 * DI + 128 * (i % 2)
        R.pa[i, :, XC : XC + 128] = R.mixer_in[:, bc : bc + 128]
        R.pa[i, :, XC + 128 : XC + 256] = R.attn_in[:, i * 128 : (i + 1) * 128]
        kv = QHEADS * HDIM + 128 * (i % 2)
        kv = R.attn_in[:, kv : kv + 128].astype(F32)
        if i >= 2:
            kv = pltpu.roll(kv, HDIM, 1)
        pick = (rows_of((MHEADS, 128)) == i * HG + lanes((MHEADS, 128)) - HDIM) & (lanes((MHEADS, 128)) >= HDIM)
        pick = pick & (lanes((MHEADS, 128)) < HDIM + HG)
        dt = nn(R.mixer_in[:, 2 * DI + 2 * STATE :], pick.astype(F32).astype(BF))
        last = jnp.where(lane < HDIM, kv, dt)
        for k in range(2):
            last = jnp.where(lane == HDIM + HG + k, gain_cols[k], last)
        R.pa[i, :, XC + 256 :] = last.astype(BF)
    for i in range(NH):
        R.pb[i, :, 0:XC] = R.mixer_in[:, i * XC : (i + 1) * XC]
        R.pb[i, :, XC : 2 * XC] = R.mixer_out[:, i * XC : (i + 1) * XC]
        R.pb[i, :, 2 * XC :] = R.attn_out[:, i * 128 : (i + 1) * 128]
        R.pc[i, :, 0:FG] = R.ffn_out[:, i * FG : (i + 1) * FG]
        R.pc[i, :, FG : 2 * FG] = R.ffn_in[:, i * FG : (i + 1) * FG]
        R.pc[i, :, 2 * FG :] = R.ffn_in[:, FF + i * FG : FF + (i + 1) * FG]


LATE_OUT = ["normed", "xin", "bc", "q", "pre", "wa", "wb", "kvh", "gw_out"]


def forward_body(nb, T, reach, local, R):
    b, h = place()
    moves = Moves(R, LATE_OUT, True)
    core, y = lax.rem(h, 2), h // 2
    tok, rpb = T // NH, D // nb
    S, nz = rpb // NH, nb // 2
    pair = (b, other(h, 1))
    peers = (other(h, 1), other(h, 2), NH - 1 - h)
    if local:
        pack_rows(R, S)
    R.cb2[...] = R.cb[...].reshape(1, DI + 256)
    R.gain2[...] = R.gain[...].reshape(1, DI)
    barrier(
        head_edges(b, h)
        + line_edges(b, h, nb)
        + [((h == NH - 1) & (b + 1 < nb), (b + 1, jnp.int32(i))) for i in range(NH)]
        + [(b >= 1, (b - 1, jnp.int32(NH - 1)))]
        + Scan.edges(b, h, nb, reach)
        + halo_edges(b, h, nb, reach)
    )
    packs, weights = (R.pa, R.pb, R.pc), (R.v_wa, R.v_wb, R.wc)
    gather_x = HeadGather(lambda m, i: R.xg.at[m, pl.ds(LAG + i * tok, tok)], b, h, members(R, "gx", 2))
    gather_c = HeadGather(lambda m, i: R.cotg.at[m, pl.ds(i * tok, tok)], b, h, members(R, "gc", 2))
    spots = [(R.v_wa, slice(XC, WA)), (R.v_wa, slice(0, XC)), (R.v_wb, slice(0, WB))] + [(R.wc, slice(k * FG, (k + 1) * FG)) for k in range(3)]
    lines = [
        LineGather(
            lambda i, w=w, cols=cols: w.at[pl.ds(i * rpb, rpb), cols], b, h, nb, members(R, f"line{k}_", 5)
        )
        for k, (w, cols) in enumerate(spots)
    ]

    def piece(k, i):
        mine = weights[k].at[pl.ds(b * rpb + h * S, S)]
        return copy_to(packs[k].at[peers[i]], mine, R.ps.at[k, i], R.pr.at[k, i], (b, peers[i]))

    def start_pieces(k):
        if local:
            for i in range(3):
                piece(k, i).start()
            weights[k][pl.ds(b * rpb + h * S, S), :] = packs[k][h]
        else:
            weights[k][pl.ds(b * rpb, rpb), :] = packs[k][...]

    def wait_pieces(k):
        if local:
            for i in range(3):
                piece(k, i).wait_recv()

    start_pieces(0)
    for m in range(2):
        R.xg[m, pl.ds(LAG + h * tok, tok), :] = R.x[m]
        R.cotg[m, pl.ds(h * tok, tok), :] = R.cot[m]
    for m in range(2):
        gather_x.begin(m)

    def edge(i):
        return copy_to(
            R.x.at[:, pl.ds(tok - LAG, LAG)], R.xg.at[:, pl.ds(0, LAG)], R.es.at[i], R.er.at[0], (b + 1, jnp.int32(i))
        )

    @pl.when((h == NH - 1) & (b + 1 < nb))
    def _():
        for i in range(NH):
            edge(i).start()

    @pl.when(b == 0)
    def _():
        R.xg[:, 0:LAG, :] = jnp.zeros((2, LAG, D), BF)

    start_pieces(1)
    wait_pieces(0)
    lines[0].begin()
    lines[1].begin()
    rope_tables(R.freq, b, T, R.cosine, R.sine)
    for m in range(2):
        gather_x.forward(m)
    for m in range(2):
        gather_x.finish(m)

    @pl.when(b >= 1)
    def _():
        edge(0).wait_recv()

    for m in range(2):
        v = R.xg[m].astype(F32)
        R.wide[m] = v * lax.rsqrt(jnp.mean(v * v, axis=1, keepdims=True) + EPS)
    share = lambda part: range(part * (nz - 1) // 3, (part + 1) * (nz - 1) // 3)

    def ahead(part, *which):
        for s in share(part):
            for k in which:
                lines[k].advance(s)

    ahead(0, 0, 1)
    wait_pieces(1)
    start_pieces(2)
    for m in range(2):
        gather_c.begin(m)
    ahead(1, 0, 1)
    lines[2].begin()
    ahead(2, 0, 1)
    lines[0].finish()

    last = R.v_wa[:, XC + 256 :].astype(F32).T
    R.gains[...] = last[HDIM + HG + 2 - 8 : HDIM + HG + 2]
    n1 = R.gains[6:7, :]
    for m in range(2):
        R.v_normed[m] = (R.wide[m] * n1).astype(BF)
    lane = lanes((T, 128))
    mine_bc = pl.ds(pl.multiple_of(core * 128, 128), 128)
    kv = [nn(R.v_normed[m, LAG:], R.v_wa[:, XC + 256 :]) for m in range(2)]
    packed = jnp.where(lane < HDIM, kv[0], pltpu.roll(kv[1], HDIM, 1))
    turned = rotate_pair(packed, R.cosine[...], R.sine[...])
    R.v_kvh[0, core] = jnp.where(core == 0, turned, packed).astype(BF)
    halo = Halo(1, lambda d: R.v_kvh.at[0, core], lambda d: R.v_kvh.at[d, core], b, h, nb, reach, members(R, "halo", 2))
    halo.begin()
    for m in range(2):
        R.v_bc[m, :, mine_bc] = nn(R.v_normed[m], R.v_wa[:, XC : XC + 128]).astype(BF)
    swap = (
        lambda: copy_to(R.v_bc.at[:, :, mine_bc], R.v_bc.at[:, :, mine_bc], R.ss.at[0], R.sr.at[0], pair),
        lambda: copy_to(R.v_kvh.at[0, core], R.v_kvh.at[0, core], R.ss.at[1], R.sr.at[1], pair),
    )
    for c in swap:
        c().start()
    wait_pieces(2)
    lines[3].begin()
    dt = [pltpu.roll(kv[0], 128 - HDIM, 1), pltpu.roll(kv[1], 128 - HDIM + 8, 1)]
    R.dt[...] = (
        jnp.where(lane < HG, dt[0], jnp.where((lane >= 8) & (lane < 8 + HG), dt[1], 0.0)).astype(BF).astype(F32)
    )
    for m in range(2):
        q = nn(R.v_normed[m, LAG:], R.v_wa[:, XC + 128 : XC + 256])
        R.v_q[m] = rotate_pair(q, R.cosine[...], R.sine[...]).astype(BF)
    lines[1].finish()
    for m in range(2):
        R.v_xin[m] = nn(R.v_normed[m], R.v_wa[:, 0:XC]).astype(BF)

    scans = [Scan(1, b, h, nb, reach, members(R, f"scan{m}_", 5)) for m in range(2)]
    sums = [HeadSum(b, h, members(R, f"sumf{m}_", 3)) for m in range(2)]
    back_sums = [HeadSum(b, h, members(R, f"sumb{m}_", 3)) for m in range(2)]
    pos = b * T + rows_of((T, 1))
    first = [doc_start(R.starts, m, pos) for m in range(2)]
    tail = [f[T - 1 :, :] for f in first]
    for d in range(1, reach + 1):

        @pl.when(b < d)
        def _():
            R.v_kvh[d] = jnp.zeros((2, T, 128), BF)

    def convolve(m, chunks):
        for chunk in chunks:
            cols = pl.ds(chunk * 128, 128)
            taps, bias = group_taps(h, R.cw, R.cb2, chunk)
            total = jnp.broadcast_to(bias, (T, 128))
            for j in range(4):
                back = 3 - j
                total = total + jnp.where(
                    pos - first[m] >= back, R.cin[m, pl.ds(LAG - back, T), cols] * taps[j : j + 1], 0.0
                )
            R.v_pre[m, :, cols] = total
            act = total * sigmoid(total)
            if chunk < XC // 128:
                R.xs[m, :, cols] = act
            elif chunk == XC // 128:
                R.bs[m] = act.astype(BF)
            else:
                R.cs[m] = act.astype(BF)

    z, step, a_neg, cum = decays_of(R.dt, R.dtb, R.alog, h, T)
    R.cumt[...] = cum.T[:16]
    R.stept[...] = step.T[:16]
    cum_last = cum[T - 1 :, :]
    kept = by_batch(lambda m: jnp.broadcast_to((pos >= tail[m]).astype(F32), (T, 128)))
    omega = jnp.exp(cum_last - cum) * step * kept
    for m in range(2):
        if m == 1:
            ahead(0, 2)
        R.cin[m, :, 0:XC] = R.v_xin[m].astype(F32)
        convolve(m, range(XC // 128))
        if m == 0:
            swap[0]().wait_recv()
        R.cin[m, :, XC:] = R.v_bc[m].astype(F32)
        convolve(m, (XC // 128, XC // 128 + 1))
        weighted = (R.xs[m] * widen(omega, 8 * m)).astype(BF)
        decay = jnp.where(tail[m] < b * T, jnp.exp(R.cumt[8 * m : 8 * m + 8, T - 1 : T]), 0.0)
        scans[m].set(tn(weighted, R.bs[m]), decay)
    lines[4].begin()

    seen = lanes((T, T)) + b * T
    lane = lanes((T, 128))

    def inside(m, between):
        both = nt(R.cs[m], R.bs[m])
        allowed = (seen <= pos) & (seen >= first[m])
        for i in range(HG):
            l = 8 * m + i
            gap = jnp.where(allowed, cum[:, l : l + 1] - R.cumt[l : l + 1, :], FAR)
            weights_ts = (jnp.exp(gap) * both * R.stept[l : l + 1, :]).astype(BF)
            R.ybuf[m, :, i * MHDIM : (i + 1) * MHDIM] = nn(weights_ts, R.xs[m, :, i * MHDIM : (i + 1) * MHDIM].astype(BF))
            if i == HG // 2 - 1:
                between()
        R.ybuf[m] = R.ybuf[m] + wide_row(R.skip, h) * R.xs[m]

    def on_to_pair(d):
        return copy_to(R.v_kvh.at[d, core], R.v_kvh.at[d, core], R.hs.at[d], R.hr.at[d], pair)

    R.lse[...] = jnp.zeros((T, 128), F32)

    def attend(m, i):
        query = R.v_q[m, :, i * HDIM : (i + 1) * HDIM]

        def score(d, top):
            at = seen - d * T
            keys = R.v_kvh[d, 0, :, m * HDIM : (m + 1) * HDIM]
            s = jnp.where((at <= pos) & (at >= first[m]), nt(query, keys) * SCALE, FAR)
            R.sbuf[d] = s
            return jnp.maximum(top, jnp.max(s, axis=1, keepdims=True))

        top = lax.fori_loop(0, reach + 1, score, jnp.full((T, 1), FAR, F32))

        def weigh(d, total):
            e = jnp.exp(R.sbuf[d] - top)
            R.sbuf[d] = e
            return total + jnp.sum(e, axis=1, keepdims=True)

        total = lax.fori_loop(0, reach + 1, weigh, jnp.zeros((T, 1), F32))
        inverse = 1.0 / total

        def take(d, acc):
            probs = (R.sbuf[d] * inverse).astype(BF)
            return acc + nn(probs, R.v_kvh[d, 1, :, m * HDIM : (m + 1) * HDIM])

        out = lax.fori_loop(0, reach + 1, take, jnp.zeros((T, HDIM), F32))
        R.attnf[m, :, i * HDIM : (i + 1) * HDIM] = out
        R.attnl[m, :, i * HDIM : (i + 1) * HDIM] = out.astype(BF)
        R.lse[...] = jnp.where(lane == 2 * m + i, top + jnp.log(total), R.lse[...])

    def mixed(m):
        gate = nn(R.v_normed[m, LAG:], R.v_wb[:, 0:XC])
        R.gate[m] = gate
        R.sin[m] = scans[m].last()[...]
        live = jnp.where(first[m] < b * T, jnp.exp(cum), 0.0)
        yv = R.ybuf[m] + nt(R.cs[m], R.sin[m, 0:XC]) * widen(live, 8 * m)
        low = yv.astype(BF)
        R.ylow[m] = low
        g = low.astype(F32) * gate * sigmoid(gate)
        R.ybuf[m] = g
        sums[m].begin(jnp.sum(g * g, axis=1, keepdims=True))

    gain = R.gain2[:, pl.ds(pl.multiple_of(h * XC, 128), XC)]
    n2 = R.gains[7:8, :]
    scales = [None, None]

    def rows(ref):
        return lambda m, head: ref[m, pl.ds(pl.multiple_of(head * tok, tok), tok), :]

    def own(ref, m):
        return ref.at[m, pl.ds(pl.multiple_of(h * tok, tok), tok), :]

    out1 = HeadScatter(rows(R.wide), b, h, members(R, "sc1_", 6))
    out2 = HeadScatter(rows(R.wide), b, h, members(R, "sc2_", 6))
    out3 = HeadScatter(rows(R.part), b, h, members(R, "sc3_", 6))
    gather_s = HeadGather(lambda m, i: R.secg.at[m, pl.ds(i * tok, tok)], b, h, members(R, "gs", 2))
    gather_h = HeadGather(lambda m, i: R.hlg.at[m, pl.ds(i * tok, tok)], b, h, members(R, "gh", 2))
    w_mix, w_att, w_out, w_in = (
        lambda: R.v_wb[:, XC : 2 * XC], lambda: R.v_wb[:, 2 * XC :], lambda: R.wc[:, 0:FG], lambda: R.wc[:, FG:]
    )

    def project(m):
        scales[m] = lax.rsqrt(sums[m].finish() * (1.0 / DI) + EPS)
        R.gated[m] = (R.ybuf[m] * scales[m] * gain).astype(BF)
        R.wide[m, 0:T, :] = nt(R.gated[m], w_mix()) + nt(R.attnl[m], w_att())
        out1.begin(m)

    def second_norm(m):
        out1.finish(m)
        value = R.x[m].astype(F32) + out1.result(m)
        R.hid[m] = value
        scale = lax.rsqrt(jnp.mean(value * value, axis=1, keepdims=True) + EPS)
        own(R.secg, m)[...] = (value * scale * n2).astype(BF)
        gather_s.begin(m)

    def feed(m):
        gather_c.finish(m)
        R.gact[m] = nn(R.cotg[m], w_out())
        gather_s.finish(m)
        a = nn(R.secg[m], R.wc[:, FG : 2 * FG])
        u = nn(R.secg[m], R.wc[:, 2 * FG :])
        sg = sigmoid(a)
        si = a * sg
        R.act[m] = (si * u).astype(BF)
        R.ggu[m, :, 0:FG] = (R.gact[m] * u * (sg * (1.0 + a * (1.0 - sg)))).astype(BF)
        R.ggu[m, :, FG:] = (R.gact[m] * si).astype(BF)
        R.wide[m, 0:T, :] = nt(R.ggu[m], w_in())
        out2.begin(m)
        R.part[m] = nt(R.act[m], w_out())

    def hidden_back(m):
        out2.finish(m)
        value = R.hid[m]
        scale = lax.rsqrt(jnp.mean(value * value, axis=1, keepdims=True) + EPS)
        grad, gain_part = norm_back(value, scale, n2, out2.result(m))
        grad = grad + R.cot[m].astype(F32)
        R.gh[m] = grad
        R.gn2[...] = gain_part if m == 0 else R.gn2[...] + gain_part
        own(R.hlg, m)[...] = grad.astype(BF)
        gather_h.begin(m)

    def project_back(m):
        gather_h.finish(m)
        R.up[m] = nn(R.hlg[m], w_mix())
        gate = R.gate[m]
        n = R.ylow[m].astype(F32) * gate * sigmoid(gate) * scales[m]
        up = R.up[m]
        part = jnp.sum(up * n, axis=0, keepdims=True)
        R.ggain[...] = part if m == 0 else R.ggain[...] + part
        back_sums[m].begin(jnp.sum(up * gain * n, axis=1, keepdims=True))
        R.gattn[m] = nn(R.hlg[m], w_att()).astype(BF)

    def mixed_back(m):
        total = back_sums[m].finish()
        gate = R.gate[m]
        sg = sigmoid(gate)
        si = gate * sg
        low = R.ylow[m].astype(F32)
        n = low * si * scales[m]
        grad = scales[m] * (R.up[m] * gain - n * (total * (1.0 / DI)))
        R.gy[m] = (grad * si).astype(BF)
        R.ggate[m] = (grad * low * (sg * (1.0 + gate * (1.0 - sg)))).astype(BF)

    def weight_grad(ref, at, left, right, cols):
        ref[:, at + cols.start : at + cols.stop] = sum(tn(left[m], right[m, :, cols]) for m in range(2)).astype(BF)

    pairs = [PairReduce(getattr(R, f"gi{k}"), members(R, f"pair{k}_", 3), b, h, nb) for k in range(2)]

    def in_grad(k, q):
        cols = slice(k * FG + q * FG // 2, k * FG + (q + 1) * FG // 2)
        grad = sum(tn(R.secg[m], R.ggu[m, :, cols]) for m in range(2)).astype(BF)
        pairs[k].src[:, :, :, q * FG // 2 : (q + 1) * FG // 2] = grad.reshape(nz, 2, rpb, FG // 2)

    moves.start("normed", "xin", "bc", "q", "pre", "wa")
    inside(0, lambda: ahead(1, 2))
    for m in range(2):
        scans[m].join(0)
    ahead(0, 3)
    lines[5].begin()
    halo.finish_recv()
    for d in range(1, reach + 1):

        @pl.when(b >= d)
        def _():
            on_to_pair(d).start()

    swap[1]().wait_recv()
    for d in range(1, reach + 1):

        @pl.when(b >= d)
        def _():
            on_to_pair(d).wait_recv()

    attend(0, 0)
    ahead(2, 2)
    for i in range(1, len(scans[0].steps) - 1):
        for m in range(2):
            scans[m].join(i)
    ahead(0, 4)
    attend(0, 1)
    ahead(1, 3)
    for m in range(2):
        gather_c.forward(m)
    inside(1, lambda: ahead(0, 5))
    lines[2].finish()
    moves.start("wb", "kvh")
    mixed(0)
    ahead(1, 4)
    attend(1, 0)
    project(0)
    ahead(2, 3)
    ahead(1, 5)
    attend(1, 1)
    out1.middle(0)
    ahead(2, 4)
    mixed(1)
    second_norm(0)
    project(1)
    ahead(2, 5)
    gather_s.forward(0)
    out1.middle(1)
    for k in range(3, 6):
        lines[k].finish()
    feed(0)
    second_norm(1)
    out2.middle(0)
    gather_s.forward(1)
    feed(1)
    out2.middle(1)
    in_grad(0, 0)
    in_grad(0, 1)
    pairs[0].begin()
    hidden_back(0)
    for m in range(2):
        out3.begin(m)
    gather_h.forward(0)
    in_grad(1, 0)
    hidden_back(1)
    in_grad(1, 1)
    pairs[1].begin()
    project_back(0)
    gather_h.forward(1)
    out3.middle(0)
    out3.middle(1)
    half = [slice(k * FG // 2, (k + 1) * FG // 2) for k in range(2)]
    for k in range(2):
        weight_grad(R.v_gw_out, FG, R.cotg, R.act, half[k])
    project_back(1)
    mixed_back(0)
    per = max(nb // NH, 1)
    mix_to, att_to = arrange(per, XC, 0), arrange(per, 128, 1)
    for m in range(2):
        R.act[m] = (nn(R.gated[m], mix_to) + nn(R.attnl[m], att_to)).astype(BF)
    for k in range(2):
        weight_grad(R.v_gw_out, 0, R.hlg, R.act, half[k])
    moves.start("gw_out")
    mixed_back(1)
    for m in range(2):
        out3.finish(m)
        R.out[m] = R.hid[m] + out3.result(m)
    for k in range(2):
        pairs[k].finish(R.gw_in, slice(k * FG, (k + 1) * FG))

    if local:
        for k in range(3):
            for i in range(3):
                piece(k, i).wait_send()

    @pl.when((h == NH - 1) & (b + 1 < nb))
    def _():
        for i in range(NH):
            edge(i).wait_send()

    for c in swap:
        c().wait_send()
    for d in range(1, reach + 1):

        @pl.when(b >= d)
        def _():
            on_to_pair(d).wait_send()

    moves.wait_all()
    for g in lines + pairs + [gather_x, gather_c, gather_s, gather_h, out1, out2, out3]:
        g.done()
    for scan in scans:
        scan.finish()
    halo.finish_send()


def forward(nb, reach, ins, local):
    tok = ins["x"].shape[1]
    T, rpb = tok * NH, D // nb
    S = rpb // NH
    dma = pltpu.SemaphoreType.DMA
    outs = dict(
        normed=vm((2, LAG + T, D), BF), xin=vm((2, LAG + T, XC), BF), bc=vm((2, LAG + T, 256), BF), q=vm((2, T, 128), BF),
        kvh=vm((reach + 1, 2, T, 128), BF), dt=vm((T, 128), F32), pre=vm((2, T, XC + 256), F32),
        sin=vm((2, Scan.ROWS, 128), BF), attnf=vm((2, T, 128), F32), lse=vm((T, 128), F32), gy=vm((2, T, XC), BF),
        ggate=vm((2, T, XC), BF), gattn=vm((2, T, 128), BF), gw_in=vm((nb // 2, rpb, 2 * FG), BF), gw_out=vm((D, 2 * FG), BF), gn2=vm((1, D), F32),
        ggain=vm((1, XC), F32), out=vm((2, tok, D), F32), gh=vm((2, tok, D), F32), wa=vm((D, WA), BF), wb=vm((D, WB), BF),
        gains=vm((8, D), F32), cosine=vm((T, 128), F32), sine=vm((T, 128), F32),
    )
    V = pltpu.VMEM
    scratch = dict(
        xg=V((2, LAG + T, D), BF), cotg=V((2, T, D), BF), wc=V((D, WC), BF), wide=V((2, LAG + T, D), F32),
        gate=V((2, T, XC), F32), cin=V((2, LAG + T, XC + 256), F32), xs=V((2, T, XC), F32), bs=V((2, T, 128), BF),
        cs=V((2, T, 128), BF), ybuf=V((2, T, XC), F32), sbuf=V((reach + 1, T, T), F32), cumt=V((16, T), F32),
        stept=V((16, T), F32), ylow=V((2, T, XC), BF), gated=V((2, T, XC), BF), attnl=V((2, T, 128), BF),
        part=V((2, T, D), F32), secg=V((2, T, D), BF), hlg=V((2, T, D), BF), act=V((2, T, FG), BF),
        ggu=V((2, T, 2 * FG), BF), gact=V((2, T, FG), F32), hid=V((2, tok, D), F32), up=V((2, T, XC), F32),
        cb2=V((1, DI + 256), F32), gain2=V((1, DI), F32),
        ps=dma((3, 3)), pr=dma((3, 3)), es=dma((NH,)), er=dma((1,)), ss=dma((2,)), sr=dma((2,)),
        hs=dma((reach + 1,)), hr=dma((reach + 1,)),
    )
    scratch.update({"v_" + n: V(outs[n].shape, outs[n].dtype) for n in LATE_OUT}, moved=dma((len(LATE_OUT),)))
    if local:
        scratch.update(pa=V((NH, S, WA), BF), pb=V((NH, S, WB), BF), pc=V((NH, S, WC), BF))
    for name in ("gx", "gc", "gs", "gh"):
        scratch.update(group(name, HeadGather.scratch()))
    for k in range(2):
        scratch.update(group(f"pair{k}_", PairReduce.scratch(nb, FG)))
        scratch[f"gi{k}"] = V((nb // 2, 2, rpb, FG), BF)
    for k in range(6):
        scratch.update(group(f"line{k}_", LineGather.scratch(nb)))
    for k in range(3):
        scratch.update(group(f"sc{k + 1}_", HeadScatter.scratch(tok)))
    for m in range(2):
        scratch.update(group(f"scan{m}_", Scan.scratch(reach)))
        scratch.update(group(f"sumf{m}_", HeadSum.scratch(T)))
        scratch.update(group(f"sumb{m}_", HeadSum.scratch(T)))
    scratch.update(group("halo", Halo.scratch(reach)))
    body = functools.partial(forward_body, nb, T, reach, local)
    return run(body, ins, outs, scratch, "forward", 1, smem=("starts", "dtb", "alog", "skip"), hbm=LATE_OUT)


LATE_IN = ["pre", "gw_out", "kvh", "normed", "ggate", "xin", "bc", "wa", "wb", "gh"]


def backward_body(nb, T, reach, easy, R):
    b, h = place()
    moves = Moves(R, LATE_IN, False)
    tok, rpb = T // NH, D // nb
    nz, per = nb // 2, nb // NH
    share = (XC + 128) // per
    core, y = lax.rem(h, 2), h // 2
    pair, across = (b, other(h, 1)), (b, other(h, 2))
    total_sum = Sum(members(R, "sum", 4), b, h, nb)
    targets = [(per * h + i, b // per) for i in range(per)] if easy else []

    def away(device):
        return (device[0] != b) | (device[1] != h)

    barrier(
        head_edges(b, h) + line_edges(b, h, nb) + Scan.edges(b, h, nb, reach) + halo_edges(b, h, nb, reach)
        + [((h == NH - 1) & (b + 1 < nb), (b + 1, jnp.int32(i))) for i in range(NH)]
        + [(b >= 1, (b - 1, jnp.int32(NH - 1)))]
        + total_sum.edges()
        + [(away(t), t) for t in targets]
    )
    lines = [
        LineReduce(src, members(R, f"line{k}_", 10 if k else 7), b, h, nb)
        for k, src in enumerate((R.gw_in, R.v_gw_out, R.gwb, R.gwx, R.gwc))
    ]

    def send_ffn():
        lines[0].finish(R.res0)
        if easy:
            for i, to in enumerate((h // 2, 2 + h // 2)):
                R.fmsg[i] = R.res0[:, i * FG : (i + 1) * FG].astype(BF)
                slot = lax.rem(h, 2)

                @pl.when(to != h)
                def _():
                    copy_to(R.fmsg.at[i], R.fgot.at[slot], R.fs.at[i], R.fr.at[slot], (b, to)).start()

                @pl.when(to == h)
                def _():
                    R.fgot[slot] = R.fmsg[i]
        else:
            R.raw[:, 0 : 2 * FG] = R.res0[...].astype(BF)

    def send_out():
        lines[1].finish(R.res1)
        if easy:
            slot = lax.rem(b, per)
            for i, to in enumerate(targets):
                for j in range(2):
                    R.msg[i, j] = R.res1[:, j * FG + i * share : j * FG + (i + 1) * share].astype(BF)

                @pl.when(away(to))
                def _():
                    copy_to(R.msg.at[i], R.got.at[slot], R.ms.at[i], R.mr.at[slot], to).start()

                @pl.when(jnp.logical_not(away(to)))
                def _():
                    R.got[slot] = R.msg[i]
        else:
            R.raw[:, 2 * FG :] = R.res1[...].astype(BF)

    gather = HeadGather(lambda m, i: (R.w1b, R.w1c)[m].at[i], b, h, members(R, "gw", 2))

    def send_gate():
        lines[2].finish(R.res2)
        R.w1b[h] = R.res2[...].astype(BF)
        gather.begin(0)

    moves.start("pre", "gw_out", "kvh", "normed", "ggate", "xin", "bc", "wa", "wb", "gh")
    lines[0].step_some(0)
    moves.wait("pre", "gw_out")
    lines[1].start_some(0)
    scans = [Scan(-1, b, h, nb, reach, members(R, f"scan{m}_", 5)) for m in range(2)]
    halo = Halo(-1, lambda d: R.gkvs.at[d], lambda d: R.gkvr.at[d], b, h, nb, reach, members(R, "halo", 2))
    pos = b * T + rows_of((T, 1))
    first = [doc_start(R.starts, m, pos) for m in range(2)]
    tail = [f[T - 1 :, :] for f in first]
    seen = lanes((T, T)) + b * T
    lane = lanes((T, 128))
    for m in range(2):
        for chunk in range((XC + 256) // 128):
            cols = pl.ds(chunk * 128, 128)
            value = R.v_pre[m, :, cols]
            act = value * sigmoid(value)
            if chunk < XC // 128:
                R.xs[m, :, cols] = act
            elif chunk == XC // 128:
                R.bs[m] = act.astype(BF)
            else:
                R.cs[m] = act.astype(BF)
    z, step, a_neg, cum = decays_of(R.dt, R.dtb, R.alog, h, T)
    R.cumt[...] = cum.T[:16]
    R.stept[...] = step.T[:16]
    cum_last = cum[T - 1 :, :]
    live = jnp.exp(cum) * by_batch(lambda m: jnp.broadcast_to((first[m] < b * T).astype(F32), (T, 128)))
    kept = jnp.exp(cum_last - cum) * by_batch(lambda m: jnp.broadcast_to((pos >= tail[m]).astype(F32), (T, 128)))
    omega = kept * step
    for m in range(2):
        u = (R.gy[m].astype(F32) * widen(live, 8 * m)).astype(BF)
        decay = jnp.where(tail[m] < b * T, jnp.exp(R.cumt[8 * m : 8 * m + 8, T - 1 : T]), 0.0)
        scans[m].set(tn(u, R.cs[m]), decay)
    lines[0].step_some(1)
    lines[1].start_some(1)
    moves.wait("kvh")

    R.gkv[...] = jnp.zeros_like(R.gkv)
    for m in range(2):
        for i in range(2):
            mine = slice(i * HDIM, (i + 1) * HDIM)
            query, grad = R.q[m, :, mine], R.gattn[m, :, mine]
            delta = jnp.sum(grad.astype(F32) * R.attnf[m, :, mine], axis=1, keepdims=True)
            lse = R.lse[:, 2 * m + i : 2 * m + i + 1]

            def block(d, acc):
                at = seen - d * T
                keys = R.v_kvh[d, 0, :, m * HDIM : (m + 1) * HDIM]
                vals = R.v_kvh[d, 1, :, m * HDIM : (m + 1) * HDIM]
                probs = jnp.where((at <= pos) & (at >= first[m]), jnp.exp(nt(query, keys) * SCALE - lse), 0.0)
                ds = (probs * (nt(grad, vals) - delta)).astype(BF)
                R.gkv[d, 0, :, m * HDIM : (m + 1) * HDIM] += tn(ds, query) * SCALE
                R.gkv[d, 1, :, m * HDIM : (m + 1) * HDIM] += tn(probs.astype(BF), grad)
                return acc + nn(ds, keys)

            R.gq[m, :, mine] = lax.fori_loop(0, reach + 1, block, jnp.zeros((T, HDIM), F32)) * SCALE
            if m == 0 and i == 1:
                lines[1].start_some(2)
            elif m == 1 and i == 0:
                lines[0].step_some(2)
            elif m == 1:
                lines[1].start_some(3)
        if m == 0:
            for scan in scans:
                scan.join(0)
    for d in range(reach + 1):
        R.pair_k[d] = R.gkv[d, 1 - core].astype(BF)
    swap_k = lambda: copy_to(R.pair_k, R.pair_kr, R.ss.at[0], R.sr.at[0], pair)
    swap_k().start()

    moves.wait("normed", "ggate")
    for m in range(2):
        R.gproj[m, 0:LAG, WA:] = jnp.zeros((LAG, XC), BF)
        R.gproj[m, LAG:, WA:] = R.v_ggate[m]
        R.gproj[m, 0:LAG, XC + 128 :WA] = jnp.zeros((LAG, 256), BF)
        R.gproj[m, LAG:, XC + 128 : XC + 256] = rotate_pair(R.gq[m], R.cosine[...], -R.sine[...]).astype(BF)


    def weight_grad(ref, at, cols):
        grad = sum(tn(R.v_normed[m], R.gproj[m, :, cols]) for m in range(2)).astype(BF)
        ref[:, :, :, at : at + cols.stop - cols.start] = grad.reshape(nz, 2, rpb, cols.stop - cols.start)

    weight_grad(R.gwb, 0, slice(WA, WA + XC))
    weight_grad(R.gwb, XC, slice(XC + 128, XC + 256))
    swap_k().wait_recv()
    for d in range(reach + 1):
        value = R.gkv[d, core] + R.pair_kr[d].astype(F32)
        if d == 0:
            R.gkv[0, core] = value
        else:
            R.gkvs[d] = value.astype(BF)
    halo.begin()
    lines[1].step_some(0)

    row_sums = jnp.zeros((T, 128), F32)
    R.rowq[...] = jnp.zeros_like(R.rowq)
    skip = wide_row(R.skip, h)
    gskip = jnp.zeros((1, 128), F32)
    for m in range(2):
        both = nt(R.cs[m], R.bs[m])
        allowed = (seen <= pos) & (seen >= first[m])
        gboth = jnp.zeros((T, T), F32)
        for i in range(HG):
            l = 8 * m + i
            mine = slice(i * MHDIM, (i + 1) * MHDIM)
            grad = R.gy[m, :, mine]
            decay = jnp.exp(jnp.where(allowed, cum[:, l : l + 1] - R.cumt[l : l + 1, :], FAR))
            srow = R.stept[l : l + 1, :]
            ld = decay * nt(grad, R.xs[m, :, mine].astype(BF))
            gboth = gboth + ld * srow
            q = ld * both
            R.rowq[l : l + 1, :] = jnp.sum(q, axis=0, keepdims=True)
            row_sums = jnp.where(lane == l, jnp.sum(q * srow, axis=1, keepdims=True), row_sums)
            R.gx[m, :, mine] = tn((decay * both * srow).astype(BF), grad)
            if i == HG // 2:
                if m == 1:
                    lines[2].start_some(2)
                    lines[2].start_some(3)
        low = gboth.astype(BF)
        R.gcm[m] = nn(low, R.bs[m])
        R.gbm[m] = tn(low, R.cs[m])
        gyf = R.gy[m].astype(F32)
        gskip = gskip + exact(jnp.sum(gyf * R.xs[m], axis=0, keepdims=True), head_select(m))
        R.gx[m] = R.gx[m] + skip * gyf
        u = gyf * widen(live, 8 * m)
        carried = nt(R.cs[m], R.sin[m, 0:XC])
        row_sums = row_sums + exact(u * carried, head_select(m))
        R.gcm[m] += nn(u.astype(BF), R.sin[m, 0:XC])
        if m == 0:
            for scan in scans:
                scan.join(1)
            lines[1].step_some(1)
            lines[2].start_some(0)
            lines[2].start_some(1)
    for scan in scans:
        for i in range(2, len(scan.steps) - 1):
            scan.join(i)

    colq = jnp.concatenate([R.rowq[...], jnp.zeros((112, T), F32)], axis=0).T
    gstep = colq
    gcum = row_sums - step * colq
    glast = jnp.zeros((1, 128), F32)
    for m in range(2):
        adjoint = scans[m].last()[0:XC, :]
        read = nt(R.bs[m], adjoint)
        wide = widen(omega, 8 * m)
        R.gx[m] += wide * read
        R.gbm[m] += nn((R.xs[m] * wide).astype(BF), adjoint)
        gw = exact(R.xs[m] * read, head_select(m))
        gstep = gstep + kept * gw
        term = omega * gw
        gcum = gcum - term
        glast = glast + jnp.sum(term, axis=0, keepdims=True)
        through = jnp.where(tail[m] < b * T, jnp.exp(cum_last), 0.0)
        overlap = adjoint.astype(F32) * R.sin[m, 0:XC].astype(F32)
        per_head = jnp.sum(
            lax.dot_general(overlap, head_select(m), (((0,), (0,)), ((), ())), precision=high, preferred_element_type=F32),
            axis=0, keepdims=True,
        )
        glast = glast + through * per_head
    gcum = gcum + jnp.where(rows_of((T, 128)) == T - 1, glast, 0.0)
    gda = exact(triangle(T, upper=True), gcum)
    gstep = gstep + gda * a_neg
    gz = jnp.where(valid_row(), gstep * sigmoid(z), 0.0)
    lines[1].step_some(2)
    moves.wait("xin", "bc")

    conv_grad = [[], []]
    R.gcin[...] = jnp.zeros_like(R.gcin)
    R.gcw[...] = jnp.zeros_like(R.gcw)
    for m in range(2):
        R.cin[:, 0:XC] = R.v_xin[m].astype(F32)
        R.cin[:, XC:] = R.v_bc[m].astype(F32)
        for chunk in range((XC + 256) // 128):
            cols = pl.ds(chunk * 128, 128)
            taps, _ = group_taps(h, R.cw, None, chunk)
            pre = R.v_pre[m, :, cols]
            sg = sigmoid(pre)
            if chunk < XC // 128:
                up = R.gx[m, :, cols]
            elif chunk == XC // 128:
                up = R.gbm[m]
            else:
                up = R.gcm[m]
            gs = up * (sg * (1.0 + pre * (1.0 - sg)))
            R.gcw[4:5, cols] += jnp.sum(gs, axis=0, keepdims=True)
            for back in range(4):
                j = 3 - back
                near = jnp.where(pos - first[m] >= back, gs, 0.0)
                R.gcw[j : j + 1, cols] += jnp.sum(near * R.cin[pl.ds(LAG - back, T), cols], axis=0, keepdims=True)
                R.gcin[m, pl.ds(LAG - back, T), cols] += near * taps[j : j + 1]

    mine_bc = pl.ds(pl.multiple_of(XC + core * 128, 128), 128)
    pair_bc = pl.ds(pl.multiple_of(XC + (1 - core) * 128, 128), 128)
    for m in range(2):
        R.pair_b[m] = R.gcin[m, :, pair_bc].astype(BF)
    swap_b = lambda: copy_to(R.pair_b, R.pair_br, R.ss.at[1], R.sr.at[1], pair)
    swap_b().start()
    for m in range(2):
        R.gproj[m, :, 0:XC] = R.gcin[m, :, 0:XC].astype(BF)
    weight_grad(R.gwx, 0, slice(0, XC))
    for k in range(4):
        lines[3].start_some(k)
    send_ffn()
    lines[2].step_some(0)
    halo.finish_recv()
    packed = R.gkv[0, core]
    for d in range(1, reach + 1):
        packed = packed + jnp.where(b + d < nb, R.gkvr[d].astype(F32), 0.0)
    turned = rotate_pair(packed, R.cosine[...], -R.sine[...])
    packed = jnp.where(core == 0, turned, packed)
    swap_b().wait_recv()
    for m in range(2):
        value = R.gcin[m, :, mine_bc] + R.pair_br[m].astype(F32)
        R.sum_b[m] = value
        R.across_b[m] = value.astype(BF)
    swap_y = lambda: copy_to(R.across_b, R.across_br, R.ss.at[2], R.sr.at[2], across)
    swap_y().start()
    for m in range(2):
        mine = packed if m == 0 else pltpu.roll(packed, HDIM, 1)
        gdt = pltpu.roll(gz, HDIM - 8 * m, 1)
        R.gproj[m, LAG:, XC + 256 : WA] = jnp.where(
            lane < HDIM, mine, jnp.where(lane < HDIM + HG, gdt, 0.0)
        ).astype(BF)
    weight_grad(R.gwc, 128, slice(XC + 256, WA))
    swap_y().wait_recv()
    half = lanes((LAG + T, 128)) // HDIM == y
    for m in range(2):
        R.gproj[m, :, XC : XC + 128] = jnp.where(half, R.sum_b[m] + R.across_br[m].astype(F32), 0.0).astype(BF)
    weight_grad(R.gwc, 0, slice(XC, XC + 128))
    for k in range(4):
        lines[4].start_some(k)
    lines[2].step_some(1)
    send_out()
    moves.wait("wa", "wb")

    scatter = HeadScatter(
        lambda m, head: R.gnp[m, pl.ds(pl.multiple_of(LAG + head * tok, LAG), tok), :], b, h, members(R, "sc", 6)
    )
    for m in range(2):
        R.gnp[m] = nt(R.gproj[m, :, 0:WA], R.v_wa[...]) + nt(R.gproj[m, :, WA:], R.v_wb[:, 0:XC])
        scatter.begin(m)
        R.edge_s[m] = R.gnp[m, 0:LAG, :].astype(BF)

    n1 = R.gains[6:7, :]
    small = jnp.concatenate(
        [
            jnp.sum(gz, axis=0, keepdims=True),
            jnp.sum(gda * step, axis=0, keepdims=True) * a_neg,
            gskip,
            jnp.zeros((5, 128), F32),
        ],
        axis=0,
    )
    small = jnp.where(lanes((8, 128)) < HG, small + pltpu.roll(small, 120, 1), 0.0)
    small = pltpu.roll(small, h * HG, 1)
    R.pay[...] = jnp.zeros_like(R.pay)
    wide_x = pl.ds(pl.multiple_of(h * XC, 128), XC)
    R.pay[0:5, wide_x] = R.gcw[0:5, 0:XC]
    R.pay[0:5, DI:] = R.gcw[0:5, XC:]
    R.pay[5:6, wide_x] = R.ggain[...]
    gn1 = sum(jnp.sum(R.gnp[m] * R.v_normed[m].astype(F32), axis=0, keepdims=True) for m in range(2))
    R.pay[6:7, 0:D] = gn1 / n1
    R.pay[7:8, 0:D] = R.gn2[...]
    for k in range(3):
        R.pay[6:7, D + 128 * k : D + 128 * (k + 1)] = small[k : k + 1]
    total_sum.begin(R.pay[...])

    def edge(i):
        return copy_to(R.edge_s, R.edge_r.at[i], R.es.at[0], R.er.at[i], (b - 1, jnp.int32(NH - 1)))

    @pl.when(b >= 1)
    def _():
        edge(h).start()

    for m in range(2):
        scatter.middle(m)
    moves.wait("gh")
    lines[2].step_some(2)
    lines[3].step_some(0)
    total_sum.step(0)
    lines[4].step_some(0)
    mine = (h == NH - 1) & (b + 1 < nb)

    @pl.when(mine)
    def _():
        for i in range(NH):
            edge(i).wait_recv()

    @pl.when(jnp.logical_not(mine))
    def _():
        R.edge_r[...] = jnp.zeros_like(R.edge_r)

    for m in range(2):
        scatter.finish(m)
        R.up[m] = scatter.result(m)
        R.up[m, tok - LAG : tok, :] += sum(R.edge_r[i, m].astype(F32) for i in range(NH))
        value = R.x[m].astype(F32)
        scale = lax.rsqrt(jnp.mean(value * value, axis=1, keepdims=True) + EPS)
        R.gin[m] = R.v_gh[m] + norm_back(value, scale, n1, R.up[m])[0]
    send_gate()
    lines[3].step_some(1)
    total_sum.step(1)
    lines[4].step_some(1)
    lines[3].step_some(2)
    total_sum.step(2)
    lines[4].step_some(2)
    gather.forward(0)
    lines[3].finish(R.res3)
    R.w1c[h, :, 0:XC] = R.res3[...].astype(BF)
    total_sum.step(3)
    lines[4].finish(R.res4)
    R.w1c[h, :, XC:] = R.res4[...].astype(BF)
    gather.begin(1)
    for k in range(4, len(total_sum.steps)):
        total_sum.step(k)
    gather.forward(1)
    R.small[...] = total_sum.result()
    if easy:
        for j in range(2):
            src = 2 * lax.rem(h, 2) + j

            @pl.when(src != h)
            def _():
                copy_to(R.fmsg.at[0], R.fgot.at[j], R.fs.at[0], R.fr.at[j], (b, src)).wait_recv()

        for j in range(per):

            @pl.when(away(targets[j]))
            def _():
                copy_to(R.msg.at[0], R.got.at[j], R.ms.at[0], R.mr.at[j], targets[j]).wait_recv()

        for i, to in enumerate((h // 2, 2 + h // 2)):

            @pl.when(to != h)
            def _():
                copy_to(R.fmsg.at[i], R.fgot.at[0], R.fs.at[i], R.fr.at[0], (b, to)).wait_send()

        for i in range(per):

            @pl.when(away(targets[i]))
            def _():
                copy_to(R.msg.at[i], R.got.at[0], R.ms.at[i], R.mr.at[0], targets[i]).wait_send()

    for m in range(2):
        gather.finish(m)
    for line in lines:
        line.done()

    @pl.when(b >= 1)
    def _():
        edge(h).wait_send()

    for c in (swap_k, swap_b, swap_y):
        c().wait_send()
    gather.done()
    scatter.done()
    for scan in scans:
        scan.finish()
    halo.finish_send()


def backward(nb, reach, ins):
    tok = ins["x"].shape[1]
    T, rpb, nz, per = tok * NH, D // nb, nb // 2, nb // NH
    share = (XC + 128) // per
    easy = share % 128 == 0
    dma, V = pltpu.SemaphoreType.DMA, pltpu.VMEM
    outs = dict(
        gin=vm((2, tok, D), F32), w1b=vm((NH, rpb, XC + 128), BF), w1c=vm((NH, rpb, XC + 256), BF),
        small=vm((8, DI + 256), F32),
    )
    if easy:
        outs.update(fgot=vm((2, rpb, FG), BF), got=vm((per, 2, rpb, share), BF))
    else:
        outs.update(raw=vm((rpb, 4 * FG), BF))
    scratch = dict(
        xs=V((2, T, XC), F32), bs=V((2, T, 128), BF), cs=V((2, T, 128), BF), cumt=V((16, T), F32), stept=V((16, T), F32),
        gkv=V((reach + 1, 2, T, 128), F32), gkvs=V((reach + 1, T, 128), BF), gkvr=V((reach + 1, T, 128), BF),
        pair_k=V((reach + 1, T, 128), BF), pair_kr=V((reach + 1, T, 128), BF), gq=V((2, T, 128), F32),
        gproj=V((2, LAG + T, WA + XC), BF), gwb=V((nz, 2, rpb, XC + 128), BF), gwx=V((nz, 2, rpb, XC), BF), gwc=V((nz, 2, rpb, 256), BF),
        rowq=V((16, T), F32), gx=V((2, T, XC), F32), gbm=V((2, T, 128), F32), gcm=V((2, T, 128), F32),
        gcin=V((2, LAG + T, XC + 256), F32), gcw=V((8, XC + 256), F32), cin=V((LAG + T, XC + 256), F32),
        pair_b=V((2, LAG + T, 128), BF), pair_br=V((2, LAG + T, 128), BF), sum_b=V((2, LAG + T, 128), F32),
        across_b=V((2, LAG + T, 128), BF), across_br=V((2, LAG + T, 128), BF), gnp=V((2, LAG + T, D), F32),
        edge_s=V((2, LAG, D), BF), edge_r=V((NH, 2, LAG, D), BF), up=V((2, tok, D), F32), pay=V((8, DI + 256), F32),
        res0=V((rpb, 2 * FG), F32), res1=V((rpb, 2 * FG), F32), res2=V((rpb, XC + 128), F32), res3=V((rpb, XC), F32), res4=V((rpb, 256), F32),
        ss=dma((3,)), sr=dma((3,)), es=dma((1,)), er=dma((NH,)), moved=dma((len(LATE_IN),)),
    )
    scratch.update({"v_" + n: V(ins[n].shape, ins[n].dtype) for n in LATE_IN})
    if easy:
        scratch.update(
            fmsg=V((2, rpb, FG), BF), msg=V((per, 2, rpb, share), BF), fs=dma((2,)), fr=dma((2,)), ms=dma((per,)), mr=dma((per,)),
        )
    for k, cols in enumerate((2 * FG, 2 * FG, XC + 128, XC, 256)):
        scratch.update(group(f"line{k}_", LineReduce.scratch(nb, cols, k > 0)))
    scratch.update(group("sum", Sum.scratch(nb, (8, DI + 256))))
    for m in range(2):
        scratch.update(group(f"scan{m}_", Scan.scratch(reach)))
    scratch.update(group("halo", Halo.scratch(reach)))
    scratch.update(group("sc", HeadScatter.scratch(tok)))
    scratch.update(group("gw", HeadGather.scratch()))
    body = functools.partial(backward_body, nb, T, reach, easy)
    return run(body, ins, outs, scratch, "backward", 2, smem=("starts", "dtb", "alog", "skip"), hbm=LATE_IN)


def finish_body(nb, R):
    h = lax.axis_index("head")
    rpb, per = D // nb, nb // NH
    R.out[...] = R.out_in[...]
    R.gin[...] = R.gin_in[...]
    kv = XC + 128
    for i in range(NH):
        first, second = R.w1b[i].astype(F32).T, R.w1c[i].astype(F32).T
        R.full[i * XC : (i + 1) * XC] = first[:XC]
        R.full[DI + i * XC : DI + (i + 1) * XC] = second[:XC]
        R.fatt[i * 128 : (i + 1) * 128] = first[XC:]
        half = HDIM * (i // 2)
        at = 2 * DI + 128 * (i % 2) + half
        R.full[at : at + HDIM] = second[XC + half : XC + half + HDIM]
        at = QHEADS * HDIM + 128 * (i % 2) + half
        R.fatt[at : at + HDIM] = second[kv : kv + HDIM]
        at = 2 * DI + 256 + i * HG
        R.full[at : at + HG] = second[kv + HDIM : kv + HDIM + HG]
    for ref, out in ((R.full, R.mix_in), (R.fatt, R.att_in)):
        width = out.shape[0]
        out[...] = ref[pl.ds(h * width, width), :]
    R.cw[...] = R.small[0:4, :]
    R.cb[...] = R.small[4:5, :].reshape(DI + 256)
    R.gain[...] = R.small[5:6, 0:DI].reshape(DI)
    R.n1[...] = R.small[6:7, 0:D].reshape(D)
    R.n2[...] = R.small[7:8, 0:D].reshape(D)
    for k, ref in enumerate((R.dtb, R.alog, R.skip)):
        ref[...] = R.small[6:7, D + 128 * k : D + 128 * k + MHEADS].reshape(MHEADS)
    if hasattr(R, "got"):
        for j in range(2):
            R.ffn[:, j * FG : (j + 1) * FG] = R.fgot[j].astype(F32)
        for j in range(per):
            cols = slice(j * rpb, (j + 1) * rpb)
            both = R.got[j, 0].astype(F32).T
            R.mix_out[:, cols] = both[: XC // per]
            R.att_out[:, cols] = both[XC // per :]
            R.ffn_out[:, cols] = R.got[j, 1].astype(F32).T


def finish(nb, ins, mix_cols, att_cols):
    rpb, per = D // nb, nb // NH
    outs = dict(
        out=vm(ins["out_in"].shape, F32), gin=vm(ins["gin_in"].shape, F32), mix_in=vm((mix_cols, rpb), F32),
        att_in=vm((att_cols, rpb), F32), cw=vm((4, DI + 256), F32), cb=vm((DI + 256,), F32), gain=vm((DI,), F32),
        n1=vm((D,), F32), n2=vm((D,), F32), dtb=vm((MHEADS,), F32), alog=vm((MHEADS,), F32), skip=vm((MHEADS,), F32),
    )
    if "got" in ins:
        outs.update(
            ffn=vm((rpb, 2 * FG), F32), mix_out=vm((XC // per, per * rpb), F32), att_out=vm((128 // per, per * rpb), F32),
            ffn_out=vm((FG // per, per * rpb), F32),
        )
    V = pltpu.VMEM
    scratch = dict(full=V((NH * mix_cols, rpb), F32), fatt=V((NH * att_cols, rpb), F32))
    return run(functools.partial(finish_body, nb), ins, outs, scratch, "finish", None)


def pack_columns(mixer_in, attn_in, mixer_out, attn_out, ffn_in, ffn_out, norm_one, norm_two):
    shard = mixer_in.shape[0]
    mix_t, att_t, ffn_t = mixer_out.T, attn_out.T, ffn_out.T
    sets = ([], [], [])
    for i in range(NH):
        kv = QHEADS * HDIM + 128 * (i % 2) + HDIM * (i // 2)
        bc, dt = 2 * DI + 128 * (i % 2), 2 * DI + 2 * STATE + i * HG
        sets[0].append(
            [
                mixer_in[:, DI + i * XC : DI + (i + 1) * XC], mixer_in[:, bc : bc + 128],
                attn_in[:, i * 128 : (i + 1) * 128], attn_in[:, kv : kv + HDIM], mixer_in[:, dt : dt + HG],
                norm_one[:, None], norm_two[:, None], jnp.zeros((shard, 128 - HDIM - HG - 2), BF),
            ]
        )
        sets[1].append(
            [
                mixer_in[:, i * XC : (i + 1) * XC], mix_t[:, i * XC : (i + 1) * XC], att_t[:, i * 128 : (i + 1) * 128],
            ]
        )
        sets[2].append(
            [
                ffn_t[:, i * FG : (i + 1) * FG], ffn_in[:, i * FG : (i + 1) * FG],
                ffn_in[:, FF + i * FG : FF + (i + 1) * FG],
            ]
        )
    out = []
    for parts in sets:
        v = jnp.stack([jnp.concatenate(p, axis=1) for p in parts])
        out.append(lax.all_to_all(v, "head", split_axis=0, concat_axis=0, tiled=True).reshape(shard * NH, v.shape[2]))
    return out


def on_device(
    inputs, cotangent, doc_starts, norm_one, mixer_in, conv_weight, conv_bias, dt_bias, a_log, d_skip, ssm_gain,
    mixer_out, attn_in, attn_out, norm_two, ffn_in, ffn_out,
):
    nb = lax.axis_size("blk")
    T = inputs.shape[1] * NH
    longest = min(MAXLEN, T * nb // 2)
    reach = (longest + T - 2) // T
    shard = mixer_in.shape[0]
    rpb, nz = shard * NH, nb // 2
    local = shard % 16 == 0

    lane = np.arange(128) % HDIM % (HDIM // 2)
    freq = jnp.asarray((10000.0 ** (-(lane.astype(np.float32) * 2.0 / HDIM))).astype(np.float32))[None, :]
    small = dict(
        starts=doc_starts, cw=conv_weight, dtb=dt_bias, alog=a_log, skip=d_skip
    )
    if local:
        weights = dict(
            mixer_in=mixer_in, attn_in=attn_in, mixer_out=mixer_out.T, attn_out=attn_out.T, ffn_in=ffn_in,
            ffn_out=ffn_out.T, n1=norm_one[None, :], n2=norm_two[None, :],
        )
    else:
        weights = dict(
            zip(("pa", "pb", "pc"), pack_columns(mixer_in, attn_in, mixer_out, attn_out, ffn_in, ffn_out, norm_one, norm_two))
        )
    f = forward(nb, reach, dict(x=inputs, cot=cotangent, freq=freq, cb=conv_bias, gain=ssm_gain, **small, **weights), local)
    shape = (nz, 2, rpb, 2 * FG)
    kept = (
        "gy", "gattn", "q", "kvh", "attnf", "lse", "pre", "xin", "bc", "dt", "sin", "ggate", "cosine", "sine", "normed", "wa",
        "wb", "gh", "gains", "gn2", "ggain",
    )
    b = backward(
        nb, reach,
        dict(
            x=inputs, gw_in=f.gw_in, gw_out=f.gw_out.reshape(shape), **small,
            **{n: getattr(f, n) for n in kept},
        ),
    )
    ins = dict(out_in=f.out, gin_in=b.gin, w1b=b.w1b, w1c=b.w1c, small=b.small)
    easy = hasattr(b, "got")
    if easy:
        ins.update(fgot=b.fgot, got=b.got)
    r = finish(nb, ins, mixer_in.shape[1] // NH, attn_in.shape[1] // NH)
    if easy:
        g_ffn_in, g_mix_out, g_att_out, g_ffn_out = r.ffn, r.mix_out, r.att_out, r.ffn_out
    else:
        per = nb // NH
        head, blk = lax.axis_index("head"), lax.axis_index("blk")
        mine = lax.all_gather(b.raw[:, : 2 * FG], "head").reshape(NH, rpb, 2, FG)
        ffn = jnp.transpose(mine, (1, 2, 0, 3)).reshape(rpb, 2 * FF)
        g_ffn_in = lax.dynamic_slice_in_dim(ffn, head * (2 * FF // NH), 2 * FF // NH, 1).astype(F32)
        outs = lax.all_gather(b.raw[:, 2 * FG :], ("blk", "head")).reshape(nb, NH, rpb, 2 * FG)
        outs = jnp.transpose(outs, (1, 3, 0, 2)).reshape(NH, 2, per, FG // per, D)
        outs = lax.dynamic_slice_in_dim(outs, head * (D // NH), D // NH, 4)
        outs = jnp.transpose(outs, (0, 2, 1, 3, 4)).reshape(nb, 2, FG // per, D // NH)
        outs = lax.dynamic_index_in_dim(outs, blk, 0, False).astype(F32)
        g_mix_out, g_att_out, g_ffn_out = outs[0, : XC // per], outs[0, XC // per :], outs[1]
    return (
        r.out, r.gin, r.n1, r.mix_in.T, r.cw, r.cb, r.dtb, r.alog, r.skip, r.gain, g_mix_out, r.att_in.T, g_att_out, r.n2,
        g_ffn_in, g_ffn_out,
    )


def solution(mesh):
    both = ("blk", "head")
    tokens, rows, cols = P(None, both, None), P(both, None), P(None, both)
    split = P("blk", "head")
    return jax.shard_map(
        on_device,
        mesh=mesh,
        in_specs=(
            tokens, tokens, P(), P(both), rows, P(), P(), P(), P(), P(), P(), cols, rows, cols, P(both), rows, cols,
        ),
        out_specs=(
            tokens, tokens, P(), split, P(), P(), P(), P(), P(), P(), split, split, split, P(), split, split,
        ),
        check_vma=False,
    )
```

```python
import functools
import types

import jax
import jax.numpy as jnp
import numpy as np
from jax import lax
from jax.experimental import pallas as pl
from jax.experimental.pallas import tpu as pltpu
from jax.sharding import PartitionSpec as P

MHEADS = 24
MHDIM = 64
STATE = 128
QHEADS = 8
HDIM = 64
FF = 2048
DI = 1536
D = 1024
MAXLEN = 4096
NH = 4
HG = MHEADS // NH
XC = HG * MHDIM
FG = FF // NH
WA = XC + 3 * 128
WB = 2 * XC + 128
WC = 3 * FG
LAG = 16
EPS = 1e-5
FAR = -1e30
SCALE = HDIM**-0.5
MESH = pl.DeviceIdType.MESH
BF = jnp.bfloat16
F32 = jnp.float32
VMEM_LIMIT = 62 * 2**20
high = lax.Precision.HIGHEST


def nn(a, b):
    return lax.dot_general(a, b, (((1,), (0,)), ((), ())), preferred_element_type=F32)


def nt(a, b):
    return lax.dot_general(a, b, (((1,), (1,)), ((), ())), preferred_element_type=F32)


def tn(a, b):
    return lax.dot_general(a, b, (((0,), (0,)), ((), ())), preferred_element_type=F32)


def other(index, step):
    return index + step - 2 * step * lax.rem(index // step, 2)


def copy_to(src, dst, send, recv, where):
    return pltpu.make_async_remote_copy(
        src_ref=src, dst_ref=dst, send_sem=send, recv_sem=recv, device_id=where, device_id_type=MESH
    )


def barrier(edges):
    sem = pltpu.get_barrier_semaphore()
    for there, where in edges:
        if there is True:
            pl.semaphore_signal(sem, inc=1, device_id=where, device_id_type=MESH)
        else:

            @pl.when(there)
            def _():
                pl.semaphore_signal(sem, inc=1, device_id=where, device_id_type=MESH)

    total = 0
    for there, _ in edges:
        total = total + (1 if there is True else there.astype(jnp.int32))
    pl.semaphore_wait(sem, total)


def lanes(shape):
    return lax.broadcasted_iota(jnp.int32, shape, len(shape) - 1)


def rows_of(shape):
    return lax.broadcasted_iota(jnp.int32, shape, len(shape) - 2)


def sigmoid(v):
    return 1.0 / (1.0 + jnp.exp(-v))


def widen(cols, first, count=HG, width=MHDIM):
    return jnp.concatenate(
        [
            jnp.broadcast_to(cols[:, first + i : first + i + 1], (cols.shape[0], width))
            for i in range(count)
        ],
        axis=1,
    )


class LineGather:
    def __init__(self, piece, b, h, nb, sems):
        self.piece, self.h, self.nz = piece, h, nb // 2
        self.z, self.x = b // 2, lax.rem(b, 2)
        self.line_recv, self.send_r, self.send_l, self.x_send, self.x_recv = sems

    @staticmethod
    def scratch(nb):
        return [pltpu.SemaphoreType.DMA((nb // 2,))] * 5

    def at(self, z, x=None):
        return self.piece(2 * z + (self.x if x is None else x))

    def to_x(self, z):
        return copy_to(
            self.at(z), self.at(z), self.x_send.at[z], self.x_recv.at[z], (2 * self.z + 1 - self.x, self.h)
        )

    def to_z(self, z, way):
        send = self.send_r if way > 0 else self.send_l
        return copy_to(
            self.at(z), self.at(z), send.at[z], self.line_recv.at[z], (2 * (self.z + way) + self.x, self.h)
        )

    def begin(self):
        self.hop(0)
        self.to_x(self.z).start()

    def hop(self, s):
        @pl.when((self.z - s >= 0) & (self.z + 1 < self.nz))
        def _():
            self.to_z(self.z - s, 1).start()

        @pl.when((self.z + s < self.nz) & (self.z >= 1))
        def _():
            self.to_z(self.z + s, -1).start()

    def advance(self, s):
        left, right = self.z - 1 - s, self.z + 1 + s
        more = s + 1 < self.nz - 1

        @pl.when(left >= 0)
        def _():
            self.to_z(left, 1).wait_recv()
            if more:

                @pl.when(self.z + 1 < self.nz)
                def _():
                    self.to_z(left, 1).start()

            self.to_x(left).start()

        @pl.when(right < self.nz)
        def _():
            self.to_z(right, -1).wait_recv()
            if more:

                @pl.when(self.z >= 1)
                def _():
                    self.to_z(right, -1).start()

            self.to_x(right).start()

    def finish(self):
        for z in range(self.nz):
            copy_to(
                self.at(z, 1 - self.x),
                self.at(z, 1 - self.x),
                self.x_send.at[z],
                self.x_recv.at[z],
                (2 * self.z + 1 - self.x, self.h),
            ).wait_recv()

    def done(self):
        for z in range(self.nz):
            self.to_x(z).wait_send()

            @pl.when((z <= self.z) & (self.z + 1 < self.nz))
            def _():
                self.to_z(z, 1).wait_send()

            @pl.when((z >= self.z) & (self.z >= 1))
            def _():
                self.to_z(z, -1).wait_send()


def line_edges(b, h, nb):
    return [
        (True, (other(b, 1), h)),
        (b >= 2, (b - 2, h)),
        (b + 2 < nb, (b + 2, h)),
    ]


def head_edges(b, h):
    return [(True, (b, other(h, 1))), (True, (b, other(h, 2))), (True, (b, NH - 1 - h))]


class HeadGather:
    def __init__(self, rows, b, h, sems):
        self.rows, self.b, self.h = rows, b, h
        self.send, self.recv = sems

    @staticmethod
    def scratch():
        return [pltpu.SemaphoreType.DMA((2, 3))] * 2

    def copy(self, m, i):
        pair, across = other(self.h, 1), other(self.h, 2)
        rows = self.rows(m, self.h if i < 2 else across)
        return copy_to(rows, rows, self.send.at[m, i], self.recv.at[m, i], (self.b, across if i == 1 else pair))

    def begin(self, m):
        self.copy(m, 1).start()
        self.copy(m, 0).start()

    def forward(self, m):
        self.copy(m, 1).wait_recv()
        self.copy(m, 2).start()

    def finish(self, m):
        self.copy(m, 0).wait_recv()
        self.copy(m, 2).wait_recv()

    def done(self):
        for m in range(2):
            for i in range(3):
                self.copy(m, i).wait_send()


class HeadScatter:
    def __init__(self, full, b, h, bufs):
        self.full, self.b, self.h = full, b, h
        self.send_c, self.recv_c, self.send_y, self.recv_y, self.send, self.recv = bufs

    @staticmethod
    def scratch(rows):
        return [
            pltpu.VMEM((2, 2, rows, D), BF),
            pltpu.VMEM((2, 2, rows, D), BF),
            pltpu.VMEM((2, rows, D), BF),
            pltpu.VMEM((2, rows, D), BF),
            pltpu.SemaphoreType.DMA((2, 2)),
            pltpu.SemaphoreType.DMA((2, 2)),
        ]

    def copy(self, m, i):
        src, dst = ((self.send_c, self.recv_c), (self.send_y, self.recv_y))[i]
        return copy_to(src.at[m], dst.at[m], self.send.at[m, i], self.recv.at[m, i], (self.b, other(self.h, i + 1)))

    def begin(self, m):
        core = lax.rem(self.h, 2)
        for y in range(2):
            self.send_c[m, y] = self.full(m, 2 * y + 1 - core).astype(BF)
        self.copy(m, 0).start()

    def middle(self, m):
        core, y = lax.rem(self.h, 2), self.h // 2
        self.copy(m, 0).wait_recv()
        self.send_y[m] = (self.full(m, 2 * (1 - y) + core) + self.recv_c[m, 1 - y].astype(F32)).astype(BF)
        self.copy(m, 1).start()

    def finish(self, m):
        self.copy(m, 1).wait_recv()

    def result(self, m):
        y = self.h // 2
        return self.full(m, self.h) + self.recv_c[m, y].astype(F32) + self.recv_y[m].astype(F32)

    def done(self):
        for m in range(2):
            for i in range(2):
                self.copy(m, i).wait_send()


class Todo:
    def __init__(self):
        self.steps = []

    def add(self, *steps):
        self.steps += steps

    def tick(self, count=1):
        for _ in range(min(count, len(self.steps))):
            self.steps.pop(0)()

    def drain(self, left=0):
        self.tick(max(len(self.steps) - left, 0))


def place():
    return lax.axis_index("blk"), lax.axis_index("head")


def rotate_pair(v, cosine, sine):
    lane = lax.rem(lanes(v.shape), HDIM)
    front = lane < HDIM // 2
    partner = jnp.where(front, pltpu.roll(v, 128 - HDIM // 2, 1), pltpu.roll(v, HDIM // 2, 1))
    return v * cosine + jnp.where(front, -partner, partner) * sine


def rope_tables(freq_ref, b, rows, ref_cos, ref_sin):
    pos = (b * rows + rows_of((rows, 128))).astype(F32)
    angle = pos * freq_ref[...]
    ref_cos[...] = jnp.cos(angle)
    ref_sin[...] = jnp.sin(angle)


def vm(shape, dtype):
    return jax.ShapeDtypeStruct(shape, dtype)


def run(body, ins, outs, scratch, name, cid, smem=(), hbm=()):
    names = list(ins) + list(outs) + list(scratch)

    def kernel(*refs):
        body(types.SimpleNamespace(**dict(zip(names, refs))))

    def space(n):
        return pl.BlockSpec(memory_space=pltpu.SMEM if n in smem else (pl.ANY if n in hbm else pltpu.VMEM))

    got = pl.pallas_call(
        kernel,
        out_shape=list(outs.values()),
        in_specs=[space(n) for n in ins],
        out_specs=[space(n) for n in outs],
        scratch_shapes=list(scratch.values()),
        compiler_params=pltpu.CompilerParams(
            collective_id=cid, has_side_effects=cid is not None, vmem_limit_bytes=VMEM_LIMIT
        ),
        name=name,
    )(*ins.values())
    return types.SimpleNamespace(**dict(zip(outs, got)))


class Moves:
    def __init__(self, refs, names, out):
        self.refs, self.names, self.out = refs, names, out
        self.waiting = []

    def copy(self, name):
        far, near = getattr(self.refs, name), getattr(self.refs, "v_" + name)
        src, dst = (near, far) if self.out else (far, near)
        return pltpu.make_async_copy(src, dst, self.refs.moved.at[self.names.index(name)])

    def start(self, *names):
        for n in names:
            self.copy(n).start()
            self.waiting.append(n)

    def wait(self, *names):
        for n in names:
            self.copy(n).wait()
            self.waiting.remove(n)

    def wait_all(self):
        self.wait(*list(self.waiting))


def group(prefix, shapes):
    return {f"{prefix}{i}": s for i, s in enumerate(shapes)}


def members(refs, prefix, count):
    return [getattr(refs, f"{prefix}{i}") for i in range(count)]


def doc_start(starts_ref, m, pos):
    first = jnp.zeros(pos.shape, jnp.int32)
    for k in range(starts_ref.shape[1]):
        s = starts_ref[m, k]
        first = jnp.where(pos >= s, s, first)
    return first


def head_row(ref, h, count=2):
    lane = lanes((1, 128))
    row = jnp.zeros((1, 128), F32)
    for i in range(HG):
        for m in range(count):
            row = jnp.where(lane == 8 * m + i, ref[h * HG + i], row)
    return row


def wide_row(ref, h):
    lane = lanes((1, XC)) // MHDIM
    row = jnp.zeros((1, XC), F32)
    for i in range(HG):
        row = jnp.where(lane == i, ref[h * HG + i], row)
    return row


def valid_row():
    lane = lanes((1, 128))
    return (lane < 16) & (lax.rem(lane, 8) < HG)


def triangle(n, upper=False):
    r, c = rows_of((n, n)), lanes((n, n))
    return ((c >= r) if upper else (c <= r)).astype(F32)


class Scan:
    ROWS = XC + 16

    def __init__(self, way, b, h, nb, reach, bufs):
        self.way, self.b, self.h, self.nb = way, b, h, nb
        self.steps = Scan.step_list(reach)
        self.send_buf, self.recv_buf, self.sums, self.send, self.recv = bufs

    @staticmethod
    def step_list(reach):
        steps, d = [], 1
        while d < reach:
            steps.append(d)
            d *= 2
        return steps + [1]

    @staticmethod
    def scratch(reach):
        n = len(Scan.step_list(reach))
        return [
            pltpu.VMEM((n, Scan.ROWS, 128), BF),
            pltpu.VMEM((n, Scan.ROWS, 128), BF),
            pltpu.VMEM((Scan.ROWS, 128), F32),
            pltpu.SemaphoreType.DMA((n,)),
            pltpu.SemaphoreType.DMA((n,)),
        ]

    @staticmethod
    def edges(b, h, nb, reach):
        out = []
        for d in sorted(set(Scan.step_list(reach))):
            out += [(b + d < nb, (b + d, h)), (b >= d, (b - d, h))]
        return out

    def has_to(self, d):
        return (self.b + d < self.nb) if self.way > 0 else (self.b >= d)

    def has_from(self, d):
        return (self.b >= d) if self.way > 0 else (self.b + d < self.nb)

    def copy(self, i):
        return copy_to(
            self.send_buf.at[i], self.recv_buf.at[i], self.send.at[i], self.recv.at[i],
            (self.b + self.way * self.steps[i], self.h),
        )

    def set(self, state, decay):
        self.sums[0:XC, :] = state
        self.sums[XC : XC + 8, :] = jnp.broadcast_to(decay, (8, 128))
        self.sums[XC + 8 :, :] = jnp.zeros((8, 128), F32)
        self.send_step(0)

    def send_step(self, i):
        self.send_buf[i] = self.sums[...].astype(BF)

        @pl.when(self.has_to(self.steps[i]))
        def _():
            self.copy(i).start()

    def receive(self, i):
        there = self.has_from(self.steps[i])

        @pl.when(there)
        def _():
            self.copy(i).wait_recv()

        @pl.when(jnp.logical_not(there))
        def _():
            self.recv_buf[i] = jnp.zeros((Scan.ROWS, 128), BF)

    def join(self, i):
        if i + 1 >= len(self.steps):
            return
        self.receive(i)
        early = self.recv_buf[i].astype(F32)
        for j in range(HG):
            mine = pl.ds(j * MHDIM, MHDIM)
            decay = self.sums[pl.ds(XC + j, 1), :]
            self.sums[mine, :] = self.sums[mine, :] + decay * early[j * MHDIM : (j + 1) * MHDIM]
        self.sums[pl.ds(XC, 8), :] = self.sums[pl.ds(XC, 8), :] * early[XC : XC + 8]
        self.send_step(i + 1)

    def last(self):
        end = len(self.steps) - 1
        self.receive(end)
        return self.recv_buf.at[end]

    def finish(self):
        for i, d in enumerate(self.steps):

            @pl.when(self.has_to(d))
            def _():
                self.copy(i).wait_send()


def halo_edges(b, h, nb, reach):
    out = []
    for d in range(1, reach + 1):
        out += [(b + d < nb, (b + d, h)), (b >= d, (b - d, h))]
    return out


class Halo:
    def __init__(self, way, src, dst, b, h, nb, reach, sems):
        self.way, self.src, self.dst, self.b, self.h, self.nb, self.reach = way, src, dst, b, h, nb, reach
        self.send, self.recv = sems

    @staticmethod
    def scratch(reach):
        return [pltpu.SemaphoreType.DMA((reach + 1,))] * 2

    def there(self, d, way):
        return (self.b + d < self.nb) if way > 0 else (self.b >= d)

    def copy(self, d):
        return copy_to(
            self.src(d), self.dst(d), self.send.at[d], self.recv.at[d], (self.b + self.way * d, self.h)
        )

    def begin(self):
        for d in range(1, self.reach + 1):

            @pl.when(self.there(d, self.way))
            def _():
                self.copy(d).start()

    def finish_recv(self):
        for d in range(1, self.reach + 1):

            @pl.when(self.there(d, -self.way))
            def _():
                self.copy(d).wait_recv()

    def finish_send(self):
        for d in range(1, self.reach + 1):

            @pl.when(self.there(d, self.way))
            def _():
                self.copy(d).wait_send()


class HeadSum:
    def __init__(self, b, h, bufs):
        self.b, self.h = b, h
        self.buf, self.send, self.recv = bufs

    @staticmethod
    def scratch(T):
        return [pltpu.VMEM((4, 8, T), F32), pltpu.SemaphoreType.DMA((3,)), pltpu.SemaphoreType.DMA((3,))]

    def copies(self):
        return [
            copy_to(self.buf.at[0], self.buf.at[1 + i], self.send.at[i], self.recv.at[i], (self.b, to))
            for i, to in enumerate((other(self.h, 1), other(self.h, 2), NH - 1 - self.h))
        ]

    def begin(self, column):
        T = self.buf.shape[2]
        self.buf[0] = jnp.broadcast_to(column, (T, 128)).T[:8]
        for c in self.copies():
            c.start()

    def finish(self):
        for c in self.copies():
            c.wait()
        T = self.buf.shape[2]
        total = self.buf[0] + self.buf[1] + self.buf[2] + self.buf[3]
        return jnp.concatenate([total, jnp.zeros((120, T), F32)], axis=0).T[:, 0:1]


def group_taps(h, w_ref, b_ref, chunk):
    if chunk < XC // 128:
        at = pl.ds(pl.multiple_of(h * XC + chunk * 128, 128), 128)
    else:
        at = pl.ds(DI + (chunk - XC // 128) * 128, 128)
    return w_ref[:, at], (None if b_ref is None else b_ref[:, at])


def decays_of(dt_ref, bias_ref, alog_ref, h, T):
    valid = valid_row()
    z = dt_ref[...] + head_row(bias_ref, h)
    step = jnp.where(valid, jnp.maximum(z, 0.0) + jnp.log1p(jnp.exp(-jnp.abs(z))), 0.0)
    a_neg = jnp.where(valid, -jnp.exp(head_row(alog_ref, h)), 0.0)
    cum = jnp.dot(triangle(T), step * a_neg, precision=high, preferred_element_type=F32)
    return z, step, a_neg, cum


def by_batch(pick):
    first, second = pick(0), pick(1)
    return jnp.where(lanes((first.shape[0], 128)) < 8, first, second)


def norm_back(value, scale, gain, upstream):
    n = value * scale
    uw = upstream * gain
    grad = scale * (uw - n * jnp.mean(n * uw, axis=1, keepdims=True))
    return grad, jnp.sum(upstream * n, axis=0, keepdims=True)


def arrange(per, width, first):
    total = XC + 128
    share, mix, att = total // per, XC // per, 128 // per
    n, src = lanes((width, total)), rows_of((width, total))
    i, u = n // share, lax.rem(n, share)
    if first == 0:
        hit = (u < mix) & (src == i * mix + u)
    else:
        hit = (u >= mix) & (src == i * att + u - mix)
    return hit.astype(F32).astype(BF)


def head_select(m):
    return (lanes((XC, 128)) == 8 * m + rows_of((XC, 128)) // MHDIM).astype(F32)


def exact(a, b):
    return jnp.dot(a, b, precision=high, preferred_element_type=F32)


class LineReduce:
    def __init__(self, src, bufs, b, h, nb):
        self.src, self.h, self.nz = src, h, nb // 2
        self.z, self.x = b // 2, lax.rem(b, 2)
        self.whole = len(bufs) == 10
        if self.whole:
            self.total, self.from_l, self.from_r, self.ls, self.lr, self.rs, self.rr, self.from_x, self.xs, self.xr = bufs
        else:
            self.total, self.from_l, self.from_r, self.ls, self.lr, self.rs, self.rr = bufs

    @staticmethod
    def scratch(nb, cols, whole=True):
        nz, rpb = nb // 2, D // nb
        buf, sem = pltpu.VMEM((nz, rpb, cols), BF), pltpu.SemaphoreType.DMA((nz,))
        return [buf] * 3 + [sem] * 4 + ([buf] + [sem] * 2 if whole else [])

    def to_x(self, z):
        return copy_to(
            self.src.at[z, 1 - self.x], self.from_x.at[z], self.xs.at[z], self.xr.at[z], (2 * self.z + 1 - self.x, self.h)
        )

    def up(self, z):
        return copy_to(
            self.total.at[z], self.from_l.at[z], self.rs.at[z], self.lr.at[z], (2 * (self.z + 1) + self.x, self.h)
        )

    def down(self, z):
        return copy_to(
            self.total.at[z], self.from_r.at[z], self.ls.at[z], self.rr.at[z], (2 * (self.z - 1) + self.x, self.h)
        )

    def start_x(self, j):
        self.to_x(jnp.where(self.z < self.nz // 2, self.nz - 1 - j, j)).start()

    def start_some(self, part, parts=4):
        for j in range(part * self.nz // parts, (part + 1) * self.nz // parts):
            self.start_x(j)

    def paired(self, z):
        if not self.whole:
            return self.src[z].astype(F32)
        self.to_x(z).wait_recv()
        return self.src[z, self.x].astype(F32) + self.from_x[z].astype(F32)

    def step(self, t):
        z_up, z_down = self.nz - 1 - t + self.z, t - (self.nz - 1) + self.z

        @pl.when(t >= self.z)
        def _():
            value = self.paired(z_up)

            @pl.when(self.z == 0)
            def _():
                self.total[z_up] = value.astype(BF)

            @pl.when(self.z > 0)
            def _():
                self.up(z_up).wait_recv()
                self.total[z_up] = (value + self.from_l[z_up].astype(F32)).astype(BF)

            self.up(z_up).start()

        @pl.when(z_down >= 0)
        def _():
            value = self.paired(z_down)

            @pl.when(self.z == self.nz - 1)
            def _():
                self.total[z_down] = value.astype(BF)

            @pl.when(self.z < self.nz - 1)
            def _():
                self.down(z_down).wait_recv()
                self.total[z_down] = (value + self.from_r[z_down].astype(F32)).astype(BF)

            self.down(z_down).start()

    def step_some(self, part, parts=3):
        for t in range(part * (self.nz - 1) // parts, (part + 1) * (self.nz - 1) // parts):
            self.step(t)

    def finish(self, result):
        z = self.z
        result[...] = self.paired(z)

        @pl.when(z >= 1)
        def _():
            self.up(z).wait_recv()
            result[...] += self.from_l[z].astype(F32)

        @pl.when(z + 1 < self.nz)
        def _():
            self.down(z).wait_recv()
            result[...] += self.from_r[z].astype(F32)

    def done(self):
        for z in range(self.nz):
            if self.whole:
                self.to_x(z).wait_send()

            @pl.when(self.z < z)
            def _():
                self.up(z).wait_send()

            @pl.when(self.z > z)
            def _():
                self.down(z).wait_send()


class PairReduce:
    def __init__(self, src, bufs, b, h, nb):
        self.src, self.h, self.nz = src, h, nb // 2
        self.z, self.x = b // 2, lax.rem(b, 2)
        self.from_x, self.xs, self.xr = bufs

    @staticmethod
    def scratch(nb, cols):
        nz, rpb = nb // 2, D // nb
        return [pltpu.VMEM((nz, rpb, cols), BF)] + [pltpu.SemaphoreType.DMA((nz,))] * 2

    def to_x(self, z):
        return copy_to(
            self.src.at[z, 1 - self.x], self.from_x.at[z], self.xs.at[z], self.xr.at[z], (2 * self.z + 1 - self.x, self.h)
        )

    def begin(self):
        for z in range(self.nz):
            self.to_x(z).start()

    def finish(self, out, cols):
        for z in range(self.nz):
            self.to_x(z).wait_recv()
            out[z, :, cols] = (self.src[z, self.x].astype(F32) + self.from_x[z].astype(F32)).astype(BF)

    def done(self):
        for z in range(self.nz):
            self.to_x(z).wait_send()


class Sum:
    def __init__(self, bufs, b, h, nb):
        self.b, self.h, self.nb = b, h, nb
        self.acc, self.got, self.send, self.recv = bufs
        self.steps = Sum.step_list(nb)

    @staticmethod
    def step_list(nb):
        steps = [("h", 1), ("h", 2)]
        d = 1
        while d < nb:
            steps.append(("b", d))
            d *= 2
        return steps

    @staticmethod
    def scratch(nb, shape):
        n = len(Sum.step_list(nb))
        return [
            pltpu.VMEM((n + 1,) + shape, F32), pltpu.VMEM((n,) + shape, F32),
            pltpu.SemaphoreType.DMA((n,)), pltpu.SemaphoreType.DMA((n,)),
        ]

    def peer(self, i):
        kind, d = self.steps[i]
        return (self.b, other(self.h, d)) if kind == "h" else (other(self.b, d), self.h)

    def edges(self):
        return [(True, self.peer(i)) for i in range(len(self.steps))]

    def copy(self, i):
        return copy_to(self.acc.at[i], self.got.at[i], self.send.at[i], self.recv.at[i], self.peer(i))

    def begin(self, value):
        self.acc[0] = value
        self.copy(0).start()

    def step(self, i):
        self.copy(i).wait()
        self.acc[i + 1] = self.acc[i] + self.got[i]
        if i + 1 < len(self.steps):
            self.copy(i + 1).start()

    def result(self):
        return self.acc[len(self.steps)]


def pack_rows(R, S):
    eye = (rows_of((S, S)) == lanes((S, S))).astype(F32)
    gain_cols = [jnp.sum(eye * ref[...].astype(F32), axis=1, keepdims=True) for ref in (R.n1, R.n2)]
    lane = lanes((S, 128))
    for i in range(NH):
        R.pa[i, :, 0:XC] = R.mixer_in[:, DI + i * XC : DI + (i + 1) * XC]
        bc = 2 * DI + 128 * (i % 2)
        R.pa[i, :, XC : XC + 128] = R.mixer_in[:, bc : bc + 128]
        R.pa[i, :, XC + 128 : XC + 256] = R.attn_in[:, i * 128 : (i + 1) * 128]
        kv = QHEADS * HDIM + 128 * (i % 2)
        kv = R.attn_in[:, kv : kv + 128].astype(F32)
        if i >= 2:
            kv = pltpu.roll(kv, HDIM, 1)
        pick = (rows_of((MHEADS, 128)) == i * HG + lanes((MHEADS, 128)) - HDIM) & (lanes((MHEADS, 128)) >= HDIM)
        pick = pick & (lanes((MHEADS, 128)) < HDIM + HG)
        dt = nn(R.mixer_in[:, 2 * DI + 2 * STATE :], pick.astype(F32).astype(BF))
        last = jnp.where(lane < HDIM, kv, dt)
        for k in range(2):
            last = jnp.where(lane == HDIM + HG + k, gain_cols[k], last)
        R.pa[i, :, XC + 256 :] = last.astype(BF)
    for i in range(NH):
        R.pb[i, :, 0:XC] = R.mixer_in[:, i * XC : (i + 1) * XC]
        R.pb[i, :, XC : 2 * XC] = R.mixer_out[:, i * XC : (i + 1) * XC]
        R.pb[i, :, 2 * XC :] = R.attn_out[:, i * 128 : (i + 1) * 128]
        R.pc[i, :, 0:FG] = R.ffn_out[:, i * FG : (i + 1) * FG]
        R.pc[i, :, FG : 2 * FG] = R.ffn_in[:, i * FG : (i + 1) * FG]
        R.pc[i, :, 2 * FG :] = R.ffn_in[:, FF + i * FG : FF + (i + 1) * FG]


LATE_OUT = ["normed", "xin", "bc", "q", "pre", "wa", "wb", "kvh", "gw_out"]


def forward_body(nb, T, reach, local, R):
    b, h = place()
    moves = Moves(R, LATE_OUT, True)
    core, y = lax.rem(h, 2), h // 2
    tok, rpb = T // NH, D // nb
    S, nz = rpb // NH, nb // 2
    pair = (b, other(h, 1))
    peers = (other(h, 1), other(h, 2), NH - 1 - h)
    if local:
        pack_rows(R, S)
    R.cb2[...] = R.cb[...].reshape(1, DI + 256)
    R.gain2[...] = R.gain[...].reshape(1, DI)
    barrier(
        head_edges(b, h)
        + line_edges(b, h, nb)
        + [((h == NH - 1) & (b + 1 < nb), (b + 1, jnp.int32(i))) for i in range(NH)]
        + [(b >= 1, (b - 1, jnp.int32(NH - 1)))]
        + Scan.edges(b, h, nb, reach)
        + halo_edges(b, h, nb, reach)
    )
    packs, weights = (R.pa, R.pb, R.pc), (R.v_wa, R.v_wb, R.wc)
    gather_x = HeadGather(lambda m, i: R.xg.at[m, pl.ds(LAG + i * tok, tok)], b, h, members(R, "gx", 2))
    gather_c = HeadGather(lambda m, i: R.cotg.at[m, pl.ds(i * tok, tok)], b, h, members(R, "gc", 2))
    spots = [(R.v_wa, slice(XC, WA)), (R.v_wa, slice(0, XC)), (R.v_wb, slice(0, WB))] + [(R.wc, slice(k * FG, (k + 1) * FG)) for k in range(3)]
    lines = [
        LineGather(
            lambda i, w=w, cols=cols: w.at[pl.ds(i * rpb, rpb), cols], b, h, nb, members(R, f"line{k}_", 5)
        )
        for k, (w, cols) in enumerate(spots)
    ]

    def piece(k, i):
        mine = weights[k].at[pl.ds(b * rpb + h * S, S)]
        return copy_to(packs[k].at[peers[i]], mine, R.ps.at[k, i], R.pr.at[k, i], (b, peers[i]))

    def start_pieces(k):
        if local:
            for i in range(3):
                piece(k, i).start()
            weights[k][pl.ds(b * rpb + h * S, S), :] = packs[k][h]
        else:
            weights[k][pl.ds(b * rpb, rpb), :] = packs[k][...]

    def wait_pieces(k):
        if local:
            for i in range(3):
                piece(k, i).wait_recv()

    start_pieces(0)
    for m in range(2):
        R.xg[m, pl.ds(LAG + h * tok, tok), :] = R.x[m]
        R.cotg[m, pl.ds(h * tok, tok), :] = R.cot[m]
    for m in range(2):
        gather_x.begin(m)

    def edge(i):
        return copy_to(
            R.x.at[:, pl.ds(tok - LAG, LAG)], R.xg.at[:, pl.ds(0, LAG)], R.es.at[i], R.er.at[0], (b + 1, jnp.int32(i))
        )

    @pl.when((h == NH - 1) & (b + 1 < nb))
    def _():
        for i in range(NH):
            edge(i).start()

    @pl.when(b == 0)
    def _():
        R.xg[:, 0:LAG, :] = jnp.zeros((2, LAG, D), BF)

    start_pieces(1)
    wait_pieces(0)
    lines[0].begin()
    lines[1].begin()
    rope_tables(R.freq, b, T, R.cosine, R.sine)
    for m in range(2):
        gather_x.forward(m)
    for m in range(2):
        gather_x.finish(m)

    @pl.when(b >= 1)
    def _():
        edge(0).wait_recv()

    for m in range(2):
        v = R.xg[m].astype(F32)
        R.wide[m] = v * lax.rsqrt(jnp.mean(v * v, axis=1, keepdims=True) + EPS)
    share = lambda part: range(part * (nz - 1) // 3, (part + 1) * (nz - 1) // 3)

    def ahead(part, *which):
        for s in share(part):
            for k in which:
                lines[k].advance(s)

    ahead(0, 0, 1)
    wait_pieces(1)
    start_pieces(2)
    for m in range(2):
        gather_c.begin(m)
    ahead(1, 0, 1)
    lines[2].begin()
    ahead(2, 0, 1)
    lines[0].finish()

    last = R.v_wa[:, XC + 256 :].astype(F32).T
    R.gains[...] = last[HDIM + HG + 2 - 8 : HDIM + HG + 2]
    n1 = R.gains[6:7, :]
    for m in range(2):
        R.v_normed[m] = (R.wide[m] * n1).astype(BF)
    lane = lanes((T, 128))
    mine_bc = pl.ds(pl.multiple_of(core * 128, 128), 128)
    kv = [nn(R.v_normed[m, LAG:], R.v_wa[:, XC + 256 :]) for m in range(2)]
    packed = jnp.where(lane < HDIM, kv[0], pltpu.roll(kv[1], HDIM, 1))
    turned = rotate_pair(packed, R.cosine[...], R.sine[...])
    R.v_kvh[0, core] = jnp.where(core == 0, turned, packed).astype(BF)
    halo = Halo(1, lambda d: R.v_kvh.at[0, core], lambda d: R.v_kvh.at[d, core], b, h, nb, reach, members(R, "halo", 2))
    halo.begin()
    for m in range(2):
        R.v_bc[m, :, mine_bc] = nn(R.v_normed[m], R.v_wa[:, XC : XC + 128]).astype(BF)
    swap = (
        lambda: copy_to(R.v_bc.at[:, :, mine_bc], R.v_bc.at[:, :, mine_bc], R.ss.at[0], R.sr.at[0], pair),
        lambda: copy_to(R.v_kvh.at[0, core], R.v_kvh.at[0, core], R.ss.at[1], R.sr.at[1], pair),
    )
    for c in swap:
        c().start()
    wait_pieces(2)
    lines[3].begin()
    dt = [pltpu.roll(kv[0], 128 - HDIM, 1), pltpu.roll(kv[1], 128 - HDIM + 8, 1)]
    R.dt[...] = (
        jnp.where(lane < HG, dt[0], jnp.where((lane >= 8) & (lane < 8 + HG), dt[1], 0.0)).astype(BF).astype(F32)
    )
    for m in range(2):
        q = nn(R.v_normed[m, LAG:], R.v_wa[:, XC + 128 : XC + 256])
        R.v_q[m] = rotate_pair(q, R.cosine[...], R.sine[...]).astype(BF)
    lines[1].finish()
    for m in range(2):
        R.v_xin[m] = nn(R.v_normed[m], R.v_wa[:, 0:XC]).astype(BF)

    scans = [Scan(1, b, h, nb, reach, members(R, f"scan{m}_", 5)) for m in range(2)]
    sums = [HeadSum(b, h, members(R, f"sumf{m}_", 3)) for m in range(2)]
    back_sums = [HeadSum(b, h, members(R, f"sumb{m}_", 3)) for m in range(2)]
    pos = b * T + rows_of((T, 1))
    first = [doc_start(R.starts, m, pos) for m in range(2)]
    tail = [f[T - 1 :, :] for f in first]
    for d in range(1, reach + 1):

        @pl.when(b < d)
        def _():
            R.v_kvh[d] = jnp.zeros((2, T, 128), BF)

    def convolve(m, chunks):
        for chunk in chunks:
            cols = pl.ds(chunk * 128, 128)
            taps, bias = group_taps(h, R.cw, R.cb2, chunk)
            total = jnp.broadcast_to(bias, (T, 128))
            for j in range(4):
                back = 3 - j
                total = total + jnp.where(
                    pos - first[m] >= back, R.cin[m, pl.ds(LAG - back, T), cols] * taps[j : j + 1], 0.0
                )
            R.v_pre[m, :, cols] = total
            act = total * sigmoid(total)
            if chunk < XC // 128:
                R.xs[m, :, cols] = act
            elif chunk == XC // 128:
                R.bs[m] = act.astype(BF)
            else:
                R.cs[m] = act.astype(BF)

    z, step, a_neg, cum = decays_of(R.dt, R.dtb, R.alog, h, T)
    R.cumt[...] = cum.T[:16]
    R.stept[...] = step.T[:16]
    cum_last = cum[T - 1 :, :]
    kept = by_batch(lambda m: jnp.broadcast_to((pos >= tail[m]).astype(F32), (T, 128)))
    omega = jnp.exp(cum_last - cum) * step * kept
    for m in range(2):
        if m == 1:
            ahead(0, 2)
        R.cin[m, :, 0:XC] = R.v_xin[m].astype(F32)
        convolve(m, range(XC // 128))
        if m == 0:
            swap[0]().wait_recv()
        R.cin[m, :, XC:] = R.v_bc[m].astype(F32)
        convolve(m, (XC // 128, XC // 128 + 1))
        weighted = (R.xs[m] * widen(omega, 8 * m)).astype(BF)
        decay = jnp.where(tail[m] < b * T, jnp.exp(R.cumt[8 * m : 8 * m + 8, T - 1 : T]), 0.0)
        scans[m].set(tn(weighted, R.bs[m]), decay)
    lines[4].begin()

    seen = lanes((T, T)) + b * T
    lane = lanes((T, 128))

    def inside(m, between):
        both = nt(R.cs[m], R.bs[m])
        allowed = (seen <= pos) & (seen >= first[m])
        for i in range(HG):
            l = 8 * m + i
            gap = jnp.where(allowed, cum[:, l : l + 1] - R.cumt[l : l + 1, :], FAR)
            weights_ts = (jnp.exp(gap) * both * R.stept[l : l + 1, :]).astype(BF)
            R.ybuf[m, :, i * MHDIM : (i + 1) * MHDIM] = nn(weights_ts, R.xs[m, :, i * MHDIM : (i + 1) * MHDIM].astype(BF))
            if i == HG // 2 - 1:
                between()
        R.ybuf[m] = R.ybuf[m] + wide_row(R.skip, h) * R.xs[m]

    def on_to_pair(d):
        return copy_to(R.v_kvh.at[d, core], R.v_kvh.at[d, core], R.hs.at[d], R.hr.at[d], pair)

    R.lse[...] = jnp.zeros((T, 128), F32)

    def attend(m, i):
        query = R.v_q[m, :, i * HDIM : (i + 1) * HDIM]

        def score(d, top):
            at = seen - d * T
            keys = R.v_kvh[d, 0, :, m * HDIM : (m + 1) * HDIM]
            s = jnp.where((at <= pos) & (at >= first[m]), nt(query, keys) * SCALE, FAR)
            R.sbuf[d] = s
            return jnp.maximum(top, jnp.max(s, axis=1, keepdims=True))

        top = lax.fori_loop(0, reach + 1, score, jnp.full((T, 1), FAR, F32))

        def weigh(d, total):
            e = jnp.exp(R.sbuf[d] - top)
            R.sbuf[d] = e
            return total + jnp.sum(e, axis=1, keepdims=True)

        total = lax.fori_loop(0, reach + 1, weigh, jnp.zeros((T, 1), F32))
        inverse = 1.0 / total

        def take(d, acc):
            probs = (R.sbuf[d] * inverse).astype(BF)
            return acc + nn(probs, R.v_kvh[d, 1, :, m * HDIM : (m + 1) * HDIM])

        out = lax.fori_loop(0, reach + 1, take, jnp.zeros((T, HDIM), F32))
        R.attnf[m, :, i * HDIM : (i + 1) * HDIM] = out
        R.attnl[m, :, i * HDIM : (i + 1) * HDIM] = out.astype(BF)
        R.lse[...] = jnp.where(lane == 2 * m + i, top + jnp.log(total), R.lse[...])

    def mixed(m):
        gate = nn(R.v_normed[m, LAG:], R.v_wb[:, 0:XC])
        R.gate[m] = gate
        R.sin[m] = scans[m].last()[...]
        live = jnp.where(first[m] < b * T, jnp.exp(cum), 0.0)
        yv = R.ybuf[m] + nt(R.cs[m], R.sin[m, 0:XC]) * widen(live, 8 * m)
        low = yv.astype(BF)
        R.ylow[m] = low
        g = low.astype(F32) * gate * sigmoid(gate)
        R.ybuf[m] = g
        sums[m].begin(jnp.sum(g * g, axis=1, keepdims=True))

    gain = R.gain2[:, pl.ds(pl.multiple_of(h * XC, 128), XC)]
    n2 = R.gains[7:8, :]
    scales = [None, None]

    def rows(ref):
        return lambda m, head: ref[m, pl.ds(pl.multiple_of(head * tok, tok), tok), :]

    def own(ref, m):
        return ref.at[m, pl.ds(pl.multiple_of(h * tok, tok), tok), :]

    out1 = HeadScatter(rows(R.wide), b, h, members(R, "sc1_", 6))
    out2 = HeadScatter(rows(R.wide), b, h, members(R, "sc2_", 6))
    out3 = HeadScatter(rows(R.part), b, h, members(R, "sc3_", 6))
    gather_s = HeadGather(lambda m, i: R.secg.at[m, pl.ds(i * tok, tok)], b, h, members(R, "gs", 2))
    gather_h = HeadGather(lambda m, i: R.hlg.at[m, pl.ds(i * tok, tok)], b, h, members(R, "gh", 2))
    w_mix, w_att, w_out, w_in = (
        lambda: R.v_wb[:, XC : 2 * XC], lambda: R.v_wb[:, 2 * XC :], lambda: R.wc[:, 0:FG], lambda: R.wc[:, FG:]
    )

    def project(m):
        scales[m] = lax.rsqrt(sums[m].finish() * (1.0 / DI) + EPS)
        R.gated[m] = (R.ybuf[m] * scales[m] * gain).astype(BF)
        R.wide[m, 0:T, :] = nt(R.gated[m], w_mix()) + nt(R.attnl[m], w_att())
        out1.begin(m)

    def second_norm(m):
        out1.finish(m)
        value = R.x[m].astype(F32) + out1.result(m)
        R.hid[m] = value
        scale = lax.rsqrt(jnp.mean(value * value, axis=1, keepdims=True) + EPS)
        own(R.secg, m)[...] = (value * scale * n2).astype(BF)
        gather_s.begin(m)

    def feed(m):
        gather_c.finish(m)
        R.gact[m] = nn(R.cotg[m], w_out())
        gather_s.finish(m)
        a = nn(R.secg[m], R.wc[:, FG : 2 * FG])
        u = nn(R.secg[m], R.wc[:, 2 * FG :])
        sg = sigmoid(a)
        si = a * sg
        R.act[m] = (si * u).astype(BF)
        R.ggu[m, :, 0:FG] = (R.gact[m] * u * (sg * (1.0 + a * (1.0 - sg)))).astype(BF)
        R.ggu[m, :, FG:] = (R.gact[m] * si).astype(BF)
        R.wide[m, 0:T, :] = nt(R.ggu[m], w_in())
        out2.begin(m)
        R.part[m] = nt(R.act[m], w_out())

    def hidden_back(m):
        out2.finish(m)
        value = R.hid[m]
        scale = lax.rsqrt(jnp.mean(value * value, axis=1, keepdims=True) + EPS)
        grad, gain_part = norm_back(value, scale, n2, out2.result(m))
        grad = grad + R.cot[m].astype(F32)
        R.gh[m] = grad
        R.gn2[...] = gain_part if m == 0 else R.gn2[...] + gain_part
        own(R.hlg, m)[...] = grad.astype(BF)
        gather_h.begin(m)

    def project_back(m):
        gather_h.finish(m)
        R.up[m] = nn(R.hlg[m], w_mix())
        gate = R.gate[m]
        n = R.ylow[m].astype(F32) * gate * sigmoid(gate) * scales[m]
        up = R.up[m]
        part = jnp.sum(up * n, axis=0, keepdims=True)
        R.ggain[...] = part if m == 0 else R.ggain[...] + part
        back_sums[m].begin(jnp.sum(up * gain * n, axis=1, keepdims=True))
        R.gattn[m] = nn(R.hlg[m], w_att()).astype(BF)

    def mixed_back(m):
        total = back_sums[m].finish()
        gate = R.gate[m]
        sg = sigmoid(gate)
        si = gate * sg
        low = R.ylow[m].astype(F32)
        n = low * si * scales[m]
        grad = scales[m] * (R.up[m] * gain - n * (total * (1.0 / DI)))
        R.gy[m] = (grad * si).astype(BF)
        R.ggate[m] = (grad * low * (sg * (1.0 + gate * (1.0 - sg)))).astype(BF)

    def weight_grad(ref, at, left, right, cols):
        ref[:, at + cols.start : at + cols.stop] = sum(tn(left[m], right[m, :, cols]) for m in range(2)).astype(BF)

    pairs = [PairReduce(getattr(R, f"gi{k}"), members(R, f"pair{k}_", 3), b, h, nb) for k in range(2)]

    def in_grad(k, q):
        cols = slice(k * FG + q * FG // 2, k * FG + (q + 1) * FG // 2)
        grad = sum(tn(R.secg[m], R.ggu[m, :, cols]) for m in range(2)).astype(BF)
        pairs[k].src[:, :, :, q * FG // 2 : (q + 1) * FG // 2] = grad.reshape(nz, 2, rpb, FG // 2)

    moves.start("normed", "xin", "bc", "q", "pre", "wa")
    inside(0, lambda: ahead(1, 2))
    for m in range(2):
        scans[m].join(0)
    ahead(0, 3)
    lines[5].begin()
    halo.finish_recv()
    for d in range(1, reach + 1):

        @pl.when(b >= d)
        def _():
            on_to_pair(d).start()

    swap[1]().wait_recv()
    for d in range(1, reach + 1):

        @pl.when(b >= d)
        def _():
            on_to_pair(d).wait_recv()

    attend(0, 0)
    ahead(2, 2)
    for i in range(1, len(scans[0].steps) - 1):
        for m in range(2):
            scans[m].join(i)
    ahead(0, 4)
    attend(0, 1)
    ahead(1, 3)
    for m in range(2):
        gather_c.forward(m)
    inside(1, lambda: ahead(0, 5))
    attend(1, 0)
    attend(1, 1)
    lines[2].finish()
    moves.start("wb", "kvh")
    mixed(0)
    ahead(1, 4)
    mixed(1)
    project(0)
    ahead(2, 3)
    ahead(1, 5)
    out1.middle(0)
    project(1)
    ahead(2, 4)
    second_norm(0)
    out1.middle(1)
    ahead(2, 5)
    gather_s.forward(0)
    for k in range(3, 6):
        lines[k].finish()
    feed(0)
    second_norm(1)
    out2.middle(0)
    gather_s.forward(1)
    feed(1)
    out2.middle(1)
    in_grad(0, 0)
    in_grad(0, 1)
    pairs[0].begin()
    hidden_back(0)
    in_grad(1, 0)
    in_grad(1, 1)
    pairs[1].begin()
    for m in range(2):
        out3.begin(m)
    gather_h.forward(0)
    hidden_back(1)
    project_back(0)
    gather_h.forward(1)
    out3.middle(0)
    out3.middle(1)
    half = [slice(k * FG // 2, (k + 1) * FG // 2) for k in range(2)]
    for k in range(2):
        weight_grad(R.v_gw_out, FG, R.cotg, R.act, half[k])
    project_back(1)
    mixed_back(0)
    per = max(nb // NH, 1)
    mix_to, att_to = arrange(per, XC, 0), arrange(per, 128, 1)
    for m in range(2):
        R.act[m] = (nn(R.gated[m], mix_to) + nn(R.attnl[m], att_to)).astype(BF)
    for k in range(2):
        weight_grad(R.v_gw_out, 0, R.hlg, R.act, half[k])
    moves.start("gw_out")
    mixed_back(1)
    for m in range(2):
        out3.finish(m)
        R.out[m] = R.hid[m] + out3.result(m)
    for k in range(2):
        pairs[k].finish(R.gw_in, slice(k * FG, (k + 1) * FG))

    if local:
        for k in range(3):
            for i in range(3):
                piece(k, i).wait_send()

    @pl.when((h == NH - 1) & (b + 1 < nb))
    def _():
        for i in range(NH):
            edge(i).wait_send()

    for c in swap:
        c().wait_send()
    for d in range(1, reach + 1):

        @pl.when(b >= d)
        def _():
            on_to_pair(d).wait_send()

    moves.wait_all()
    for g in lines + pairs + [gather_x, gather_c, gather_s, gather_h, out1, out2, out3]:
        g.done()
    for scan in scans:
        scan.finish()
    halo.finish_send()


def forward(nb, reach, ins, local):
    tok = ins["x"].shape[1]
    T, rpb = tok * NH, D // nb
    S = rpb // NH
    dma = pltpu.SemaphoreType.DMA
    outs = dict(
        normed=vm((2, LAG + T, D), BF), xin=vm((2, LAG + T, XC), BF), bc=vm((2, LAG + T, 256), BF), q=vm((2, T, 128), BF),
        kvh=vm((reach + 1, 2, T, 128), BF), dt=vm((T, 128), F32), pre=vm((2, T, XC + 256), F32),
        sin=vm((2, Scan.ROWS, 128), BF), attnf=vm((2, T, 128), F32), lse=vm((T, 128), F32), gy=vm((2, T, XC), BF),
        ggate=vm((2, T, XC), BF), gattn=vm((2, T, 128), BF), gw_in=vm((nb // 2, rpb, 2 * FG), BF), gw_out=vm((D, 2 * FG), BF), gn2=vm((1, D), F32),
        ggain=vm((1, XC), F32), out=vm((2, tok, D), F32), gh=vm((2, tok, D), F32), wa=vm((D, WA), BF), wb=vm((D, WB), BF),
        gains=vm((8, D), F32), cosine=vm((T, 128), F32), sine=vm((T, 128), F32),
    )
    V = pltpu.VMEM
    scratch = dict(
        xg=V((2, LAG + T, D), BF), cotg=V((2, T, D), BF), wc=V((D, WC), BF), wide=V((2, LAG + T, D), F32),
        gate=V((2, T, XC), F32), cin=V((2, LAG + T, XC + 256), F32), xs=V((2, T, XC), F32), bs=V((2, T, 128), BF),
        cs=V((2, T, 128), BF), ybuf=V((2, T, XC), F32), sbuf=V((reach + 1, T, T), F32), cumt=V((16, T), F32),
        stept=V((16, T), F32), ylow=V((2, T, XC), BF), gated=V((2, T, XC), BF), attnl=V((2, T, 128), BF),
        part=V((2, T, D), F32), secg=V((2, T, D), BF), hlg=V((2, T, D), BF), act=V((2, T, FG), BF),
        ggu=V((2, T, 2 * FG), BF), gact=V((2, T, FG), F32), hid=V((2, tok, D), F32), up=V((2, T, XC), F32),
        cb2=V((1, DI + 256), F32), gain2=V((1, DI), F32),
        ps=dma((3, 3)), pr=dma((3, 3)), es=dma((NH,)), er=dma((1,)), ss=dma((2,)), sr=dma((2,)),
        hs=dma((reach + 1,)), hr=dma((reach + 1,)),
    )
    scratch.update({"v_" + n: V(outs[n].shape, outs[n].dtype) for n in LATE_OUT}, moved=dma((len(LATE_OUT),)))
    if local:
        scratch.update(pa=V((NH, S, WA), BF), pb=V((NH, S, WB), BF), pc=V((NH, S, WC), BF))
    for name in ("gx", "gc", "gs", "gh"):
        scratch.update(group(name, HeadGather.scratch()))
    for k in range(2):
        scratch.update(group(f"pair{k}_", PairReduce.scratch(nb, FG)))
        scratch[f"gi{k}"] = V((nb // 2, 2, rpb, FG), BF)
    for k in range(6):
        scratch.update(group(f"line{k}_", LineGather.scratch(nb)))
    for k in range(3):
        scratch.update(group(f"sc{k + 1}_", HeadScatter.scratch(tok)))
    for m in range(2):
        scratch.update(group(f"scan{m}_", Scan.scratch(reach)))
        scratch.update(group(f"sumf{m}_", HeadSum.scratch(T)))
        scratch.update(group(f"sumb{m}_", HeadSum.scratch(T)))
    scratch.update(group("halo", Halo.scratch(reach)))
    body = functools.partial(forward_body, nb, T, reach, local)
    return run(body, ins, outs, scratch, "forward", 1, smem=("starts", "dtb", "alog", "skip"), hbm=LATE_OUT)


LATE_IN = ["pre", "gw_out", "kvh", "normed", "ggate", "xin", "bc", "wa", "wb", "gh"]


def backward_body(nb, T, reach, easy, R):
    b, h = place()
    moves = Moves(R, LATE_IN, False)
    tok, rpb = T // NH, D // nb
    nz, per = nb // 2, nb // NH
    share = (XC + 128) // per
    core = lax.rem(h, 2)
    pair = (b, other(h, 1))
    total_sum = Sum(members(R, "sum", 4), b, h, nb)
    targets = [(per * h + i, b // per) for i in range(per)] if easy else []

    def away(device):
        return (device[0] != b) | (device[1] != h)

    barrier(
        head_edges(b, h) + line_edges(b, h, nb) + Scan.edges(b, h, nb, reach) + halo_edges(b, h, nb, reach)
        + [((h == NH - 1) & (b + 1 < nb), (b + 1, jnp.int32(i))) for i in range(NH)]
        + [(b >= 1, (b - 1, jnp.int32(NH - 1)))]
        + total_sum.edges()
        + [(away(t), t) for t in targets]
    )
    lines = [
        LineReduce(src, members(R, f"line{k}_", 10 if k else 7), b, h, nb)
        for k, src in enumerate((R.gw_in, R.v_gw_out, R.gwb, R.gwx, R.gwc))
    ]

    def send_ffn():
        lines[0].finish(R.res0)
        if easy:
            for i, to in enumerate((h // 2, 2 + h // 2)):
                R.fmsg[i] = R.res0[:, i * FG : (i + 1) * FG].astype(BF)
                slot = lax.rem(h, 2)

                @pl.when(to != h)
                def _():
                    copy_to(R.fmsg.at[i], R.fgot.at[slot], R.fs.at[i], R.fr.at[slot], (b, to)).start()

                @pl.when(to == h)
                def _():
                    R.fgot[slot] = R.fmsg[i]
        else:
            R.raw[:, 0 : 2 * FG] = R.res0[...].astype(BF)

    def send_out():
        lines[1].finish(R.res1)
        if easy:
            slot = lax.rem(b, per)
            for i, to in enumerate(targets):
                for j in range(2):
                    R.msg[i, j] = R.res1[:, j * FG + i * share : j * FG + (i + 1) * share].astype(BF)

                @pl.when(away(to))
                def _():
                    copy_to(R.msg.at[i], R.got.at[slot], R.ms.at[i], R.mr.at[slot], to).start()

                @pl.when(jnp.logical_not(away(to)))
                def _():
                    R.got[slot] = R.msg[i]
        else:
            R.raw[:, 2 * FG :] = R.res1[...].astype(BF)

    gather = HeadGather(lambda m, i: (R.w1b, R.w1c)[m].at[i], b, h, members(R, "gw", 2))

    def send_gate():
        lines[2].finish(R.res2)
        R.w1b[h] = R.res2[...].astype(BF)
        gather.begin(0)

    moves.start("pre", "gw_out", "kvh", "normed", "ggate", "xin", "bc", "wa", "wb", "gh")
    lines[0].step_some(0)
    moves.wait("pre", "gw_out")
    lines[1].start_some(0)
    scans = [Scan(-1, b, h, nb, reach, members(R, f"scan{m}_", 5)) for m in range(2)]
    halo = Halo(-1, lambda d: R.gkvs.at[d], lambda d: R.gkvr.at[d], b, h, nb, reach, members(R, "halo", 2))
    pos = b * T + rows_of((T, 1))
    first = [doc_start(R.starts, m, pos) for m in range(2)]
    tail = [f[T - 1 :, :] for f in first]
    seen = lanes((T, T)) + b * T
    lane = lanes((T, 128))
    for m in range(2):
        for chunk in range((XC + 256) // 128):
            cols = pl.ds(chunk * 128, 128)
            value = R.v_pre[m, :, cols]
            act = value * sigmoid(value)
            if chunk < XC // 128:
                R.xs[m, :, cols] = act
            elif chunk == XC // 128:
                R.bs[m] = act.astype(BF)
            else:
                R.cs[m] = act.astype(BF)
    z, step, a_neg, cum = decays_of(R.dt, R.dtb, R.alog, h, T)
    R.cumt[...] = cum.T[:16]
    R.stept[...] = step.T[:16]
    cum_last = cum[T - 1 :, :]
    live = jnp.exp(cum) * by_batch(lambda m: jnp.broadcast_to((first[m] < b * T).astype(F32), (T, 128)))
    kept = jnp.exp(cum_last - cum) * by_batch(lambda m: jnp.broadcast_to((pos >= tail[m]).astype(F32), (T, 128)))
    omega = kept * step
    for m in range(2):
        u = (R.gy[m].astype(F32) * widen(live, 8 * m)).astype(BF)
        decay = jnp.where(tail[m] < b * T, jnp.exp(R.cumt[8 * m : 8 * m + 8, T - 1 : T]), 0.0)
        scans[m].set(tn(u, R.cs[m]), decay)
    lines[0].step_some(1)
    lines[1].start_some(1)
    lines[1].start_some(2)
    moves.wait("kvh")

    R.gkv[...] = jnp.zeros_like(R.gkv)
    for m in range(2):
        for i in range(2):
            mine = slice(i * HDIM, (i + 1) * HDIM)
            query, grad = R.q[m, :, mine], R.gattn[m, :, mine]
            delta = jnp.sum(grad.astype(F32) * R.attnf[m, :, mine], axis=1, keepdims=True)
            lse = R.lse[:, 2 * m + i : 2 * m + i + 1]

            def block(d, acc):
                at = seen - d * T
                keys = R.v_kvh[d, 0, :, m * HDIM : (m + 1) * HDIM]
                vals = R.v_kvh[d, 1, :, m * HDIM : (m + 1) * HDIM]
                probs = jnp.where((at <= pos) & (at >= first[m]), jnp.exp(nt(query, keys) * SCALE - lse), 0.0)
                ds = (probs * (nt(grad, vals) - delta)).astype(BF)
                R.gkv[d, 0, :, m * HDIM : (m + 1) * HDIM] += tn(ds, query) * SCALE
                R.gkv[d, 1, :, m * HDIM : (m + 1) * HDIM] += tn(probs.astype(BF), grad)
                return acc + nn(ds, keys)

            R.gq[m, :, mine] = lax.fori_loop(0, reach + 1, block, jnp.zeros((T, HDIM), F32)) * SCALE
            if m == 0 and i == 1:
                lines[1].start_some(3)
            elif m == 1 and i == 0:
                lines[0].step_some(2)
        if m == 0:
            for scan in scans:
                scan.join(0)
    for d in range(reach + 1):
        R.pair_k[d] = R.gkv[d, 1 - core].astype(BF)
    swap_k = lambda: copy_to(R.pair_k, R.pair_kr, R.ss.at[0], R.sr.at[0], pair)
    swap_k().start()

    moves.wait("normed", "ggate")
    for m in range(2):
        R.gproj[m, 0:LAG, WA:] = jnp.zeros((LAG, XC), BF)
        R.gproj[m, LAG:, WA:] = R.v_ggate[m]
        R.gproj[m, 0:LAG, XC + 128 :WA] = jnp.zeros((LAG, 256), BF)
        R.gproj[m, LAG:, XC + 128 : XC + 256] = rotate_pair(R.gq[m], R.cosine[...], -R.sine[...]).astype(BF)


    def weight_grad(ref, at, cols):
        grad = sum(tn(R.v_normed[m], R.gproj[m, :, cols]) for m in range(2)).astype(BF)
        ref[:, :, :, at : at + cols.stop - cols.start] = grad.reshape(nz, 2, rpb, cols.stop - cols.start)

    weight_grad(R.gwb, 0, slice(WA, WA + XC))
    weight_grad(R.gwb, XC, slice(XC + 128, XC + 256))
    swap_k().wait_recv()
    for d in range(reach + 1):
        value = R.gkv[d, core] + R.pair_kr[d].astype(F32)
        if d == 0:
            R.gkv[0, core] = value
        else:
            R.gkvs[d] = value.astype(BF)
    halo.begin()
    lines[1].step_some(0)

    row_sums = jnp.zeros((T, 128), F32)
    R.rowq[...] = jnp.zeros_like(R.rowq)
    skip = wide_row(R.skip, h)
    gskip = jnp.zeros((1, 128), F32)
    for m in range(2):
        both = nt(R.cs[m], R.bs[m])
        allowed = (seen <= pos) & (seen >= first[m])
        gboth = jnp.zeros((T, T), F32)
        for i in range(HG):
            l = 8 * m + i
            mine = slice(i * MHDIM, (i + 1) * MHDIM)
            grad = R.gy[m, :, mine]
            decay = jnp.exp(jnp.where(allowed, cum[:, l : l + 1] - R.cumt[l : l + 1, :], FAR))
            srow = R.stept[l : l + 1, :]
            ld = decay * nt(grad, R.xs[m, :, mine].astype(BF))
            gboth = gboth + ld * srow
            q = ld * both
            R.rowq[l : l + 1, :] = jnp.sum(q, axis=0, keepdims=True)
            row_sums = jnp.where(lane == l, jnp.sum(q * srow, axis=1, keepdims=True), row_sums)
            R.gx[m, :, mine] = tn((decay * both * srow).astype(BF), grad)
            if i == HG // 2:
                if m == 1:
                    lines[2].start_some(2)
                    lines[2].start_some(3)
        low = gboth.astype(BF)
        R.gcm[m] = nn(low, R.bs[m])
        R.gbm[m] = tn(low, R.cs[m])
        gyf = R.gy[m].astype(F32)
        gskip = gskip + exact(jnp.sum(gyf * R.xs[m], axis=0, keepdims=True), head_select(m))
        R.gx[m] = R.gx[m] + skip * gyf
        u = gyf * widen(live, 8 * m)
        carried = nt(R.cs[m], R.sin[m, 0:XC])
        row_sums = row_sums + exact(u * carried, head_select(m))
        R.gcm[m] += nn(u.astype(BF), R.sin[m, 0:XC])
        if m == 0:
            for scan in scans:
                scan.join(1)
            lines[1].step_some(1)
            lines[2].start_some(0)
            lines[2].start_some(1)
    for scan in scans:
        for i in range(2, len(scan.steps) - 1):
            scan.join(i)

    colq = jnp.concatenate([R.rowq[...], jnp.zeros((112, T), F32)], axis=0).T
    gstep = colq
    gcum = row_sums - step * colq
    glast = jnp.zeros((1, 128), F32)
    for m in range(2):
        adjoint = scans[m].last()[0:XC, :]
        read = nt(R.bs[m], adjoint)
        wide = widen(omega, 8 * m)
        R.gx[m] += wide * read
        R.gbm[m] += nn((R.xs[m] * wide).astype(BF), adjoint)
        gw = exact(R.xs[m] * read, head_select(m))
        gstep = gstep + kept * gw
        term = omega * gw
        gcum = gcum - term
        glast = glast + jnp.sum(term, axis=0, keepdims=True)
        through = jnp.where(tail[m] < b * T, jnp.exp(cum_last), 0.0)
        overlap = adjoint.astype(F32) * R.sin[m, 0:XC].astype(F32)
        per_head = jnp.sum(
            lax.dot_general(overlap, head_select(m), (((0,), (0,)), ((), ())), precision=high, preferred_element_type=F32),
            axis=0, keepdims=True,
        )
        glast = glast + through * per_head
    gcum = gcum + jnp.where(rows_of((T, 128)) == T - 1, glast, 0.0)
    gda = exact(triangle(T, upper=True), gcum)
    gstep = gstep + gda * a_neg
    gz = jnp.where(valid_row(), gstep * sigmoid(z), 0.0)
    lines[1].step_some(2)
    moves.wait("xin", "bc")

    conv_grad = [[], []]
    R.gcin[...] = jnp.zeros_like(R.gcin)
    R.gcw[...] = jnp.zeros_like(R.gcw)
    for m in range(2):
        R.cin[:, 0:XC] = R.v_xin[m].astype(F32)
        R.cin[:, XC:] = R.v_bc[m].astype(F32)
        for chunk in range((XC + 256) // 128):
            cols = pl.ds(chunk * 128, 128)
            taps, _ = group_taps(h, R.cw, None, chunk)
            pre = R.v_pre[m, :, cols]
            sg = sigmoid(pre)
            if chunk < XC // 128:
                up = R.gx[m, :, cols]
            elif chunk == XC // 128:
                up = R.gbm[m]
            else:
                up = R.gcm[m]
            gs = up * (sg * (1.0 + pre * (1.0 - sg)))
            R.gcw[4:5, cols] += jnp.sum(gs, axis=0, keepdims=True)
            for back in range(4):
                j = 3 - back
                near = jnp.where(pos - first[m] >= back, gs, 0.0)
                R.gcw[j : j + 1, cols] += jnp.sum(near * R.cin[pl.ds(LAG - back, T), cols], axis=0, keepdims=True)
                R.gcin[m, pl.ds(LAG - back, T), cols] += near * taps[j : j + 1]

    mine_bc = pl.ds(pl.multiple_of(XC + core * 128, 128), 128)
    pair_bc = pl.ds(pl.multiple_of(XC + (1 - core) * 128, 128), 128)
    for m in range(2):
        R.pair_b[m] = R.gcin[m, :, pair_bc].astype(BF)
    swap_b = lambda: copy_to(R.pair_b, R.pair_br, R.ss.at[1], R.sr.at[1], pair)
    swap_b().start()
    for m in range(2):
        R.gproj[m, :, 0:XC] = R.gcin[m, :, 0:XC].astype(BF)
    weight_grad(R.gwx, 0, slice(0, XC))
    for k in range(4):
        lines[3].start_some(k)
    send_ffn()
    lines[2].step_some(0)
    halo.finish_recv()
    packed = R.gkv[0, core]
    for d in range(1, reach + 1):
        packed = packed + jnp.where(b + d < nb, R.gkvr[d].astype(F32), 0.0)
    turned = rotate_pair(packed, R.cosine[...], -R.sine[...])
    packed = jnp.where(core == 0, turned, packed)
    swap_b().wait_recv()
    for m in range(2):
        R.gproj[m, :, XC : XC + 128] = (R.gcin[m, :, mine_bc] + R.pair_br[m].astype(F32)).astype(BF)
    for m in range(2):
        mine = packed if m == 0 else pltpu.roll(packed, HDIM, 1)
        gdt = pltpu.roll(gz, HDIM - 8 * m, 1)
        R.gproj[m, LAG:, XC + 256 : WA] = jnp.where(
            lane < HDIM, mine, jnp.where(lane < HDIM + HG, gdt, 0.0)
        ).astype(BF)
    weight_grad(R.gwc, 128, slice(XC + 256, WA))
    weight_grad(R.gwc, 0, slice(XC, XC + 128))
    for k in range(4):
        lines[4].start_some(k)
    lines[2].step_some(1)
    send_out()
    moves.wait("wa", "wb")

    scatter = HeadScatter(
        lambda m, head: R.gnp[m, pl.ds(pl.multiple_of(LAG + head * tok, LAG), tok), :], b, h, members(R, "sc", 6)
    )
    for m in range(2):
        R.gnp[m] = nt(R.gproj[m, :, 0:WA], R.v_wa[...]) + nt(R.gproj[m, :, WA:], R.v_wb[:, 0:XC])
        scatter.begin(m)
        R.edge_s[m] = R.gnp[m, 0:LAG, :].astype(BF)

    n1 = R.gains[6:7, :]
    small = jnp.concatenate(
        [
            jnp.sum(gz, axis=0, keepdims=True),
            jnp.sum(gda * step, axis=0, keepdims=True) * a_neg,
            gskip,
            jnp.zeros((5, 128), F32),
        ],
        axis=0,
    )
    small = jnp.where(lanes((8, 128)) < HG, small + pltpu.roll(small, 120, 1), 0.0)
    small = pltpu.roll(small, h * HG, 1)
    R.pay[...] = jnp.zeros_like(R.pay)
    wide_x = pl.ds(pl.multiple_of(h * XC, 128), XC)
    R.pay[0:5, wide_x] = R.gcw[0:5, 0:XC]
    R.pay[0:5, DI:] = R.gcw[0:5, XC:]
    R.pay[5:6, wide_x] = R.ggain[...]
    gn1 = sum(jnp.sum(R.gnp[m] * R.v_normed[m].astype(F32), axis=0, keepdims=True) for m in range(2))
    R.pay[6:7, 0:D] = gn1 / n1
    R.pay[7:8, 0:D] = R.gn2[...]
    for k in range(3):
        R.pay[6:7, D + 128 * k : D + 128 * (k + 1)] = small[k : k + 1]
    total_sum.begin(R.pay[...])

    def edge(i):
        return copy_to(R.edge_s, R.edge_r.at[i], R.es.at[0], R.er.at[i], (b - 1, jnp.int32(NH - 1)))

    @pl.when(b >= 1)
    def _():
        edge(h).start()

    for m in range(2):
        scatter.middle(m)
    moves.wait("gh")
    lines[2].step_some(2)
    lines[3].step_some(0)
    total_sum.step(0)
    lines[4].step_some(0)
    mine = (h == NH - 1) & (b + 1 < nb)

    @pl.when(mine)
    def _():
        for i in range(NH):
            edge(i).wait_recv()

    @pl.when(jnp.logical_not(mine))
    def _():
        R.edge_r[...] = jnp.zeros_like(R.edge_r)

    for m in range(2):
        scatter.finish(m)
        R.up[m] = scatter.result(m)
        R.up[m, tok - LAG : tok, :] += sum(R.edge_r[i, m].astype(F32) for i in range(NH))
        value = R.x[m].astype(F32)
        scale = lax.rsqrt(jnp.mean(value * value, axis=1, keepdims=True) + EPS)
        R.gin[m] = R.v_gh[m] + norm_back(value, scale, n1, R.up[m])[0]
    send_gate()
    lines[3].step_some(1)
    total_sum.step(1)
    lines[4].step_some(1)
    lines[3].step_some(2)
    total_sum.step(2)
    lines[4].step_some(2)
    gather.forward(0)
    lines[3].finish(R.res3)
    R.w1c[h, :, 0:XC] = R.res3[...].astype(BF)
    total_sum.step(3)
    lines[4].finish(R.res4)
    R.w1c[h, :, XC:] = R.res4[...].astype(BF)
    gather.begin(1)
    for k in range(4, len(total_sum.steps)):
        total_sum.step(k)
    gather.forward(1)
    R.small[...] = total_sum.result()
    if easy:
        for j in range(2):
            src = 2 * lax.rem(h, 2) + j

            @pl.when(src != h)
            def _():
                copy_to(R.fmsg.at[0], R.fgot.at[j], R.fs.at[0], R.fr.at[j], (b, src)).wait_recv()

        for j in range(per):

            @pl.when(away(targets[j]))
            def _():
                copy_to(R.msg.at[0], R.got.at[j], R.ms.at[0], R.mr.at[j], targets[j]).wait_recv()

        for i, to in enumerate((h // 2, 2 + h // 2)):

            @pl.when(to != h)
            def _():
                copy_to(R.fmsg.at[i], R.fgot.at[0], R.fs.at[i], R.fr.at[0], (b, to)).wait_send()

        for i in range(per):

            @pl.when(away(targets[i]))
            def _():
                copy_to(R.msg.at[i], R.got.at[0], R.ms.at[i], R.mr.at[0], targets[i]).wait_send()

    for m in range(2):
        gather.finish(m)
    for line in lines:
        line.done()

    @pl.when(b >= 1)
    def _():
        edge(h).wait_send()

    for c in (swap_k, swap_b):
        c().wait_send()
    gather.done()
    scatter.done()
    for scan in scans:
        scan.finish()
    halo.finish_send()


def backward(nb, reach, ins):
    tok = ins["x"].shape[1]
    T, rpb, nz, per = tok * NH, D // nb, nb // 2, nb // NH
    share = (XC + 128) // per
    easy = share % 128 == 0
    dma, V = pltpu.SemaphoreType.DMA, pltpu.VMEM
    outs = dict(
        gin=vm((2, tok, D), F32), w1b=vm((NH, rpb, XC + 128), BF), w1c=vm((NH, rpb, XC + 256), BF),
        small=vm((8, DI + 256), F32),
    )
    if easy:
        outs.update(fgot=vm((2, rpb, FG), BF), got=vm((per, 2, rpb, share), BF))
    else:
        outs.update(raw=vm((rpb, 4 * FG), BF))
    scratch = dict(
        xs=V((2, T, XC), F32), bs=V((2, T, 128), BF), cs=V((2, T, 128), BF), cumt=V((16, T), F32), stept=V((16, T), F32),
        gkv=V((reach + 1, 2, T, 128), F32), gkvs=V((reach + 1, T, 128), BF), gkvr=V((reach + 1, T, 128), BF),
        pair_k=V((reach + 1, T, 128), BF), pair_kr=V((reach + 1, T, 128), BF), gq=V((2, T, 128), F32),
        gproj=V((2, LAG + T, WA + XC), BF), gwb=V((nz, 2, rpb, XC + 128), BF), gwx=V((nz, 2, rpb, XC), BF), gwc=V((nz, 2, rpb, 256), BF),
        rowq=V((16, T), F32), gx=V((2, T, XC), F32), gbm=V((2, T, 128), F32), gcm=V((2, T, 128), F32),
        gcin=V((2, LAG + T, XC + 256), F32), gcw=V((8, XC + 256), F32), cin=V((LAG + T, XC + 256), F32),
        pair_b=V((2, LAG + T, 128), BF), pair_br=V((2, LAG + T, 128), BF), gnp=V((2, LAG + T, D), F32),
        edge_s=V((2, LAG, D), BF), edge_r=V((NH, 2, LAG, D), BF), up=V((2, tok, D), F32), pay=V((8, DI + 256), F32),
        res0=V((rpb, 2 * FG), F32), res1=V((rpb, 2 * FG), F32), res2=V((rpb, XC + 128), F32), res3=V((rpb, XC), F32), res4=V((rpb, 256), F32),
        ss=dma((2,)), sr=dma((2,)), es=dma((1,)), er=dma((NH,)), moved=dma((len(LATE_IN),)),
    )
    scratch.update({"v_" + n: V(ins[n].shape, ins[n].dtype) for n in LATE_IN})
    if easy:
        scratch.update(
            fmsg=V((2, rpb, FG), BF), msg=V((per, 2, rpb, share), BF), fs=dma((2,)), fr=dma((2,)), ms=dma((per,)), mr=dma((per,)),
        )
    for k, cols in enumerate((2 * FG, 2 * FG, XC + 128, XC, 256)):
        scratch.update(group(f"line{k}_", LineReduce.scratch(nb, cols, k > 0)))
    scratch.update(group("sum", Sum.scratch(nb, (8, DI + 256))))
    for m in range(2):
        scratch.update(group(f"scan{m}_", Scan.scratch(reach)))
    scratch.update(group("halo", Halo.scratch(reach)))
    scratch.update(group("sc", HeadScatter.scratch(tok)))
    scratch.update(group("gw", HeadGather.scratch()))
    body = functools.partial(backward_body, nb, T, reach, easy)
    return run(body, ins, outs, scratch, "backward", 2, smem=("starts", "dtb", "alog", "skip"), hbm=LATE_IN)


def finish_body(nb, R):
    h = lax.axis_index("head")
    rpb, per = D // nb, nb // NH
    R.out[...] = R.out_in[...]
    R.gin[...] = R.gin_in[...]
    kv = XC + 128
    for i in range(NH):
        first, second = R.w1b[i].astype(F32).T, R.w1c[i].astype(F32).T
        R.full[i * XC : (i + 1) * XC] = first[:XC]
        R.full[DI + i * XC : DI + (i + 1) * XC] = second[:XC]
        R.fatt[i * 128 : (i + 1) * 128] = first[XC:]
        at = 2 * DI + 128 * (i % 2)
        R.full[at : at + 128] = second[XC:kv] if i < 2 else R.full[at : at + 128] + second[XC:kv]
        at = QHEADS * HDIM + 128 * (i % 2) + HDIM * (i // 2)
        R.fatt[at : at + HDIM] = second[kv : kv + HDIM]
        at = 2 * DI + 256 + i * HG
        R.full[at : at + HG] = second[kv + HDIM : kv + HDIM + HG]
    for ref, out in ((R.full, R.mix_in), (R.fatt, R.att_in)):
        width = out.shape[0]
        out[...] = ref[pl.ds(h * width, width), :]
    R.cw[...] = R.small[0:4, :]
    R.cb[...] = R.small[4:5, :].reshape(DI + 256)
    R.gain[...] = R.small[5:6, 0:DI].reshape(DI)
    R.n1[...] = R.small[6:7, 0:D].reshape(D)
    R.n2[...] = R.small[7:8, 0:D].reshape(D)
    for k, ref in enumerate((R.dtb, R.alog, R.skip)):
        ref[...] = R.small[6:7, D + 128 * k : D + 128 * k + MHEADS].reshape(MHEADS)
    if hasattr(R, "got"):
        for j in range(2):
            R.ffn[:, j * FG : (j + 1) * FG] = R.fgot[j].astype(F32)
        for j in range(per):
            cols = slice(j * rpb, (j + 1) * rpb)
            both = R.got[j, 0].astype(F32).T
            R.mix_out[:, cols] = both[: XC // per]
            R.att_out[:, cols] = both[XC // per :]
            R.ffn_out[:, cols] = R.got[j, 1].astype(F32).T


def finish(nb, ins, mix_cols, att_cols):
    rpb, per = D // nb, nb // NH
    outs = dict(
        out=vm(ins["out_in"].shape, F32), gin=vm(ins["gin_in"].shape, F32), mix_in=vm((mix_cols, rpb), F32),
        att_in=vm((att_cols, rpb), F32), cw=vm((4, DI + 256), F32), cb=vm((DI + 256,), F32), gain=vm((DI,), F32),
        n1=vm((D,), F32), n2=vm((D,), F32), dtb=vm((MHEADS,), F32), alog=vm((MHEADS,), F32), skip=vm((MHEADS,), F32),
    )
    if "got" in ins:
        outs.update(
            ffn=vm((rpb, 2 * FG), F32), mix_out=vm((XC // per, per * rpb), F32), att_out=vm((128 // per, per * rpb), F32),
            ffn_out=vm((FG // per, per * rpb), F32),
        )
    V = pltpu.VMEM
    scratch = dict(full=V((NH * mix_cols, rpb), F32), fatt=V((NH * att_cols, rpb), F32))
    return run(functools.partial(finish_body, nb), ins, outs, scratch, "finish", None)


def pack_columns(mixer_in, attn_in, mixer_out, attn_out, ffn_in, ffn_out, norm_one, norm_two):
    shard = mixer_in.shape[0]
    mix_t, att_t, ffn_t = mixer_out.T, attn_out.T, ffn_out.T
    sets = ([], [], [])
    for i in range(NH):
        kv = QHEADS * HDIM + 128 * (i % 2) + HDIM * (i // 2)
        bc, dt = 2 * DI + 128 * (i % 2), 2 * DI + 2 * STATE + i * HG
        sets[0].append(
            [
                mixer_in[:, DI + i * XC : DI + (i + 1) * XC], mixer_in[:, bc : bc + 128],
                attn_in[:, i * 128 : (i + 1) * 128], attn_in[:, kv : kv + HDIM], mixer_in[:, dt : dt + HG],
                norm_one[:, None], norm_two[:, None], jnp.zeros((shard, 128 - HDIM - HG - 2), BF),
            ]
        )
        sets[1].append(
            [
                mixer_in[:, i * XC : (i + 1) * XC], mix_t[:, i * XC : (i + 1) * XC], att_t[:, i * 128 : (i + 1) * 128],
            ]
        )
        sets[2].append(
            [
                ffn_t[:, i * FG : (i + 1) * FG], ffn_in[:, i * FG : (i + 1) * FG],
                ffn_in[:, FF + i * FG : FF + (i + 1) * FG],
            ]
        )
    out = []
    for parts in sets:
        v = jnp.stack([jnp.concatenate(p, axis=1) for p in parts])
        out.append(lax.all_to_all(v, "head", split_axis=0, concat_axis=0, tiled=True).reshape(shard * NH, v.shape[2]))
    return out


def on_device(
    inputs, cotangent, doc_starts, norm_one, mixer_in, conv_weight, conv_bias, dt_bias, a_log, d_skip, ssm_gain,
    mixer_out, attn_in, attn_out, norm_two, ffn_in, ffn_out,
):
    nb = lax.axis_size("blk")
    T = inputs.shape[1] * NH
    longest = min(MAXLEN, T * nb // 2)
    reach = (longest + T - 2) // T
    shard = mixer_in.shape[0]
    rpb, nz = shard * NH, nb // 2
    local = shard % 16 == 0

    lane = np.arange(128) % HDIM % (HDIM // 2)
    freq = jnp.asarray((10000.0 ** (-(lane.astype(np.float32) * 2.0 / HDIM))).astype(np.float32))[None, :]
    small = dict(
        starts=doc_starts, cw=conv_weight, dtb=dt_bias, alog=a_log, skip=d_skip
    )
    if local:
        weights = dict(
            mixer_in=mixer_in, attn_in=attn_in, mixer_out=mixer_out.T, attn_out=attn_out.T, ffn_in=ffn_in,
            ffn_out=ffn_out.T, n1=norm_one[None, :], n2=norm_two[None, :],
        )
    else:
        weights = dict(
            zip(("pa", "pb", "pc"), pack_columns(mixer_in, attn_in, mixer_out, attn_out, ffn_in, ffn_out, norm_one, norm_two))
        )
    f = forward(nb, reach, dict(x=inputs, cot=cotangent, freq=freq, cb=conv_bias, gain=ssm_gain, **small, **weights), local)
    shape = (nz, 2, rpb, 2 * FG)
    kept = (
        "gy", "gattn", "q", "kvh", "attnf", "lse", "pre", "xin", "bc", "dt", "sin", "ggate", "cosine", "sine", "normed", "wa",
        "wb", "gh", "gains", "gn2", "ggain",
    )
    b = backward(
        nb, reach,
        dict(
            x=inputs, gw_in=f.gw_in, gw_out=f.gw_out.reshape(shape), **small,
            **{n: getattr(f, n) for n in kept},
        ),
    )
    ins = dict(out_in=f.out, gin_in=b.gin, w1b=b.w1b, w1c=b.w1c, small=b.small)
    easy = hasattr(b, "got")
    if easy:
        ins.update(fgot=b.fgot, got=b.got)
    r = finish(nb, ins, mixer_in.shape[1] // NH, attn_in.shape[1] // NH)
    if easy:
        g_ffn_in, g_mix_out, g_att_out, g_ffn_out = r.ffn, r.mix_out, r.att_out, r.ffn_out
    else:
        per = nb // NH
        head, blk = lax.axis_index("head"), lax.axis_index("blk")
        mine = lax.all_gather(b.raw[:, : 2 * FG], "head").reshape(NH, rpb, 2, FG)
        ffn = jnp.transpose(mine, (1, 2, 0, 3)).reshape(rpb, 2 * FF)
        g_ffn_in = lax.dynamic_slice_in_dim(ffn, head * (2 * FF // NH), 2 * FF // NH, 1).astype(F32)
        outs = lax.all_gather(b.raw[:, 2 * FG :], ("blk", "head")).reshape(nb, NH, rpb, 2 * FG)
        outs = jnp.transpose(outs, (1, 3, 0, 2)).reshape(NH, 2, per, FG // per, D)
        outs = lax.dynamic_slice_in_dim(outs, head * (D // NH), D // NH, 4)
        outs = jnp.transpose(outs, (0, 2, 1, 3, 4)).reshape(nb, 2, FG // per, D // NH)
        outs = lax.dynamic_index_in_dim(outs, blk, 0, False).astype(F32)
        g_mix_out, g_att_out, g_ffn_out = outs[0, : XC // per], outs[0, XC // per :], outs[1]
    return (
        r.out, r.gin, r.n1, r.mix_in.T, r.cw, r.cb, r.dtb, r.alog, r.skip, r.gain, g_mix_out, r.att_in.T, g_att_out, r.n2,
        g_ffn_in, g_ffn_out,
    )


def solution(mesh):
    both = ("blk", "head")
    tokens, rows, cols = P(None, both, None), P(both, None), P(None, both)
    split = P("blk", "head")
    return jax.shard_map(
        on_device,
        mesh=mesh,
        in_specs=(
            tokens, tokens, P(), P(both), rows, P(), P(), P(), P(), P(), P(), cols, rows, cols, P(both), rows, cols,
        ),
        out_specs=(
            tokens, tokens, P(), split, P(), P(), P(), P(), P(), P(), split, split, split, P(), split, split,
        ),
        check_vma=False,
    )
```

```python
import functools
import types

import jax
import jax.numpy as jnp
import numpy as np
from jax import lax
from jax.experimental import pallas as pl
from jax.experimental.pallas import tpu as pltpu
from jax.sharding import PartitionSpec as P

MHEADS = 24
MHDIM = 64
STATE = 128
QHEADS = 8
HDIM = 64
FF = 2048
DI = 1536
D = 1024
MAXLEN = 4096
NH = 4
HG = MHEADS // NH
XC = HG * MHDIM
FG = FF // NH
WA = XC + 3 * 128
WB = 2 * XC + 128
WC = 3 * FG
LAG = 16
EPS = 1e-5
FAR = -1e30
SCALE = HDIM**-0.5
MESH = pl.DeviceIdType.MESH
BF = jnp.bfloat16
F32 = jnp.float32
VMEM_LIMIT = 62 * 2**20
high = lax.Precision.HIGHEST


def nn(a, b):
    return lax.dot_general(a, b, (((1,), (0,)), ((), ())), preferred_element_type=F32)


def nt(a, b):
    return lax.dot_general(a, b, (((1,), (1,)), ((), ())), preferred_element_type=F32)


def tn(a, b):
    return lax.dot_general(a, b, (((0,), (0,)), ((), ())), preferred_element_type=F32)


def other(index, step):
    return index + step - 2 * step * lax.rem(index // step, 2)


def copy_to(src, dst, send, recv, where):
    return pltpu.make_async_remote_copy(
        src_ref=src, dst_ref=dst, send_sem=send, recv_sem=recv, device_id=where, device_id_type=MESH
    )


def barrier(edges):
    sem = pltpu.get_barrier_semaphore()
    for there, where in edges:
        if there is True:
            pl.semaphore_signal(sem, inc=1, device_id=where, device_id_type=MESH)
        else:

            @pl.when(there)
            def _():
                pl.semaphore_signal(sem, inc=1, device_id=where, device_id_type=MESH)

    total = 0
    for there, _ in edges:
        total = total + (1 if there is True else there.astype(jnp.int32))
    pl.semaphore_wait(sem, total)


def lanes(shape):
    return lax.broadcasted_iota(jnp.int32, shape, len(shape) - 1)


def rows_of(shape):
    return lax.broadcasted_iota(jnp.int32, shape, len(shape) - 2)


def sigmoid(v):
    return 1.0 / (1.0 + jnp.exp(-v))


def widen(cols, first, count=HG, width=MHDIM):
    return jnp.concatenate(
        [
            jnp.broadcast_to(cols[:, first + i : first + i + 1], (cols.shape[0], width))
            for i in range(count)
        ],
        axis=1,
    )


class LineGather:
    def __init__(self, piece, b, h, nb, sems):
        self.piece, self.h, self.nz = piece, h, nb // 2
        self.z, self.x = b // 2, lax.rem(b, 2)
        self.line_recv, self.send_r, self.send_l, self.x_send, self.x_recv = sems

    @staticmethod
    def scratch(nb):
        return [pltpu.SemaphoreType.DMA((nb // 2,))] * 5

    def at(self, z, x=None):
        return self.piece(2 * z + (self.x if x is None else x))

    def to_x(self, z):
        return copy_to(
            self.at(z), self.at(z), self.x_send.at[z], self.x_recv.at[z], (2 * self.z + 1 - self.x, self.h)
        )

    def to_z(self, z, way):
        send = self.send_r if way > 0 else self.send_l
        return copy_to(
            self.at(z), self.at(z), send.at[z], self.line_recv.at[z], (2 * (self.z + way) + self.x, self.h)
        )

    def begin(self):
        self.hop(0)
        self.to_x(self.z).start()

    def hop(self, s):
        @pl.when((self.z - s >= 0) & (self.z + 1 < self.nz))
        def _():
            self.to_z(self.z - s, 1).start()

        @pl.when((self.z + s < self.nz) & (self.z >= 1))
        def _():
            self.to_z(self.z + s, -1).start()

    def advance(self, s):
        left, right = self.z - 1 - s, self.z + 1 + s
        more = s + 1 < self.nz - 1

        @pl.when(left >= 0)
        def _():
            self.to_z(left, 1).wait_recv()
            if more:

                @pl.when(self.z + 1 < self.nz)
                def _():
                    self.to_z(left, 1).start()

            self.to_x(left).start()

        @pl.when(right < self.nz)
        def _():
            self.to_z(right, -1).wait_recv()
            if more:

                @pl.when(self.z >= 1)
                def _():
                    self.to_z(right, -1).start()

            self.to_x(right).start()

    def finish(self):
        for z in range(self.nz):
            copy_to(
                self.at(z, 1 - self.x),
                self.at(z, 1 - self.x),
                self.x_send.at[z],
                self.x_recv.at[z],
                (2 * self.z + 1 - self.x, self.h),
            ).wait_recv()

    def done(self):
        for z in range(self.nz):
            self.to_x(z).wait_send()

            @pl.when((z <= self.z) & (self.z + 1 < self.nz))
            def _():
                self.to_z(z, 1).wait_send()

            @pl.when((z >= self.z) & (self.z >= 1))
            def _():
                self.to_z(z, -1).wait_send()


def line_edges(b, h, nb):
    return [
        (True, (other(b, 1), h)),
        (b >= 2, (b - 2, h)),
        (b + 2 < nb, (b + 2, h)),
    ]


def head_edges(b, h):
    return [(True, (b, other(h, 1))), (True, (b, other(h, 2))), (True, (b, NH - 1 - h))]


class HeadGather:
    def __init__(self, rows, b, h, sems, count=2):
        self.rows, self.b, self.h, self.count = rows, b, h, count
        self.send, self.recv = sems

    @staticmethod
    def scratch(count=2):
        return [pltpu.SemaphoreType.DMA((count, 3))] * 2

    def copy(self, m, i):
        pair, across = other(self.h, 1), other(self.h, 2)
        rows = self.rows(m, self.h if i < 2 else across)
        return copy_to(rows, rows, self.send.at[m, i], self.recv.at[m, i], (self.b, across if i == 1 else pair))

    def begin(self, m):
        self.copy(m, 1).start()
        self.copy(m, 0).start()

    def forward(self, m):
        self.copy(m, 1).wait_recv()
        self.copy(m, 2).start()

    def finish(self, m):
        self.copy(m, 0).wait_recv()
        self.copy(m, 2).wait_recv()

    def done(self):
        for m in range(self.count):
            for i in range(3):
                self.copy(m, i).wait_send()


class HeadScatter:
    def __init__(self, full, b, h, bufs):
        self.full, self.b, self.h = full, b, h
        self.send_c, self.recv_c, self.send_y, self.recv_y, self.send, self.recv = bufs

    @staticmethod
    def scratch(rows):
        return [
            pltpu.VMEM((2, 2, rows, D), BF),
            pltpu.VMEM((2, 2, rows, D), BF),
            pltpu.VMEM((2, rows, D), BF),
            pltpu.VMEM((2, rows, D), BF),
            pltpu.SemaphoreType.DMA((2, 2)),
            pltpu.SemaphoreType.DMA((2, 2)),
        ]

    def copy(self, m, i):
        src, dst = ((self.send_c, self.recv_c), (self.send_y, self.recv_y))[i]
        return copy_to(src.at[m], dst.at[m], self.send.at[m, i], self.recv.at[m, i], (self.b, other(self.h, i + 1)))

    def begin(self, m):
        core = lax.rem(self.h, 2)
        for y in range(2):
            self.send_c[m, y] = self.full(m, 2 * y + 1 - core).astype(BF)
        self.copy(m, 0).start()

    def middle(self, m):
        core, y = lax.rem(self.h, 2), self.h // 2
        self.copy(m, 0).wait_recv()
        self.send_y[m] = (self.full(m, 2 * (1 - y) + core) + self.recv_c[m, 1 - y].astype(F32)).astype(BF)
        self.copy(m, 1).start()

    def finish(self, m):
        self.copy(m, 1).wait_recv()

    def result(self, m):
        y = self.h // 2
        return self.full(m, self.h) + self.recv_c[m, y].astype(F32) + self.recv_y[m].astype(F32)

    def done(self):
        for m in range(2):
            for i in range(2):
                self.copy(m, i).wait_send()


class Todo:
    def __init__(self):
        self.steps = []

    def add(self, *steps):
        self.steps += steps

    def tick(self, count=1):
        for _ in range(min(count, len(self.steps))):
            self.steps.pop(0)()

    def drain(self, left=0):
        self.tick(max(len(self.steps) - left, 0))


def place():
    return lax.axis_index("blk"), lax.axis_index("head")


def rotate_pair(v, cosine, sine):
    lane = lax.rem(lanes(v.shape), HDIM)
    front = lane < HDIM // 2
    partner = jnp.where(front, pltpu.roll(v, 128 - HDIM // 2, 1), pltpu.roll(v, HDIM // 2, 1))
    return v * cosine + jnp.where(front, -partner, partner) * sine


def rope_tables(freq_ref, b, rows, ref_cos, ref_sin):
    pos = (b * rows + rows_of((rows, 128))).astype(F32)
    angle = pos * freq_ref[...]
    ref_cos[...] = jnp.cos(angle)
    ref_sin[...] = jnp.sin(angle)


def vm(shape, dtype):
    return jax.ShapeDtypeStruct(shape, dtype)


def run(body, ins, outs, scratch, name, cid, smem=(), hbm=()):
    names = list(ins) + list(outs) + list(scratch)

    def kernel(*refs):
        body(types.SimpleNamespace(**dict(zip(names, refs))))

    def space(n):
        return pl.BlockSpec(memory_space=pltpu.SMEM if n in smem else (pl.ANY if n in hbm else pltpu.VMEM))

    got = pl.pallas_call(
        kernel,
        out_shape=list(outs.values()),
        in_specs=[space(n) for n in ins],
        out_specs=[space(n) for n in outs],
        scratch_shapes=list(scratch.values()),
        compiler_params=pltpu.CompilerParams(
            collective_id=cid, has_side_effects=cid is not None, vmem_limit_bytes=VMEM_LIMIT
        ),
        name=name,
    )(*ins.values())
    return types.SimpleNamespace(**dict(zip(outs, got)))


class Moves:
    def __init__(self, refs, names, out):
        self.refs, self.names, self.out = refs, names, out
        self.waiting = []

    def copy(self, name):
        far, near = getattr(self.refs, name), getattr(self.refs, "v_" + name)
        src, dst = (near, far) if self.out else (far, near)
        return pltpu.make_async_copy(src, dst, self.refs.moved.at[self.names.index(name)])

    def start(self, *names):
        for n in names:
            self.copy(n).start()
            self.waiting.append(n)

    def wait(self, *names):
        for n in names:
            self.copy(n).wait()
            self.waiting.remove(n)

    def wait_all(self):
        self.wait(*list(self.waiting))


def group(prefix, shapes):
    return {f"{prefix}{i}": s for i, s in enumerate(shapes)}


def members(refs, prefix, count):
    return [getattr(refs, f"{prefix}{i}") for i in range(count)]


def doc_start(starts_ref, m, pos):
    first = jnp.zeros(pos.shape, jnp.int32)
    for k in range(starts_ref.shape[1]):
        s = starts_ref[m, k]
        first = jnp.where(pos >= s, s, first)
    return first


def head_row(ref, h, count=2):
    lane = lanes((1, 128))
    row = jnp.zeros((1, 128), F32)
    for i in range(HG):
        for m in range(count):
            row = jnp.where(lane == 8 * m + i, ref[h * HG + i], row)
    return row


def wide_row(ref, h):
    lane = lanes((1, XC)) // MHDIM
    row = jnp.zeros((1, XC), F32)
    for i in range(HG):
        row = jnp.where(lane == i, ref[h * HG + i], row)
    return row


def valid_row():
    lane = lanes((1, 128))
    return (lane < 16) & (lax.rem(lane, 8) < HG)


def triangle(n, upper=False):
    r, c = rows_of((n, n)), lanes((n, n))
    return ((c >= r) if upper else (c <= r)).astype(F32)


class Scan:
    ROWS = XC + 16

    def __init__(self, way, b, h, nb, reach, bufs):
        self.way, self.b, self.h, self.nb = way, b, h, nb
        self.steps = Scan.step_list(reach)
        self.send_buf, self.recv_buf, self.sums, self.send, self.recv = bufs

    @staticmethod
    def step_list(reach):
        steps, d = [], 1
        while d < reach:
            steps.append(d)
            d *= 2
        return steps + [1]

    @staticmethod
    def scratch(reach):
        n = len(Scan.step_list(reach))
        return [
            pltpu.VMEM((n, Scan.ROWS, 128), BF),
            pltpu.VMEM((n, Scan.ROWS, 128), BF),
            pltpu.VMEM((Scan.ROWS, 128), F32),
            pltpu.SemaphoreType.DMA((n,)),
            pltpu.SemaphoreType.DMA((n,)),
        ]

    @staticmethod
    def edges(b, h, nb, reach):
        out = []
        for d in sorted(set(Scan.step_list(reach))):
            out += [(b + d < nb, (b + d, h)), (b >= d, (b - d, h))]
        return out

    def has_to(self, d):
        return (self.b + d < self.nb) if self.way > 0 else (self.b >= d)

    def has_from(self, d):
        return (self.b >= d) if self.way > 0 else (self.b + d < self.nb)

    def copy(self, i):
        return copy_to(
            self.send_buf.at[i], self.recv_buf.at[i], self.send.at[i], self.recv.at[i],
            (self.b + self.way * self.steps[i], self.h),
        )

    def set(self, state, decay):
        self.sums[0:XC, :] = state
        self.sums[XC : XC + 8, :] = jnp.broadcast_to(decay, (8, 128))
        self.sums[XC + 8 :, :] = jnp.zeros((8, 128), F32)
        self.send_step(0)

    def send_step(self, i):
        self.send_buf[i] = self.sums[...].astype(BF)

        @pl.when(self.has_to(self.steps[i]))
        def _():
            self.copy(i).start()

    def receive(self, i):
        there = self.has_from(self.steps[i])

        @pl.when(there)
        def _():
            self.copy(i).wait_recv()

        @pl.when(jnp.logical_not(there))
        def _():
            self.recv_buf[i] = jnp.zeros((Scan.ROWS, 128), BF)

    def join(self, i):
        if i + 1 >= len(self.steps):
            return
        self.receive(i)
        early = self.recv_buf[i].astype(F32)
        for j in range(HG):
            mine = pl.ds(j * MHDIM, MHDIM)
            decay = self.sums[pl.ds(XC + j, 1), :]
            self.sums[mine, :] = self.sums[mine, :] + decay * early[j * MHDIM : (j + 1) * MHDIM]
        self.sums[pl.ds(XC, 8), :] = self.sums[pl.ds(XC, 8), :] * early[XC : XC + 8]
        self.send_step(i + 1)

    def last(self):
        end = len(self.steps) - 1
        self.receive(end)
        return self.recv_buf.at[end]

    def finish(self):
        for i, d in enumerate(self.steps):

            @pl.when(self.has_to(d))
            def _():
                self.copy(i).wait_send()


def halo_edges(b, h, nb, reach):
    out = []
    for d in range(1, reach + 1):
        out += [(b + d < nb, (b + d, h)), (b >= d, (b - d, h))]
    return out


class Halo:
    def __init__(self, way, src, dst, b, h, nb, reach, sems):
        self.way, self.src, self.dst, self.b, self.h, self.nb, self.reach = way, src, dst, b, h, nb, reach
        self.send, self.recv = sems

    @staticmethod
    def scratch(reach):
        return [pltpu.SemaphoreType.DMA((reach + 1,))] * 2

    def there(self, d, way):
        return (self.b + d < self.nb) if way > 0 else (self.b >= d)

    def copy(self, d):
        return copy_to(
            self.src(d), self.dst(d), self.send.at[d], self.recv.at[d], (self.b + self.way * d, self.h)
        )

    def begin(self):
        for d in range(1, self.reach + 1):

            @pl.when(self.there(d, self.way))
            def _():
                self.copy(d).start()

    def finish_recv(self):
        for d in range(1, self.reach + 1):

            @pl.when(self.there(d, -self.way))
            def _():
                self.copy(d).wait_recv()

    def finish_send(self):
        for d in range(1, self.reach + 1):

            @pl.when(self.there(d, self.way))
            def _():
                self.copy(d).wait_send()


class HeadSum:
    def __init__(self, b, h, bufs):
        self.b, self.h = b, h
        self.buf, self.send, self.recv = bufs

    @staticmethod
    def scratch(T):
        return [pltpu.VMEM((4, 8, T), F32), pltpu.SemaphoreType.DMA((3,)), pltpu.SemaphoreType.DMA((3,))]

    def copies(self):
        return [
            copy_to(self.buf.at[0], self.buf.at[1 + i], self.send.at[i], self.recv.at[i], (self.b, to))
            for i, to in enumerate((other(self.h, 1), other(self.h, 2), NH - 1 - self.h))
        ]

    def begin(self, column):
        T = self.buf.shape[2]
        self.buf[0] = jnp.broadcast_to(column, (T, 128)).T[:8]
        for c in self.copies():
            c.start()

    def finish(self):
        for c in self.copies():
            c.wait()
        T = self.buf.shape[2]
        total = self.buf[0] + self.buf[1] + self.buf[2] + self.buf[3]
        return jnp.concatenate([total, jnp.zeros((120, T), F32)], axis=0).T[:, 0:1]


def group_taps(h, w_ref, b_ref, chunk):
    if chunk < XC // 128:
        at = pl.ds(pl.multiple_of(h * XC + chunk * 128, 128), 128)
    else:
        at = pl.ds(DI + (chunk - XC // 128) * 128, 128)
    return w_ref[:, at], (None if b_ref is None else b_ref[:, at])


def decays_of(dt_ref, bias_ref, alog_ref, h, T):
    valid = valid_row()
    z = dt_ref[...] + head_row(bias_ref, h)
    step = jnp.where(valid, jnp.maximum(z, 0.0) + jnp.log1p(jnp.exp(-jnp.abs(z))), 0.0)
    a_neg = jnp.where(valid, -jnp.exp(head_row(alog_ref, h)), 0.0)
    cum = jnp.dot(triangle(T), step * a_neg, precision=high, preferred_element_type=F32)
    return z, step, a_neg, cum


def by_batch(pick):
    first, second = pick(0), pick(1)
    return jnp.where(lanes((first.shape[0], 128)) < 8, first, second)


def norm_back(value, scale, gain, upstream):
    n = value * scale
    uw = upstream * gain
    grad = scale * (uw - n * jnp.mean(n * uw, axis=1, keepdims=True))
    return grad, jnp.sum(upstream * n, axis=0, keepdims=True)


def arrange(per, width, first):
    total = XC + 128
    share, mix, att = total // per, XC // per, 128 // per
    n, src = lanes((width, total)), rows_of((width, total))
    i, u = n // share, lax.rem(n, share)
    if first == 0:
        hit = (u < mix) & (src == i * mix + u)
    else:
        hit = (u >= mix) & (src == i * att + u - mix)
    return hit.astype(F32).astype(BF)


def head_select(m):
    return (lanes((XC, 128)) == 8 * m + rows_of((XC, 128)) // MHDIM).astype(F32)


def exact(a, b):
    return jnp.dot(a, b, precision=high, preferred_element_type=F32)


class LineReduce:
    def __init__(self, src, bufs, b, h, nb):
        self.src, self.h, self.nz = src, h, nb // 2
        self.z, self.x = b // 2, lax.rem(b, 2)
        self.whole = len(bufs) == 10
        if self.whole:
            self.total, self.from_l, self.from_r, self.ls, self.lr, self.rs, self.rr, self.from_x, self.xs, self.xr = bufs
        else:
            self.total, self.from_l, self.from_r, self.ls, self.lr, self.rs, self.rr = bufs

    @staticmethod
    def scratch(nb, cols, whole=True):
        nz, rpb = nb // 2, D // nb
        buf, sem = pltpu.VMEM((nz, rpb, cols), BF), pltpu.SemaphoreType.DMA((nz,))
        return [buf] * 3 + [sem] * 4 + ([buf] + [sem] * 2 if whole else [])

    def to_x(self, z):
        return copy_to(
            self.src.at[z, 1 - self.x], self.from_x.at[z], self.xs.at[z], self.xr.at[z], (2 * self.z + 1 - self.x, self.h)
        )

    def up(self, z):
        return copy_to(
            self.total.at[z], self.from_l.at[z], self.rs.at[z], self.lr.at[z], (2 * (self.z + 1) + self.x, self.h)
        )

    def down(self, z):
        return copy_to(
            self.total.at[z], self.from_r.at[z], self.ls.at[z], self.rr.at[z], (2 * (self.z - 1) + self.x, self.h)
        )

    def start_x(self, j):
        self.to_x(jnp.where(self.z < self.nz // 2, self.nz - 1 - j, j)).start()

    def start_some(self, part, parts=4):
        for j in range(part * self.nz // parts, (part + 1) * self.nz // parts):
            self.start_x(j)

    def paired(self, z):
        if not self.whole:
            return self.src[z].astype(F32)
        self.to_x(z).wait_recv()
        return self.src[z, self.x].astype(F32) + self.from_x[z].astype(F32)

    def step(self, t):
        z_up, z_down = self.nz - 1 - t + self.z, t - (self.nz - 1) + self.z

        @pl.when(t >= self.z)
        def _():
            value = self.paired(z_up)

            @pl.when(self.z == 0)
            def _():
                self.total[z_up] = value.astype(BF)

            @pl.when(self.z > 0)
            def _():
                self.up(z_up).wait_recv()
                self.total[z_up] = (value + self.from_l[z_up].astype(F32)).astype(BF)

            self.up(z_up).start()

        @pl.when(z_down >= 0)
        def _():
            value = self.paired(z_down)

            @pl.when(self.z == self.nz - 1)
            def _():
                self.total[z_down] = value.astype(BF)

            @pl.when(self.z < self.nz - 1)
            def _():
                self.down(z_down).wait_recv()
                self.total[z_down] = (value + self.from_r[z_down].astype(F32)).astype(BF)

            self.down(z_down).start()

    def step_some(self, part, parts=3):
        for t in range(part * (self.nz - 1) // parts, (part + 1) * (self.nz - 1) // parts):
            self.step(t)

    def finish(self, result):
        z = self.z
        result[...] = self.paired(z)

        @pl.when(z >= 1)
        def _():
            self.up(z).wait_recv()
            result[...] += self.from_l[z].astype(F32)

        @pl.when(z + 1 < self.nz)
        def _():
            self.down(z).wait_recv()
            result[...] += self.from_r[z].astype(F32)

    def done(self):
        for z in range(self.nz):
            if self.whole:
                self.to_x(z).wait_send()

            @pl.when(self.z < z)
            def _():
                self.up(z).wait_send()

            @pl.when(self.z > z)
            def _():
                self.down(z).wait_send()


class PairReduce:
    def __init__(self, src, bufs, b, h, nb):
        self.src, self.h, self.nz = src, h, nb // 2
        self.z, self.x = b // 2, lax.rem(b, 2)
        self.from_x, self.xs, self.xr = bufs

    @staticmethod
    def scratch(nb, cols):
        nz, rpb = nb // 2, D // nb
        return [pltpu.VMEM((nz, rpb, cols), BF)] + [pltpu.SemaphoreType.DMA((nz,))] * 2

    def to_x(self, z):
        return copy_to(
            self.src.at[z, 1 - self.x], self.from_x.at[z], self.xs.at[z], self.xr.at[z], (2 * self.z + 1 - self.x, self.h)
        )

    def begin(self):
        for z in range(self.nz):
            self.to_x(z).start()

    def finish(self, out, cols):
        for z in range(self.nz):
            self.to_x(z).wait_recv()
            out[z, :, cols] = (self.src[z, self.x].astype(F32) + self.from_x[z].astype(F32)).astype(BF)

    def done(self):
        for z in range(self.nz):
            self.to_x(z).wait_send()


class Sum:
    def __init__(self, bufs, b, h, nb):
        self.b, self.h, self.nb = b, h, nb
        self.acc, self.got, self.send, self.recv = bufs
        self.steps = Sum.step_list(nb)

    @staticmethod
    def step_list(nb):
        steps = [("h", 1), ("h", 2)]
        d = 1
        while d < nb:
            steps.append(("b", d))
            d *= 2
        return steps

    @staticmethod
    def scratch(nb, shape):
        n = len(Sum.step_list(nb))
        return [
            pltpu.VMEM((n + 1,) + shape, F32), pltpu.VMEM((n,) + shape, F32),
            pltpu.SemaphoreType.DMA((n,)), pltpu.SemaphoreType.DMA((n,)),
        ]

    def peer(self, i):
        kind, d = self.steps[i]
        return (self.b, other(self.h, d)) if kind == "h" else (other(self.b, d), self.h)

    def edges(self):
        return [(True, self.peer(i)) for i in range(len(self.steps))]

    def copy(self, i):
        return copy_to(self.acc.at[i], self.got.at[i], self.send.at[i], self.recv.at[i], self.peer(i))

    def begin(self, value):
        self.acc[0] = value
        self.copy(0).start()

    def step(self, i):
        self.copy(i).wait()
        self.acc[i + 1] = self.acc[i] + self.got[i]
        if i + 1 < len(self.steps):
            self.copy(i + 1).start()

    def result(self):
        return self.acc[len(self.steps)]


def pack_rows(R, S):
    eye = (rows_of((S, S)) == lanes((S, S))).astype(F32)
    gain_cols = [jnp.sum(eye * ref[...].astype(F32), axis=1, keepdims=True) for ref in (R.n1, R.n2)]
    lane = lanes((S, 128))
    for i in range(NH):
        R.pa[i, :, 0:XC] = R.mixer_in[:, DI + i * XC : DI + (i + 1) * XC]
        bc = 2 * DI + 128 * (i % 2)
        R.pa[i, :, XC : XC + 128] = R.mixer_in[:, bc : bc + 128]
        R.pa[i, :, XC + 128 : XC + 256] = R.attn_in[:, i * 128 : (i + 1) * 128]
        kv = QHEADS * HDIM + 128 * (i % 2)
        kv = R.attn_in[:, kv : kv + 128].astype(F32)
        if i >= 2:
            kv = pltpu.roll(kv, HDIM, 1)
        pick = (rows_of((MHEADS, 128)) == i * HG + lanes((MHEADS, 128)) - HDIM) & (lanes((MHEADS, 128)) >= HDIM)
        pick = pick & (lanes((MHEADS, 128)) < HDIM + HG)
        dt = nn(R.mixer_in[:, 2 * DI + 2 * STATE :], pick.astype(F32).astype(BF))
        last = jnp.where(lane < HDIM, kv, dt)
        for k in range(2):
            last = jnp.where(lane == HDIM + HG + k, gain_cols[k], last)
        R.pa[i, :, XC + 256 :] = last.astype(BF)
    for i in range(NH):
        R.pb[i, :, 0:XC] = R.mixer_in[:, i * XC : (i + 1) * XC]
        R.pb[i, :, XC : 2 * XC] = R.mixer_out[:, i * XC : (i + 1) * XC]
        R.pb[i, :, 2 * XC :] = R.attn_out[:, i * 128 : (i + 1) * 128]
        R.pc[i, :, 0:FG] = R.ffn_out[:, i * FG : (i + 1) * FG]
        R.pc[i, :, FG : 2 * FG] = R.ffn_in[:, i * FG : (i + 1) * FG]
        R.pc[i, :, 2 * FG :] = R.ffn_in[:, FF + i * FG : FF + (i + 1) * FG]


LATE_OUT = ["normed", "xin", "bc", "q", "pre", "wa", "wb", "kvh", "gw_out"]


def forward_body(nb, T, reach, local, R):
    b, h = place()
    moves = Moves(R, LATE_OUT, True)
    core, y = lax.rem(h, 2), h // 2
    tok, rpb = T // NH, D // nb
    S, nz = rpb // NH, nb // 2
    pair = (b, other(h, 1))
    peers = (other(h, 1), other(h, 2), NH - 1 - h)
    if local:
        pack_rows(R, S)
    R.cb2[...] = R.cb[...].reshape(1, DI + 256)
    R.gain2[...] = R.gain[...].reshape(1, DI)
    barrier(
        head_edges(b, h)
        + line_edges(b, h, nb)
        + [((h == NH - 1) & (b + 1 < nb), (b + 1, jnp.int32(i))) for i in range(NH)]
        + [(b >= 1, (b - 1, jnp.int32(NH - 1)))]
        + Scan.edges(b, h, nb, reach)
        + halo_edges(b, h, nb, reach)
    )
    packs, weights = (R.pa, R.pb, R.pc), (R.v_wa, R.v_wb, R.wc)
    gather_x = HeadGather(lambda m, i: R.xg.at[m, pl.ds(LAG + i * tok, tok)], b, h, members(R, "gx", 2))
    gather_c = HeadGather(lambda m, i: R.cotg.at[m, pl.ds(i * tok, tok)], b, h, members(R, "gc", 2))
    spots = [(R.v_wa, slice(XC, WA)), (R.v_wa, slice(0, XC)), (R.v_wb, slice(0, WB))] + [(R.wc, slice(k * FG, (k + 1) * FG)) for k in range(3)]
    lines = [
        LineGather(
            lambda i, w=w, cols=cols: w.at[pl.ds(i * rpb, rpb), cols], b, h, nb, members(R, f"line{k}_", 5)
        )
        for k, (w, cols) in enumerate(spots)
    ]

    def piece(k, i):
        mine = weights[k].at[pl.ds(b * rpb + h * S, S)]
        return copy_to(packs[k].at[peers[i]], mine, R.ps.at[k, i], R.pr.at[k, i], (b, peers[i]))

    def start_pieces(k):
        if local:
            for i in range(3):
                piece(k, i).start()
            weights[k][pl.ds(b * rpb + h * S, S), :] = packs[k][h]
        else:
            weights[k][pl.ds(b * rpb, rpb), :] = packs[k][...]

    def wait_pieces(k):
        if local:
            for i in range(3):
                piece(k, i).wait_recv()

    start_pieces(0)
    for m in range(2):
        R.xg[m, pl.ds(LAG + h * tok, tok), :] = R.x[m]
        R.cotg[m, pl.ds(h * tok, tok), :] = R.cot[m]
    for m in range(2):
        gather_x.begin(m)

    def edge(i):
        return copy_to(
            R.x.at[:, pl.ds(tok - LAG, LAG)], R.xg.at[:, pl.ds(0, LAG)], R.es.at[i], R.er.at[0], (b + 1, jnp.int32(i))
        )

    @pl.when((h == NH - 1) & (b + 1 < nb))
    def _():
        for i in range(NH):
            edge(i).start()

    @pl.when(b == 0)
    def _():
        R.xg[:, 0:LAG, :] = jnp.zeros((2, LAG, D), BF)

    start_pieces(1)
    wait_pieces(0)
    lines[0].begin()
    lines[1].begin()
    rope_tables(R.freq, b, T, R.cosine, R.sine)
    for m in range(2):
        gather_x.forward(m)
    for m in range(2):
        gather_x.finish(m)

    @pl.when(b >= 1)
    def _():
        edge(0).wait_recv()

    for m in range(2):
        v = R.xg[m].astype(F32)
        R.wide[m] = v * lax.rsqrt(jnp.mean(v * v, axis=1, keepdims=True) + EPS)
    share = lambda part: range(part * (nz - 1) // 3, (part + 1) * (nz - 1) // 3)

    def ahead(part, *which):
        for s in share(part):
            for k in which:
                lines[k].advance(s)

    ahead(0, 0, 1)
    wait_pieces(1)
    start_pieces(2)
    for m in range(2):
        gather_c.begin(m)
    ahead(1, 0, 1)
    lines[2].begin()
    ahead(2, 0, 1)
    lines[0].finish()

    last = R.v_wa[:, XC + 256 :].astype(F32).T
    R.gains[...] = last[HDIM + HG + 2 - 8 : HDIM + HG + 2]
    n1 = R.gains[6:7, :]
    for m in range(2):
        R.v_normed[m] = (R.wide[m] * n1).astype(BF)
    lane = lanes((T, 128))
    mine_bc = pl.ds(pl.multiple_of(core * 128, 128), 128)
    kv = [nn(R.v_normed[m, LAG:], R.v_wa[:, XC + 256 :]) for m in range(2)]
    packed = jnp.where(lane < HDIM, kv[0], pltpu.roll(kv[1], HDIM, 1))
    turned = rotate_pair(packed, R.cosine[...], R.sine[...])
    R.v_kvh[0, core] = jnp.where(core == 0, turned, packed).astype(BF)
    halo = Halo(1, lambda d: R.v_kvh.at[0, core], lambda d: R.v_kvh.at[d, core], b, h, nb, reach, members(R, "halo", 2))
    halo.begin()
    for m in range(2):
        R.v_bc[m, :, mine_bc] = nn(R.v_normed[m], R.v_wa[:, XC : XC + 128]).astype(BF)
    swap = (
        lambda: copy_to(R.v_bc.at[:, :, mine_bc], R.v_bc.at[:, :, mine_bc], R.ss.at[0], R.sr.at[0], pair),
        lambda: copy_to(R.v_kvh.at[0, core], R.v_kvh.at[0, core], R.ss.at[1], R.sr.at[1], pair),
    )
    for c in swap:
        c().start()
    wait_pieces(2)
    lines[3].begin()
    dt = [pltpu.roll(kv[0], 128 - HDIM, 1), pltpu.roll(kv[1], 128 - HDIM + 8, 1)]
    R.dt[...] = (
        jnp.where(lane < HG, dt[0], jnp.where((lane >= 8) & (lane < 8 + HG), dt[1], 0.0)).astype(BF).astype(F32)
    )
    for m in range(2):
        q = nn(R.v_normed[m, LAG:], R.v_wa[:, XC + 128 : XC + 256])
        R.v_q[m] = rotate_pair(q, R.cosine[...], R.sine[...]).astype(BF)
    lines[1].finish()
    for m in range(2):
        R.v_xin[m] = nn(R.v_normed[m], R.v_wa[:, 0:XC]).astype(BF)

    scans = [Scan(1, b, h, nb, reach, members(R, f"scan{m}_", 5)) for m in range(2)]
    sums = [HeadSum(b, h, members(R, f"sumf{m}_", 3)) for m in range(2)]
    back_sums = [HeadSum(b, h, members(R, f"sumb{m}_", 3)) for m in range(2)]
    pos = b * T + rows_of((T, 1))
    first = [doc_start(R.starts, m, pos) for m in range(2)]
    tail = [f[T - 1 :, :] for f in first]
    for d in range(1, reach + 1):

        @pl.when(b < d)
        def _():
            R.v_kvh[d] = jnp.zeros((2, T, 128), BF)

    def convolve(m, chunks):
        for chunk in chunks:
            cols = pl.ds(chunk * 128, 128)
            taps, bias = group_taps(h, R.cw, R.cb2, chunk)
            total = jnp.broadcast_to(bias, (T, 128))
            for j in range(4):
                back = 3 - j
                total = total + jnp.where(
                    pos - first[m] >= back, R.cin[m, pl.ds(LAG - back, T), cols] * taps[j : j + 1], 0.0
                )
            R.v_pre[m, :, cols] = total
            act = total * sigmoid(total)
            if chunk < XC // 128:
                R.xs[m, :, cols] = act
            elif chunk == XC // 128:
                R.bs[m] = act.astype(BF)
            else:
                R.cs[m] = act.astype(BF)

    z, step, a_neg, cum = decays_of(R.dt, R.dtb, R.alog, h, T)
    R.cumt[...] = cum.T[:16]
    R.stept[...] = step.T[:16]
    cum_last = cum[T - 1 :, :]
    kept = by_batch(lambda m: jnp.broadcast_to((pos >= tail[m]).astype(F32), (T, 128)))
    omega = jnp.exp(cum_last - cum) * step * kept
    for m in range(2):
        if m == 1:
            ahead(0, 2)
        R.cin[m, :, 0:XC] = R.v_xin[m].astype(F32)
        convolve(m, range(XC // 128))
        if m == 0:
            swap[0]().wait_recv()
        R.cin[m, :, XC:] = R.v_bc[m].astype(F32)
        convolve(m, (XC // 128, XC // 128 + 1))
        weighted = (R.xs[m] * widen(omega, 8 * m)).astype(BF)
        decay = jnp.where(tail[m] < b * T, jnp.exp(R.cumt[8 * m : 8 * m + 8, T - 1 : T]), 0.0)
        scans[m].set(tn(weighted, R.bs[m]), decay)
    lines[4].begin()

    seen = lanes((T, T)) + b * T
    lane = lanes((T, 128))

    def inside(m, between):
        both = nt(R.cs[m], R.bs[m])
        allowed = (seen <= pos) & (seen >= first[m])
        for i in range(HG):
            l = 8 * m + i
            gap = jnp.where(allowed, cum[:, l : l + 1] - R.cumt[l : l + 1, :], FAR)
            weights_ts = (jnp.exp(gap) * both * R.stept[l : l + 1, :]).astype(BF)
            R.ybuf[m, :, i * MHDIM : (i + 1) * MHDIM] = nn(weights_ts, R.xs[m, :, i * MHDIM : (i + 1) * MHDIM].astype(BF))
            if i == HG // 2 - 1:
                between()
        R.ybuf[m] = R.ybuf[m] + wide_row(R.skip, h) * R.xs[m]

    def on_to_pair(d):
        return copy_to(R.v_kvh.at[d, core], R.v_kvh.at[d, core], R.hs.at[d], R.hr.at[d], pair)

    R.lse[...] = jnp.zeros((T, 128), F32)

    def attend(m, i):
        query = R.v_q[m, :, i * HDIM : (i + 1) * HDIM]

        def score(d, top):
            at = seen - d * T
            keys = R.v_kvh[d, 0, :, m * HDIM : (m + 1) * HDIM]
            s = jnp.where((at <= pos) & (at >= first[m]), nt(query, keys) * SCALE, FAR)
            R.sbuf[d] = s
            return jnp.maximum(top, jnp.max(s, axis=1, keepdims=True))

        top = lax.fori_loop(0, reach + 1, score, jnp.full((T, 1), FAR, F32))

        def weigh(d, total):
            e = jnp.exp(R.sbuf[d] - top)
            R.sbuf[d] = e
            return total + jnp.sum(e, axis=1, keepdims=True)

        total = lax.fori_loop(0, reach + 1, weigh, jnp.zeros((T, 1), F32))
        inverse = 1.0 / total

        def take(d, acc):
            probs = (R.sbuf[d] * inverse).astype(BF)
            return acc + nn(probs, R.v_kvh[d, 1, :, m * HDIM : (m + 1) * HDIM])

        out = lax.fori_loop(0, reach + 1, take, jnp.zeros((T, HDIM), F32))
        R.attnf[m, :, i * HDIM : (i + 1) * HDIM] = out
        R.attnl[m, :, i * HDIM : (i + 1) * HDIM] = out.astype(BF)
        R.lse[...] = jnp.where(lane == 2 * m + i, top + jnp.log(total), R.lse[...])

    def mixed(m):
        gate = nn(R.v_normed[m, LAG:], R.v_wb[:, 0:XC])
        R.gate[m] = gate
        R.sin[m] = scans[m].last()[...]
        live = jnp.where(first[m] < b * T, jnp.exp(cum), 0.0)
        yv = R.ybuf[m] + nt(R.cs[m], R.sin[m, 0:XC]) * widen(live, 8 * m)
        low = yv.astype(BF)
        R.ylow[m] = low
        g = low.astype(F32) * gate * sigmoid(gate)
        R.ybuf[m] = g
        sums[m].begin(jnp.sum(g * g, axis=1, keepdims=True))

    gain = R.gain2[:, pl.ds(pl.multiple_of(h * XC, 128), XC)]
    n2 = R.gains[7:8, :]
    scales = [None, None]

    def rows(ref):
        return lambda m, head: ref[m, pl.ds(pl.multiple_of(head * tok, tok), tok), :]

    def own(ref, m):
        return ref.at[m, pl.ds(pl.multiple_of(h * tok, tok), tok), :]

    out1 = HeadScatter(rows(R.wide), b, h, members(R, "sc1_", 6))
    out2 = HeadScatter(rows(R.wide), b, h, members(R, "sc2_", 6))
    out3 = HeadScatter(rows(R.part), b, h, members(R, "sc3_", 6))
    gather_s = HeadGather(lambda m, i: R.secg.at[m, pl.ds(i * tok, tok)], b, h, members(R, "gs", 2))
    gather_h = HeadGather(lambda m, i: R.hlg.at[m, pl.ds(i * tok, tok)], b, h, members(R, "gh", 2))
    w_mix, w_att, w_out, w_in = (
        lambda: R.v_wb[:, XC : 2 * XC], lambda: R.v_wb[:, 2 * XC :], lambda: R.wc[:, 0:FG], lambda: R.wc[:, FG:]
    )

    def project(m):
        scales[m] = lax.rsqrt(sums[m].finish() * (1.0 / DI) + EPS)
        R.gated[m] = (R.ybuf[m] * scales[m] * gain).astype(BF)
        R.wide[m, 0:T, :] = nt(R.gated[m], w_mix()) + nt(R.attnl[m], w_att())
        out1.begin(m)

    def second_norm(m):
        out1.finish(m)
        value = R.x[m].astype(F32) + out1.result(m)
        R.hid[m] = value
        scale = lax.rsqrt(jnp.mean(value * value, axis=1, keepdims=True) + EPS)
        own(R.secg, m)[...] = (value * scale * n2).astype(BF)
        gather_s.begin(m)

    def feed(m):
        gather_c.finish(m)
        R.gact[m] = nn(R.cotg[m], w_out())
        gather_s.finish(m)
        a = nn(R.secg[m], R.wc[:, FG : 2 * FG])
        u = nn(R.secg[m], R.wc[:, 2 * FG :])
        sg = sigmoid(a)
        si = a * sg
        R.act[m] = (si * u).astype(BF)
        R.ggu[m, :, 0:FG] = (R.gact[m] * u * (sg * (1.0 + a * (1.0 - sg)))).astype(BF)
        R.ggu[m, :, FG:] = (R.gact[m] * si).astype(BF)
        R.wide[m, 0:T, :] = nt(R.ggu[m], w_in())
        out2.begin(m)
        R.part[m] = nt(R.act[m], w_out())

    def hidden_back(m):
        out2.finish(m)
        value = R.hid[m]
        scale = lax.rsqrt(jnp.mean(value * value, axis=1, keepdims=True) + EPS)
        grad, gain_part = norm_back(value, scale, n2, out2.result(m))
        grad = grad + R.cot[m].astype(F32)
        R.gh[m] = grad
        R.gn2[...] = gain_part if m == 0 else R.gn2[...] + gain_part
        own(R.hlg, m)[...] = grad.astype(BF)
        gather_h.begin(m)

    def project_back(m):
        gather_h.finish(m)
        R.up[m] = nn(R.hlg[m], w_mix())
        gate = R.gate[m]
        n = R.ylow[m].astype(F32) * gate * sigmoid(gate) * scales[m]
        up = R.up[m]
        part = jnp.sum(up * n, axis=0, keepdims=True)
        R.ggain[...] = part if m == 0 else R.ggain[...] + part
        back_sums[m].begin(jnp.sum(up * gain * n, axis=1, keepdims=True))
        R.gattn[m] = nn(R.hlg[m], w_att()).astype(BF)

    def mixed_back(m):
        total = back_sums[m].finish()
        gate = R.gate[m]
        sg = sigmoid(gate)
        si = gate * sg
        low = R.ylow[m].astype(F32)
        n = low * si * scales[m]
        grad = scales[m] * (R.up[m] * gain - n * (total * (1.0 / DI)))
        R.gy[m] = (grad * si).astype(BF)
        R.ggate[m] = (grad * low * (sg * (1.0 + gate * (1.0 - sg)))).astype(BF)

    def weight_grad(ref, at, left, right, cols):
        ref[:, at + cols.start : at + cols.stop] = sum(tn(left[m], right[m, :, cols]) for m in range(2)).astype(BF)

    pairs = [PairReduce(getattr(R, f"gi{k}"), members(R, f"pair{k}_", 3), b, h, nb) for k in range(2)]

    def in_grad(k, q):
        cols = slice(k * FG + q * FG // 2, k * FG + (q + 1) * FG // 2)
        grad = sum(tn(R.secg[m], R.ggu[m, :, cols]) for m in range(2)).astype(BF)
        pairs[k].src[:, :, :, q * FG // 2 : (q + 1) * FG // 2] = grad.reshape(nz, 2, rpb, FG // 2)

    moves.start("normed", "xin", "bc", "q", "pre", "wa")
    inside(0, lambda: ahead(1, 2))
    for m in range(2):
        scans[m].join(0)
    ahead(0, 3)
    lines[5].begin()
    halo.finish_recv()
    for d in range(1, reach + 1):

        @pl.when(b >= d)
        def _():
            on_to_pair(d).start()

    swap[1]().wait_recv()
    for d in range(1, reach + 1):

        @pl.when(b >= d)
        def _():
            on_to_pair(d).wait_recv()

    attend(0, 0)
    ahead(2, 2)
    for i in range(1, len(scans[0].steps) - 1):
        for m in range(2):
            scans[m].join(i)
    ahead(0, 4)
    attend(0, 1)
    ahead(1, 3)
    for m in range(2):
        gather_c.forward(m)
    inside(1, lambda: ahead(0, 5))
    attend(1, 0)
    attend(1, 1)
    lines[2].finish()
    moves.start("wb", "kvh")
    mixed(0)
    ahead(1, 4)
    mixed(1)
    project(0)
    ahead(2, 3)
    ahead(1, 5)
    out1.middle(0)
    project(1)
    ahead(2, 4)
    second_norm(0)
    out1.middle(1)
    ahead(2, 5)
    gather_s.forward(0)
    for k in range(3, 6):
        lines[k].finish()
    feed(0)
    second_norm(1)
    out2.middle(0)
    gather_s.forward(1)
    feed(1)
    out2.middle(1)
    in_grad(0, 0)
    in_grad(0, 1)
    pairs[0].begin()
    hidden_back(0)
    in_grad(1, 0)
    in_grad(1, 1)
    pairs[1].begin()
    for m in range(2):
        out3.begin(m)
    gather_h.forward(0)
    hidden_back(1)
    project_back(0)
    gather_h.forward(1)
    out3.middle(0)
    out3.middle(1)
    half = [slice(k * FG // 2, (k + 1) * FG // 2) for k in range(2)]
    for k in range(2):
        weight_grad(R.v_gw_out, FG, R.cotg, R.act, half[k])
    project_back(1)
    mixed_back(0)
    per = max(nb // NH, 1)
    mix_to, att_to = arrange(per, XC, 0), arrange(per, 128, 1)
    for m in range(2):
        R.act[m] = (nn(R.gated[m], mix_to) + nn(R.attnl[m], att_to)).astype(BF)
    for k in range(2):
        weight_grad(R.v_gw_out, 0, R.hlg, R.act, half[k])
    moves.start("gw_out")
    mixed_back(1)
    for m in range(2):
        out3.finish(m)
        R.out[m] = R.hid[m] + out3.result(m)
    for k in range(2):
        pairs[k].finish(R.gw_in, slice(k * FG, (k + 1) * FG))

    if local:
        for k in range(3):
            for i in range(3):
                piece(k, i).wait_send()

    @pl.when((h == NH - 1) & (b + 1 < nb))
    def _():
        for i in range(NH):
            edge(i).wait_send()

    for c in swap:
        c().wait_send()
    for d in range(1, reach + 1):

        @pl.when(b >= d)
        def _():
            on_to_pair(d).wait_send()

    moves.wait_all()
    for g in lines + pairs + [gather_x, gather_c, gather_s, gather_h, out1, out2, out3]:
        g.done()
    for scan in scans:
        scan.finish()
    halo.finish_send()


def forward(nb, reach, ins, local):
    tok = ins["x"].shape[1]
    T, rpb = tok * NH, D // nb
    S = rpb // NH
    dma = pltpu.SemaphoreType.DMA
    outs = dict(
        normed=vm((2, LAG + T, D), BF), xin=vm((2, LAG + T, XC), BF), bc=vm((2, LAG + T, 256), BF), q=vm((2, T, 128), BF),
        kvh=vm((reach + 1, 2, T, 128), BF), dt=vm((T, 128), F32), pre=vm((2, T, XC + 256), F32),
        sin=vm((2, Scan.ROWS, 128), BF), attnf=vm((2, T, 128), F32), lse=vm((T, 128), F32), gy=vm((2, T, XC), BF),
        ggate=vm((2, T, XC), BF), gattn=vm((2, T, 128), BF), gw_in=vm((nb // 2, rpb, 2 * FG), BF), gw_out=vm((D, 2 * FG), BF), gn2=vm((1, D), F32),
        ggain=vm((1, XC), F32), out=vm((2, tok, D), F32), gh=vm((2, tok, D), F32), wa=vm((D, WA), BF), wb=vm((D, WB), BF),
        gains=vm((8, D), F32), cosine=vm((T, 128), F32), sine=vm((T, 128), F32),
    )
    V = pltpu.VMEM
    scratch = dict(
        xg=V((2, LAG + T, D), BF), cotg=V((2, T, D), BF), wc=V((D, WC), BF), wide=V((2, LAG + T, D), F32),
        gate=V((2, T, XC), F32), cin=V((2, LAG + T, XC + 256), F32), xs=V((2, T, XC), F32), bs=V((2, T, 128), BF),
        cs=V((2, T, 128), BF), ybuf=V((2, T, XC), F32), sbuf=V((reach + 1, T, T), F32), cumt=V((16, T), F32),
        stept=V((16, T), F32), ylow=V((2, T, XC), BF), gated=V((2, T, XC), BF), attnl=V((2, T, 128), BF),
        part=V((2, T, D), F32), secg=V((2, T, D), BF), hlg=V((2, T, D), BF), act=V((2, T, FG), BF),
        ggu=V((2, T, 2 * FG), BF), gact=V((2, T, FG), F32), hid=V((2, tok, D), F32), up=V((2, T, XC), F32),
        cb2=V((1, DI + 256), F32), gain2=V((1, DI), F32),
        ps=dma((3, 3)), pr=dma((3, 3)), es=dma((NH,)), er=dma((1,)), ss=dma((2,)), sr=dma((2,)),
        hs=dma((reach + 1,)), hr=dma((reach + 1,)),
    )
    scratch.update({"v_" + n: V(outs[n].shape, outs[n].dtype) for n in LATE_OUT}, moved=dma((len(LATE_OUT),)))
    if local:
        scratch.update(pa=V((NH, S, WA), BF), pb=V((NH, S, WB), BF), pc=V((NH, S, WC), BF))
    for name in ("gx", "gc", "gs", "gh"):
        scratch.update(group(name, HeadGather.scratch()))
    for k in range(2):
        scratch.update(group(f"pair{k}_", PairReduce.scratch(nb, FG)))
        scratch[f"gi{k}"] = V((nb // 2, 2, rpb, FG), BF)
    for k in range(6):
        scratch.update(group(f"line{k}_", LineGather.scratch(nb)))
    for k in range(3):
        scratch.update(group(f"sc{k + 1}_", HeadScatter.scratch(tok)))
    for m in range(2):
        scratch.update(group(f"scan{m}_", Scan.scratch(reach)))
        scratch.update(group(f"sumf{m}_", HeadSum.scratch(T)))
        scratch.update(group(f"sumb{m}_", HeadSum.scratch(T)))
    scratch.update(group("halo", Halo.scratch(reach)))
    body = functools.partial(forward_body, nb, T, reach, local)
    return run(body, ins, outs, scratch, "forward", 1, smem=("starts", "dtb", "alog", "skip"), hbm=LATE_OUT)


LATE_IN = ["pre", "gw_out", "kvh", "normed", "ggate", "xin", "bc", "wa", "wb", "gh"]


def backward_body(nb, T, reach, easy, R):
    b, h = place()
    moves = Moves(R, LATE_IN, False)
    tok, rpb = T // NH, D // nb
    nz, per = nb // 2, nb // NH
    share = (XC + 128) // per
    core = lax.rem(h, 2)
    pair = (b, other(h, 1))
    total_sum = Sum(members(R, "sum", 4), b, h, nb)
    targets = [(per * h + i, b // per) for i in range(per)] if easy else []

    def away(device):
        return (device[0] != b) | (device[1] != h)

    barrier(
        head_edges(b, h) + line_edges(b, h, nb) + Scan.edges(b, h, nb, reach) + halo_edges(b, h, nb, reach)
        + [((h == NH - 1) & (b + 1 < nb), (b + 1, jnp.int32(i))) for i in range(NH)]
        + [(b >= 1, (b - 1, jnp.int32(NH - 1)))]
        + total_sum.edges()
        + [(away(t), t) for t in targets]
    )
    lines = [
        LineReduce(src, members(R, f"line{k}_", 10 if k else 7), b, h, nb)
        for k, src in enumerate((R.gw_in, R.v_gw_out, R.gwb, R.gwx, R.gwc))
    ]

    def send_ffn():
        lines[0].finish(R.res0)
        if easy:
            for i, to in enumerate((h // 2, 2 + h // 2)):
                R.fmsg[i] = R.res0[:, i * FG : (i + 1) * FG].astype(BF)
                slot = lax.rem(h, 2)

                @pl.when(to != h)
                def _():
                    copy_to(R.fmsg.at[i], R.fgot.at[slot], R.fs.at[i], R.fr.at[slot], (b, to)).start()

                @pl.when(to == h)
                def _():
                    R.fgot[slot] = R.fmsg[i]
        else:
            R.raw[:, 0 : 2 * FG] = R.res0[...].astype(BF)

    def send_out():
        lines[1].finish(R.res1)
        if easy:
            slot = lax.rem(b, per)
            for i, to in enumerate(targets):
                for j in range(2):
                    R.msg[i, j] = R.res1[:, j * FG + i * share : j * FG + (i + 1) * share].astype(BF)

                @pl.when(away(to))
                def _():
                    copy_to(R.msg.at[i], R.got.at[slot], R.ms.at[i], R.mr.at[slot], to).start()

                @pl.when(jnp.logical_not(away(to)))
                def _():
                    R.got[slot] = R.msg[i]
        else:
            R.raw[:, 2 * FG :] = R.res1[...].astype(BF)

    gather = HeadGather(
        lambda m, i: (R.w1b.at[i], R.w1c.at[i, :, 0:XC], R.w1c.at[i, :, XC:])[m], b, h, members(R, "gw", 2), 3
    )

    def send_gate():
        lines[2].finish(R.res2)
        R.w1b[h] = R.res2[...].astype(BF)
        gather.begin(0)

    moves.start("pre", "gw_out", "kvh", "normed", "ggate", "xin", "bc", "wa", "wb", "gh")
    lines[0].step_some(0)
    moves.wait("pre", "gw_out")
    lines[1].start_some(0)
    scans = [Scan(-1, b, h, nb, reach, members(R, f"scan{m}_", 5)) for m in range(2)]
    halo = Halo(-1, lambda d: R.gkvs.at[d], lambda d: R.gkvr.at[d], b, h, nb, reach, members(R, "halo", 2))
    pos = b * T + rows_of((T, 1))
    first = [doc_start(R.starts, m, pos) for m in range(2)]
    tail = [f[T - 1 :, :] for f in first]
    seen = lanes((T, T)) + b * T
    lane = lanes((T, 128))
    for m in range(2):
        for chunk in range((XC + 256) // 128):
            cols = pl.ds(chunk * 128, 128)
            value = R.v_pre[m, :, cols]
            act = value * sigmoid(value)
            if chunk < XC // 128:
                R.xs[m, :, cols] = act
            elif chunk == XC // 128:
                R.bs[m] = act.astype(BF)
            else:
                R.cs[m] = act.astype(BF)
    z, step, a_neg, cum = decays_of(R.dt, R.dtb, R.alog, h, T)
    R.cumt[...] = cum.T[:16]
    R.stept[...] = step.T[:16]
    cum_last = cum[T - 1 :, :]
    live = jnp.exp(cum) * by_batch(lambda m: jnp.broadcast_to((first[m] < b * T).astype(F32), (T, 128)))
    kept = jnp.exp(cum_last - cum) * by_batch(lambda m: jnp.broadcast_to((pos >= tail[m]).astype(F32), (T, 128)))
    omega = kept * step
    for m in range(2):
        u = (R.gy[m].astype(F32) * widen(live, 8 * m)).astype(BF)
        decay = jnp.where(tail[m] < b * T, jnp.exp(R.cumt[8 * m : 8 * m + 8, T - 1 : T]), 0.0)
        scans[m].set(tn(u, R.cs[m]), decay)
    lines[0].step_some(1)
    lines[1].start_some(1)
    lines[1].start_some(2)
    moves.wait("kvh")

    R.gkv[...] = jnp.zeros_like(R.gkv)
    for m in range(2):
        for i in range(2):
            mine = slice(i * HDIM, (i + 1) * HDIM)
            query, grad = R.q[m, :, mine], R.gattn[m, :, mine]
            delta = jnp.sum(grad.astype(F32) * R.attnf[m, :, mine], axis=1, keepdims=True)
            lse = R.lse[:, 2 * m + i : 2 * m + i + 1]

            def block(d, acc):
                at = seen - d * T
                keys = R.v_kvh[d, 0, :, m * HDIM : (m + 1) * HDIM]
                vals = R.v_kvh[d, 1, :, m * HDIM : (m + 1) * HDIM]
                probs = jnp.where((at <= pos) & (at >= first[m]), jnp.exp(nt(query, keys) * SCALE - lse), 0.0)
                ds = (probs * (nt(grad, vals) - delta)).astype(BF)
                R.gkv[d, 0, :, m * HDIM : (m + 1) * HDIM] += tn(ds, query) * SCALE
                R.gkv[d, 1, :, m * HDIM : (m + 1) * HDIM] += tn(probs.astype(BF), grad)
                return acc + nn(ds, keys)

            R.gq[m, :, mine] = lax.fori_loop(0, reach + 1, block, jnp.zeros((T, HDIM), F32)) * SCALE
            if m == 0 and i == 1:
                lines[1].start_some(3)
            elif m == 1 and i == 0:
                lines[0].step_some(2)
        if m == 0:
            for scan in scans:
                scan.join(0)
    for d in range(reach + 1):
        R.pair_k[d] = R.gkv[d, 1 - core].astype(BF)
    swap_k = lambda: copy_to(R.pair_k, R.pair_kr, R.ss.at[0], R.sr.at[0], pair)
    swap_k().start()

    moves.wait("normed", "ggate")
    for m in range(2):
        R.gproj[m, 0:LAG, WA:] = jnp.zeros((LAG, XC), BF)
        R.gproj[m, LAG:, WA:] = R.v_ggate[m]
        R.gproj[m, 0:LAG, XC + 128 :WA] = jnp.zeros((LAG, 256), BF)
        R.gproj[m, LAG:, XC + 128 : XC + 256] = rotate_pair(R.gq[m], R.cosine[...], -R.sine[...]).astype(BF)


    def weight_grad(ref, at, cols):
        grad = sum(tn(R.v_normed[m], R.gproj[m, :, cols]) for m in range(2)).astype(BF)
        ref[:, :, :, at : at + cols.stop - cols.start] = grad.reshape(nz, 2, rpb, cols.stop - cols.start)

    weight_grad(R.gwb, 0, slice(WA, WA + XC))
    weight_grad(R.gwb, XC, slice(XC + 128, XC + 256))
    swap_k().wait_recv()
    for d in range(reach + 1):
        value = R.gkv[d, core] + R.pair_kr[d].astype(F32)
        if d == 0:
            R.gkv[0, core] = value
        else:
            R.gkvs[d] = value.astype(BF)
    halo.begin()
    lines[1].step_some(0)

    row_sums = jnp.zeros((T, 128), F32)
    R.rowq[...] = jnp.zeros_like(R.rowq)
    skip = wide_row(R.skip, h)
    gskip = jnp.zeros((1, 128), F32)
    for m in range(2):
        both = nt(R.cs[m], R.bs[m])
        allowed = (seen <= pos) & (seen >= first[m])
        gboth = jnp.zeros((T, T), F32)
        for i in range(HG):
            l = 8 * m + i
            mine = slice(i * MHDIM, (i + 1) * MHDIM)
            grad = R.gy[m, :, mine]
            decay = jnp.exp(jnp.where(allowed, cum[:, l : l + 1] - R.cumt[l : l + 1, :], FAR))
            srow = R.stept[l : l + 1, :]
            ld = decay * nt(grad, R.xs[m, :, mine].astype(BF))
            gboth = gboth + ld * srow
            q = ld * both
            R.rowq[l : l + 1, :] = jnp.sum(q, axis=0, keepdims=True)
            row_sums = jnp.where(lane == l, jnp.sum(q * srow, axis=1, keepdims=True), row_sums)
            R.gx[m, :, mine] = tn((decay * both * srow).astype(BF), grad)
            if i == HG // 2:
                if m == 1:
                    lines[2].start_some(2)
                    lines[2].start_some(3)
        low = gboth.astype(BF)
        R.gcm[m] = nn(low, R.bs[m])
        R.gbm[m] = tn(low, R.cs[m])
        gyf = R.gy[m].astype(F32)
        gskip = gskip + exact(jnp.sum(gyf * R.xs[m], axis=0, keepdims=True), head_select(m))
        R.gx[m] = R.gx[m] + skip * gyf
        u = gyf * widen(live, 8 * m)
        carried = nt(R.cs[m], R.sin[m, 0:XC])
        row_sums = row_sums + exact(u * carried, head_select(m))
        R.gcm[m] += nn(u.astype(BF), R.sin[m, 0:XC])
        if m == 0:
            for scan in scans:
                scan.join(1)
            lines[1].step_some(1)
            lines[2].start_some(0)
            lines[2].start_some(1)
    for scan in scans:
        for i in range(2, len(scan.steps) - 1):
            scan.join(i)

    colq = jnp.concatenate([R.rowq[...], jnp.zeros((112, T), F32)], axis=0).T
    gstep = colq
    gcum = row_sums - step * colq
    glast = jnp.zeros((1, 128), F32)
    for m in range(2):
        adjoint = scans[m].last()[0:XC, :]
        read = nt(R.bs[m], adjoint)
        wide = widen(omega, 8 * m)
        R.gx[m] += wide * read
        R.gbm[m] += nn((R.xs[m] * wide).astype(BF), adjoint)
        gw = exact(R.xs[m] * read, head_select(m))
        gstep = gstep + kept * gw
        term = omega * gw
        gcum = gcum - term
        glast = glast + jnp.sum(term, axis=0, keepdims=True)
        through = jnp.where(tail[m] < b * T, jnp.exp(cum_last), 0.0)
        overlap = adjoint.astype(F32) * R.sin[m, 0:XC].astype(F32)
        per_head = jnp.sum(
            lax.dot_general(overlap, head_select(m), (((0,), (0,)), ((), ())), precision=high, preferred_element_type=F32),
            axis=0, keepdims=True,
        )
        glast = glast + through * per_head
    gcum = gcum + jnp.where(rows_of((T, 128)) == T - 1, glast, 0.0)
    gda = exact(triangle(T, upper=True), gcum)
    gstep = gstep + gda * a_neg
    gz = jnp.where(valid_row(), gstep * sigmoid(z), 0.0)
    lines[1].step_some(2)
    moves.wait("xin", "bc")

    conv_grad = [[], []]
    R.gcin[...] = jnp.zeros_like(R.gcin)
    R.gcw[...] = jnp.zeros_like(R.gcw)
    for m in range(2):
        R.cin[:, 0:XC] = R.v_xin[m].astype(F32)
        R.cin[:, XC:] = R.v_bc[m].astype(F32)
        for chunk in range((XC + 256) // 128):
            cols = pl.ds(chunk * 128, 128)
            taps, _ = group_taps(h, R.cw, None, chunk)
            pre = R.v_pre[m, :, cols]
            sg = sigmoid(pre)
            if chunk < XC // 128:
                up = R.gx[m, :, cols]
            elif chunk == XC // 128:
                up = R.gbm[m]
            else:
                up = R.gcm[m]
            gs = up * (sg * (1.0 + pre * (1.0 - sg)))
            R.gcw[4:5, cols] += jnp.sum(gs, axis=0, keepdims=True)
            for back in range(4):
                j = 3 - back
                near = jnp.where(pos - first[m] >= back, gs, 0.0)
                R.gcw[j : j + 1, cols] += jnp.sum(near * R.cin[pl.ds(LAG - back, T), cols], axis=0, keepdims=True)
                R.gcin[m, pl.ds(LAG - back, T), cols] += near * taps[j : j + 1]

    mine_bc = pl.ds(pl.multiple_of(XC + core * 128, 128), 128)
    pair_bc = pl.ds(pl.multiple_of(XC + (1 - core) * 128, 128), 128)
    for m in range(2):
        R.pair_b[m] = R.gcin[m, :, pair_bc].astype(BF)
    swap_b = lambda: copy_to(R.pair_b, R.pair_br, R.ss.at[1], R.sr.at[1], pair)
    swap_b().start()
    for m in range(2):
        R.gproj[m, :, 0:XC] = R.gcin[m, :, 0:XC].astype(BF)
    weight_grad(R.gwx, 0, slice(0, XC))
    for k in range(4):
        lines[3].start_some(k)
    send_ffn()
    lines[2].step_some(0)
    halo.finish_recv()
    packed = R.gkv[0, core]
    for d in range(1, reach + 1):
        packed = packed + jnp.where(b + d < nb, R.gkvr[d].astype(F32), 0.0)
    turned = rotate_pair(packed, R.cosine[...], -R.sine[...])
    packed = jnp.where(core == 0, turned, packed)
    swap_b().wait_recv()
    for m in range(2):
        R.gproj[m, :, XC : XC + 128] = (R.gcin[m, :, mine_bc] + R.pair_br[m].astype(F32)).astype(BF)
    for m in range(2):
        mine = packed if m == 0 else pltpu.roll(packed, HDIM, 1)
        gdt = pltpu.roll(gz, HDIM - 8 * m, 1)
        R.gproj[m, LAG:, XC + 256 : WA] = jnp.where(
            lane < HDIM, mine, jnp.where(lane < HDIM + HG, gdt, 0.0)
        ).astype(BF)
    weight_grad(R.gwc, 128, slice(XC + 256, WA))
    weight_grad(R.gwc, 0, slice(XC, XC + 128))
    for k in range(4):
        lines[4].start_some(k)
    lines[2].step_some(1)
    send_out()
    moves.wait("wa", "wb")

    scatter = HeadScatter(
        lambda m, head: R.gnp[m, pl.ds(pl.multiple_of(LAG + head * tok, LAG), tok), :], b, h, members(R, "sc", 6)
    )
    for m in range(2):
        R.gnp[m] = nt(R.gproj[m, :, 0:WA], R.v_wa[...]) + nt(R.gproj[m, :, WA:], R.v_wb[:, 0:XC])
        scatter.begin(m)
        R.edge_s[m] = R.gnp[m, 0:LAG, :].astype(BF)

    n1 = R.gains[6:7, :]
    small = jnp.concatenate(
        [
            jnp.sum(gz, axis=0, keepdims=True),
            jnp.sum(gda * step, axis=0, keepdims=True) * a_neg,
            gskip,
            jnp.zeros((5, 128), F32),
        ],
        axis=0,
    )
    small = jnp.where(lanes((8, 128)) < HG, small + pltpu.roll(small, 120, 1), 0.0)
    small = pltpu.roll(small, h * HG, 1)
    R.pay[...] = jnp.zeros_like(R.pay)
    wide_x = pl.ds(pl.multiple_of(h * XC, 128), XC)
    R.pay[0:5, wide_x] = R.gcw[0:5, 0:XC]
    R.pay[0:5, DI:] = R.gcw[0:5, XC:]
    R.pay[5:6, wide_x] = R.ggain[...]
    gn1 = sum(jnp.sum(R.gnp[m] * R.v_normed[m].astype(F32), axis=0, keepdims=True) for m in range(2))
    R.pay[6:7, 0:D] = gn1 / n1
    R.pay[7:8, 0:D] = R.gn2[...]
    for k in range(3):
        R.pay[6:7, D + 128 * k : D + 128 * (k + 1)] = small[k : k + 1]
    total_sum.begin(R.pay[...])

    def edge(i):
        return copy_to(R.edge_s, R.edge_r.at[i], R.es.at[0], R.er.at[i], (b - 1, jnp.int32(NH - 1)))

    @pl.when(b >= 1)
    def _():
        edge(h).start()

    for m in range(2):
        scatter.middle(m)
    moves.wait("gh")
    lines[2].step_some(2)
    lines[3].step_some(0)
    total_sum.step(0)
    lines[4].step_some(0)
    mine = (h == NH - 1) & (b + 1 < nb)

    @pl.when(mine)
    def _():
        for i in range(NH):
            edge(i).wait_recv()

    @pl.when(jnp.logical_not(mine))
    def _():
        R.edge_r[...] = jnp.zeros_like(R.edge_r)

    for m in range(2):
        scatter.finish(m)
        R.up[m] = scatter.result(m)
        R.up[m, tok - LAG : tok, :] += sum(R.edge_r[i, m].astype(F32) for i in range(NH))
        value = R.x[m].astype(F32)
        scale = lax.rsqrt(jnp.mean(value * value, axis=1, keepdims=True) + EPS)
        R.gin[m] = R.v_gh[m] + norm_back(value, scale, n1, R.up[m])[0]
    send_gate()
    lines[3].step_some(1)
    total_sum.step(1)
    lines[4].step_some(1)
    lines[3].step_some(2)
    total_sum.step(2)
    lines[4].step_some(2)
    gather.forward(0)
    lines[3].finish(R.res3)
    R.w1c[h, :, 0:XC] = R.res3[...].astype(BF)
    gather.begin(1)
    total_sum.step(3)
    lines[4].finish(R.res4)
    R.w1c[h, :, XC:] = R.res4[...].astype(BF)
    gather.begin(2)
    gather.forward(1)
    for k in range(4, len(total_sum.steps)):
        total_sum.step(k)
    gather.forward(2)
    R.small[...] = total_sum.result()
    if easy:
        for j in range(2):
            src = 2 * lax.rem(h, 2) + j

            @pl.when(src != h)
            def _():
                copy_to(R.fmsg.at[0], R.fgot.at[j], R.fs.at[0], R.fr.at[j], (b, src)).wait_recv()

        for j in range(per):

            @pl.when(away(targets[j]))
            def _():
                copy_to(R.msg.at[0], R.got.at[j], R.ms.at[0], R.mr.at[j], targets[j]).wait_recv()

        for i, to in enumerate((h // 2, 2 + h // 2)):

            @pl.when(to != h)
            def _():
                copy_to(R.fmsg.at[i], R.fgot.at[0], R.fs.at[i], R.fr.at[0], (b, to)).wait_send()

        for i in range(per):

            @pl.when(away(targets[i]))
            def _():
                copy_to(R.msg.at[i], R.got.at[0], R.ms.at[i], R.mr.at[0], targets[i]).wait_send()

    for m in range(3):
        gather.finish(m)
    for line in lines:
        line.done()

    @pl.when(b >= 1)
    def _():
        edge(h).wait_send()

    for c in (swap_k, swap_b):
        c().wait_send()
    gather.done()
    scatter.done()
    for scan in scans:
        scan.finish()
    halo.finish_send()


def backward(nb, reach, ins):
    tok = ins["x"].shape[1]
    T, rpb, nz, per = tok * NH, D // nb, nb // 2, nb // NH
    share = (XC + 128) // per
    easy = share % 128 == 0
    dma, V = pltpu.SemaphoreType.DMA, pltpu.VMEM
    outs = dict(
        gin=vm((2, tok, D), F32), w1b=vm((NH, rpb, XC + 128), BF), w1c=vm((NH, rpb, XC + 256), BF),
        small=vm((8, DI + 256), F32),
    )
    if easy:
        outs.update(fgot=vm((2, rpb, FG), BF), got=vm((per, 2, rpb, share), BF))
    else:
        outs.update(raw=vm((rpb, 4 * FG), BF))
    scratch = dict(
        xs=V((2, T, XC), F32), bs=V((2, T, 128), BF), cs=V((2, T, 128), BF), cumt=V((16, T), F32), stept=V((16, T), F32),
        gkv=V((reach + 1, 2, T, 128), F32), gkvs=V((reach + 1, T, 128), BF), gkvr=V((reach + 1, T, 128), BF),
        pair_k=V((reach + 1, T, 128), BF), pair_kr=V((reach + 1, T, 128), BF), gq=V((2, T, 128), F32),
        gproj=V((2, LAG + T, WA + XC), BF), gwb=V((nz, 2, rpb, XC + 128), BF), gwx=V((nz, 2, rpb, XC), BF), gwc=V((nz, 2, rpb, 256), BF),
        rowq=V((16, T), F32), gx=V((2, T, XC), F32), gbm=V((2, T, 128), F32), gcm=V((2, T, 128), F32),
        gcin=V((2, LAG + T, XC + 256), F32), gcw=V((8, XC + 256), F32), cin=V((LAG + T, XC + 256), F32),
        pair_b=V((2, LAG + T, 128), BF), pair_br=V((2, LAG + T, 128), BF), gnp=V((2, LAG + T, D), F32),
        edge_s=V((2, LAG, D), BF), edge_r=V((NH, 2, LAG, D), BF), up=V((2, tok, D), F32), pay=V((8, DI + 256), F32),
        res0=V((rpb, 2 * FG), F32), res1=V((rpb, 2 * FG), F32), res2=V((rpb, XC + 128), F32), res3=V((rpb, XC), F32), res4=V((rpb, 256), F32),
        ss=dma((2,)), sr=dma((2,)), es=dma((1,)), er=dma((NH,)), moved=dma((len(LATE_IN),)),
    )
    scratch.update({"v_" + n: V(ins[n].shape, ins[n].dtype) for n in LATE_IN})
    if easy:
        scratch.update(
            fmsg=V((2, rpb, FG), BF), msg=V((per, 2, rpb, share), BF), fs=dma((2,)), fr=dma((2,)), ms=dma((per,)), mr=dma((per,)),
        )
    for k, cols in enumerate((2 * FG, 2 * FG, XC + 128, XC, 256)):
        scratch.update(group(f"line{k}_", LineReduce.scratch(nb, cols, k > 0)))
    scratch.update(group("sum", Sum.scratch(nb, (8, DI + 256))))
    for m in range(2):
        scratch.update(group(f"scan{m}_", Scan.scratch(reach)))
    scratch.update(group("halo", Halo.scratch(reach)))
    scratch.update(group("sc", HeadScatter.scratch(tok)))
    scratch.update(group("gw", HeadGather.scratch(3)))
    body = functools.partial(backward_body, nb, T, reach, easy)
    return run(body, ins, outs, scratch, "backward", 2, smem=("starts", "dtb", "alog", "skip"), hbm=LATE_IN)


def finish_body(nb, R):
    h = lax.axis_index("head")
    rpb, per = D // nb, nb // NH
    R.out[...] = R.out_in[...]
    R.gin[...] = R.gin_in[...]
    kv = XC + 128
    for i in range(NH):
        first, second = R.w1b[i].astype(F32).T, R.w1c[i].astype(F32).T
        R.full[i * XC : (i + 1) * XC] = first[:XC]
        R.full[DI + i * XC : DI + (i + 1) * XC] = second[:XC]
        R.fatt[i * 128 : (i + 1) * 128] = first[XC:]
        at = 2 * DI + 128 * (i % 2)
        R.full[at : at + 128] = second[XC:kv] if i < 2 else R.full[at : at + 128] + second[XC:kv]
        at = QHEADS * HDIM + 128 * (i % 2) + HDIM * (i // 2)
        R.fatt[at : at + HDIM] = second[kv : kv + HDIM]
        at = 2 * DI + 256 + i * HG
        R.full[at : at + HG] = second[kv + HDIM : kv + HDIM + HG]
    for ref, out in ((R.full, R.mix_in), (R.fatt, R.att_in)):
        width = out.shape[0]
        out[...] = ref[pl.ds(h * width, width), :]
    R.cw[...] = R.small[0:4, :]
    R.cb[...] = R.small[4:5, :].reshape(DI + 256)
    R.gain[...] = R.small[5:6, 0:DI].reshape(DI)
    R.n1[...] = R.small[6:7, 0:D].reshape(D)
    R.n2[...] = R.small[7:8, 0:D].reshape(D)
    for k, ref in enumerate((R.dtb, R.alog, R.skip)):
        ref[...] = R.small[6:7, D + 128 * k : D + 128 * k + MHEADS].reshape(MHEADS)
    if hasattr(R, "got"):
        for j in range(2):
            R.ffn[:, j * FG : (j + 1) * FG] = R.fgot[j].astype(F32)
        for j in range(per):
            cols = slice(j * rpb, (j + 1) * rpb)
            both = R.got[j, 0].astype(F32).T
            R.mix_out[:, cols] = both[: XC // per]
            R.att_out[:, cols] = both[XC // per :]
            R.ffn_out[:, cols] = R.got[j, 1].astype(F32).T


def finish(nb, ins, mix_cols, att_cols):
    rpb, per = D // nb, nb // NH
    outs = dict(
        out=vm(ins["out_in"].shape, F32), gin=vm(ins["gin_in"].shape, F32), mix_in=vm((mix_cols, rpb), F32),
        att_in=vm((att_cols, rpb), F32), cw=vm((4, DI + 256), F32), cb=vm((DI + 256,), F32), gain=vm((DI,), F32),
        n1=vm((D,), F32), n2=vm((D,), F32), dtb=vm((MHEADS,), F32), alog=vm((MHEADS,), F32), skip=vm((MHEADS,), F32),
    )
    if "got" in ins:
        outs.update(
            ffn=vm((rpb, 2 * FG), F32), mix_out=vm((XC // per, per * rpb), F32), att_out=vm((128 // per, per * rpb), F32),
            ffn_out=vm((FG // per, per * rpb), F32),
        )
    V = pltpu.VMEM
    scratch = dict(full=V((NH * mix_cols, rpb), F32), fatt=V((NH * att_cols, rpb), F32))
    return run(functools.partial(finish_body, nb), ins, outs, scratch, "finish", None)


def pack_columns(mixer_in, attn_in, mixer_out, attn_out, ffn_in, ffn_out, norm_one, norm_two):
    shard = mixer_in.shape[0]
    mix_t, att_t, ffn_t = mixer_out.T, attn_out.T, ffn_out.T
    sets = ([], [], [])
    for i in range(NH):
        kv = QHEADS * HDIM + 128 * (i % 2) + HDIM * (i // 2)
        bc, dt = 2 * DI + 128 * (i % 2), 2 * DI + 2 * STATE + i * HG
        sets[0].append(
            [
                mixer_in[:, DI + i * XC : DI + (i + 1) * XC], mixer_in[:, bc : bc + 128],
                attn_in[:, i * 128 : (i + 1) * 128], attn_in[:, kv : kv + HDIM], mixer_in[:, dt : dt + HG],
                norm_one[:, None], norm_two[:, None], jnp.zeros((shard, 128 - HDIM - HG - 2), BF),
            ]
        )
        sets[1].append(
            [
                mixer_in[:, i * XC : (i + 1) * XC], mix_t[:, i * XC : (i + 1) * XC], att_t[:, i * 128 : (i + 1) * 128],
            ]
        )
        sets[2].append(
            [
                ffn_t[:, i * FG : (i + 1) * FG], ffn_in[:, i * FG : (i + 1) * FG],
                ffn_in[:, FF + i * FG : FF + (i + 1) * FG],
            ]
        )
    out = []
    for parts in sets:
        v = jnp.stack([jnp.concatenate(p, axis=1) for p in parts])
        out.append(lax.all_to_all(v, "head", split_axis=0, concat_axis=0, tiled=True).reshape(shard * NH, v.shape[2]))
    return out


def on_device(
    inputs, cotangent, doc_starts, norm_one, mixer_in, conv_weight, conv_bias, dt_bias, a_log, d_skip, ssm_gain,
    mixer_out, attn_in, attn_out, norm_two, ffn_in, ffn_out,
):
    nb = lax.axis_size("blk")
    T = inputs.shape[1] * NH
    longest = min(MAXLEN, T * nb // 2)
    reach = (longest + T - 2) // T
    shard = mixer_in.shape[0]
    rpb, nz = shard * NH, nb // 2
    local = shard % 16 == 0

    lane = np.arange(128) % HDIM % (HDIM // 2)
    freq = jnp.asarray((10000.0 ** (-(lane.astype(np.float32) * 2.0 / HDIM))).astype(np.float32))[None, :]
    small = dict(
        starts=doc_starts, cw=conv_weight, dtb=dt_bias, alog=a_log, skip=d_skip
    )
    if local:
        weights = dict(
            mixer_in=mixer_in, attn_in=attn_in, mixer_out=mixer_out.T, attn_out=attn_out.T, ffn_in=ffn_in,
            ffn_out=ffn_out.T, n1=norm_one[None, :], n2=norm_two[None, :],
        )
    else:
        weights = dict(
            zip(("pa", "pb", "pc"), pack_columns(mixer_in, attn_in, mixer_out, attn_out, ffn_in, ffn_out, norm_one, norm_two))
        )
    f = forward(nb, reach, dict(x=inputs, cot=cotangent, freq=freq, cb=conv_bias, gain=ssm_gain, **small, **weights), local)
    shape = (nz, 2, rpb, 2 * FG)
    kept = (
        "gy", "gattn", "q", "kvh", "attnf", "lse", "pre", "xin", "bc", "dt", "sin", "ggate", "cosine", "sine", "normed", "wa",
        "wb", "gh", "gains", "gn2", "ggain",
    )
    b = backward(
        nb, reach,
        dict(
            x=inputs, gw_in=f.gw_in, gw_out=f.gw_out.reshape(shape), **small,
            **{n: getattr(f, n) for n in kept},
        ),
    )
    ins = dict(out_in=f.out, gin_in=b.gin, w1b=b.w1b, w1c=b.w1c, small=b.small)
    easy = hasattr(b, "got")
    if easy:
        ins.update(fgot=b.fgot, got=b.got)
    r = finish(nb, ins, mixer_in.shape[1] // NH, attn_in.shape[1] // NH)
    if easy:
        g_ffn_in, g_mix_out, g_att_out, g_ffn_out = r.ffn, r.mix_out, r.att_out, r.ffn_out
    else:
        per = nb // NH
        head, blk = lax.axis_index("head"), lax.axis_index("blk")
        mine = lax.all_gather(b.raw[:, : 2 * FG], "head").reshape(NH, rpb, 2, FG)
        ffn = jnp.transpose(mine, (1, 2, 0, 3)).reshape(rpb, 2 * FF)
        g_ffn_in = lax.dynamic_slice_in_dim(ffn, head * (2 * FF // NH), 2 * FF // NH, 1).astype(F32)
        outs = lax.all_gather(b.raw[:, 2 * FG :], ("blk", "head")).reshape(nb, NH, rpb, 2 * FG)
        outs = jnp.transpose(outs, (1, 3, 0, 2)).reshape(NH, 2, per, FG // per, D)
        outs = lax.dynamic_slice_in_dim(outs, head * (D // NH), D // NH, 4)
        outs = jnp.transpose(outs, (0, 2, 1, 3, 4)).reshape(nb, 2, FG // per, D // NH)
        outs = lax.dynamic_index_in_dim(outs, blk, 0, False).astype(F32)
        g_mix_out, g_att_out, g_ffn_out = outs[0, : XC // per], outs[0, XC // per :], outs[1]
    return (
        r.out, r.gin, r.n1, r.mix_in.T, r.cw, r.cb, r.dtb, r.alog, r.skip, r.gain, g_mix_out, r.att_in.T, g_att_out, r.n2,
        g_ffn_in, g_ffn_out,
    )


def solution(mesh):
    both = ("blk", "head")
    tokens, rows, cols = P(None, both, None), P(both, None), P(None, both)
    split = P("blk", "head")
    return jax.shard_map(
        on_device,
        mesh=mesh,
        in_specs=(
            tokens, tokens, P(), P(both), rows, P(), P(), P(), P(), P(), P(), cols, rows, cols, P(both), rows, cols,
        ),
        out_specs=(
            tokens, tokens, P(), split, P(), P(), P(), P(), P(), P(), split, split, split, P(), split, split,
        ),
        check_vma=False,
    )
```
